32 devices in a mesh: fsdp: 8 (over z, x), ns: 4 (over y, core).
Axes of the slice: x: 2, y: 2, z: 4, core: 2. Of those that a mesh axis runs over, the one named last changes fastest.
Arguments:
- images: bfloat16 [2, 32, 3, 160, 160], P(None, ('fsdp', 'ns')), may hold values from -6 to 6
- group_ids: int32 [32], P(('fsdp', 'ns')), may hold values from 0 to 2
- labels: int32 [2, 32], P(None, ('fsdp', 'ns')), may hold values from 0 to 999
- partners: int32 [2, 32], P(None, ('fsdp', 'ns')), may hold values from 0 to 1
- mix_weights: float32 [2, 32], P(None, ('fsdp', 'ns')), may hold values from 0.3 to 1
- valid: int32 [2, 32], P(None, ('fsdp', 'ns')), may hold values 0 or 1
- flat_params: float32 [2449408], P(('fsdp', 'ns'))
- flat_first: float32 [2449408], P(('fsdp', 'ns'))
- flat_second: float32 [2449408], P(('fsdp', 'ns')), as said below
- mlp_weights: float32 [2, 512, 2048], P(None, None, ('fsdp', 'ns')), may hold values from -0.25 to 0.25
- mlp_momentum: float32 [2, 512, 2048], P(None, None, ('fsdp', 'ns'))
Outputs:
- loss_sum: float32 [], replicated
- flat_params_new: float32 [2449408], P(('fsdp', 'ns'))
- flat_first_new: float32 [2449408], P(('fsdp', 'ns'))
- flat_second_new: float32 [2449408], P(('fsdp', 'ns'))
- mlp_weights_new: float32 [2, 512, 2048], P(None, None, ('fsdp', 'ns'))
- mlp_momentum_new: float32 [2, 512, 2048], P(None, None, ('fsdp', 'ns'))
The draws below stay inside these ranges and needn't reach their ends.
Inputs may be any that keep to these rules, and one draw needn't show every extreme that they name: `flat_second`: second moments are positive.
All inputs are finite; a program needn't handle non-finite values. No bound on the sum of `valid` on one device may be relied on, other than what follows from the above.
Results may differ from the reference program's by a relative error of at most 0.003.
The reference program's roundings to bfloat16 on the way count: a program that leaves them out, or rounds other values in their place, can miss the bound.
Values may be sent and summed in bfloat16 or wider, within the bound.
No kernel may reach another device: no remote copies, remote signals or barrier semaphores. Data moves between devices by JAX's collectives and lax.ppermute only.
A program may use at most 704 MiB of HBM per device.

```python
import math
import jax
import jax.numpy as jnp
from jax import lax

C1 = 64
C2 = 128
C3 = 320
C4 = 512
HID = 2048
CLS = 1000
IN_CH = 3
RES_S = 96
RES_M = 128
RES_L = 160
MICRO = 2
NS_ITERS = 5
STEP = 10
IMGS = 32
FLAT = 2447016
FLAT_PAD = 2449408


def flat_layout():
    return [('weight', C1 * IN_CH * 49, IN_CH * 49), ('bias', C1, 1), ('weight', C2 * C1 * 9, C1 * 9), ('bias', C2, 1), ('weight', C3 * C2 * 9, C2 * 9), ('bias', C3, 1), ('weight', C4 * C3 * 9, C3 * 9), ('bias', C4, 1), ('gain', C4, 1), ('bias', C4, 1), ('scale', C4, 1), ('gain', C4, 1), ('bias', C4, 1), ('scale', C4, 1), ('bias', HID, 1), ('bias', C4, 1), ('gain', C4, 1), ('bias', C4, 1), ('head', C4 * CLS, C4), ('bias', CLS, 1)]


def signed_noise(sub_key, amount):
    return jax.random.normal(sub_key, (amount,), jnp.float32)


def draw_flat_params(key, part):
    segments = []
    for position, (segment_kind, amount, fan_width) in enumerate(flat_layout()):
        sub_key = jax.random.fold_in(key, position)
        if segment_kind == 'weight':
            segments.append(signed_noise(sub_key, amount) * fan_width ** (-0.5))
        elif segment_kind == 'head':
            segments.append(signed_noise(sub_key, amount) * 4.0 * fan_width ** (-0.5))
        elif segment_kind == 'bias':
            segments.append(signed_noise(sub_key, amount) * 0.3)
        else:
            segments.append(jax.random.uniform(sub_key, (amount,), jnp.float32, 0.5, 1.5))
    segments.append(jnp.zeros((FLAT_PAD - FLAT,), jnp.float32))
    return jnp.concatenate(segments)


def draw_flat_first(key, part):
    scale = 0.05 / (IMGS * MICRO) ** 0.5
    return signed_noise(jax.random.fold_in(key, 11), FLAT_PAD) * 0.111 * scale


def draw_flat_second(key, part):
    scale = 0.05 / (IMGS * MICRO) ** 0.5
    factor = jax.random.uniform(jax.random.fold_in(key, 12), (FLAT_PAD,), jnp.float32, 1.0, 4.0)
    return factor * 0.001001 * scale * scale


def draw_mlp_momentum(key, part):
    scale = 0.02 / (IMGS * MICRO) ** 0.5
    noise = jax.random.normal(jax.random.fold_in(key, 13), (2, C4, HID), jnp.float32)
    return noise * scale


def plant(values, rng, least, top_value):
    longest = values.shape.index(max(values.shape))
    spots = []
    for shift in (0, 1):
        where = [jax.random.randint(jax.random.fold_in(rng, axis), (), 0, length) for axis, length in enumerate(values.shape)]
        where[longest] = (where[longest] + shift) % values.shape[longest]
        spots.append(tuple(where))
    return values.at[spots[0]].set(least).at[spots[1]].set(top_value)


def level_of(own_key, extent, split, smallest, top_value):
    loudness = 1.0
    for dim, blocks in split:
        steps = jax.random.uniform(jax.random.fold_in(jax.random.fold_in(own_key, 6), dim), (blocks,), jnp.float32, smallest / len(split), top_value / len(split))
        loudness = loudness * jnp.repeat(jnp.exp(steps), extent[dim] // blocks).reshape((-1,) + (1,) * (len(extent) - 1 - dim))
    return loudness


def gaussian(stream_key, extent, deviation, limit, cuts=(), kind=jnp.bfloat16):
    level = level_of(stream_key, extent, cuts, -0.22, 0.18) if cuts else 1.0
    values = jax.random.normal(stream_key, extent, jnp.float32) * deviation * level
    return jnp.minimum(jnp.maximum(values, -limit), limit).astype(kind)


def setup_inputs(seed: int = 0) -> dict:
    streams_of = jax.random.split(jax.random.key(seed), 12)
    return {
        "images": gaussian(streams_of[0], (MICRO, IMGS, IN_CH, RES_L, RES_L), 1.0, 6.0, ((1, 32),)),
        "group_ids": plant(jax.random.randint(streams_of[1], (IMGS,), 0, 3), jax.random.fold_in(streams_of[1], 1), 0, 2).astype(jnp.int32),
        "labels": plant(jax.random.randint(streams_of[2], (MICRO, IMGS), 0, CLS), jax.random.fold_in(streams_of[2], 1), 0, CLS - 1).astype(jnp.int32),
        "partners": plant(jax.random.randint(streams_of[3], (MICRO, IMGS), 0, MICRO), jax.random.fold_in(streams_of[3], 1), 0, MICRO - 1).astype(jnp.int32),
        "mix_weights": jnp.clip(0.3 + 0.7 * jax.random.uniform(streams_of[4], (MICRO, IMGS), jnp.float32) ** level_of(streams_of[4], (MICRO, IMGS), ((1, 32),), -0.2, 0.2), 0.3, 1.0),
        "valid": plant((jax.random.randint(streams_of[5], (MICRO, IMGS), 0, 4) < 3).astype(jnp.int32), jax.random.fold_in(streams_of[5], 1), 0, 1),
        "flat_params": draw_flat_params(jax.random.fold_in(streams_of[11], 71), 0),
        "flat_first": draw_flat_first(jax.random.fold_in(streams_of[11], 71), 0),
        "flat_second": draw_flat_second(jax.random.fold_in(streams_of[11], 71), 0),
        "mlp_weights": gaussian(streams_of[9], (2, C4, HID), C4 ** -0.5, 0.25, ((2, 32),), jnp.float32),
        "mlp_momentum": draw_mlp_momentum(jax.random.fold_in(streams_of[11], 71), 0),
    }


highest = lax.Precision.HIGHEST
norm_epsilon = 1e-05

@jax.custom_vjp
def low(v):
    return lax.optimization_barrier(v.astype(jnp.bfloat16)).astype(jnp.float32)

@jax.custom_vjp
def low_back(v):
    return v

def low_keep(v):
    return (low(v), None)

def low_pass(kept, grad):
    return (grad,)

def back_keep(v):
    return (v, None)

def back_low(kept, grad):
    return (low(grad),)
low.defvjp(low_keep, low_pass)
low_back.defvjp(back_keep, back_low)

def unpack(flat_vec):
    layouts = [(C1, IN_CH * 49), (C1,), (C2, C1 * 9), (C2,), (C3, C2 * 9), (C3,), (C4, C3 * 9), (C4,), (6, C4), (HID,), (C4,), (2, C4), (C4, CLS), (CLS,)]
    pieces = []
    offset = 0
    for layout in layouts:
        amount = math.prod(layout)
        pieces.append(flat_vec[offset:offset + amount].reshape(layout))
        offset = offset + amount
    return pieces

def convolve(inputs, kernel, bias, size, stride, padding):
    channels, height, width = inputs.shape
    out_height = (height + 2 * padding - size) // stride + 1
    out_width = (width + 2 * padding - size) // stride + 1
    padded = jnp.pad(inputs, ((0, 0), (padding, padding), (padding, padding)))
    columns = []
    for row_shift in range(size):
        for col_shift in range(size):
            columns.append(lax.slice(padded, (0, row_shift, col_shift), (channels, row_shift + stride * (out_height - 1) + 1, col_shift + stride * (out_width - 1) + 1), (1, stride, stride)))
    stacked = jnp.stack(columns, axis=1).reshape(channels * size * size, out_height * out_width)
    result = jnp.dot(kernel, stacked, precision=highest) + bias[:, None]
    return result.reshape(kernel.shape[0], out_height, out_width)

def group_norm(values, gain, shift):
    center = values - jnp.mean(values)
    variance = jnp.mean(center * center)
    return center * lax.rsqrt(variance + norm_epsilon) * gain[:, None, None] + shift[:, None, None]

def pool_mixer(values):
    channels, height, width = values.shape
    padded = jnp.pad(values, ((0, 0), (1, 1), (1, 1)))
    ones_pad = jnp.pad(jnp.ones((height, width), jnp.float32), 1)
    total = jnp.zeros_like(values)
    counted = jnp.zeros((height, width), jnp.float32)
    for row_shift in range(3):
        for col_shift in range(3):
            total = total + padded[:, row_shift:row_shift + height, col_shift:col_shift + width]
            counted = counted + ones_pad[row_shift:row_shift + height, col_shift:col_shift + width]
    return total / counted - values

def image_loss(pieces, matrices, pixels, target, rounder):
    stem_kernel, stem_bias, first_kernel, first_bias, second_kernel, second_bias, third_kernel, third_bias, block_vec, ffn_bias_one, ffn_bias_two, final_vec, head_kernel, head_bias = pieces
    section = convolve(rounder(pixels), stem_kernel, stem_bias, 7, 4, 2)
    section = convolve(rounder(section), first_kernel, first_bias, 3, 2, 1)
    section = convolve(rounder(section), second_kernel, second_bias, 3, 2, 1)
    stream = convolve(rounder(section), third_kernel, third_bias, 3, 2, 1)
    stream = stream + block_vec[2][:, None, None] * pool_mixer(group_norm(stream, block_vec[0], block_vec[1]))
    channels, height, width = stream.shape
    normed = rounder(group_norm(stream, block_vec[3], block_vec[4]).reshape(channels, height * width))
    hidden = jnp.dot(matrices[0].T, normed, precision=highest) + ffn_bias_one[:, None]
    active = rounder(jax.nn.gelu(hidden, approximate=False))
    branch = jnp.dot(matrices[1], active, precision=highest) + ffn_bias_two[:, None]
    stream = stream + block_vec[5][:, None, None] * branch.reshape(channels, height, width)
    pooled = rounder(lax.optimization_barrier(jnp.mean(group_norm(stream, final_vec[0], final_vec[1]), axis=(1, 2))))
    logits = jnp.dot(pooled, head_kernel, precision=highest) + head_bias
    return -jnp.sum(target * jax.nn.log_softmax(logits))

def device_loss(pieces, matrices, pictures, group, label_col, partner_col, mix_col, valid_col, rounder):

    def branch_for(resolution):

        def compute(operands):
            pieces_in, matrices_in = operands
            total = jnp.zeros((), jnp.float32)
            for micro_index in range(MICRO):
                partner = partner_col[micro_index]
                mixing = mix_col[micro_index]
                own = pictures[micro_index, :, :resolution, :resolution].astype(jnp.float32)
                other = jnp.take(pictures, partner, axis=0)[:, :resolution, :resolution].astype(jnp.float32)
                pixels = mixing * own + (1.0 - mixing) * other
                target = mixing * jax.nn.one_hot(label_col[micro_index], CLS, dtype=jnp.float32) + (1.0 - mixing) * jax.nn.one_hot(jnp.take(label_col, partner), CLS, dtype=jnp.float32)
                total = total + valid_col[micro_index].astype(jnp.float32) * image_loss(pieces_in, matrices_in, pixels, target, rounder)
            return total
        return compute
    return lax.switch(group, [branch_for(RES_S), branch_for(RES_M), branch_for(RES_L)], (pieces, matrices))

def newton_schulz(ortho):
    for iteration in range(NS_ITERS):
        gram = jnp.einsum('bik,bjk->bij', ortho, ortho, precision=highest)
        poly = -4.775 * gram + 2.0315 * jnp.einsum('bij,bjk->bik', gram, gram, precision=highest)
        ortho = 3.4445 * ortho + jnp.einsum('bij,bjk->bik', poly, ortho, precision=highest)
    return ortho

def reference(images, group_ids, labels, partners, mix_weights, valid, flat_params, flat_first, flat_second, mlp_weights, mlp_momentum):
    valid_total = jnp.maximum(jnp.sum(valid).astype(jnp.float32), 1.0)
    columns = (jnp.swapaxes(images, 0, 1), group_ids, labels.T, partners.T, mix_weights.T, valid.T)

    def objective(flat_vec, matrices):
        pieces = unpack(low(flat_vec))
        rounded_mats = low(matrices)

        def per_device(carry, inputs):
            return (carry + device_loss(pieces, rounded_mats, *inputs, low), None)
        total, unused = lax.scan(jax.checkpoint(per_device), jnp.zeros((), jnp.float32), columns)
        return (total / valid_total, total)
    unused_obj, pullback, loss_total = jax.vjp(objective, flat_params, mlp_weights, has_aux=True)
    grad_flat, grad_mlp = pullback(jnp.ones((), jnp.float32))
    first_new = 0.9 * flat_first + 0.1 * grad_flat
    second_new = 0.999 * flat_second + 0.001 * grad_flat * grad_flat
    first_hat = first_new / (1.0 - 0.9 ** STEP)
    second_hat = second_new / (1.0 - 0.999 ** STEP)
    params_new = flat_params - 0.02 * (first_hat / (jnp.sqrt(second_hat) + 1e-08) + 0.05 * flat_params)
    momentum_new = 0.95 * mlp_momentum + grad_mlp
    ortho = grad_mlp + 0.95 * momentum_new
    norms = jnp.sqrt(lax.optimization_barrier(jnp.sum(ortho * ortho, axis=(1, 2))))
    ortho = newton_schulz(ortho / (norms + 1e-07)[:, None, None])
    weights_new = mlp_weights * (1.0 - 0.1 * 0.05) - 0.1 * 0.2 * math.sqrt(HID) * ortho
    return (loss_total, params_new, first_new, second_new, weights_new, momentum_new)
```

```python
import functools
import math

import jax
import jax.numpy as jnp
import numpy as np
from jax import lax
from jax.experimental import pallas as pl
from jax.experimental.pallas import tpu as pltpu
from jax.sharding import PartitionSpec as P

C1 = 64
C2 = 128
C3 = 320
C4 = 512
HID = 2048
CLS = 1000
IN_CH = 3
RES_S = 96
RES_L = 160
RES_STEP = 32
MICRO = 2
NS_ITERS = 5
STEP = 10
FLAT = 2447016

AXES = ("fsdp", "ns")
LANES = 128
SIDE = 5
ROWS = 32
BOTH = MICRO * ROWS
C3P = 384
CLSP = 1024
K3P = 2944
TAPS = 9

f32 = jnp.float32
bf16 = jnp.bfloat16
highest = lax.Precision.HIGHEST
norm_epsilon = 1e-05

SIZES = [
    ("stem", C1 * IN_CH * 49),
    ("b0", C1),
    ("k1", C2 * C1 * 9),
    ("b1", C2),
    ("k2", C3 * C2 * 9),
    ("b2", C3),
    ("k3", C4 * C3 * 9),
    ("b3", C4),
    ("block", 6 * C4),
    ("fb1", HID),
    ("fb2", C4),
    ("final", 2 * C4),
    ("head", C4 * CLS),
    ("hb", CLS),
]


def dot_nn(a, b):
    return lax.dot_general(a, b, (((1,), (0,)), ((), ())), preferred_element_type=f32)


def dot_nt(a, b):
    return lax.dot_general(a, b, (((1,), (1,)), ((), ())), preferred_element_type=f32)


def dot_tn(a, b):
    return lax.dot_general(a, b, (((0,), (0,)), ((), ())), preferred_element_type=f32)


def split2(x):
    hi = x.astype(bf16)
    return hi, (x - hi.astype(f32)).astype(bf16)


def split3(x):
    hi = x.astype(bf16)
    rest = x - hi.astype(f32)
    mid = rest.astype(bf16)
    return hi, mid, (rest - mid.astype(f32)).astype(bf16)


def two(dot, pair, other):
    return dot(pair[0], other) + dot(pair[1], other)


def borrow(bits):
    out = list(bits)
    for at, bit in enumerate(out):
        if bit:
            out[at] = 0
            return tuple(out), 0
        out[at] = 1
    return tuple(out), 1


def tap_source(tap, row_bits, col_bits):
    r, c = divmod(tap, 3)
    src_r, down_r = (row_bits, 0) if r else borrow(row_bits)
    src_c, down_c = (col_bits, 0) if c else borrow(col_bits)
    return (int(r != 1), int(c != 1)), src_r, src_c, down_r, down_c


def plane_of(row_bits, col_bits):
    at = 0
    for r, c in zip(row_bits, col_bits):
        at = at * 4 + r * 2 + c
    return at


def all_bits(pairs):
    for at in range(4**pairs):
        digits = [(at >> (2 * (pairs - 1 - k))) & 3 for k in range(pairs)]
        yield at, tuple(d >> 1 for d in digits), tuple(d & 1 for d in digits)


def moved(value, down_r, down_c, marks):
    if not (down_r or down_c):
        return value
    step = SIDE * down_r + down_c
    column = {(1, 0): 1, (0, 1): 2, (1, 1): 3}[(down_r, down_c)]
    return pltpu.roll(value, step, 0) * marks[:, column : column + 1]


def moved_back(value, down_r, down_c, marks):
    if not (down_r or down_c):
        return value
    step = SIDE * down_r + down_c
    column = {(1, 0): 1, (0, 1): 2, (1, 1): 3}[(down_r, down_c)]
    return pltpu.roll(value * marks[:, column : column + 1], BOTH - step, 0)


def erf(x):
    x = jnp.clip(x, -3.832506856900711, 3.832506856900711)
    s = x * x
    top = 2.2905065861350646e-4
    for coef in (3.4082910107109506e-3, 5.0955695062380861e-2, 1.8520832239976145e-1, 1.128379143519084):
        top = top * s + coef
    low = -1.1791602954361697e-7
    for coef in (
        2.3547966471313185e-5,
        1.0179625278914885e-3,
        1.4070470171167667e-2,
        1.1098505178285362e-1,
        4.9746925110067538e-1,
        1.0,
    ):
        low = low * s + coef
    return x * top / low


def total(x):
    return jnp.sum(jnp.sum(x, axis=1, keepdims=True), axis=0, keepdims=True)


def norm_images(value, mask, count):
    parts, scales = [], []
    for m in range(MICRO):
        v = value[m * ROWS : (m + 1) * ROWS]
        k = mask[m * ROWS : (m + 1) * ROWS]
        center = (v - total(v * k) / count) * k
        scale = lax.rsqrt(total(center * center) / count + norm_epsilon)
        parts.append(center * scale)
        scales.append(scale)
    return jnp.concatenate(parts, axis=0), scales


def norm_images_back(grad, hat, scales, gain, mask, count):
    parts = []
    for m in range(MICRO):
        at = slice(m * ROWS, (m + 1) * ROWS)
        g = grad[at] * gain
        h = hat[at]
        parts.append((g - total(g) / count - h * (total(g * h) / count)) * scales[m] * mask[at])
    return jnp.concatenate(parts, axis=0)


def rowsum(x):
    return jnp.sum(x, axis=0, keepdims=True)


def forward_kernel(
    whole_ref,
    real_ref,
    p0_ref,
    w0_ref,
    k1_ref,
    k2_ref,
    k3_ref,
    w1_ref,
    w2_ref,
    tm_ref,
    t64_ref,
    marks_ref,
    near_ref,
    b0_ref,
    b1_ref,
    b2_ref,
    b3_ref,
    block_ref,
    fb1_ref,
    fb2_ref,
    final_ref,
    head_ref,
    hb_ref,
    p1_ref,
    p2_ref,
    p3_ref,
    k1t_ref,
    dstream_ref,
    dmlp_ref,
    dhead_ref,
    dblock_ref,
    dfb1_ref,
    dfb2_ref,
    dfinal_ref,
    dhb_ref,
    db3_ref,
    loss_ref,
    s1_ref,
    s2_ref,
    s3_ref,
    t2_ref,
    t3_ref,
    hid_ref,
):
    marks = marks_ref[...]
    lane = lax.broadcasted_iota(jnp.int32, (BOTH, LANES), 1)
    quarter = 16 * BOTH
    for at in range(4):
        rows = pl.ds(at * quarter, quarter)
        s1_ref[rows, :] = (dot_nt(p0_ref[rows, :], w0_ref[...]) + b0_ref[...]).astype(bf16).astype(f32)

    def tap_value(ref, pairs, tap, row_bits, col_bits, cols):
        q, src_r, src_c, down_r, down_c = tap_source(tap, row_bits, col_bits)
        at = (q[0] * 2 + q[1]) * 4**pairs + plane_of(src_r, src_c)
        return moved(ref[pl.ds(at * BOTH, BOTH), cols], down_r, down_c, marks)

    k1t_ref[...] = dot_nn(k1_ref[...], t64_ref[...]).astype(bf16)
    everything = slice(None)
    for at, rb, cb in all_bits(2):
        for pair in range(5):
            left = tap_value(s1_ref, 2, 2 * pair, rb, cb, everything)
            if pair < 4:
                right = tap_value(s1_ref, 2, 2 * pair + 1, rb, cb, everything)
            else:
                right = jnp.zeros_like(left)
            p1_ref[pl.ds(at * BOTH, BOTH), pl.ds(pair * LANES, LANES)] = jnp.where(
                lane < C1, left, right
            ).astype(bf16)
    s2_ref[...] = (dot_nt(p1_ref[...], k1t_ref[...]) + b1_ref[...]).astype(bf16).astype(f32)
    for at, rb, cb in all_bits(1):
        for tap in range(TAPS):
            t2_ref[pl.ds(at * BOTH, BOTH), pl.ds(tap * LANES, LANES)] = tap_value(
                s2_ref, 1, tap, rb, cb, everything
            ).astype(bf16)
    p2_ref[...] = dot_nn(t2_ref[...], tm_ref[...]).astype(bf16)
    s3_ref[...] = (dot_nt(p2_ref[...], k2_ref[...]) + b2_ref[...]).astype(bf16).astype(f32)
    for part in range(3):
        for tap in range(TAPS):
            t3_ref[pl.ds(part * BOTH, BOTH), pl.ds(tap * LANES, LANES)] = tap_value(
                s3_ref, 0, tap, (), (), pl.ds(part * LANES, LANES)
            ).astype(bf16)
    spread = dot_nn(t3_ref[...], tm_ref[...]).astype(bf16)
    for part in range(3):
        p3_ref[:, pl.ds(part * TAPS * LANES, TAPS * LANES)] = spread[part * BOTH : (part + 1) * BOTH]
    stream = dot_nt(p3_ref[:, pl.ds(0, K3P)], k3_ref[...]) + b3_ref[...]

    mask = marks[:, 0:1]
    per_count = marks[:, 4:5]
    cells = real_ref[4]
    count = real_ref[5]
    near = near_ref[...]
    gain1, shift1, scale1 = block_ref[0:1, :], block_ref[1:2, :], block_ref[2:3, :]
    gain2, shift2, scale2 = block_ref[3:4, :], block_ref[4:5, :], block_ref[5:6, :]
    hat1, rs1 = norm_images(stream, mask, count)
    u = (hat1 * gain1 + shift1) * mask
    u3 = split3(u)
    around = dot_nn(near, u3[0]) + (dot_nn(near, u3[1]) + dot_nn(near, u3[2]))
    pool = around * per_count - u
    stream1 = stream + scale1 * pool
    hat2, rs2 = norm_images(stream1, mask, count)
    normed = ((hat2 * gain2 + shift2) * mask).astype(bf16)
    hid_ref[...] = dot_nt(normed, w1_ref[...]) + fb1_ref[...]
    hidden = hid_ref[...]
    half = 0.5 * (1.0 + erf(hidden * math.sqrt(0.5)))
    active = (hidden * half).astype(bf16)
    branch = dot_nn(active, w2_ref[...]) + fb2_ref[...]
    stream2 = stream1 + scale2 * branch
    hat3, rs3 = norm_images(stream2, mask, count)
    outs = (hat3 * final_ref[0:1, :] + final_ref[1:2, :]) * mask
    row8 = lax.broadcasted_iota(jnp.int32, (8, 1), 0)
    first, second = row8 == 0, row8 == 1

    def by_row(a, b):
        return jnp.where(first, a, jnp.where(second, b, 0.0))

    pooled = (by_row(rowsum(outs[:ROWS]), rowsum(outs[ROWS:])) / cells).astype(bf16)
    logits = dot_nn(pooled, head_ref[...]) + hb_ref[...]
    column = lax.broadcasted_iota(jnp.int32, (8, CLSP), 1)
    logits = jnp.where(column < CLS, logits, -1e30)
    top = jnp.max(logits, axis=1, keepdims=True)
    powers = jnp.exp(logits - top)
    mass = jnp.sum(powers, axis=1, keepdims=True)
    own = jnp.where(first, whole_ref[0], whole_ref[1])
    other = jnp.where(first, whole_ref[2], whole_ref[3])
    mix = by_row(real_ref[0], real_ref[1])
    target = jnp.where(column == own, mix, 0.0) + jnp.where(column == other, 1.0 - mix, 0.0)
    valid = by_row(real_ref[2], real_ref[3])
    logp = logits - top - jnp.log(mass)
    losses = -jnp.sum(target * logp, axis=1, keepdims=True) * valid
    loss_ref[...] = jnp.broadcast_to(jnp.sum(losses, axis=0, keepdims=True), (8, LANES))
    dlogits = (powers / mass * jnp.sum(target, axis=1, keepdims=True) - target) * valid
    dlog = split2(dlogits)
    dhb_ref[...] = jnp.broadcast_to(rowsum(dlogits), (8, CLSP))
    dhead_ref[...] = dot_tn(pooled, dlog[0]) + dot_tn(pooled, dlog[1])
    dpooled = two(dot_nt, dlog, head_ref[...]) / cells
    douts = jnp.concatenate(
        [
            jnp.broadcast_to(dpooled[0:1], (ROWS, C4)),
            jnp.broadcast_to(dpooled[1:2], (ROWS, C4)),
        ],
        axis=0,
    ) * mask
    row8w = lax.broadcasted_iota(jnp.int32, (8, C4), 0)

    def stack8(values):
        out = jnp.zeros((8, C4), f32)
        for at, v in enumerate(values):
            out = jnp.where(row8w == at, v, out)
        return out

    dfinal_ref[...] = stack8([rowsum(douts * hat3), rowsum(douts)])
    dstream2 = norm_images_back(douts, hat3, rs3, final_ref[0:1, :], mask, count)
    dscale2 = rowsum(dstream2 * branch)
    dbranch = dstream2 * scale2
    dfb2_ref[...] = jnp.broadcast_to(rowsum(dbranch), (8, C4))
    dbr = split2(dbranch)
    dactive = two(dot_nt, dbr, w2_ref[...])
    hidden = hid_ref[...]
    slope = 0.5 * (1.0 + erf(hidden * math.sqrt(0.5))) + hidden * (
        jnp.exp(-0.5 * hidden * hidden) * (1.0 / math.sqrt(2.0 * math.pi))
    )
    dhidden = dactive * slope
    dfb1_ref[...] = jnp.broadcast_to(rowsum(dhidden), (8, HID))
    dhid = split2(dhidden)
    for at in range(HID // LANES):
        cols = slice(at * LANES, (at + 1) * LANES)
        first_part = dot_tn(dhid[0][:, cols], normed) + dot_tn(dhid[1][:, cols], normed)
        second_part = dot_tn(active[:, cols], dbr[0]) + dot_tn(active[:, cols], dbr[1])
        dmlp_ref[0, pl.ds(at * LANES, LANES), :] = first_part
        dmlp_ref[1, pl.ds(at * LANES, LANES), :] = second_part
    dnormed = two(dot_nn, dhid, w1_ref[...])
    dgain2, dshift2 = rowsum(dnormed * hat2), rowsum(dnormed * mask)
    dstream1 = dstream2 + norm_images_back(dnormed, hat2, rs2, gain2, mask, count)
    dscale1 = rowsum(dstream1 * pool)
    dpool = dstream1 * scale1
    back = split3(dpool * per_count)
    du = dot_nn(near, back[0]) + (dot_nn(near, back[1]) + dot_nn(near, back[2])) - dpool
    dgain1, dshift1 = rowsum(du * hat1), rowsum(du)
    dstream = dstream1 + norm_images_back(du, hat1, rs1, gain1, mask, count)
    dblock_ref[...] = stack8([dgain1, dshift1, dscale1, dgain2, dshift2, dscale2])
    db3_ref[...] = jnp.broadcast_to(rowsum(dstream), (8, C4))
    dstream_ref[...] = dstream


def backward_kernel(
    dstream_ref,
    p0_ref,
    p1_ref,
    p2_ref,
    p3_ref,
    k1t_ref,
    k2_ref,
    k3_ref,
    tm_ref,
    t64_ref,
    marks_ref,
    dstem_ref,
    dk1_ref,
    dk2_ref,
    dk3_ref,
    db0_ref,
    db1_ref,
    db2_ref,
    ds3_ref,
    ds2_ref,
    ds1_ref,
    dt_ref,
    dk1t_ref,
):
    marks = marks_ref[...]
    lane = lax.broadcasted_iota(jnp.int32, (BOTH, LANES), 1)
    wide = TAPS * LANES
    grad = split2(dstream_ref[...])
    step = 512
    for start in range(0, K3P, step):
        cols = pl.ds(start, min(step, K3P - start))
        dk3_ref[:, cols] = dot_tn(grad[0], p3_ref[:, cols]) + dot_tn(grad[1], p3_ref[:, cols])
    ds3_ref[...] = jnp.zeros_like(ds3_ref)
    for part in range(3):
        width = min(wide, K3P - part * wide)
        nat = two(dot_nn, grad, k3_ref[:, pl.ds(part * wide, width)])
        if width < wide:
            keep = lax.broadcasted_iota(jnp.int32, (BOTH, width), 1) < C3 * TAPS - part * wide
            nat = jnp.where(keep, nat, 0.0)
        pieces = split2(nat)
        by_tap = dot_nt(pieces[0], tm_ref[:, pl.ds(0, width)]) + dot_nt(pieces[1], tm_ref[:, pl.ds(0, width)])
        for tap in range(TAPS):
            q, src_r, src_c, down_r, down_c = tap_source(tap, (), ())
            at = q[0] * 2 + q[1]
            ds3_ref[pl.ds(at * BOTH, BOTH), pl.ds(part * LANES, LANES)] += moved_back(
                by_tap[:, tap * LANES : (tap + 1) * LANES], down_r, down_c, marks
            )
    db2_ref[...] = jnp.broadcast_to(rowsum(ds3_ref[...]), (8, C3P))
    grad = split2(ds3_ref[...])
    dk2_ref[...] = dot_tn(grad[0], p2_ref[...]) + dot_tn(grad[1], p2_ref[...])
    pieces = split2(two(dot_nn, grad, k2_ref[...]))
    dt_ref[...] = two(dot_nt, pieces, tm_ref[...])
    ds2_ref[...] = jnp.zeros_like(ds2_ref)
    for at, rb, cb in all_bits(1):
        for tap in range(TAPS):
            q, src_r, src_c, down_r, down_c = tap_source(tap, rb, cb)
            to = (q[0] * 2 + q[1]) * 4 + plane_of(src_r, src_c)
            ds2_ref[pl.ds(to * BOTH, BOTH), :] += moved_back(
                dt_ref[pl.ds(at * BOTH, BOTH), pl.ds(tap * LANES, LANES)], down_r, down_c, marks
            )
    db1_ref[...] = jnp.broadcast_to(rowsum(ds2_ref[...]), (8, C2))
    grad = split2(ds2_ref[...])
    dk1t_ref[...] = dot_tn(grad[0], p1_ref[...]) + dot_tn(grad[1], p1_ref[...])
    dk1_ref[...] = two(dot_nt, split2(dk1t_ref[...]), t64_ref[...])
    ds1_ref[...] = jnp.zeros_like(ds1_ref)
    for pair in range(5):
        values = two(dot_nn, grad, k1t_ref[:, pl.ds(pair * LANES, LANES)])
        for at, rb, cb in all_bits(2):
            here = values[at * BOTH : (at + 1) * BOTH]
            for side in range(2):
                tap = 2 * pair + side
                if tap >= TAPS:
                    continue
                q, src_r, src_c, down_r, down_c = tap_source(tap, rb, cb)
                to = (q[0] * 2 + q[1]) * 16 + plane_of(src_r, src_c)
                mine = (lane < C1) if side == 0 else (lane >= C1)
                ds1_ref[pl.ds(to * BOTH, BOTH), :] += moved_back(
                    jnp.where(mine, here, 0.0), down_r, down_c, marks
                )
    db0_ref[...] = jnp.broadcast_to(rowsum(ds1_ref[...]), (8, LANES))
    stem = jnp.zeros((LANES, 2 * LANES), f32)
    for at in range(4):
        rows = pl.ds(at * 16 * BOTH, 16 * BOTH)
        grad = split2(ds1_ref[rows, :])
        stem = stem + (dot_tn(grad[0], p0_ref[rows, :]) + dot_tn(grad[1], p0_ref[rows, :]))
    dstem_ref[...] = stem[:C1] + stem[C1:]


def shape(*dims, dtype=f32):
    return jax.ShapeDtypeStruct(dims, dtype)


def kernel_call(body, outs, scratch, smem, count, flops):
    vmem = pl.BlockSpec(memory_space=pltpu.VMEM)
    scalar = pl.BlockSpec(memory_space=pltpu.SMEM)
    return pl.pallas_call(
        body,
        out_shape=outs,
        in_specs=[scalar] * smem + [vmem] * (count - smem),
        out_specs=[vmem] * len(outs),
        scratch_shapes=scratch,
        compiler_params=pltpu.CompilerParams(vmem_limit_bytes=60 * 1024 * 1024),
        cost_estimate=pl.CostEstimate(flops=flops, bytes_accessed=20_000_000, transcendentals=0),
    )


def run_forward(args):
    outs = [
        shape(16 * BOTH, 5 * LANES, dtype=bf16),
        shape(4 * BOTH, TAPS * LANES, dtype=bf16),
        shape(BOTH, 3 * TAPS * LANES, dtype=bf16),
        shape(C2, 5 * LANES, dtype=bf16),
        shape(BOTH, C4),
        shape(2, HID, C4),
        shape(C4, CLSP),
        shape(8, C4),
        shape(8, HID),
        shape(8, C4),
        shape(8, C4),
        shape(8, CLSP),
        shape(8, C4),
        shape(8, LANES),
    ]
    scratch = [
        pltpu.VMEM((64 * BOTH, LANES), f32),
        pltpu.VMEM((16 * BOTH, LANES), f32),
        pltpu.VMEM((4 * BOTH, C3P), f32),
        pltpu.VMEM((4 * BOTH, TAPS * LANES), bf16),
        pltpu.VMEM((3 * BOTH, TAPS * LANES), bf16),
        pltpu.VMEM((BOTH, HID), f32),
    ]
    return kernel_call(forward_kernel, outs, scratch, 2, len(args), 10**9)(*args)


def run_backward(args):
    outs = [
        shape(C1, 2 * LANES),
        shape(C2, TAPS * C1),
        shape(C3P, TAPS * LANES),
        shape(C4, K3P),
        shape(8, LANES),
        shape(8, C2),
        shape(8, C3P),
    ]
    scratch = [
        pltpu.VMEM((4 * BOTH, C3P), f32),
        pltpu.VMEM((16 * BOTH, LANES), f32),
        pltpu.VMEM((64 * BOTH, LANES), f32),
        pltpu.VMEM((4 * BOTH, TAPS * LANES), f32),
        pltpu.VMEM((C2, 5 * LANES), f32),
    ]
    return kernel_call(backward_kernel, outs, scratch, 0, len(args), 10**9)(*args)


def patches(images, resolution, partner_col, mix_col):
    pictures = images[:, 0].astype(f32)
    dims = (1, 1, RES_L, RES_L)
    inside = (lax.broadcasted_iota(jnp.int32, dims, 2) < resolution) & (
        lax.broadcasted_iota(jnp.int32, dims, 3) < resolution
    )
    mixing = mix_col[:, None, None, None]
    other = jnp.where(partner_col[:, None, None, None] == 0, pictures[0][None], pictures[1][None])
    pixels = jnp.where(inside, mixing * pictures + (1.0 - mixing) * other, 0.0).astype(bf16)
    depth = IN_CH * 49
    pick = jnp.eye(depth, dtype=bf16).reshape(IN_CH, 7, 7, depth).transpose(1, 2, 0, 3)
    columns = lax.conv_general_dilated(
        pixels,
        pick,
        (4, 4),
        ((2, 2), (2, 2)),
        dimension_numbers=("NCHW", "HWIO", "NHWC"),
        preferred_element_type=f32,
    ).astype(bf16)
    columns = columns.reshape(MICRO, SIDE, 2, 2, 2, SIDE, 2, 2, 2, depth)
    columns = columns.transpose(4, 8, 3, 7, 2, 6, 0, 1, 5, 9).reshape(64, MICRO, SIDE * SIDE, depth)
    columns = jnp.pad(columns, ((0, 0), (0, 0), (0, ROWS - SIDE * SIDE), (0, 2 * LANES - depth)))
    return columns.reshape(64 * BOTH, 2 * LANES)


def tap_orders():
    row = lax.broadcasted_iota(jnp.int32, (TAPS * LANES, TAPS * LANES), 0)
    col = lax.broadcasted_iota(jnp.int32, (TAPS * LANES, TAPS * LANES), 1)
    forth = ((row % LANES) * TAPS + row // LANES == col).astype(bf16)
    row = lax.broadcasted_iota(jnp.int32, (TAPS * C1, 5 * LANES), 0)
    col = lax.broadcasted_iota(jnp.int32, (TAPS * C1, 5 * LANES), 1)
    back = (((row % TAPS) * C1 + row // TAPS == col)).astype(bf16)
    return forth, back


def grid_marks(side):
    row = np.arange(BOTH)
    image, q = row // ROWS, row % ROWS
    y, x = q // SIDE, q % SIDE
    real = q < SIDE * SIDE
    fixed = np.stack([real & (y > 0), real & (x > 0), real & (y > 0) & (x > 0)], 1).astype(np.float32)
    close = (
        (image[:, None] == image[None])
        & (abs(y[:, None] - y[None]) <= 1)
        & (abs(x[:, None] - x[None]) <= 1)
        & real[:, None]
        & real[None]
    )
    inside = jnp.asarray(real) & (jnp.asarray(y) < side) & (jnp.asarray(x) < side)
    near = jnp.where(jnp.asarray(close) & inside[:, None] & inside[None], 1.0, 0.0)
    cells = jnp.maximum(jnp.sum(near, axis=1), 1.0)
    marks = jnp.concatenate(
        [inside.astype(f32)[:, None], jnp.asarray(fixed), (1.0 / cells)[:, None]], axis=1
    )
    return jnp.pad(marks, ((0, 0), (0, LANES - marks.shape[1]))), near.astype(bf16)


def local_gradients(images, group, label_col, partner_col, mix_col, valid_col, flat, mats):
    side = RES_S // RES_STEP + group
    columns = patches(images, side * RES_STEP, partner_col, mix_col)
    forth, back = tap_orders()
    marks, near = grid_marks(side)
    piece = {}
    offset = 0
    for name, amount in SIZES:
        piece[name] = flat[offset : offset + amount]
        offset += amount
    stem = jnp.pad(piece["stem"].reshape(C1, IN_CH * 49), ((0, 0), (0, 2 * LANES - IN_CH * 49)))
    w0 = jnp.concatenate([stem, stem], axis=0)
    k1 = piece["k1"].reshape(C2, C1 * 9)
    k2 = jnp.pad(piece["k2"].reshape(C3, C2 * 9), ((0, C3P - C3), (0, 0)))
    k3 = jnp.pad(piece["k3"].reshape(C4, C3 * 9), ((0, 0), (0, K3P - C3 * 9)))
    b0 = piece["b0"].astype(f32)
    b0 = jnp.concatenate([b0, b0])[None]
    b1 = piece["b1"].astype(f32)[None]
    b2 = jnp.pad(piece["b2"].astype(f32), (0, C3P - C3))[None]
    b3 = piece["b3"].astype(f32)[None]
    block = jnp.pad(piece["block"].astype(f32).reshape(6, C4), ((0, 2), (0, 0)))
    fb1 = piece["fb1"].astype(f32)[None]
    fb2 = piece["fb2"].astype(f32)[None]
    final = jnp.pad(piece["final"].astype(f32).reshape(2, C4), ((0, 6), (0, 0)))
    head = jnp.pad(piece["head"].reshape(C4, CLS), ((0, 0), (0, CLSP - CLS)))
    hb = jnp.pad(piece["hb"].astype(f32), (0, CLSP - CLS))[None]
    whole = jnp.concatenate([label_col, jnp.where(partner_col == 0, label_col[0], label_col[1])])
    cells = (side * side).astype(f32)
    real = jnp.concatenate(
        [mix_col, valid_col.astype(f32), jnp.stack([cells, cells * C4])]
    )
    (
        p1,
        p2,
        p3,
        k1t,
        dstream,
        dmlp,
        dhead,
        dblock,
        dfb1,
        dfb2,
        dfinal,
        dhb,
        db3,
        loss,
    ) = run_forward(
        [
            whole,
            real,
            columns,
            w0,
            k1,
            k2,
            k3,
            mats[0],
            mats[1],
            forth,
            back,
            marks,
            near,
            b0,
            b1,
            b2,
            b3,
            block,
            fb1,
            fb2,
            final,
            head,
            hb,
        ]
    )
    dstem, dk1, dk2, dk3, db0, db1, db2 = run_backward(
        [dstream, columns, p1, p2, p3, k1t, k2, k3, forth, back, marks]
    )
    pieces = [
        dstem[:, : IN_CH * 49],
        db0[0, :C1] + db0[0, C1:],
        dk1,
        db1[0],
        dk2[:C3],
        db2[0, :C3],
        dk3[:, : C3 * 9],
        db3[0],
        dblock[:6],
        dfb1[0],
        dfb2[0],
        dfinal[:2],
        dhead[:, :CLS],
        dhb[0, :CLS],
    ]
    dflat = jnp.concatenate([p.reshape(-1) for p in pieces])
    dflat = jnp.pad(dflat, (0, flat.shape[0] - dflat.shape[0]))
    return loss[0, 0], dflat, dmlp


def matmul(a, b):
    return jnp.einsum("bij,bjk->bik", a, b, precision=highest)


def orthogonalize(ortho, devices):
    gram = lax.psum(jnp.einsum("bki,bkj->bij", ortho, ortho, precision=highest), devices)
    diagonal = jnp.sum(jnp.where(jnp.eye(C4, dtype=bool)[None], gram, 0.0), axis=(1, 2))
    inverse = 1.0 / (jnp.sqrt(diagonal) + 1e-07)
    gram = gram * (inverse * inverse)[:, None, None]
    eye = jnp.eye(C4, dtype=f32)[None]
    product = None
    for iteration in range(NS_ITERS):
        poly = 3.4445 * eye - 4.775 * gram + 2.0315 * matmul(gram, gram)
        product = poly if product is None else matmul(poly, product)
        if iteration < NS_ITERS - 1:
            gram = matmul(matmul(poly, gram), poly)
    return jnp.einsum("bki,bij->bkj", ortho, product, precision=highest) * inverse[:, None, None]


def per_device(
    devices_count,
    images,
    group_ids,
    labels,
    partners,
    mix_weights,
    valid,
    flat_params,
    flat_first,
    flat_second,
    mlp_weights,
    mlp_momentum,
):
    share = mlp_weights.shape[2]
    flat_share = flat_params.shape[0]
    mats = mlp_weights.transpose(0, 2, 1)
    blocks = mats.reshape(2, share, C4 // LANES, LANES).transpose(0, 2, 1, 3).astype(bf16)
    counted = jnp.sum(valid).astype(f32)
    rows = 2 * share * C4 // LANES
    flat_rows = -(-flat_share // LANES)
    spare = flat_rows * LANES - flat_share
    sent = jnp.concatenate(
        [
            blocks.reshape(rows, LANES),
            jnp.pad(flat_params.astype(bf16), (0, spare)).reshape(flat_rows, LANES),
            jnp.full((-(rows + flat_rows) % 8 or 8, LANES), counted).astype(bf16),
        ]
    )
    got = lax.all_gather(sent, AXES, axis=0, tiled=False)
    whole_mats = (
        got[:, :rows]
        .reshape(devices_count, 2, C4 // LANES, share, LANES)
        .transpose(1, 0, 3, 2, 4)
        .reshape(2, HID, C4)
    )
    whole_flat = (
        got[:, rows : rows + flat_rows]
        .reshape(devices_count, flat_rows * LANES)[:, :flat_share]
        .reshape(devices_count * flat_share)
    )
    valid_total = jnp.maximum(jnp.sum(got[:, rows + flat_rows, 0].astype(f32)), 1.0)
    scale = 1.0 / valid_total

    loss, dflat, dmlp = local_gradients(
        images,
        group_ids[0],
        labels[:, 0],
        partners[:, 0],
        mix_weights[:, 0],
        valid[:, 0],
        whole_flat,
        whole_mats,
    )
    sum_mlp = lax.psum_scatter(
        dmlp.reshape(2, devices_count, share, C4), AXES, scatter_dimension=1, tiled=False
    ) * scale
    extra = jnp.full((devices_count, -flat_rows % 8 or 8, LANES), loss)
    dflat = jnp.pad(dflat.reshape(devices_count, flat_share), ((0, 0), (0, spare)))
    dflat = jnp.concatenate([dflat.reshape(devices_count, flat_rows, LANES), extra], axis=1)
    sum_flat = lax.psum_scatter(dflat, AXES, scatter_dimension=0, tiled=False)
    loss_total = sum_flat[flat_rows, 0]
    sum_flat = sum_flat[:flat_rows].reshape(flat_rows * LANES)[:flat_share] * scale
    first_new = 0.9 * flat_first + 0.1 * sum_flat
    second_new = 0.999 * flat_second + 0.001 * sum_flat * sum_flat
    first_hat = first_new / (1.0 - 0.9**STEP)
    second_hat = second_new / (1.0 - 0.999**STEP)
    params_new = flat_params - 0.02 * (
        first_hat / (jnp.sqrt(second_hat) + 1e-08) + 0.05 * flat_params
    )
    momentum_new = 0.95 * mlp_momentum.transpose(0, 2, 1) + sum_mlp
    ortho = orthogonalize(sum_mlp + 0.95 * momentum_new, AXES)
    weights_new = mats * (1.0 - 0.1 * 0.05) - 0.1 * 0.2 * math.sqrt(HID) * ortho
    return (
        loss_total,
        params_new,
        first_new,
        second_new,
        weights_new.transpose(0, 2, 1),
        momentum_new.transpose(0, 2, 1),
    )


def solution(mesh):
    placed = (
        P(None, AXES, None, None, None),
        P(AXES),
        P(None, AXES),
        P(None, AXES),
        P(None, AXES),
        P(None, AXES),
        P(AXES),
        P(AXES),
        P(AXES),
        P(None, None, AXES),
        P(None, None, AXES),
    )
    devices_count = math.prod(mesh.shape[axis] for axis in AXES)
    return jax.shard_map(
        functools.partial(per_device, devices_count),
        mesh=mesh,
        in_specs=placed,
        out_specs=(
            P(),
            P(AXES),
            P(AXES),
            P(AXES),
            P(None, None, AXES),
            P(None, None, AXES),
        ),
        check_vma=False,
    )
```

```python
import functools
import math

import jax
import jax.numpy as jnp
import numpy as np
from jax import lax
from jax.experimental import pallas as pl
from jax.experimental.pallas import tpu as pltpu
from jax.sharding import PartitionSpec as P

C1 = 64
C2 = 128
C3 = 320
C4 = 512
HID = 2048
CLS = 1000
IN_CH = 3
RES_S = 96
RES_L = 160
RES_STEP = 32
MICRO = 2
NS_ITERS = 5
STEP = 10

AXES = ("fsdp", "ns")
LANES = 128
SIDE = 5
ROWS = 32
BOTH = MICRO * ROWS
C3P = 384
CLSP = 1024
K3P = 2944
TAPS = 9

f32 = jnp.float32
bf16 = jnp.bfloat16
norm_epsilon = 1e-05

NARROW = C1 * IN_CH * 49
ROW_B0 = NARROW // LANES
ROW_K1 = 74
ROW_B1 = 650
ROW_K2 = 651
ROW_B2 = 3531
ROW_K3 = 3533
ROW_B3 = 15053
REST = {"b3": 0, "block": 4, "fb1": 28, "fb2": 44, "final": 48, "head": 56, "hb": 4056, "end": 4064}
GROUP = 16
SPAN = GROUP * CLS // LANES
PAIRS = [(i, j) for i in range(4) for j in range(i, 4)]


def dot_nn(a, b):
    return lax.dot_general(a, b, (((1,), (0,)), ((), ())), preferred_element_type=f32)


def dot_nt(a, b):
    return lax.dot_general(a, b, (((1,), (1,)), ((), ())), preferred_element_type=f32)


def dot_tn(a, b):
    return lax.dot_general(a, b, (((0,), (0,)), ((), ())), preferred_element_type=f32)


def split2(x):
    hi = x.astype(bf16)
    return hi, (x - hi.astype(f32)).astype(bf16)


def split3(x):
    hi = x.astype(bf16)
    rest = x - hi.astype(f32)
    mid = rest.astype(bf16)
    return hi, mid, (rest - mid.astype(f32)).astype(bf16)


def two(dot, pair, other):
    return dot(pair[0], other) + dot(pair[1], other)


def borrow(bits):
    out = list(bits)
    for at, bit in enumerate(out):
        if bit:
            out[at] = 0
            return tuple(out), 0
        out[at] = 1
    return tuple(out), 1


def tap_source(tap, row_bits, col_bits):
    r, c = divmod(tap, 3)
    src_r, down_r = (row_bits, 0) if r else borrow(row_bits)
    src_c, down_c = (col_bits, 0) if c else borrow(col_bits)
    return (int(r != 1), int(c != 1)), src_r, src_c, down_r, down_c


def plane_of(row_bits, col_bits):
    at = 0
    for r, c in zip(row_bits, col_bits):
        at = at * 4 + r * 2 + c
    return at


def all_bits(pairs):
    for at in range(4**pairs):
        digits = [(at >> (2 * (pairs - 1 - k))) & 3 for k in range(pairs)]
        yield at, tuple(d >> 1 for d in digits), tuple(d & 1 for d in digits)


def moved(value, down_r, down_c, marks):
    if not (down_r or down_c):
        return value
    step = SIDE * down_r + down_c
    column = {(1, 0): 1, (0, 1): 2, (1, 1): 3}[(down_r, down_c)]
    return pltpu.roll(value, step, 0) * marks[:, column : column + 1]


def moved_back(value, down_r, down_c, marks):
    if not (down_r or down_c):
        return value
    step = SIDE * down_r + down_c
    column = {(1, 0): 1, (0, 1): 2, (1, 1): 3}[(down_r, down_c)]
    return pltpu.roll(value * marks[:, column : column + 1], BOTH - step, 0)


def erf(x):
    x = jnp.clip(x, -3.832506856900711, 3.832506856900711)
    s = x * x
    top = 2.2905065861350646e-4
    for coef in (3.4082910107109506e-3, 5.0955695062380861e-2, 1.8520832239976145e-1, 1.128379143519084):
        top = top * s + coef
    low = -1.1791602954361697e-7
    for coef in (
        2.3547966471313185e-5,
        1.0179625278914885e-3,
        1.4070470171167667e-2,
        1.1098505178285362e-1,
        4.9746925110067538e-1,
        1.0,
    ):
        low = low * s + coef
    return x * top / low


def total(x):
    return jnp.sum(jnp.sum(x, axis=1, keepdims=True), axis=0, keepdims=True)


def norm_images(value, mask, count):
    parts, scales = [], []
    for m in range(MICRO):
        v = value[m * ROWS : (m + 1) * ROWS]
        k = mask[m * ROWS : (m + 1) * ROWS]
        center = (v - total(v * k) / count) * k
        scale = lax.rsqrt(total(center * center) / count + norm_epsilon)
        parts.append(center * scale)
        scales.append(scale)
    return jnp.concatenate(parts, axis=0), scales


def norm_images_back(grad, hat, scales, gain, mask, count):
    parts = []
    for m in range(MICRO):
        at = slice(m * ROWS, (m + 1) * ROWS)
        g = grad[at] * gain
        h = hat[at]
        parts.append((g - total(g) / count - h * (total(g * h) / count)) * scales[m] * mask[at])
    return jnp.concatenate(parts, axis=0)


def rowsum(x):
    return jnp.sum(x, axis=0, keepdims=True)


def halves(low, high):
    lane = lax.broadcasted_iota(jnp.int32, low.shape, 1)
    return jnp.where(lane < LANES // 2, pltpu.roll(low, LANES // 2, 1), pltpu.roll(high, LANES // 2, 1))


def lanes_of(ref, row, count):
    return jnp.concatenate([ref[row + at : row + at + 1, :] for at in range(count)], axis=1)


def head_masks():
    row = lax.broadcasted_iota(jnp.int32, (C4 // GROUP, C4), 0)
    col = lax.broadcasted_iota(jnp.int32, (C4 // GROUP, C4), 1)
    return col // GROUP == row, col % GROUP == row // MICRO, row % MICRO == 0


def forward_kernel(
    rows,
    share,
    flat_share,
    whole_ref,
    real_ref,
    got_ref,
    p0_ref,
    *refs,
):
    if flat_share % LANES:
        forward_body(rows, share, None, whole_ref, real_ref, got_ref, p0_ref, *refs)
    else:
        forward_body(rows, share, flat_share, whole_ref, real_ref, got_ref, p0_ref, refs[-1], *refs[:-1])


def forward_body(
    rows,
    share,
    flat_share,
    whole_ref,
    real_ref,
    got_ref,
    p0_ref,
    flat_ref,
    tm_ref,
    t64_ref,
    pm_ref,
    marks_ref,
    near_ref,
    p1_ref,
    p2_ref,
    p3e_ref,
    p3o_ref,
    k1t_ref,
    k2_ref,
    k3e_ref,
    k3o_ref,
    dstream_ref,
    keep_a_ref,
    keep_b_ref,
    send_a_ref,
    send_b_ref,
    dblock_ref,
    dfb1_ref,
    small_ref,
    pooled_ref,
    dlog_ref,
    loss_ref,
    s1_ref,
    s2_ref,
    s3_ref,
    t2_ref,
    t3_ref,
    hid_ref,
    w0_ref,
    k1f_ref,
    rest_ref,
    wide_ref,
    z_ref,
    mats_ref,
    sems,
    *flat_refs,
):
    if flat_share is not None:
        near_refs = flat_refs
        flat_copy = pltpu.make_async_copy(
            got_ref.at[:, pl.ds(rows, near_refs[0].shape[1]), :], near_refs[0], near_refs[1].at[0]
        )
        flat_copy.start()
    copies = []
    for mat in range(2):
        for part in range(C4 // LANES):
            copy = pltpu.make_async_copy(
                got_ref.at[:, pl.ds((mat * (C4 // LANES) + part) * share, share), :],
                mats_ref.at[mat, part],
                sems.at[mat * (C4 // LANES) + part],
            )
            copy.start()
            copies.append(copy)
    if flat_share is not None:
        flat_copy.wait()
        flat_rows = flat_share // LANES
        for at in range(near_refs[0].shape[0]):
            flat_ref[pl.ds(at * flat_rows, flat_rows), :] = near_refs[0][at, pl.ds(0, flat_rows), :].astype(f32)
    marks = marks_ref[...]
    lane = lax.broadcasted_iota(jnp.int32, (BOTH, LANES), 1)
    lane1 = lax.broadcasted_iota(jnp.int32, (1, LANES), 1)
    depth = IN_CH * 49
    for at in range(C1):
        row, shift = divmod(depth * at, LANES)
        line = lanes_of(flat_ref, row, 3)
        if shift:
            line = pltpu.roll(line, 3 * LANES - shift, 1)
        w0_ref[at : at + 1, :] = line[:, : 2 * LANES]
    w0 = w0_ref[...].astype(bf16)
    w0 = jnp.concatenate([w0, w0], axis=0)
    b0 = flat_ref[ROW_B0 : ROW_B0 + 1, :]
    b0 = jnp.where(lane1 < C1, pltpu.roll(b0, C1, 1), b0)
    quarter = 16 * BOTH
    for at in range(4):
        span = pl.ds(at * quarter, quarter)
        s1_ref[span, :] = (dot_nt(p0_ref[span, :], w0) + b0).astype(bf16).astype(f32)

    def tap_value(ref, pairs, tap, row_bits, col_bits, cols):
        q, src_r, src_c, down_r, down_c = tap_source(tap, row_bits, col_bits)
        at = (q[0] * 2 + q[1]) * 4**pairs + plane_of(src_r, src_c)
        return moved(ref[pl.ds(at * BOTH, BOTH), cols], down_r, down_c, marks)

    half = C2 // 2
    for odd in range(2):
        block = jnp.concatenate(
            [flat_ref[pl.ds(ROW_K1 + 4 * odd + j, half, stride=9), :].astype(bf16) for j in range(5)], axis=1
        )
        block = dot_nn(block, t64_ref[odd])
        for j in range(5):
            k1f_ref[j, pl.ds(odd, half, stride=2), :] = block[:, j * LANES : (j + 1) * LANES]
    for j in range(5):
        k1t_ref[:, pl.ds(j * LANES, LANES)] = k1f_ref[j].astype(bf16)
    everything = slice(None)
    for at, rb, cb in all_bits(2):
        for pair in range(5):
            left = tap_value(s1_ref, 2, 2 * pair, rb, cb, everything)
            if pair < 4:
                right = tap_value(s1_ref, 2, 2 * pair + 1, rb, cb, everything)
            else:
                right = jnp.zeros_like(left)
            p1_ref[pl.ds(at * BOTH, BOTH), pl.ds(pair * LANES, LANES)] = jnp.where(
                lane < C1, left, right
            ).astype(bf16)
    b1 = flat_ref[ROW_B1 : ROW_B1 + 1, :]
    s2_ref[...] = (dot_nt(p1_ref[...], k1t_ref[...]) + b1).astype(bf16).astype(f32)
    for j in range(TAPS):
        k2_ref[pl.ds(0, C3), pl.ds(j * LANES, LANES)] = flat_ref[pl.ds(ROW_K2 + j, C3, stride=TAPS), :].astype(bf16)
    k2_ref[pl.ds(C3, C3P - C3), :] = jnp.zeros((C3P - C3, TAPS * LANES), bf16)
    b2 = lanes_of(flat_ref, ROW_B2, 3)
    b2 = jnp.where(lax.broadcasted_iota(jnp.int32, b2.shape, 1) < C3, b2, 0.0)
    for at, rb, cb in all_bits(1):
        for tap in range(TAPS):
            t2_ref[pl.ds(at * BOTH, BOTH), pl.ds(tap * LANES, LANES)] = tap_value(
                s2_ref, 1, tap, rb, cb, everything
            ).astype(bf16)
    p2_ref[...] = dot_nn(t2_ref[...], tm_ref[...]).astype(bf16)
    s3_ref[...] = (dot_nt(p2_ref[...], k2_ref[...]) + b2).astype(bf16).astype(f32)
    for part in range(3):
        for tap in range(TAPS):
            t3_ref[pl.ds(part * BOTH, BOTH), pl.ds(tap * LANES, LANES)] = tap_value(
                s3_ref, 0, tap, (), (), pl.ds(part * LANES, LANES)
            ).astype(bf16)
    spread = dot_nn(t3_ref[...], tm_ref[...])
    spread = jnp.concatenate([spread[part * BOTH : (part + 1) * BOTH] for part in range(3)], axis=1)
    p3o_ref[...] = spread[:, :K3P].astype(bf16)
    p3e_ref[...] = pltpu.roll(spread, LANES // 2, 1)[:, :K3P].astype(bf16)
    for j in range(K3P // LANES):
        cols = pl.ds(j * LANES, LANES)
        k3e_ref[:, cols] = flat_ref[pl.ds(ROW_K3 + j, C4 // 2, stride=45), :].astype(bf16)
        k3o_ref[:, cols] = flat_ref[pl.ds(ROW_K3 + 23 + j, C4 // 2, stride=45), :].astype(bf16)
    apart = split3(
        jnp.concatenate([dot_nt(p3e_ref[...], k3e_ref[...]), dot_nt(p3o_ref[...], k3o_ref[...])], axis=1)
    )
    stream = dot_nn(apart[0], pm_ref[...]) + (dot_nn(apart[1], pm_ref[...]) + dot_nn(apart[2], pm_ref[...]))

    amount = REST["head"]
    rest_ref[...] = halves(flat_ref[ROW_B3 : ROW_B3 + amount, :], flat_ref[ROW_B3 + 1 : ROW_B3 + 1 + amount, :])
    b3 = lanes_of(rest_ref, REST["b3"], 4)
    gain1, shift1, scale1, gain2, shift2, scale2 = (lanes_of(rest_ref, REST["block"] + 4 * k, 4) for k in range(6))
    fb1 = lanes_of(rest_ref, REST["fb1"], HID // LANES)
    fb2 = lanes_of(rest_ref, REST["fb2"], 4)
    gain3, shift3 = (lanes_of(rest_ref, REST["final"] + 4 * k, 4) for k in range(2))

    stream = stream + b3
    mask = marks[:, 0:1]
    per_count = marks[:, 4:5]
    cells = real_ref[4]
    count = real_ref[5]
    near = near_ref[...]
    hat1, rs1 = norm_images(stream, mask, count)
    u = (hat1 * gain1 + shift1) * mask
    u3 = split3(u)
    around = dot_nn(near, u3[0]) + (dot_nn(near, u3[1]) + dot_nn(near, u3[2]))
    pool = around * per_count - u
    stream1 = stream + scale1 * pool
    hat2, rs2 = norm_images(stream1, mask, count)
    normed = ((hat2 * gain2 + shift2) * mask).astype(bf16)
    for copy in copies:
        copy.wait()
    blocks = C4 // LANES

    def matrix(mat, part):
        return mats_ref[mat, part].reshape(HID, LANES)

    def lanes(x, part):
        return x[:, part * LANES : (part + 1) * LANES]

    hidden = fb1
    for part in range(blocks):
        hidden = hidden + dot_nt(lanes(normed, part), matrix(0, part))
    hid_ref[...] = hidden
    active = (hidden * (0.5 * (1.0 + erf(hidden * math.sqrt(0.5))))).astype(bf16)
    branch = jnp.concatenate([dot_nn(active, matrix(1, part)) for part in range(blocks)], axis=1) + fb2
    stream2 = stream1 + scale2 * branch
    hat3, rs3 = norm_images(stream2, mask, count)
    outs = (hat3 * gain3 + shift3) * mask
    row8 = lax.broadcasted_iota(jnp.int32, (8, 1), 0)
    first, second = row8 == 0, row8 == 1

    def by_row(a, b):
        return jnp.where(first, a, jnp.where(second, b, 0.0))

    pooled = (by_row(rowsum(outs[:ROWS]), rowsum(outs[ROWS:])) / cells).astype(bf16)
    pooled_f = pooled.astype(f32)
    pooled_ref[...] = pooled_f
    groups = C4 // GROUP
    in_group, in_place, own_row = head_masks()
    picked = jnp.where(in_place, jnp.where(own_row, pooled_f[0:1, :], pooled_f[1:2, :]), 0.0).astype(bf16)
    by_place = dot_nt(picked, in_group.astype(bf16)).astype(bf16)
    row_head = ROW_B3 + REST["head"]
    low = pltpu.roll(flat_ref[pl.ds(row_head, groups, stride=SPAN), :], LANES // 2, 1)
    lane32 = lax.broadcasted_iota(jnp.int32, (groups, LANES), 1)
    for at in range(SPAN):
        high = pltpu.roll(flat_ref[pl.ds(row_head + at + 1, groups, stride=SPAN), :], LANES // 2, 1)
        wide_ref[:, pl.ds(at * LANES, LANES)] = jnp.where(lane32 < LANES // 2, low, high).astype(bf16)
        low = high
    wide_ref[:, pl.ds(SPAN * LANES, LANES)] = jnp.zeros((groups, LANES), bf16)
    z_ref[...] = dot_nn(by_place, wide_ref[...])
    column = lax.broadcasted_iota(jnp.int32, (8, CLSP), 1)
    row_hb = ROW_B3 + REST["hb"]
    hb = jnp.concatenate(
        [halves(flat_ref[row_hb + k : row_hb + k + 1, :], flat_ref[row_hb + k + 1 : row_hb + k + 2, :]) for k in range(8)],
        axis=1,
    )
    logits = jnp.zeros((MICRO, CLSP), f32)
    for place in range(GROUP):
        at, shift = divmod(CLS * place, LANES)
        window = z_ref[pl.ds(MICRO * place, MICRO), pl.ds(at * LANES, CLSP + LANES)]
        if shift:
            window = pltpu.roll(window, CLSP + LANES - shift, 1)
        logits = logits + window[:, :CLSP]
    logits = by_row(logits[0:1], logits[1:2]) + hb
    logits = jnp.where(column < CLS, logits, -1e30)
    top = jnp.max(logits, axis=1, keepdims=True)
    powers = jnp.exp(logits - top)
    mass = jnp.sum(powers, axis=1, keepdims=True)
    own = jnp.where(first, whole_ref[0], whole_ref[1])
    other = jnp.where(first, whole_ref[2], whole_ref[3])
    mix = by_row(real_ref[0], real_ref[1])
    target = jnp.where(column == own, mix, 0.0) + jnp.where(column == other, 1.0 - mix, 0.0)
    valid = by_row(real_ref[2], real_ref[3])
    logp = logits - top - jnp.log(mass)
    losses = -jnp.sum(target * logp, axis=1, keepdims=True) * valid
    loss_ref[...] = jnp.broadcast_to(jnp.sum(losses, axis=0, keepdims=True), (8, LANES))
    dlogits = (powers / mass * jnp.sum(target, axis=1, keepdims=True) - target) * valid
    dlog_ref[...] = dlogits
    dpooled = jnp.zeros((8, C4), f32)
    padded = jnp.concatenate([dlogits, jnp.zeros((8, LANES), f32)], axis=1)
    place_col = lax.broadcasted_iota(jnp.int32, (8, C4), 1) % GROUP
    spread_groups = in_group.astype(bf16)
    for place in range(GROUP):
        at, shift = divmod(CLS * place, LANES)
        window = pltpu.roll(padded, shift, 1) if shift else padded
        per_group = two(dot_nt, split2(window), wide_ref[:, pl.ds(at * LANES, CLSP + LANES)])
        z3 = split3(per_group)
        by_channel = dot_nn(z3[0], spread_groups) + (dot_nn(z3[1], spread_groups) + dot_nn(z3[2], spread_groups))
        dpooled = jnp.where(place_col == place, by_channel, dpooled)
    dpooled = dpooled / cells
    douts = jnp.concatenate(
        [
            jnp.broadcast_to(dpooled[0:1], (ROWS, C4)),
            jnp.broadcast_to(dpooled[1:2], (ROWS, C4)),
        ],
        axis=0,
    ) * mask
    row8w = lax.broadcasted_iota(jnp.int32, (8, C4), 0)

    def stack8(values):
        out = jnp.zeros((8, C4), f32)
        for at, v in enumerate(values):
            out = jnp.where(row8w == at, v, out)
        return out

    dgain3, dshift3 = rowsum(douts * hat3), rowsum(douts)
    dstream2 = norm_images_back(douts, hat3, rs3, gain3, mask, count)
    dscale2 = rowsum(dstream2 * branch)
    dbranch = dstream2 * scale2
    dfb2 = rowsum(dbranch)
    dbr = split2(dbranch)
    dactive = None
    for part in range(blocks):
        term = two(dot_nt, (lanes(dbr[0], part), lanes(dbr[1], part)), matrix(1, part))
        dactive = term if dactive is None else dactive + term
    hidden = hid_ref[...]
    slope = 0.5 * (1.0 + erf(hidden * math.sqrt(0.5))) + hidden * (
        jnp.exp(-0.5 * hidden * hidden) * (1.0 / math.sqrt(2.0 * math.pi))
    )
    dhidden = dactive * slope
    dfb1_ref[...] = jnp.broadcast_to(rowsum(dhidden), (8, HID))
    dhid = split2(dhidden)

    def gradients(refs):
        for at in range(HID // LANES):
            cols = slice(at * LANES, (at + 1) * LANES)
            span = pl.ds(at * LANES, LANES)
            one = dot_tn(dhid[0][:, cols], normed) + dot_tn(dhid[1][:, cols], normed)
            two_ = dot_tn(active[:, cols], dbr[0]) + dot_tn(active[:, cols], dbr[1])
            refs[0][span, :] = one[:, : C4 // 2]
            refs[1][span, :] = one[:, C4 // 2 :]
            refs[2][span, :] = two_[:, : C4 // 2]
            refs[3][span, :] = two_[:, C4 // 2 :]

    core = whole_ref[4]

    @pl.when(core == 0)
    def _():
        gradients((keep_a_ref, keep_b_ref, send_a_ref, send_b_ref))

    @pl.when(core != 0)
    def _():
        gradients((send_a_ref, send_b_ref, keep_a_ref, keep_b_ref))

    dnormed = jnp.concatenate([two(dot_nn, dhid, matrix(0, part)) for part in range(blocks)], axis=1)
    dgain2, dshift2 = rowsum(dnormed * hat2), rowsum(dnormed * mask)
    dstream1 = dstream2 + norm_images_back(dnormed, hat2, rs2, gain2, mask, count)
    dscale1 = rowsum(dstream1 * pool)
    dpool = dstream1 * scale1
    back = split3(dpool * per_count)
    du = dot_nn(near, back[0]) + (dot_nn(near, back[1]) + dot_nn(near, back[2])) - dpool
    dgain1, dshift1 = rowsum(du * hat1), rowsum(du)
    dstream = dstream1 + norm_images_back(du, hat1, rs1, gain1, mask, count)
    dblock_ref[...] = stack8([dgain1, dshift1, dscale1, dgain2, dshift2, dscale2])
    small_ref[...] = stack8([rowsum(dstream), dfb2, dgain3, dshift3])
    dstream_ref[...] = dstream


def backward_kernel(
    unused_one_ref,
    unused_two_ref,
    dstream_ref,
    p0_ref,
    p1_ref,
    p2_ref,
    p3e_ref,
    p3o_ref,
    k1t_ref,
    k2_ref,
    k3e_ref,
    k3o_ref,
    tm_ref,
    t64_ref,
    pm_ref,
    marks_ref,
    dblock_ref,
    dfb1_ref,
    small_ref,
    pooled_ref,
    dlog_ref,
    out_ref,
    ds3_ref,
    ds2_ref,
    ds1_ref,
    dt_ref,
    dk1t_ref,
    rest_ref,
):
    marks = marks_ref[...]
    lane = lax.broadcasted_iota(jnp.int32, (BOTH, LANES), 1)
    lane1 = lax.broadcasted_iota(jnp.int32, (1, LANES), 1)
    wide = TAPS * LANES
    grad3 = split3(dstream_ref[...])
    apart = dot_nt(grad3[0], pm_ref[...]) + (dot_nt(grad3[1], pm_ref[...]) + dot_nt(grad3[2], pm_ref[...]))
    half = C4 // 2
    even, odd = split2(apart[:, :half]), split2(apart[:, half:])
    last = K3P // LANES - 1
    for j in range(last):
        cols = pl.ds(j * LANES, LANES)
        value = dot_tn(odd[0], p3o_ref[:, cols]) + dot_tn(odd[1], p3o_ref[:, cols])
        out_ref[pl.ds(ROW_K3 + 23 + j, half, stride=45), :] = value
        if j:
            value = dot_tn(even[0], p3e_ref[:, cols]) + dot_tn(even[1], p3e_ref[:, cols])
            out_ref[pl.ds(ROW_K3 + j, half, stride=45), :] = value
    cols = pl.ds(last * LANES, LANES)
    value = dot_tn(even[0], p3e_ref[:, cols]) + dot_tn(even[1], p3e_ref[:, cols])
    out_ref[pl.ds(ROW_K3 + last, half, stride=45), :] = value
    tail = dot_tn(odd[0], p3o_ref[:, cols]) + dot_tn(odd[1], p3o_ref[:, cols])
    cols = pl.ds(0, LANES)
    begin = dot_tn(even[0], p3e_ref[:, cols]) + dot_tn(even[1], p3e_ref[:, cols])
    rows = lax.broadcasted_iota(jnp.int32, (half, LANES), 0)
    out_ref[pl.ds(ROW_K3, half, stride=45), :] = begin + jnp.where(rows == 0, 0.0, pltpu.roll(tail, 1, 0))
    tail = tail[half - 1 : half]
    ds3_ref[...] = jnp.zeros_like(ds3_ref)
    position = lax.broadcasted_iota(jnp.int32, (BOTH, K3P), 1)
    nat = jnp.where(position < LANES // 2, 0.0, two(dot_nn, even, k3e_ref[...]))
    nat = pltpu.roll(nat, K3P - LANES // 2, 1) + jnp.where(
        position < C3 * TAPS, two(dot_nn, odd, k3o_ref[...]), 0.0
    )
    for part in range(3):
        width = min(wide, K3P - part * wide)
        pieces = split2(nat[:, part * wide : part * wide + width])
        by_tap = dot_nt(pieces[0], tm_ref[:, pl.ds(0, width)]) + dot_nt(pieces[1], tm_ref[:, pl.ds(0, width)])
        for tap in range(TAPS):
            q, src_r, src_c, down_r, down_c = tap_source(tap, (), ())
            at = q[0] * 2 + q[1]
            ds3_ref[pl.ds(at * BOTH, BOTH), pl.ds(part * LANES, LANES)] += moved_back(
                by_tap[:, tap * LANES : (tap + 1) * LANES], down_r, down_c, marks
            )
    db2 = rowsum(ds3_ref[...])
    for k in range(2):
        out_ref[ROW_B2 + k : ROW_B2 + k + 1, :] = db2[:, k * LANES : (k + 1) * LANES]
    out_ref[ROW_K3 : ROW_K3 + 1, :] += jnp.where(lane1 < LANES // 2, db2[:, 2 * LANES :], 0.0)
    grad = split2(ds3_ref[...])
    grad_real = (grad[0][:, :C3], grad[1][:, :C3])
    for j in range(TAPS):
        cols = pl.ds(j * LANES, LANES)
        value = dot_tn(grad[0], p2_ref[:, cols]) + dot_tn(grad[1], p2_ref[:, cols])
        out_ref[pl.ds(ROW_K2 + j, C3, stride=TAPS), :] = value[:C3]
    pieces = split2(two(dot_nn, grad, k2_ref[...]))
    dt_ref[...] = two(dot_nt, pieces, tm_ref[...])
    ds2_ref[...] = jnp.zeros_like(ds2_ref)
    for at, rb, cb in all_bits(1):
        for tap in range(TAPS):
            q, src_r, src_c, down_r, down_c = tap_source(tap, rb, cb)
            to = (q[0] * 2 + q[1]) * 4 + plane_of(src_r, src_c)
            ds2_ref[pl.ds(to * BOTH, BOTH), :] += moved_back(
                dt_ref[pl.ds(at * BOTH, BOTH), pl.ds(tap * LANES, LANES)], down_r, down_c, marks
            )
    out_ref[ROW_B1 : ROW_B1 + 1, :] = rowsum(ds2_ref[...])
    grad = split2(ds2_ref[...])
    few = C2 // 2
    for j in range(5):
        cols = pl.ds(j * LANES, LANES)
        dk1t_ref[j] = dot_tn(grad[0], p1_ref[:, cols]) + dot_tn(grad[1], p1_ref[:, cols])
    evens, odds = (
        two(
            dot_nt,
            split2(jnp.concatenate([dk1t_ref[j, pl.ds(odd, few, stride=2), :] for j in range(5)], axis=1)),
            t64_ref[odd],
        )
        for odd in range(2)
    )
    for j in range(9):
        if j < 4:
            value = evens[:, j * LANES : (j + 1) * LANES]
        elif j == 4:
            value = evens[:, 4 * LANES :] + odds[:, :LANES]
        else:
            value = odds[:, (j - 4) * LANES : (j - 3) * LANES]
        out_ref[pl.ds(ROW_K1 + j, few, stride=9), :] = value
    ds1_ref[...] = jnp.zeros_like(ds1_ref)
    for pair in range(5):
        values = two(dot_nn, grad, k1t_ref[:, pl.ds(pair * LANES, LANES)])
        for at, rb, cb in all_bits(2):
            here = values[at * BOTH : (at + 1) * BOTH]
            for side in range(2):
                tap = 2 * pair + side
                if tap >= TAPS:
                    continue
                q, src_r, src_c, down_r, down_c = tap_source(tap, rb, cb)
                to = (q[0] * 2 + q[1]) * 16 + plane_of(src_r, src_c)
                mine = (lane < C1) if side == 0 else (lane >= C1)
                ds1_ref[pl.ds(to * BOTH, BOTH), :] += moved_back(
                    jnp.where(mine, here, 0.0), down_r, down_c, marks
                )
    db0 = rowsum(ds1_ref[...])
    db0 = db0 + pltpu.roll(db0, LANES // 2, 1)
    stem = jnp.zeros((LANES, 2 * LANES), f32)
    for at in range(4):
        span = pl.ds(at * 16 * BOTH, 16 * BOTH)
        grad = split2(ds1_ref[span, :])
        stem = stem + (dot_tn(grad[0], p0_ref[span, :]) + dot_tn(grad[1], p0_ref[span, :]))
    stem = stem[:C1] + stem[C1:]
    depth = IN_CH * 49
    held = jnp.zeros((1, 3 * LANES), f32)
    done = 0
    for at in range(C1):
        row, shift = divmod(depth * at, LANES)
        line = jnp.concatenate([stem[at : at + 1], jnp.zeros((1, LANES), f32)], axis=1)
        if shift:
            line = pltpu.roll(line, shift, 1)
        while done < row:
            out_ref[done : done + 1, :] = held[:, :LANES]
            held = jnp.concatenate([held[:, LANES:], jnp.zeros((1, LANES), f32)], axis=1)
            done += 1
        held = held + line
    out_ref[done : done + 1, :] = held[:, :LANES]
    if done < ROW_B0:
        out_ref[ROW_B0 : ROW_B0 + 1, :] = held[:, LANES : 2 * LANES]
    out_ref[ROW_B0 : ROW_B0 + 1, :] += jnp.where(lane1 < LANES // 2, 0.0, db0)

    lead = 5

    def put(name, value):
        for k in range(value.shape[1] // LANES):
            at = lead + REST[name] + k
            rest_ref[at : at + 1, :] = value[:, k * LANES : (k + 1) * LANES]

    rest_ref[0:8, :] = jnp.zeros((8, LANES), f32)
    put("b3", small_ref[0:1, :])
    for k in range(6):
        at = lead + REST["block"] + 4 * k
        for i in range(4):
            rest_ref[at + i : at + i + 1, :] = dblock_ref[k : k + 1, i * LANES : (i + 1) * LANES]
    put("fb1", dfb1_ref[0:1, :])
    put("fb2", small_ref[1:2, :])
    put("final", jnp.concatenate([small_ref[2:3, :], small_ref[3:4, :]], axis=1))
    dlog = dlog_ref[...]
    put("hb", dlog[0:1] + dlog[1:2])
    rest_ref[lead + REST["end"] : lead + REST["end"] + 11, :] = jnp.zeros((11, LANES), f32)
    pooled = pooled_ref[...]
    in_group, in_place, own_row = head_masks()
    picked = jnp.where(in_place, jnp.where(own_row, pooled[0:1, :], pooled[1:2, :]), 0.0).astype(bf16)
    by_group = dot_nt(in_group.astype(bf16), picked)
    padded = jnp.concatenate([dlog, jnp.zeros((8, LANES), f32)], axis=1)
    groups = C4 // GROUP
    written = -1
    for place in range(GROUP):
        at, shift = divmod(CLS * place, LANES)
        window = pltpu.roll(padded, shift, 1) if shift else padded
        ours = by_group[:, MICRO * place : MICRO * place + 1]
        others = by_group[:, MICRO * place + 1 : MICRO * place + 2]
        for k in range(CLSP // LANES + 1):
            if (at + k) * LANES >= CLS * (place + 1):
                break
            block = slice(k * LANES, (k + 1) * LANES)
            value = ours * window[0:1, block] + others * window[1:2, block]
            target = pl.ds(lead + REST["head"] + at + k, groups, stride=SPAN)
            if at + k == written:
                rest_ref[target, :] += value
            else:
                rest_ref[target, :] = value
            written = at + k
    first = ROW_B3 + 3
    out_ref[ROW_B3 : first, :] = halves(rest_ref[lead - 1 : lead + 2, :], rest_ref[lead : lead + 3, :])
    out_ref[ROW_B3 : ROW_B3 + 1, :] += tail
    step = 508
    for at in range(0, REST["end"], step):
        out_ref[first + at : first + at + step, :] = halves(
            rest_ref[lead + 2 + at : lead + 2 + at + step, :], rest_ref[lead + 3 + at : lead + 3 + at + step, :]
        )
    end = first + REST["end"]
    out_ref[end : out_ref.shape[0], :] = jnp.zeros((out_ref.shape[0] - end, LANES), f32)


def passes(a, b, dot, many):
    small = dot(a[0], b[1]) + dot(a[1], b[0])
    if many:
        small = small + (dot(a[0], b[2]) + dot(a[1], b[1]) + dot(a[2], b[0]))
    return dot(a[0], b[0]) + small


def gram_kernel(scale_ref, sums_ref, momentum_ref, loss_ref, ortho_ref, new_ref, packed_ref):
    grad = sums_ref[...] * scale_ref[0]
    new = 0.95 * momentum_ref[...] + grad
    new_ref[...] = new
    ortho = grad + 0.95 * new
    ortho_ref[...] = ortho
    parts = split3(ortho)

    def cut(k):
        return tuple(p[:, k * LANES : (k + 1) * LANES] for p in parts)

    for at, (i, j) in enumerate(PAIRS):
        block = passes(cut(i), cut(j), dot_tn, True)
        if at == 0:
            row = lax.broadcasted_iota(jnp.int32, block.shape, 0)
            col = lax.broadcasted_iota(jnp.int32, block.shape, 1)
            block = jnp.where((row == LANES - 1) & (col == 0), loss_ref[0:1, 0:1], block)
        packed_ref[pl.ds(at * LANES, LANES), :] = block


def newton_steps(gram, ortho, steps, last):
    wide_row = lax.broadcasted_iota(jnp.int32, (C4, C4), 0)
    wide_col = lax.broadcasted_iota(jnp.int32, (C4, C4), 1)
    for iteration in steps:
        many = iteration == 0
        split = split3 if many else split2
        parts = split(gram)
        poly = jnp.where(wide_row == wide_col, 3.4445, 0.0) + (
            -4.775 * gram + 2.0315 * passes(parts, parts, dot_nn, many)
        )
        poly_parts = split(poly)
        ortho = passes(split(ortho), poly_parts, dot_nn, many)
        if iteration < last:
            gram = passes(split(passes(poly_parts, parts, dot_nn, many)), poly_parts, dot_nn, many)
    return gram, ortho


def newton_first_kernel(steps, packed_ref, ortho_ref, out_ref, gram_ref, loss_ref):
    row = lax.broadcasted_iota(jnp.int32, (LANES, LANES), 0)
    col = lax.broadcasted_iota(jnp.int32, (LANES, LANES), 1)
    trace = jnp.zeros((1, 1), f32)
    for at, (i, j) in enumerate(PAIRS):
        block = packed_ref[pl.ds(at * LANES, LANES), :]
        if at == 0:
            loss_ref[...] = jnp.broadcast_to(block[LANES - 1 : LANES, 0:1], (8, LANES))
            block = jnp.where((row == LANES - 1) & (col == 0), block.T, block)
        gram_ref[pl.ds(i * LANES, LANES), pl.ds(j * LANES, LANES)] = block
        if i == j:
            trace = trace + total(jnp.where(row == col, block, 0.0))
        else:
            gram_ref[pl.ds(j * LANES, LANES), pl.ds(i * LANES, LANES)] = block.T
    inverse = 1.0 / (jnp.sqrt(trace) + 1e-07)
    gram, ortho = newton_steps(
        gram_ref[...] * (inverse * inverse), ortho_ref[...] * inverse, range(steps), NS_ITERS - 1
    )
    gram_ref[...] = gram
    out_ref[...] = ortho


def newton_last_kernel(steps, unused_ref, gram_ref, ortho_ref, out_ref):
    unused_gram, ortho = newton_steps(gram_ref[...], ortho_ref[...], range(steps, NS_ITERS), NS_ITERS - 1)
    out_ref[...] = ortho


def shape(*dims, dtype=f32):
    return jax.ShapeDtypeStruct(dims, dtype)


def kernel_call(body, outs, scratch, smem, kept, count, micros):
    vmem = pl.BlockSpec(memory_space=pltpu.VMEM)
    scalar = pl.BlockSpec(memory_space=pltpu.SMEM)
    anywhere = pl.BlockSpec(memory_space=pl.ANY)
    return pl.pallas_call(
        body,
        out_shape=outs,
        in_specs=[scalar] * smem + [anywhere] * kept + [vmem] * (count - smem - kept),
        out_specs=[vmem] * len(outs),
        scratch_shapes=scratch,
        compiler_params=pltpu.CompilerParams(vmem_limit_bytes=60 * 1024 * 1024),
        cost_estimate=pl.CostEstimate(flops=10**6, bytes_accessed=micros * 3_000_000, transcendentals=0),
    )


def pack_kernel(valid_ref, mats_ref, flat_ref, out_ref):
    share = mats_ref.shape[2]
    for mat in range(2):
        turned = mats_ref[mat].T.astype(bf16)
        for part in range(C4 // LANES):
            at = (mat * (C4 // LANES) + part) * share
            out_ref[pl.ds(at, share), :] = turned[:, part * LANES : (part + 1) * LANES]
    rows = 2 * share * C4 // LANES
    count = flat_ref.shape[0]
    out_ref[pl.ds(rows, count), :] = flat_ref[...].astype(bf16)
    left = out_ref.shape[0] - rows - count
    counted = (valid_ref[0] + valid_ref[1]).astype(f32)
    out_ref[pl.ds(rows + count, left), :] = jnp.full((left, LANES), counted, f32).astype(bf16)


def run_pack(valid, mats, flat):
    rows = 2 * mats.shape[2] * C4 // LANES + flat.shape[0]
    outs = [shape((rows // 16 + 1) * 16, LANES, dtype=bf16)]
    return kernel_call(pack_kernel, outs, [], 1, 0, 3, 2)(valid, mats, flat)[0]


def run_forward(args, rows, share, flat_share):
    half = C4 // 2
    outs = [
        shape(16 * BOTH, 5 * LANES, dtype=bf16),
        shape(4 * BOTH, TAPS * LANES, dtype=bf16),
        shape(BOTH, K3P, dtype=bf16),
        shape(BOTH, K3P, dtype=bf16),
        shape(C2, 5 * LANES, dtype=bf16),
        shape(C3P, TAPS * LANES, dtype=bf16),
        shape(half, K3P, dtype=bf16),
        shape(half, K3P, dtype=bf16),
        shape(BOTH, C4),
        shape(HID, half),
        shape(HID, half),
        shape(HID, half),
        shape(HID, half),
        shape(8, C4),
        shape(8, HID),
        shape(8, C4),
        shape(8, C4),
        shape(8, CLSP),
        shape(8, LANES),
    ]
    scratch = [
        pltpu.VMEM((64 * BOTH, LANES), f32),
        pltpu.VMEM((16 * BOTH, LANES), f32),
        pltpu.VMEM((4 * BOTH, C3P), f32),
        pltpu.VMEM((4 * BOTH, TAPS * LANES), bf16),
        pltpu.VMEM((3 * BOTH, TAPS * LANES), bf16),
        pltpu.VMEM((BOTH, HID), f32),
        pltpu.VMEM((C1, 2 * LANES), f32),
        pltpu.VMEM((5, C2, LANES), f32),
        pltpu.VMEM((REST["head"], LANES), f32),
        pltpu.VMEM((C4 // GROUP, (SPAN + 1) * LANES), bf16),
        pltpu.VMEM((C4 // GROUP, (SPAN + 1) * LANES), f32),
        pltpu.VMEM((2, C4 // LANES, HID // share, share, LANES), bf16),
        pltpu.SemaphoreType.DMA((2 * C4 // LANES,)),
    ]
    if flat_share % LANES == 0:
        got = args[2]
        scratch += [
            pltpu.VMEM((got.shape[0], got.shape[1] - rows, LANES), bf16),
            pltpu.SemaphoreType.DMA((1,)),
            pltpu.VMEM((got.shape[0] * flat_share // LANES, LANES), f32),
        ]
    body = functools.partial(forward_kernel, rows, share, flat_share)
    return kernel_call(body, outs, scratch, 2, 1, len(args), 25)(*args)


def run_backward(args, flat_rows):
    scratch = [
        pltpu.VMEM((4 * BOTH, C3P), f32),
        pltpu.VMEM((16 * BOTH, LANES), f32),
        pltpu.VMEM((64 * BOTH, LANES), f32),
        pltpu.VMEM((4 * BOTH, TAPS * LANES), f32),
        pltpu.VMEM((5, C2, LANES), f32),
        pltpu.VMEM((REST["end"] + 16, LANES), f32),
    ]
    outs = [shape(flat_rows, LANES)]
    return kernel_call(backward_kernel, outs, scratch, 0, 2, len(args), 20)(*args)[0]


def run_gram(scale, sums, momentum, loss):
    rows = momentum.shape[0]
    outs = [shape(rows, C4), shape(rows, C4), shape(len(PAIRS) * LANES, LANES)]
    return kernel_call(gram_kernel, outs, [], 1, 0, 4, 4)(scale, sums, momentum, loss)


def run_newton_first(packed, ortho, steps):
    outs = [shape(*ortho.shape), shape(C4, C4), shape(8, LANES)]
    return kernel_call(functools.partial(newton_first_kernel, steps), outs, [], 0, 0, 2, 12)(packed, ortho)


def run_newton_last(tie, gram, ortho, steps):
    outs = [shape(*ortho.shape)]
    return kernel_call(functools.partial(newton_last_kernel, steps), outs, [], 0, 1, 3, 8)(tie, gram, ortho)[0]


def patches(images, resolution, partner_col, mix_col):
    pictures = images[:, 0].astype(f32)
    dims = (1, 1, RES_L, RES_L)
    inside = (lax.broadcasted_iota(jnp.int32, dims, 2) < resolution) & (
        lax.broadcasted_iota(jnp.int32, dims, 3) < resolution
    )
    mixing = mix_col[:, None, None, None]
    other = jnp.where(partner_col[:, None, None, None] == 0, pictures[0][None], pictures[1][None])
    pixels = jnp.where(inside, mixing * pictures + (1.0 - mixing) * other, 0.0).astype(bf16)
    depth = IN_CH * 49
    pick = jnp.eye(depth, dtype=bf16).reshape(IN_CH, 7, 7, depth).transpose(1, 2, 0, 3)
    columns = lax.conv_general_dilated(
        pixels,
        pick,
        (4, 4),
        ((2, 2), (2, 2)),
        dimension_numbers=("NCHW", "HWIO", "NHWC"),
        preferred_element_type=f32,
    ).astype(bf16)
    columns = columns.reshape(MICRO, SIDE, 2, 2, 2, SIDE, 2, 2, 2, depth)
    columns = columns.transpose(4, 8, 3, 7, 2, 6, 0, 1, 5, 9).reshape(64, MICRO, SIDE * SIDE, depth)
    columns = jnp.pad(columns, ((0, 0), (0, 0), (0, ROWS - SIDE * SIDE), (0, 2 * LANES - depth)))
    return columns.reshape(64 * BOTH, 2 * LANES)


def tap_orders():
    row = lax.broadcasted_iota(jnp.int32, (TAPS * LANES, TAPS * LANES), 0)
    col = lax.broadcasted_iota(jnp.int32, (TAPS * LANES, TAPS * LANES), 1)
    forth = ((row % LANES) * TAPS + row // LANES == col).astype(bf16)
    dims = (2, 5 * LANES, 5 * LANES)
    row = lax.broadcasted_iota(jnp.int32, dims, 1) - C1 * lax.broadcasted_iota(jnp.int32, dims, 0)
    col = lax.broadcasted_iota(jnp.int32, dims, 2)
    real = (row >= 0) & (row < TAPS * C1)
    row = jnp.maximum(row, 0)
    back = (real & ((row % TAPS) * C1 + row // TAPS == col)).astype(bf16)
    row = lax.broadcasted_iota(jnp.int32, (C4, C4), 0)
    col = lax.broadcasted_iota(jnp.int32, (C4, C4), 1)
    merge = ((row % (C4 // 2)) * 2 + row // (C4 // 2) == col).astype(bf16)
    return forth, back, merge


def grid_marks(side):
    row = np.arange(BOTH)
    image, q = row // ROWS, row % ROWS
    y, x = q // SIDE, q % SIDE
    real = q < SIDE * SIDE
    fixed = np.stack([real & (y > 0), real & (x > 0), real & (y > 0) & (x > 0)], 1).astype(np.float32)
    close = (
        (image[:, None] == image[None])
        & (abs(y[:, None] - y[None]) <= 1)
        & (abs(x[:, None] - x[None]) <= 1)
        & real[:, None]
        & real[None]
    )
    inside = jnp.asarray(real) & (jnp.asarray(y) < side) & (jnp.asarray(x) < side)
    near = jnp.where(jnp.asarray(close) & inside[:, None] & inside[None], 1.0, 0.0)
    cells = jnp.maximum(jnp.sum(near, axis=1), 1.0)
    marks = jnp.concatenate(
        [inside.astype(f32)[:, None], jnp.asarray(fixed), (1.0 / cells)[:, None]], axis=1
    )
    return jnp.pad(marks, ((0, 0), (0, LANES - marks.shape[1]))), near.astype(bf16)


def local_inputs(images, group, label_col, partner_col, mix_col, valid_col, core):
    side = RES_S // RES_STEP + group
    columns = patches(images, side * RES_STEP, partner_col, mix_col)
    orders = tap_orders()
    marks, near = grid_marks(side)
    other = jnp.where(partner_col == 0, label_col[0], label_col[1])
    whole = jnp.concatenate([label_col, other, core.astype(jnp.int32)[None]])
    cells = (side * side).astype(f32)
    real = jnp.concatenate([mix_col, valid_col.astype(f32), jnp.stack([cells, cells * C4])])
    return whole, real, columns, orders, marks, near


def first_half(prepared, got, flat, rows, share, flat_share):
    whole, real, columns, (forth, back, merge), marks, near = prepared
    args = [whole, real, got, columns] + flat + [forth, back, merge, marks, near]
    return run_forward(args, rows, share, flat_share)


def second_half(prepared, made, flat_rows, ties):
    columns, (forth, back, merge), marks = prepared[2], prepared[3], prepared[4]
    p1, p2, p3e, p3o, k1t, k2, k3e, k3o, dstream = made[:9]
    args = [dstream, columns, p1, p2, p3e, p3o, k1t, k2, k3e, k3o, forth, back, merge, marks]
    return run_backward(list(ties) + args + list(made[13:18]), flat_rows)


class Ring:
    def __init__(self, count):
        self.count = count
        self.squares = count // 8
        me = lax.axis_index(AXES)
        self.me = me
        self.core = me % 2
        self.low = (me // 2) % 2
        self.high = (me // 4) % 2
        self.corner = (me // 2) % 4
        self.square = me // 8

    def swap(self, value, bits):
        return lax.ppermute(value, AXES, [(i, i ^ bits) for i in range(self.count)])


def pick(value, at, axis):
    return lax.dynamic_index_in_dim(value, at, axis, keepdims=False)


class Scatter:
    def __init__(self, ring, value, high_first):
        self.ring = ring
        self.value = value
        self.order = [(1, ring.high, 4), (2, ring.low, 2)] if high_first else [(2, ring.low, 2), (1, ring.high, 4)]
        self.sent = None

    def prepare(self):
        axis, mine, self.bits = self.order.pop(0)
        if not self.order:
            axis = 1
        self.sent = pick(self.value, 1 - mine, axis)
        self.value = pick(self.value, mine, axis)

    def send(self):
        self.got = self.ring.swap(self.sent, self.bits)

    def add(self):
        self.value = self.value + self.got


def sum_squares(ring, value):
    got = [ring.swap(pick(value, ring.square ^ j, 0), 8 * j) for j in range(1, ring.squares)]
    return functools.reduce(jnp.add, got, pick(value, ring.square, 0))


def together(scatters, *others):
    values = lax.optimization_barrier(tuple(x.value for x in scatters) + tuple(others))
    for x, value in zip(scatters, values):
        x.value = value
    return values[len(scatters) :]


class ChipSum:
    def __init__(self, ring, value):
        self.ring = ring
        self.shape = value.shape
        self.value = value.reshape(ring.squares, 4, value.shape[0] // (4 * ring.squares), value.shape[1])

    def scatter_corners(self):
        ring = self.ring
        got = [ring.swap(pick(self.value, ring.corner ^ j, 1), 2 * j) for j in range(1, 4)]
        self.value = functools.reduce(jnp.add, got, pick(self.value, ring.corner, 1))

    def scatter_squares(self):
        ring = self.ring
        got = [ring.swap(pick(self.value, ring.square ^ j, 0), 8 * j) for j in range(1, ring.squares)]
        self.value = functools.reduce(jnp.add, got, pick(self.value, ring.square, 0))

    def gather_squares(self):
        ring = self.ring
        held = jnp.stack([self.value] + [ring.swap(self.value, 8 * j) for j in range(1, ring.squares)])
        self.value = jnp.stack([pick(held, ring.square ^ j, 0) for j in range(ring.squares)])

    def gather_corners(self):
        ring = self.ring
        held = jnp.stack([self.value] + [ring.swap(self.value, 2 * j) for j in range(1, 4)])
        held = jnp.stack([pick(held, ring.corner ^ j, 0) for j in range(4)], axis=1)
        return held.reshape(self.shape)


def per_device(
    devices_count,
    images,
    group_ids,
    labels,
    partners,
    mix_weights,
    valid,
    flat_params,
    flat_first,
    flat_second,
    mlp_weights,
    mlp_momentum,
):
    ring = Ring(devices_count)
    chips = devices_count // 2
    share = mlp_weights.shape[2]
    flat_share = flat_params.shape[0]
    rows = 2 * share * C4 // LANES
    flat_rows = -(-flat_share // LANES)
    spare = flat_rows * LANES - flat_share
    mine = jnp.pad(flat_params, (0, spare)) if spare else flat_params
    sent = run_pack(valid.reshape(MICRO), mlp_weights, mine.reshape(flat_rows, LANES))
    got = lax.all_gather(sent, AXES, axis=0, tiled=False)
    prepared = local_inputs(
        images, group_ids[0], labels[:, 0], partners[:, 0], mix_weights[:, 0], valid[:, 0], ring.core
    )
    momentum = mlp_momentum.transpose(0, 2, 1)

    def of_both_cores(mine, theirs):
        at_first = ring.core == 0
        return jnp.concatenate([jnp.where(at_first, mine, theirs), jnp.where(at_first, theirs, mine)])

    momentum_rows = of_both_cores(
        pick(momentum, ring.core, 0), ring.swap(pick(momentum, 1 - ring.core, 0), 1)
    )
    if flat_share % LANES:
        whole_flat = [
            got[:, rows : rows + flat_rows]
            .astype(f32)
            .reshape(devices_count, flat_rows * LANES)[:, :flat_share]
            .reshape(devices_count * flat_share // LANES, LANES)
        ]
    else:
        whole_flat = []
    valid_total = jnp.maximum(jnp.sum(got[:, rows + flat_rows, 0].astype(f32)), 1.0)
    scale = 1.0 / valid_total

    made = first_half(prepared, got, whole_flat, rows, share, flat_share)
    keep_a, keep_b, send_a, send_b = made[9:13]
    loss = made[18]
    loss = loss + ring.swap(loss, 1)
    square = (ring.squares, 2, 2, 2 * share, C4 // 2)
    core_a = (keep_a + ring.swap(send_a, 1)).reshape(square)
    core_b = (keep_b + ring.swap(send_b, 1)).reshape(square)
    mlp = [Scatter(ring, core_a, True), Scatter(ring, core_b, False)]
    for x in mlp:
        x.prepare()
        x.send()

    each = -(-(devices_count * flat_share) // (devices_count * LANES * 8)) * 8
    ties = [x.sent[(0,) * (x.sent.ndim - 2)][:8, :LANES] for x in mlp]
    dflat = second_half(prepared, made, devices_count * each, ties)
    dflat = dflat.reshape(chips, 2, each, LANES)
    for x in mlp:
        x.add()
    (dflat,) = together(mlp, dflat)
    for x in mlp:
        x.prepare()
        x.send()
    dflat = pick(dflat, ring.core, 1) + ring.swap(pick(dflat, 1 - ring.core, 1), 1)
    dflat = dflat.reshape(ring.squares, 2, 2, each, LANES)
    cut = -(-each // 16) * 8
    flat = [Scatter(ring, dflat[:, :, :, :cut], True), Scatter(ring, dflat[:, :, :, cut:], False)]
    for x in mlp:
        x.add()
    together(mlp + flat)
    for x in flat:
        x.prepare()
        x.send()
    sums = sum_squares(ring, jnp.concatenate([x.value for x in mlp], axis=2))
    ortho, momentum_new, packed = run_gram(scale[None], sums, momentum_rows, loss)
    grams = ChipSum(ring, packed)
    grams.scatter_corners()
    for x in flat:
        x.add()
    together([grams] + flat)
    grams.scatter_squares()
    for x in flat:
        x.prepare()
        x.send()
    grams.gather_squares()
    for x in flat:
        x.add()
    together([grams] + flat)
    sum_flat = sum_squares(ring, jnp.concatenate([x.value for x in flat], axis=1))
    steps = 2
    ortho, gram, loss_total = run_newton_first(grams.gather_corners(), ortho, steps)
    lag = (devices_count - 1) * (each * LANES - flat_share)
    hops = -(-lag // (each * LANES))
    tail = min(each, -(-lag // (8 * LANES)) * 8)
    before = [
        lax.ppermute(sum_flat[each - tail :], AXES, [(i, i + h) for i in range(devices_count - h)])
        for h in range(hops, 0, -1)
    ]
    ortho = run_newton_last(sum_flat[each - 8 :], gram, ortho, steps)
    sum_flat = jnp.concatenate(before + [sum_flat])
    start = len(before) * tail * LANES - ring.me * (each * LANES - flat_share)
    if flat_share % LANES == 0:
        sum_flat = lax.dynamic_slice_in_dim(sum_flat, start // LANES, flat_rows, 0).reshape(-1)
    else:
        sum_flat = lax.dynamic_slice_in_dim(sum_flat.reshape(-1), start, flat_share, 0)
    sum_flat = sum_flat * scale
    first_new = 0.9 * flat_first + 0.1 * sum_flat
    second_new = 0.999 * flat_second + 0.001 * sum_flat * sum_flat
    first_hat = first_new / (1.0 - 0.9**STEP)
    second_hat = second_new / (1.0 - 0.999**STEP)
    params_new = flat_params - 0.02 * (
        first_hat / (jnp.sqrt(second_hat) + 1e-08) + 0.05 * flat_params
    )

    def to_owners(by_chip):
        parts = by_chip.reshape(2, share, C4)
        mine, theirs = pick(parts, ring.core, 0), ring.swap(pick(parts, 1 - ring.core, 0), 1)
        at_first = ring.core == 0
        return jnp.stack([jnp.where(at_first, mine, theirs), jnp.where(at_first, theirs, mine)])

    mats = mlp_weights.transpose(0, 2, 1)
    weights_new = mats * (1.0 - 0.1 * 0.05) - 0.1 * 0.2 * math.sqrt(HID) * to_owners(ortho)
    return (
        loss_total[0, 0],
        params_new,
        first_new,
        second_new,
        weights_new.transpose(0, 2, 1),
        to_owners(momentum_new).transpose(0, 2, 1),
    )


def solution(mesh):
    placed = (
        P(None, AXES, None, None, None),
        P(AXES),
        P(None, AXES),
        P(None, AXES),
        P(None, AXES),
        P(None, AXES),
        P(AXES),
        P(AXES),
        P(AXES),
        P(None, None, AXES),
        P(None, None, AXES),
    )
    devices_count = math.prod(mesh.shape[axis] for axis in AXES)
    return jax.shard_map(
        functools.partial(per_device, devices_count),
        mesh=mesh,
        in_specs=placed,
        out_specs=(
            P(),
            P(AXES),
            P(AXES),
            P(AXES),
            P(None, None, AXES),
            P(None, None, AXES),
        ),
        check_vma=False,
    )
```

```python
import functools
import math

import jax
import jax.numpy as jnp
import numpy as np
from jax import lax
from jax.experimental import pallas as pl
from jax.experimental.pallas import tpu as pltpu
from jax.sharding import PartitionSpec as P

C1 = 64
C2 = 128
C3 = 320
C4 = 512
HID = 2048
CLS = 1000
IN_CH = 3
RES_S = 96
RES_L = 160
RES_STEP = 32
MICRO = 2
NS_ITERS = 5
STEP = 10

AXES = ("fsdp", "ns")
LANES = 128
SIDE = 5
ROWS = 32
BOTH = MICRO * ROWS
C3P = 384
CLSP = 1024
K3P = 2944
TAPS = 9

f32 = jnp.float32
bf16 = jnp.bfloat16
norm_epsilon = 1e-05

NARROW = C1 * IN_CH * 49
ROW_B0 = NARROW // LANES
ROW_K1 = 74
ROW_B1 = 650
ROW_K2 = 651
ROW_B2 = 3531
ROW_K3 = 3533
ROW_B3 = 15053
REST = {"b3": 0, "block": 4, "fb1": 28, "fb2": 44, "final": 48, "head": 56, "hb": 4056, "end": 4064}
GROUP = 16
SPAN = GROUP * CLS // LANES
PAIRS = [(i, j) for i in range(4) for j in range(i, 4)]


def dot_nn(a, b):
    return lax.dot_general(a, b, (((1,), (0,)), ((), ())), preferred_element_type=f32)


def dot_nt(a, b):
    return lax.dot_general(a, b, (((1,), (1,)), ((), ())), preferred_element_type=f32)


def dot_tn(a, b):
    return lax.dot_general(a, b, (((0,), (0,)), ((), ())), preferred_element_type=f32)


def split2(x):
    hi = x.astype(bf16)
    return hi, (x - hi.astype(f32)).astype(bf16)


def split3(x):
    hi = x.astype(bf16)
    rest = x - hi.astype(f32)
    mid = rest.astype(bf16)
    return hi, mid, (rest - mid.astype(f32)).astype(bf16)


def two(dot, pair, other):
    return dot(pair[0], other) + dot(pair[1], other)


def borrow(bits):
    out = list(bits)
    for at, bit in enumerate(out):
        if bit:
            out[at] = 0
            return tuple(out), 0
        out[at] = 1
    return tuple(out), 1


def tap_source(tap, row_bits, col_bits):
    r, c = divmod(tap, 3)
    src_r, down_r = (row_bits, 0) if r else borrow(row_bits)
    src_c, down_c = (col_bits, 0) if c else borrow(col_bits)
    return (int(r != 1), int(c != 1)), src_r, src_c, down_r, down_c


def plane_of(row_bits, col_bits):
    at = 0
    for r, c in zip(row_bits, col_bits):
        at = at * 4 + r * 2 + c
    return at


def stem_plane(quarter, row_bits, col_bits):
    row = quarter[0] + 2 * row_bits[0] + 4 * row_bits[1]
    return row * 8 + quarter[1] + 2 * col_bits[0] + 4 * col_bits[1]


def all_bits(pairs):
    for at in range(4**pairs):
        digits = [(at >> (2 * (pairs - 1 - k))) & 3 for k in range(pairs)]
        yield at, tuple(d >> 1 for d in digits), tuple(d & 1 for d in digits)


def moved(value, down_r, down_c, marks):
    if not (down_r or down_c):
        return value
    step = SIDE * down_r + down_c
    column = {(1, 0): 1, (0, 1): 2, (1, 1): 3}[(down_r, down_c)]
    return pltpu.roll(value, step, 0) * marks[:, column : column + 1]


def moved_back(value, down_r, down_c, marks):
    if not (down_r or down_c):
        return value
    step = SIDE * down_r + down_c
    column = {(1, 0): 1, (0, 1): 2, (1, 1): 3}[(down_r, down_c)]
    return pltpu.roll(value * marks[:, column : column + 1], BOTH - step, 0)


def erf(x):
    x = jnp.clip(x, -3.832506856900711, 3.832506856900711)
    s = x * x
    top = 2.2905065861350646e-4
    for coef in (3.4082910107109506e-3, 5.0955695062380861e-2, 1.8520832239976145e-1, 1.128379143519084):
        top = top * s + coef
    low = -1.1791602954361697e-7
    for coef in (
        2.3547966471313185e-5,
        1.0179625278914885e-3,
        1.4070470171167667e-2,
        1.1098505178285362e-1,
        4.9746925110067538e-1,
        1.0,
    ):
        low = low * s + coef
    return x * top / low


def total(x):
    return jnp.sum(jnp.sum(x, axis=1, keepdims=True), axis=0, keepdims=True)


def norm_images(value, mask, count):
    parts, scales = [], []
    for m in range(MICRO):
        v = value[m * ROWS : (m + 1) * ROWS]
        k = mask[m * ROWS : (m + 1) * ROWS]
        center = (v - total(v * k) / count) * k
        scale = lax.rsqrt(total(center * center) / count + norm_epsilon)
        parts.append(center * scale)
        scales.append(scale)
    return jnp.concatenate(parts, axis=0), scales


def norm_images_back(grad, hat, scales, gain, mask, count):
    parts = []
    for m in range(MICRO):
        at = slice(m * ROWS, (m + 1) * ROWS)
        g = grad[at] * gain
        h = hat[at]
        parts.append((g - total(g) / count - h * (total(g * h) / count)) * scales[m] * mask[at])
    return jnp.concatenate(parts, axis=0)


def rowsum(x):
    return jnp.sum(x, axis=0, keepdims=True)


def halves(low, high):
    lane = lax.broadcasted_iota(jnp.int32, low.shape, 1)
    return jnp.where(lane < LANES // 2, pltpu.roll(low, LANES // 2, 1), pltpu.roll(high, LANES // 2, 1))


def lanes_of(ref, row, count):
    return jnp.concatenate([ref[row + at : row + at + 1, :] for at in range(count)], axis=1)


def head_masks():
    row = lax.broadcasted_iota(jnp.int32, (C4 // GROUP, C4), 0)
    col = lax.broadcasted_iota(jnp.int32, (C4 // GROUP, C4), 1)
    return col // GROUP == row, col % GROUP == row // MICRO, row % MICRO == 0


class Copies:
    def __init__(self, sems):
        self.sems = sems
        self.count = 2

    def start_shared(self, source, target):
        pltpu.make_async_copy(source, target, self.sems.at[0]).start()

    def start_out(self, source, target):
        pltpu.make_async_copy(source, target, self.sems.at[1]).start()

    def out(self, source):
        return pltpu.make_async_copy(source, source, self.sems.at[1])

    def shared(self, target):
        return pltpu.make_async_copy(target, target, self.sems.at[0])

    def start(self, source, target):
        copy = self.make(source, target)
        copy.start()
        return copy

    def make(self, source, target):
        copy = pltpu.make_async_copy(source, target, self.sems.at[self.count])
        self.count += 1
        return copy


def pieces_of(gathered):
    for number, (unused_array, masks, base) in enumerate(gathered):
        for place in range(2 ** len(masks)):
            index, owner = [], base
            for k, mask in enumerate(masks):
                bit = (place >> k) & 1
                index.append(bit)
                owner ^= mask * bit
            yield number, tuple(index), owner


def conv_kernel(flat_share, *refs):
    if flat_share % LANES:
        conv_body(None, None, *refs)
    else:
        conv_body(flat_share, refs[1], refs[0], refs[-1], *refs[2:-1])


def conv_body(
    flat_share,
    got_hbm,
    whole_ref,
    flat_ref,
    p0_hbm,
    tm_hbm,
    t64_hbm,
    pm_hbm,
    marks_ref,
    p1_hbm,
    p2_hbm,
    p3e_hbm,
    p3o_hbm,
    k1t_hbm,
    k2_hbm,
    k3e_hbm,
    k3o_hbm,
    stream_ref,
    rest_ref,
    wide_ref,
    hb_ref,
    count_ref,
    p0_ref,
    tm_ref,
    t64_ref,
    pm_ref,
    p1_ref,
    p2_ref,
    p3e_ref,
    p3o_ref,
    k1t_ref,
    k2_ref,
    k3e_ref,
    k3o_ref,
    s1_ref,
    s2_ref,
    s3_ref,
    t2_ref,
    t3_ref,
    w0_ref,
    k1f_ref,
    sems,
    *near_refs,
):
    copies = Copies(sems)
    if got_hbm is not None:
        near_ref = near_refs[0]
        flat_copy = copies.start(got_hbm, near_ref)
    p0_copy = copies.start(p0_hbm, p0_ref)
    t64_copy = copies.start(t64_hbm, t64_ref)
    tm_copy = copies.start(tm_hbm, tm_ref)
    pm_copy = copies.start(pm_hbm, pm_ref)
    outward = []
    if got_hbm is not None:
        flat_copy.wait()
        flat_rows = flat_share // LANES
        counted = jnp.zeros((1, LANES), f32)
        for at in range(near_ref.shape[0]):
            flat_ref[pl.ds(at * flat_rows, flat_rows), :] = near_ref[at, pl.ds(0, flat_rows), :].astype(f32)
            counted = counted + near_ref[at, pl.ds(flat_rows, 1), :].astype(f32)
        count_ref[...] = jnp.broadcast_to(counted, (8, LANES))
    else:
        count_ref[...] = jnp.zeros((8, LANES), f32)
    marks = marks_ref[...]
    lane = lax.broadcasted_iota(jnp.int32, (BOTH, LANES), 1)
    lane1 = lax.broadcasted_iota(jnp.int32, (1, LANES), 1)
    depth = IN_CH * 49
    for at in range(C1):
        row, shift = divmod(depth * at, LANES)
        line = lanes_of(flat_ref, row, 3)
        if shift:
            line = pltpu.roll(line, 3 * LANES - shift, 1)
        w0_ref[at : at + 1, :] = line[:, : 2 * LANES]
    w0 = w0_ref[...].astype(bf16)
    w0 = jnp.concatenate([w0, w0], axis=0)
    b0 = flat_ref[ROW_B0 : ROW_B0 + 1, :]
    b0 = jnp.where(lane1 < C1, pltpu.roll(b0, C1, 1), b0)
    quarter = 16 * BOTH
    p0_copy.wait()
    for at in range(4):
        span = pl.ds(at * quarter, quarter)
        s1_ref[span, :] = (dot_nt(p0_ref[span, :], w0) + b0).astype(bf16).astype(f32)

    def tap_value(ref, pairs, tap, row_bits, col_bits, cols):
        q, src_r, src_c, down_r, down_c = tap_source(tap, row_bits, col_bits)
        if pairs == 2:
            at = stem_plane(q, src_r, src_c)
        else:
            at = (q[0] * 2 + q[1]) * 4**pairs + plane_of(src_r, src_c)
        return moved(ref[pl.ds(at * BOTH, BOTH), cols], down_r, down_c, marks)

    half = C2 // 2
    t64_copy.wait()
    for odd in range(2):
        block = jnp.concatenate(
            [flat_ref[pl.ds(ROW_K1 + 4 * odd + j, half, stride=9), :].astype(bf16) for j in range(5)], axis=1
        )
        block = dot_nn(block, t64_ref[pl.ds(C1 * (1 - odd), 5 * LANES), :])
        for j in range(5):
            k1f_ref[j, pl.ds(odd, half, stride=2), :] = block[:, j * LANES : (j + 1) * LANES]
    for j in range(5):
        k1t_ref[:, pl.ds(j * LANES, LANES)] = k1f_ref[j].astype(bf16)
    outward.append(copies.start(k1t_ref, k1t_hbm))
    everything = slice(None)
    for at, rb, cb in all_bits(2):
        for pair in range(5):
            left = tap_value(s1_ref, 2, 2 * pair, rb, cb, everything)
            if pair < 4:
                right = tap_value(s1_ref, 2, 2 * pair + 1, rb, cb, everything)
            else:
                right = jnp.zeros_like(left)
            p1_ref[pl.ds(at * BOTH, BOTH), pl.ds(pair * LANES, LANES)] = jnp.where(
                lane < C1, left, right
            ).astype(bf16)
    outward.append(copies.start(p1_ref, p1_hbm))
    b1 = flat_ref[ROW_B1 : ROW_B1 + 1, :]
    s2_ref[...] = (dot_nt(p1_ref[...], k1t_ref[...]) + b1).astype(bf16).astype(f32)
    for j in range(TAPS):
        k2_ref[pl.ds(0, C3), pl.ds(j * LANES, LANES)] = flat_ref[pl.ds(ROW_K2 + j, C3, stride=TAPS), :].astype(bf16)
    k2_ref[pl.ds(C3, C3P - C3), :] = jnp.zeros((C3P - C3, TAPS * LANES), bf16)
    outward.append(copies.start(k2_ref, k2_hbm))
    b2 = lanes_of(flat_ref, ROW_B2, 3)
    b2 = jnp.where(lax.broadcasted_iota(jnp.int32, b2.shape, 1) < C3, b2, 0.0)
    for at, rb, cb in all_bits(1):
        for tap in range(TAPS):
            t2_ref[pl.ds(at * BOTH, BOTH), pl.ds(tap * LANES, LANES)] = tap_value(
                s2_ref, 1, tap, rb, cb, everything
            ).astype(bf16)
    tm_copy.wait()
    p2_ref[...] = dot_nn(t2_ref[...], tm_ref[...]).astype(bf16)
    outward.append(copies.start(p2_ref, p2_hbm))
    s3_ref[...] = (dot_nt(p2_ref[...], k2_ref[...]) + b2).astype(bf16).astype(f32)
    for part in range(3):
        for tap in range(TAPS):
            t3_ref[pl.ds(part * BOTH, BOTH), pl.ds(tap * LANES, LANES)] = tap_value(
                s3_ref, 0, tap, (), (), pl.ds(part * LANES, LANES)
            ).astype(bf16)
    spread = dot_nn(t3_ref[...], tm_ref[...])
    spread = jnp.concatenate([spread[part * BOTH : (part + 1) * BOTH] for part in range(3)], axis=1)
    p3o_ref[...] = spread[:, :K3P].astype(bf16)
    p3e_ref[...] = pltpu.roll(spread, LANES // 2, 1)[:, :K3P].astype(bf16)
    for j in range(K3P // LANES):
        cols = pl.ds(j * LANES, LANES)
        k3e_ref[:, cols] = flat_ref[pl.ds(ROW_K3 + j, C4 // 2, stride=45), :].astype(bf16)
        k3o_ref[:, cols] = flat_ref[pl.ds(ROW_K3 + 23 + j, C4 // 2, stride=45), :].astype(bf16)
    for source, target in ((p3e_ref, p3e_hbm), (p3o_ref, p3o_hbm), (k3e_ref, k3e_hbm), (k3o_ref, k3o_hbm)):
        outward.append(copies.start(source, target))
    pm_copy.wait()
    apart = split3(
        jnp.concatenate([dot_nt(p3e_ref[...], k3e_ref[...]), dot_nt(p3o_ref[...], k3o_ref[...])], axis=1)
    )
    stream = dot_nn(apart[0], pm_ref[...]) + (dot_nn(apart[1], pm_ref[...]) + dot_nn(apart[2], pm_ref[...]))

    stream_ref[...] = stream

    amount = REST["head"]
    rest_ref[...] = halves(flat_ref[ROW_B3 : ROW_B3 + amount, :], flat_ref[ROW_B3 + 1 : ROW_B3 + 1 + amount, :])
    row_hb = ROW_B3 + REST["hb"]
    hb_ref[...] = halves(flat_ref[row_hb : row_hb + 8, :], flat_ref[row_hb + 1 : row_hb + 9, :])
    groups = C4 // GROUP
    row_head = ROW_B3 + REST["head"]
    low = pltpu.roll(flat_ref[pl.ds(row_head, groups, stride=SPAN), :], LANES // 2, 1)
    lane32 = lax.broadcasted_iota(jnp.int32, (groups, LANES), 1)
    for at in range(SPAN):
        high = pltpu.roll(flat_ref[pl.ds(row_head + at + 1, groups, stride=SPAN), :], LANES // 2, 1)
        wide_ref[:, pl.ds(at * LANES, LANES)] = jnp.where(lane32 < LANES // 2, low, high).astype(bf16)
        low = high
    wide_ref[:, pl.ds(SPAN * LANES, LANES)] = jnp.zeros((groups, LANES), bf16)
    for copy in outward:
        copy.wait()


def block_kernel(
    share,
    gathered,
    whole_ref,
    real_ref,
    *refs,
):
    count = [len(half) for half in gathered]
    held = [refs[: count[0]], refs[count[0] : sum(count)]]
    block_body(share, gathered, held, whole_ref, real_ref, *refs[sum(count) :])


def block_body(
    share,
    gathered,
    held,
    whole_ref,
    real_ref,
    stream_ref,
    rest_ref,
    wide_ref,
    hb_ref,
    marks_ref,
    near_ref,
    keep_own_a,
    keep_own_b,
    keep_other_a,
    keep_other_b,
    send_own_a,
    send_own_b,
    send_other_a,
    send_other_b,
    dstream_ref,
    dblock_ref,
    dfb1_ref,
    small_ref,
    pooled_ref,
    dlog_ref,
    loss_ref,
    dmlp_ref,
    hid_ref,
    z_ref,
    per_ref,
    mats_ref,
    sems,
):
    copies = Copies(sems)
    me = whole_ref[5]
    for mat in range(2):
        for number, index, owner in pieces_of(gathered[mat]):
            copies.start_shared(held[mat][number].at[index], mats_ref.at[mat, :, me ^ owner])
    mats_copy = copies.shared(mats_ref)
    marks = marks_ref[...]
    stream = stream_ref[...]
    b3 = lanes_of(rest_ref, REST["b3"], 4)
    gain1, shift1, scale1, gain2, shift2, scale2 = (lanes_of(rest_ref, REST["block"] + 4 * k, 4) for k in range(6))
    fb1 = lanes_of(rest_ref, REST["fb1"], HID // LANES)
    fb2 = lanes_of(rest_ref, REST["fb2"], 4)
    gain3, shift3 = (lanes_of(rest_ref, REST["final"] + 4 * k, 4) for k in range(2))

    stream = stream + b3
    mask = marks[:, 0:1]
    per_count = marks[:, 4:5]
    cells = real_ref[4]
    count = real_ref[5]
    near = near_ref[...]
    hat1, rs1 = norm_images(stream, mask, count)
    u = (hat1 * gain1 + shift1) * mask
    u3 = split3(u)
    around = dot_nn(near, u3[0]) + (dot_nn(near, u3[1]) + dot_nn(near, u3[2]))
    pool = around * per_count - u
    stream1 = stream + scale1 * pool
    hat2, rs2 = norm_images(stream1, mask, count)
    normed = ((hat2 * gain2 + shift2) * mask).astype(bf16)
    mats_copy.wait()
    blocks = C4 // LANES

    def matrix(mat, part):
        return mats_ref[mat, part].reshape(HID, LANES)

    def lanes(x, part):
        return x[:, part * LANES : (part + 1) * LANES]

    hidden = fb1
    for part in range(blocks):
        hidden = hidden + dot_nt(lanes(normed, part), matrix(0, part))
    hid_ref[...] = hidden
    active = (hidden * (0.5 * (1.0 + erf(hidden * math.sqrt(0.5))))).astype(bf16)
    branch = jnp.concatenate([dot_nn(active, matrix(1, part)) for part in range(blocks)], axis=1) + fb2
    stream2 = stream1 + scale2 * branch
    hat3, rs3 = norm_images(stream2, mask, count)
    outs = (hat3 * gain3 + shift3) * mask
    row8 = lax.broadcasted_iota(jnp.int32, (8, 1), 0)
    first, second = row8 == 0, row8 == 1

    def by_row(a, b):
        return jnp.where(first, a, jnp.where(second, b, 0.0))

    pooled = (by_row(rowsum(outs[:ROWS]), rowsum(outs[ROWS:])) / cells).astype(bf16)
    pooled_f = pooled.astype(f32)
    pooled_ref[...] = pooled_f
    in_group, in_place, own_row = head_masks()
    picked = jnp.where(in_place, jnp.where(own_row, pooled_f[0:1, :], pooled_f[1:2, :]), 0.0).astype(bf16)
    by_place = dot_nt(picked, in_group.astype(bf16)).astype(bf16)
    z_ref[...] = dot_nn(by_place, wide_ref[...])
    column = lax.broadcasted_iota(jnp.int32, (8, CLSP), 1)
    hb = lanes_of(hb_ref, 0, 8)
    logits = jnp.zeros((MICRO, CLSP), f32)
    for place in range(GROUP):
        at, shift = divmod(CLS * place, LANES)
        window = z_ref[pl.ds(MICRO * place, MICRO), pl.ds(at * LANES, CLSP + LANES)]
        if shift:
            window = pltpu.roll(window, CLSP + LANES - shift, 1)
        logits = logits + window[:, :CLSP]
    logits = by_row(logits[0:1], logits[1:2]) + hb
    logits = jnp.where(column < CLS, logits, -1e30)
    top = jnp.max(logits, axis=1, keepdims=True)
    powers = jnp.exp(logits - top)
    mass = jnp.sum(powers, axis=1, keepdims=True)
    own = jnp.where(first, whole_ref[0], whole_ref[1])
    other = jnp.where(first, whole_ref[2], whole_ref[3])
    mix = by_row(real_ref[0], real_ref[1])
    target = jnp.where(column == own, mix, 0.0) + jnp.where(column == other, 1.0 - mix, 0.0)
    valid = by_row(real_ref[2], real_ref[3])
    logp = logits - top - jnp.log(mass)
    losses = -jnp.sum(target * logp, axis=1, keepdims=True) * valid
    loss_ref[...] = jnp.broadcast_to(jnp.sum(losses, axis=0, keepdims=True), (8, LANES))
    dlogits = (powers / mass * jnp.sum(target, axis=1, keepdims=True) - target) * valid
    dlog_ref[...] = dlogits
    padded = jnp.concatenate([dlogits, jnp.zeros((8, LANES), f32)], axis=1)
    for place in range(GROUP):
        at, shift = divmod(CLS * place, LANES)
        window = pltpu.roll(padded, shift, 1) if shift else padded
        per_group = two(dot_nt, split2(window), wide_ref[:, pl.ds(at * LANES, CLSP + LANES)])
        per_ref[pl.ds(MICRO * place, MICRO), :] = per_group[:MICRO]
    per3 = split3(per_ref[...])
    ones = in_group.astype(bf16)
    by_channel = dot_nn(per3[0], ones) + (dot_nn(per3[1], ones) + dot_nn(per3[2], ones))
    dpooled = by_row(
        rowsum(jnp.where(in_place & own_row, by_channel, 0.0)),
        rowsum(jnp.where(in_place & ~own_row, by_channel, 0.0)),
    )
    dpooled = dpooled / cells
    douts = jnp.concatenate(
        [
            jnp.broadcast_to(dpooled[0:1], (ROWS, C4)),
            jnp.broadcast_to(dpooled[1:2], (ROWS, C4)),
        ],
        axis=0,
    ) * mask
    row8w = lax.broadcasted_iota(jnp.int32, (8, C4), 0)

    def stack8(values):
        out = jnp.zeros((8, C4), f32)
        for at, v in enumerate(values):
            out = jnp.where(row8w == at, v, out)
        return out

    dgain3, dshift3 = rowsum(douts * hat3), rowsum(douts)
    dstream2 = norm_images_back(douts, hat3, rs3, gain3, mask, count)
    dscale2 = rowsum(dstream2 * branch)
    dbranch = dstream2 * scale2
    dfb2 = rowsum(dbranch)
    dbr = split2(dbranch)
    dactive = None
    for part in range(blocks):
        term = two(dot_nt, (lanes(dbr[0], part), lanes(dbr[1], part)), matrix(1, part))
        dactive = term if dactive is None else dactive + term
    hidden = hid_ref[...]
    slope = 0.5 * (1.0 + erf(hidden * math.sqrt(0.5))) + hidden * (
        jnp.exp(-0.5 * hidden * hidden) * (1.0 / math.sqrt(2.0 * math.pi))
    )
    dhidden = dactive * slope
    dfb1_ref[...] = jnp.broadcast_to(rowsum(dhidden), (8, HID))
    dhid = split2(dhidden)

    tall_dhid = jnp.concatenate(dhid, axis=0)
    tall_normed = jnp.concatenate([normed, normed], axis=0)
    tall_active = jnp.concatenate([active, active], axis=0)
    tall_dbr = jnp.concatenate(dbr, axis=0)
    core, corner_high, corner_low = whole_ref[4], (me // 4) % 2, (me // 2) % 2
    half = C4 // 2
    targets = (
        ((keep_own_a, keep_own_b), (keep_other_a, keep_other_b)),
        ((send_own_a, send_own_b), (send_other_a, send_other_b)),
    )
    each = 2 * share
    batch = max(each, LANES)
    for at in range(HID // LANES):
        cols = slice(at * LANES, (at + 1) * LANES)
        span = pl.ds(at * LANES, LANES)
        for mat, (one, other) in enumerate(((tall_dhid, tall_normed), (tall_active, tall_dbr))):
            value = dot_tn(one[:, cols], other)
            dmlp_ref[mat, 0, span, :] = value[:, :half]
            dmlp_ref[mat, 1, span, :] = value[:, half:]
        if (at + 1) * LANES % batch:
            continue
        for chip in range(((at + 1) * LANES - batch) // each, (at + 1) * LANES // each):
            square, high, low = chip // 4, (chip // 2) % 2, chip % 2
            for side, (bit, mine, place) in enumerate(((high, corner_high, low), (low, corner_low, high))):
                for mat in range(2):
                    for sent in range(2):
                        for away in range(2):
                            copy = (
                                dmlp_ref.at[mat, side, pl.ds(chip * each, each), :],
                                targets[sent][away][side].at[square, place],
                            )
                            pl.when((core == mat ^ sent) & (mine == bit ^ away))(
                                functools.partial(copies.start_out, *copy)
                            )
    dnormed = jnp.concatenate([two(dot_nn, dhid, matrix(0, part)) for part in range(blocks)], axis=1)
    dgain2, dshift2 = rowsum(dnormed * hat2), rowsum(dnormed * mask)
    dstream1 = dstream2 + norm_images_back(dnormed, hat2, rs2, gain2, mask, count)
    dscale1 = rowsum(dstream1 * pool)
    dpool = dstream1 * scale1
    back = split3(dpool * per_count)
    du = dot_nn(near, back[0]) + (dot_nn(near, back[1]) + dot_nn(near, back[2])) - dpool
    dgain1, dshift1 = rowsum(du * hat1), rowsum(du)
    dstream = dstream1 + norm_images_back(du, hat1, rs1, gain1, mask, count)
    dblock_ref[...] = stack8([dgain1, dshift1, dscale1, dgain2, dshift2, dscale2])
    small_ref[...] = stack8([rowsum(dstream), dfb2, dgain3, dshift3])
    dstream_ref[...] = dstream
    copies.out(dmlp_ref).wait()


def backward_kernel(
    unused_one_ref,
    unused_two_ref,
    dstream_ref,
    p0_ref,
    p1_ref,
    p2_ref,
    p3e_ref,
    p3o_ref,
    k1t_ref,
    k2_ref,
    k3e_ref,
    k3o_ref,
    tm_ref,
    t64_ref,
    pm_ref,
    marks_ref,
    dblock_ref,
    dfb1_ref,
    small_ref,
    pooled_ref,
    dlog_ref,
    whole_ref,
    keep_a_hbm,
    keep_b_hbm,
    send_a_hbm,
    send_b_hbm,
    out_ref,
    ds3_ref,
    ds2_ref,
    ds1_ref,
    dt_ref,
    dk1t_ref,
    rest_ref,
    sems,
):
    marks = marks_ref[...]
    lane = lax.broadcasted_iota(jnp.int32, (BOTH, LANES), 1)
    lane1 = lax.broadcasted_iota(jnp.int32, (1, LANES), 1)
    wide = TAPS * LANES
    grad3 = split3(dstream_ref[...])
    apart = dot_nt(grad3[0], pm_ref[...]) + (dot_nt(grad3[1], pm_ref[...]) + dot_nt(grad3[2], pm_ref[...]))
    half = C4 // 2
    even, odd = split2(apart[:, :half]), split2(apart[:, half:])
    tall_even, tall_odd = jnp.concatenate(even, axis=0), jnp.concatenate(odd, axis=0)

    def by_even(cols):
        return dot_tn(tall_even, jnp.concatenate([p3e_ref[:, cols]] * 2, axis=0))

    def by_odd(cols):
        return dot_tn(tall_odd, jnp.concatenate([p3o_ref[:, cols]] * 2, axis=0))

    last = K3P // LANES - 1
    for j in range(last):
        cols = pl.ds(j * LANES, LANES)
        out_ref[pl.ds(ROW_K3 + 23 + j, half, stride=45), :] = by_odd(cols)
        if j:
            out_ref[pl.ds(ROW_K3 + j, half, stride=45), :] = by_even(cols)
    cols = pl.ds(last * LANES, LANES)
    out_ref[pl.ds(ROW_K3 + last, half, stride=45), :] = by_even(cols)
    tail = by_odd(cols)
    begin = by_even(pl.ds(0, LANES))
    rows = lax.broadcasted_iota(jnp.int32, (half, LANES), 0)
    out_ref[pl.ds(ROW_K3, half, stride=45), :] = begin + jnp.where(rows == 0, 0.0, pltpu.roll(tail, 1, 0))
    tail = tail[half - 1 : half]
    ds3_ref[...] = jnp.zeros_like(ds3_ref)
    position = lax.broadcasted_iota(jnp.int32, (BOTH, K3P), 1)
    nat = jnp.where(position < LANES // 2, 0.0, two(dot_nn, even, k3e_ref[...]))
    nat = pltpu.roll(nat, K3P - LANES // 2, 1) + jnp.where(
        position < C3 * TAPS, two(dot_nn, odd, k3o_ref[...]), 0.0
    )
    for part in range(3):
        width = min(wide, K3P - part * wide)
        pieces = split2(nat[:, part * wide : part * wide + width])
        by_tap = dot_nt(pieces[0], tm_ref[:, pl.ds(0, width)]) + dot_nt(pieces[1], tm_ref[:, pl.ds(0, width)])
        for tap in range(TAPS):
            q, src_r, src_c, down_r, down_c = tap_source(tap, (), ())
            at = q[0] * 2 + q[1]
            ds3_ref[pl.ds(at * BOTH, BOTH), pl.ds(part * LANES, LANES)] += moved_back(
                by_tap[:, tap * LANES : (tap + 1) * LANES], down_r, down_c, marks
            )
    db2 = rowsum(ds3_ref[...])
    for k in range(2):
        out_ref[ROW_B2 + k : ROW_B2 + k + 1, :] = db2[:, k * LANES : (k + 1) * LANES]
    out_ref[ROW_K3 : ROW_K3 + 1, :] += jnp.where(lane1 < LANES // 2, db2[:, 2 * LANES :], 0.0)
    grad = split2(ds3_ref[...])
    grad_real = (grad[0][:, :C3], grad[1][:, :C3])
    for j in range(TAPS):
        cols = pl.ds(j * LANES, LANES)
        value = dot_tn(grad[0], p2_ref[:, cols]) + dot_tn(grad[1], p2_ref[:, cols])
        out_ref[pl.ds(ROW_K2 + j, C3, stride=TAPS), :] = value[:C3]
    pieces = split2(two(dot_nn, grad, k2_ref[...]))
    dt_ref[...] = two(dot_nt, pieces, tm_ref[...])
    ds2_ref[...] = jnp.zeros_like(ds2_ref)
    for at, rb, cb in all_bits(1):
        for tap in range(TAPS):
            q, src_r, src_c, down_r, down_c = tap_source(tap, rb, cb)
            to = (q[0] * 2 + q[1]) * 4 + plane_of(src_r, src_c)
            ds2_ref[pl.ds(to * BOTH, BOTH), :] += moved_back(
                dt_ref[pl.ds(at * BOTH, BOTH), pl.ds(tap * LANES, LANES)], down_r, down_c, marks
            )
    out_ref[ROW_B1 : ROW_B1 + 1, :] = rowsum(ds2_ref[...])
    grad = split2(ds2_ref[...])
    few = C2 // 2
    for j in range(5):
        cols = pl.ds(j * LANES, LANES)
        dk1t_ref[j] = dot_tn(grad[0], p1_ref[:, cols]) + dot_tn(grad[1], p1_ref[:, cols])
    evens, odds = (
        two(
            dot_nt,
            split2(jnp.concatenate([dk1t_ref[j, pl.ds(odd, few, stride=2), :] for j in range(5)], axis=1)),
            t64_ref[pl.ds(C1 * (1 - odd), 5 * LANES), :],
        )
        for odd in range(2)
    )
    for j in range(9):
        if j < 4:
            value = evens[:, j * LANES : (j + 1) * LANES]
        elif j == 4:
            value = evens[:, 4 * LANES :] + odds[:, :LANES]
        else:
            value = odds[:, (j - 4) * LANES : (j - 3) * LANES]
        out_ref[pl.ds(ROW_K1 + j, few, stride=9), :] = value
    ds1_ref[...] = jnp.zeros_like(ds1_ref)
    for pair in range(5):
        values = two(dot_nn, grad, k1t_ref[:, pl.ds(pair * LANES, LANES)])
        for at, rb, cb in all_bits(2):
            here = values[at * BOTH : (at + 1) * BOTH]
            for side in range(2):
                tap = 2 * pair + side
                if tap >= TAPS:
                    continue
                q, src_r, src_c, down_r, down_c = tap_source(tap, rb, cb)
                to = stem_plane(q, src_r, src_c)
                mine = (lane < C1) if side == 0 else (lane >= C1)
                ds1_ref[pl.ds(to * BOTH, BOTH), :] += moved_back(
                    jnp.where(mine, here, 0.0), down_r, down_c, marks
                )
    db0 = rowsum(ds1_ref[...])
    db0 = db0 + pltpu.roll(db0, LANES // 2, 1)
    stem = jnp.zeros((LANES, 2 * LANES), f32)
    for at in range(4):
        span = pl.ds(at * 16 * BOTH, 16 * BOTH)
        grad = split2(ds1_ref[span, :])
        stem = stem + (dot_tn(grad[0], p0_ref[span, :]) + dot_tn(grad[1], p0_ref[span, :]))
    stem = stem[:C1] + stem[C1:]
    depth = IN_CH * 49
    held = jnp.zeros((1, 3 * LANES), f32)
    done = 0
    for at in range(C1):
        row, shift = divmod(depth * at, LANES)
        line = jnp.concatenate([stem[at : at + 1], jnp.zeros((1, LANES), f32)], axis=1)
        if shift:
            line = pltpu.roll(line, shift, 1)
        while done < row:
            out_ref[done : done + 1, :] = held[:, :LANES]
            held = jnp.concatenate([held[:, LANES:], jnp.zeros((1, LANES), f32)], axis=1)
            done += 1
        held = held + line
    out_ref[done : done + 1, :] = held[:, :LANES]
    if done < ROW_B0:
        out_ref[ROW_B0 : ROW_B0 + 1, :] = held[:, LANES : 2 * LANES]
    out_ref[ROW_B0 : ROW_B0 + 1, :] += jnp.where(lane1 < LANES // 2, 0.0, db0)

    lead = 5

    def put(name, value):
        for k in range(value.shape[1] // LANES):
            at = lead + REST[name] + k
            rest_ref[at : at + 1, :] = value[:, k * LANES : (k + 1) * LANES]

    rest_ref[0:8, :] = jnp.zeros((8, LANES), f32)
    put("b3", small_ref[0:1, :])
    for k in range(6):
        at = lead + REST["block"] + 4 * k
        for i in range(4):
            rest_ref[at + i : at + i + 1, :] = dblock_ref[k : k + 1, i * LANES : (i + 1) * LANES]
    put("fb1", dfb1_ref[0:1, :])
    put("fb2", small_ref[1:2, :])
    put("final", jnp.concatenate([small_ref[2:3, :], small_ref[3:4, :]], axis=1))
    dlog = dlog_ref[...]
    put("hb", dlog[0:1] + dlog[1:2])
    rest_ref[lead + REST["end"] : lead + REST["end"] + 11, :] = jnp.zeros((11, LANES), f32)
    pooled = pooled_ref[...]
    in_group, in_place, own_row = head_masks()
    picked = jnp.where(in_place, jnp.where(own_row, pooled[0:1, :], pooled[1:2, :]), 0.0).astype(bf16)
    by_group = dot_nt(in_group.astype(bf16), picked)
    padded = jnp.concatenate([dlog, jnp.zeros((8, LANES), f32)], axis=1)
    groups = C4 // GROUP
    written = -1
    for place in range(GROUP):
        at, shift = divmod(CLS * place, LANES)
        window = pltpu.roll(padded, shift, 1) if shift else padded
        ours = by_group[:, MICRO * place : MICRO * place + 1]
        others = by_group[:, MICRO * place + 1 : MICRO * place + 2]
        for k in range(CLSP // LANES + 1):
            if (at + k) * LANES >= CLS * (place + 1):
                break
            block = slice(k * LANES, (k + 1) * LANES)
            value = ours * window[0:1, block] + others * window[1:2, block]
            target = pl.ds(lead + REST["head"] + at + k, groups, stride=SPAN)
            if at + k == written:
                rest_ref[target, :] += value
            else:
                rest_ref[target, :] = value
            written = at + k
    first = ROW_B3 + 3
    out_ref[ROW_B3 : first, :] = halves(rest_ref[lead - 1 : lead + 2, :], rest_ref[lead : lead + 3, :])
    out_ref[ROW_B3 : ROW_B3 + 1, :] += tail
    step = 508
    for at in range(0, REST["end"], step):
        out_ref[first + at : first + at + step, :] = halves(
            rest_ref[lead + 2 + at : lead + 2 + at + step, :], rest_ref[lead + 3 + at : lead + 3 + at + step, :]
        )
    end = first + REST["end"]
    out_ref[end : out_ref.shape[0], :] = jnp.zeros((out_ref.shape[0] - end, LANES), f32)
    chips, cut, unused_lanes = keep_a_hbm.shape
    each = cut + keep_b_hbm.shape[1]
    core = whole_ref[4]
    copies = Copies(sems)
    for chunk in range(2 * chips):
        for keep, send, at, rows in ((keep_a_hbm, send_a_hbm, 0, cut), (keep_b_hbm, send_b_hbm, cut, each - cut)):
            source = out_ref.at[pl.ds(chunk * each + at, rows), :]
            ours, theirs = (keep, send) if chunk % 2 == 0 else (send, keep)
            pl.when(core == 0)(functools.partial(copies.start_out, source, ours.at[chunk // 2]))
            pl.when(core != 0)(functools.partial(copies.start_out, source, theirs.at[chunk // 2]))
    copies.out(out_ref).wait()


def passes(a, b, dot, many):
    small = dot(a[0], b[1]) + dot(a[1], b[0])
    if many:
        small = small + (dot(a[0], b[2]) + dot(a[1], b[1]) + dot(a[2], b[0]))
    return dot(a[0], b[0]) + small


def gram_kernel(scale_ref, kept_a_ref, got_a_ref, kept_b_ref, got_b_ref, momentum_ref, loss_ref, ortho_ref, new_ref, packed_ref):
    grad = jnp.concatenate([kept_a_ref[...] + got_a_ref[...], kept_b_ref[...] + got_b_ref[...]], axis=1) * scale_ref[0]
    new = 0.95 * momentum_ref[...] + grad
    new_ref[...] = new
    ortho = grad + 0.95 * new
    ortho_ref[...] = ortho
    parts = split3(ortho)

    def cut(k):
        return tuple(p[:, k * LANES : (k + 1) * LANES] for p in parts)

    for at, (i, j) in enumerate(PAIRS):
        block = passes(cut(i), cut(j), dot_tn, True)
        if at == 0:
            row = lax.broadcasted_iota(jnp.int32, block.shape, 0)
            col = lax.broadcasted_iota(jnp.int32, block.shape, 1)
            block = jnp.where((row == LANES - 1) & (col == 0), loss_ref[0:1, 0:1], block)
        packed_ref[pl.ds(at * LANES, LANES), :] = block


def newton_steps(gram, ortho, steps, last):
    wide_row = lax.broadcasted_iota(jnp.int32, (C4, C4), 0)
    wide_col = lax.broadcasted_iota(jnp.int32, (C4, C4), 1)
    for iteration in steps:
        many = iteration == 0
        split = split3 if many else split2
        parts = split(gram)
        poly = jnp.where(wide_row == wide_col, 3.4445, 0.0) + (
            -4.775 * gram + 2.0315 * passes(parts, parts, dot_nn, many)
        )
        poly_parts = split(poly)
        ortho = passes(split(ortho), poly_parts, dot_nn, many)
        if iteration < last:
            gram = passes(split(passes(poly_parts, parts, dot_nn, many)), poly_parts, dot_nn, many)
    return gram, ortho


def newton_first_kernel(steps, packed_ref, ortho_ref, out_ref, gram_ref, loss_ref):
    row = lax.broadcasted_iota(jnp.int32, (LANES, LANES), 0)
    col = lax.broadcasted_iota(jnp.int32, (LANES, LANES), 1)
    trace = jnp.zeros((1, 1), f32)
    for at, (i, j) in enumerate(PAIRS):
        block = packed_ref[pl.ds(at * LANES, LANES), :]
        if at == 0:
            loss_ref[...] = jnp.broadcast_to(block[LANES - 1 : LANES, 0:1], (8, LANES))
            block = jnp.where((row == LANES - 1) & (col == 0), block.T, block)
        gram_ref[pl.ds(i * LANES, LANES), pl.ds(j * LANES, LANES)] = block
        if i == j:
            trace = trace + total(jnp.where(row == col, block, 0.0))
        else:
            gram_ref[pl.ds(j * LANES, LANES), pl.ds(i * LANES, LANES)] = block.T
    inverse = 1.0 / (jnp.sqrt(trace) + 1e-07)
    gram, ortho = newton_steps(
        gram_ref[...] * (inverse * inverse), ortho_ref[...] * inverse, range(steps), NS_ITERS - 1
    )
    gram_ref[...] = gram
    out_ref[...] = ortho


def newton_last_kernel(steps, unused_ref, gram_ref, ortho_ref, out_ref):
    unused_gram, ortho = newton_steps(gram_ref[...], ortho_ref[...], range(steps, NS_ITERS), NS_ITERS - 1)
    out_ref[...] = ortho


def shape(*dims, dtype=f32):
    return jax.ShapeDtypeStruct(dims, dtype)


def kernel_call(body, outs, scratch, smem, kept, count, micros, outs_kept=0):
    vmem = pl.BlockSpec(memory_space=pltpu.VMEM)
    scalar = pl.BlockSpec(memory_space=pltpu.SMEM)
    anywhere = pl.BlockSpec(memory_space=pl.ANY)
    if isinstance(kept, int):
        specs = [anywhere] * kept + [vmem] * (count - smem - kept)
    else:
        specs = [anywhere if k else vmem for k in kept[smem:]] + [vmem] * (count - len(kept))
    return pl.pallas_call(
        body,
        out_shape=outs,
        in_specs=[scalar] * smem + specs,
        out_specs=[anywhere] * outs_kept + [vmem] * (len(outs) - outs_kept),
        scratch_shapes=scratch,
        compiler_params=pltpu.CompilerParams(vmem_limit_bytes=60 * 1024 * 1024),
        cost_estimate=pl.CostEstimate(flops=10**6, bytes_accessed=micros * 3_000_000, transcendentals=0),
    )


def pack_kernel(valid_ref, mats_ref, flat_ref, one_ref, two_ref, out_ref):
    share = mats_ref.shape[2]
    for mat, to_ref in enumerate((one_ref, two_ref)):
        turned = mats_ref[mat].T.astype(bf16)
        for part in range(C4 // LANES):
            to_ref[part] = turned[:, part * LANES : (part + 1) * LANES]
    count = flat_ref.shape[0]
    out_ref[pl.ds(0, count), :] = flat_ref[...].astype(bf16)
    left = out_ref.shape[0] - count
    counted = (valid_ref[0] + valid_ref[1]).astype(f32)
    out_ref[pl.ds(count, left), :] = jnp.full((left, LANES), counted, f32).astype(bf16)


def run_pack(valid, mats, flat):
    rows = (flat.shape[0] // 16 + 1) * 16
    outs = [shape(C4 // LANES, mats.shape[2], LANES, dtype=bf16)] * 2 + [shape(rows, LANES, dtype=bf16)]
    return kernel_call(pack_kernel, outs, [], 1, 0, 3, 2)(valid, mats, flat)


def run_conv(whole, flat, moved, marks, flat_share):
    half = C4 // 2
    moved_outs = [
        shape(16 * BOTH, 5 * LANES, dtype=bf16),
        shape(4 * BOTH, TAPS * LANES, dtype=bf16),
        shape(BOTH, K3P, dtype=bf16),
        shape(BOTH, K3P, dtype=bf16),
        shape(C2, 5 * LANES, dtype=bf16),
        shape(C3P, TAPS * LANES, dtype=bf16),
        shape(half, K3P, dtype=bf16),
        shape(half, K3P, dtype=bf16),
    ]
    outs = moved_outs + [
        shape(BOTH, C4),
        shape(REST["head"], LANES),
        shape(C4 // GROUP, (SPAN + 1) * LANES, dtype=bf16),
        shape(8, LANES),
        shape(8, LANES),
    ]
    scratch = [pltpu.VMEM(a.shape, a.dtype) for a in moved + moved_outs]
    scratch += [
        pltpu.VMEM((64 * BOTH, LANES), f32),
        pltpu.VMEM((16 * BOTH, LANES), f32),
        pltpu.VMEM((4 * BOTH, C3P), f32),
        pltpu.VMEM((4 * BOTH, TAPS * LANES), bf16),
        pltpu.VMEM((3 * BOTH, TAPS * LANES), bf16),
        pltpu.VMEM((C1, 2 * LANES), f32),
        pltpu.VMEM((5, C2, LANES), f32),
        pltpu.SemaphoreType.DMA((16,)),
    ]
    args = [whole, flat] + moved + [marks]
    if flat_share % LANES:
        kept = [False, False] + [True] * 4
    else:
        kept = [False] + [True] * 5
        scratch += [
            pltpu.VMEM(flat.shape, bf16),
            pltpu.VMEM((flat.shape[0] * flat_share // LANES, LANES), f32),
        ]
    body = functools.partial(conv_kernel, flat_share)
    return kernel_call(body, outs, scratch, 1, kept, len(args), 12, 8)(*args)


def run_block(whole, real, gathered, made, marks, near, share, devices_count):
    half = C4 // 2
    outs = [shape(devices_count // 8, 2, 2 * share, half)] * 8 + [
        shape(BOTH, C4),
        shape(8, C4),
        shape(8, HID),
        shape(8, C4),
        shape(8, C4),
        shape(8, CLSP),
        shape(8, LANES),
    ]
    scratch = [
        pltpu.VMEM((2, 2, HID, half), f32),
        pltpu.VMEM((BOTH, HID), f32),
        pltpu.VMEM((C4 // GROUP, (SPAN + 1) * LANES), f32),
        pltpu.VMEM((MICRO * GROUP, C4 // GROUP), f32),
        pltpu.VMEM((2, C4 // LANES, HID // share, share, LANES), bf16),
        pltpu.SemaphoreType.DMA((2,)),
    ]
    arrays = [array for side in gathered for array, *unused in side]
    args = [whole, real] + arrays + list(made) + [marks, near]
    kept = [False] * 2 + [True] * len(arrays)
    body = functools.partial(block_kernel, share, gathered)
    return kernel_call(body, outs, scratch, 2, kept, len(args), 12, 8)(*args)


def run_backward(args, chips, each):
    scratch = [
        pltpu.VMEM((2 * chips * each, LANES), f32),
        pltpu.VMEM((4 * BOTH, C3P), f32),
        pltpu.VMEM((16 * BOTH, LANES), f32),
        pltpu.VMEM((64 * BOTH, LANES), f32),
        pltpu.VMEM((4 * BOTH, TAPS * LANES), f32),
        pltpu.VMEM((5, C2, LANES), f32),
        pltpu.VMEM((REST["end"] + 16, LANES), f32),
        pltpu.SemaphoreType.DMA((2,)),
    ]
    cut = -(-each // 16) * 8
    outs = [shape(chips, cut, LANES), shape(chips, each - cut, LANES)] * 2

    def body(*refs):
        backward_kernel(*refs[1 : len(args)], refs[0], *refs[len(args) :])

    return kernel_call(body, outs, scratch, 1, 2, len(args), 20, 4)(*args)


def run_gram(scale, sums, momentum, loss):
    rows = momentum.shape[0]
    outs = [shape(rows, C4), shape(rows, C4), shape(len(PAIRS) * LANES, LANES)]
    return kernel_call(gram_kernel, outs, [], 1, 0, 7, 4)(scale, *sums, momentum, loss)


def run_newton_first(packed, ortho, steps):
    outs = [shape(*ortho.shape), shape(C4, C4), shape(8, LANES)]
    return kernel_call(functools.partial(newton_first_kernel, steps), outs, [], 0, 0, 2, 12)(packed, ortho)


def run_newton_last(tie, gram, ortho, steps):
    outs = [shape(*ortho.shape)]
    return kernel_call(functools.partial(newton_last_kernel, steps), outs, [], 0, 1, 3, 8)(tie, gram, ortho)[0]


def patches(images, resolution, partner_col, mix_col):
    pictures = images[:, 0].astype(f32)
    dims = (1, 1, RES_L, RES_L)
    inside = (lax.broadcasted_iota(jnp.int32, dims, 2) < resolution) & (
        lax.broadcasted_iota(jnp.int32, dims, 3) < resolution
    )
    mixing = mix_col[:, None, None, None]
    other = jnp.where(partner_col[:, None, None, None] == 0, pictures[0][None], pictures[1][None])
    pixels = jnp.where(inside, mixing * pictures + (1.0 - mixing) * other, 0.0).astype(bf16)
    padded = jnp.pad(pixels, ((0, 0), (0, 0), (2, 1), (2, 1)))
    size = RES_STEP + 3
    blocks = [
        padded[:, :, RES_STEP * i : RES_STEP * i + size, RES_STEP * j : RES_STEP * j + size]
        for i in range(SIDE)
        for j in range(SIDE)
    ]
    blocks = jnp.stack(blocks, axis=1).reshape(MICRO * SIDE * SIDE, IN_CH, size, size)
    depth = IN_CH * 49
    choose = jnp.eye(depth, dtype=bf16).reshape(IN_CH, 7, 7, depth).transpose(1, 2, 0, 3)
    columns = lax.conv_general_dilated(
        blocks,
        choose,
        (4, 4),
        ((0, 0), (0, 0)),
        dimension_numbers=("NCHW", "HWIO", "HWNC"),
        preferred_element_type=f32,
    ).astype(bf16)
    columns = columns.reshape(64, MICRO, SIDE * SIDE, depth)
    columns = jnp.pad(columns, ((0, 0), (0, 0), (0, ROWS - SIDE * SIDE), (0, 2 * LANES - depth)))
    return columns.reshape(64 * BOTH, 2 * LANES)


def tap_orders():
    row = lax.broadcasted_iota(jnp.int32, (TAPS * LANES, TAPS * LANES), 0)
    col = lax.broadcasted_iota(jnp.int32, (TAPS * LANES, TAPS * LANES), 1)
    forth = ((row % LANES) * TAPS + row // LANES == col).astype(bf16)
    dims = (5 * LANES + C1, 5 * LANES)
    row = lax.broadcasted_iota(jnp.int32, dims, 0) - C1
    col = lax.broadcasted_iota(jnp.int32, dims, 1)
    real = (row >= 0) & (row < TAPS * C1)
    row = jnp.maximum(row, 0)
    back = (real & ((row % TAPS) * C1 + row // TAPS == col)).astype(bf16)
    row = lax.broadcasted_iota(jnp.int32, (C4, C4), 0)
    col = lax.broadcasted_iota(jnp.int32, (C4, C4), 1)
    merge = ((row % (C4 // 2)) * 2 + row // (C4 // 2) == col).astype(bf16)
    return forth, back, merge


def grid_marks(side):
    row = np.arange(BOTH)
    image, q = row // ROWS, row % ROWS
    y, x = q // SIDE, q % SIDE
    real = q < SIDE * SIDE
    fixed = np.stack([real & (y > 0), real & (x > 0), real & (y > 0) & (x > 0)], 1).astype(np.float32)
    close = (
        (image[:, None] == image[None])
        & (abs(y[:, None] - y[None]) <= 1)
        & (abs(x[:, None] - x[None]) <= 1)
        & real[:, None]
        & real[None]
    )
    inside = jnp.asarray(real) & (jnp.asarray(y) < side) & (jnp.asarray(x) < side)
    near = jnp.where(jnp.asarray(close) & inside[:, None] & inside[None], 1.0, 0.0)
    cells = jnp.maximum(jnp.sum(near, axis=1), 1.0)
    marks = jnp.concatenate(
        [inside.astype(f32)[:, None], jnp.asarray(fixed), (1.0 / cells)[:, None]], axis=1
    )
    return jnp.pad(marks, ((0, 0), (0, LANES - marks.shape[1]))), near.astype(bf16)


def local_inputs(images, group, label_col, partner_col, mix_col, valid_col, me):
    side = RES_S // RES_STEP + group
    columns = patches(images, side * RES_STEP, partner_col, mix_col)
    orders = tap_orders()
    marks, near = grid_marks(side)
    other = jnp.where(partner_col == 0, label_col[0], label_col[1])
    whole = jnp.concatenate([label_col, other, jnp.stack([me % 2, me]).astype(jnp.int32)])
    cells = (side * side).astype(f32)
    real = jnp.concatenate([mix_col, valid_col.astype(f32), jnp.stack([cells, cells * C4])])
    return whole, real, columns, orders, marks, near


def second_half(prepared, convs, made, chips, each, ties):
    columns, (forth, back, merge), marks = prepared[2], prepared[3], prepared[4]
    p1, p2, p3e, p3o, k1t, k2, k3e, k3o = convs[:8]
    args = [made[8], columns, p1, p2, p3e, p3o, k1t, k2, k3e, k3o, forth, back, merge, marks]
    return run_backward([prepared[0]] + list(ties) + args + list(made[9:14]), chips, each)


class Ring:
    def __init__(self, count):
        self.count = count
        self.squares = count // 8
        me = lax.axis_index(AXES)
        self.me = me
        self.core = me % 2
        self.low = (me // 2) % 2
        self.high = (me // 4) % 2
        self.corner = (me // 2) % 4
        self.square = me // 8

    def swap(self, value, bits):
        return lax.ppermute(value, AXES, [(i, i ^ bits) for i in range(self.count)])


def pick(value, at, axis):
    return lax.dynamic_index_in_dim(value, at, axis, keepdims=False)


class Scatter:
    def __init__(self, ring, terms, high_first):
        self.ring = ring
        self.terms = terms
        self.order = [(1, ring.high, 4), (2, ring.low, 2)] if high_first else [(2, ring.low, 2), (1, ring.high, 4)]
        self.sent = None

    def begin(self, sent):
        self.bits = self.order.pop(0)[2]
        self.sent = functools.reduce(jnp.add, sent)

    def prepare(self):
        axis, mine, self.bits = self.order.pop(0)
        if not self.order:
            axis = 1
        self.sent = functools.reduce(jnp.add, [pick(x, 1 - mine, axis) for x in self.terms])
        self.terms = [pick(x, mine, axis) for x in self.terms]

    def send(self):
        self.terms.append(self.ring.swap(self.sent, self.bits))

    def add(self):
        self.terms = [functools.reduce(jnp.add, self.terms)]


def sum_squares(ring, value, far_first):
    bits = ring.squares.bit_length() - 1
    order = list(range(bits))
    if far_first:
        order.reverse()
    held = order.copy()
    value = value.reshape((2,) * bits + value.shape[1:])
    got = None
    for bit in order:
        axis = len(held) - 1 - sorted(held).index(bit)
        held.remove(bit)
        mine = (ring.square >> bit) & 1
        if got is not None:
            value = value + got
        got = ring.swap(pick(value, 1 - mine, axis), 8 << bit)
        value = pick(value, mine, axis)
    return value, got


class Gather:
    def __init__(self, ring, value, far_first, high_first):
        self.ring = ring
        self.value = value
        self.masks = []
        bits = list(range(ring.squares.bit_length() - 1))
        self.squares = [8 << bit for bit in (reversed(bits) if far_first else bits)]
        self.corners = (4, 2) if high_first else (2, 4)
        self.pieces = []

    def exchange(self, mask):
        self.value = jnp.stack([self.value, self.ring.swap(self.value, mask)])
        self.masks = [mask] + self.masks

    def between_squares(self):
        for mask in self.squares:
            self.exchange(mask)

    def first_corner(self):
        self.exchange(self.corners[0])

    def second_corner(self):
        got = self.ring.swap(self.value, self.corners[1])
        self.pieces = [(self.value, self.masks, 0), (got, self.masks, self.corners[1])]

    def between_cores(self):
        self.pieces += [(self.ring.swap(array, 1), masks, base | 1) for array, masks, base in self.pieces]


def together(scatters, *others):
    counts = [len(x.terms) for x in scatters]
    values = lax.optimization_barrier(tuple(t for x in scatters for t in x.terms) + tuple(others))
    at = 0
    for x, count in zip(scatters, counts):
        x.terms = list(values[at : at + count])
        at += count
    return values[at:]


class ChipSum:
    def __init__(self, ring, value):
        self.ring = ring
        self.shape = value.shape
        self.terms = [value.reshape(4, value.shape[0] // 4, value.shape[1])]

    def scatter_corners(self):
        ring = self.ring
        got = [ring.swap(pick(self.terms[0], ring.corner ^ j, 0), 2 * j) for j in range(1, 4)]
        self.terms = [functools.reduce(jnp.add, got, pick(self.terms[0], ring.corner, 0))]

    def sum_squares(self):
        ring = self.ring
        got = [ring.swap(self.terms[0], 8 * j) for j in range(1, ring.squares)]
        self.terms = [functools.reduce(jnp.add, got, self.terms[0])]


    def gather_corners(self):
        ring = self.ring
        held = jnp.stack([self.terms[0]] + [ring.swap(self.terms[0], 2 * j) for j in range(1, 4)])
        return jnp.stack([pick(held, ring.corner ^ j, 0) for j in range(4)]).reshape(self.shape)


def per_device(
    devices_count,
    images,
    group_ids,
    labels,
    partners,
    mix_weights,
    valid,
    flat_params,
    flat_first,
    flat_second,
    mlp_weights,
    mlp_momentum,
):
    ring = Ring(devices_count)
    chips = devices_count // 2
    share = mlp_weights.shape[2]
    flat_share = flat_params.shape[0]
    flat_rows = -(-flat_share // LANES)
    spare = flat_rows * LANES - flat_share
    mine = jnp.pad(flat_params, (0, spare)) if spare else flat_params
    mats_one, mats_two, sent = run_pack(
        valid.reshape(MICRO), mlp_weights, mine.reshape(flat_rows, LANES)
    )
    prepared = local_inputs(
        images, group_ids[0], labels[:, 0], partners[:, 0], mix_weights[:, 0], valid[:, 0], ring.me
    )
    whole, real, columns, orders, marks, near = prepared
    momentum = mlp_momentum.transpose(0, 2, 1)

    def of_both_cores(mine, theirs):
        at_first = ring.core == 0
        return jnp.concatenate([jnp.where(at_first, mine, theirs), jnp.where(at_first, theirs, mine)])

    momentum_rows = of_both_cores(
        pick(momentum, ring.core, 0), ring.swap(pick(momentum, 1 - ring.core, 0), 1)
    )
    mats = [Gather(ring, mats_one, False, True), Gather(ring, mats_two, True, False)]
    got = lax.all_gather(sent, AXES, axis=0, tiled=False)
    for x in mats:
        x.between_squares()
    for x in mats:
        x.first_corner()
    for x in mats:
        x.second_corner()
    for x in mats:
        x.between_cores()
    moved = [columns, *orders]
    if flat_share % LANES:
        whole_flat = (
            got[:, :flat_rows]
            .astype(f32)
            .reshape(devices_count, flat_rows * LANES)[:, :flat_share]
            .reshape(devices_count * flat_share // LANES, LANES)
        )
        convs = run_conv(whole, whole_flat, moved, marks, flat_share)
        counted = jnp.sum(got[:, flat_rows, 0].astype(f32))
    else:
        convs = run_conv(whole, got, moved, marks, flat_share)
        counted = convs[12][0, 0]
    scale = 1.0 / jnp.maximum(counted, 1.0)
    made = run_block(whole, real, [x.pieces for x in mats], convs[8:12], marks, near, share, devices_count)
    keep_own, keep_other, send_own, send_other = (made[2 * k : 2 * k + 2] for k in range(4))
    loss = made[14]
    got_other = [ring.swap(x, 1) for x in send_other]
    got_own = [ring.swap(x, 1) for x in send_own]
    mlp = []
    for side in range(2):
        x = Scatter(ring, [keep_own[side], got_own[side]], side == 0)
        x.begin([keep_other[side], got_other[side]])
        x.send()
        mlp.append(x)

    each = -(-(devices_count * flat_share) // (devices_count * LANES * 8)) * 8
    ties = [x.sent[(0,) * (x.sent.ndim - 2)][:8, :LANES] for x in mlp]
    keep_a, keep_b, send_a, send_b = second_half(prepared, convs, made, chips, each, ties)
    loss = loss + ring.swap(loss, 1)
    for x in mlp:
        x.add()
    send_a, send_b = together(mlp, send_a, send_b)
    for x in mlp:
        x.prepare()
        x.send()
    flat = []
    for keep, send, first in ((keep_a, send_a, True), (keep_b, send_b, False)):
        square = (ring.squares, 2, 2) + keep.shape[1:]
        flat.append(Scatter(ring, [keep.reshape(square), ring.swap(send, 1).reshape(square)], first))
    for x in mlp:
        x.add()
    together(mlp + flat)
    sums = [sum_squares(ring, x.terms[0], far) for x, far in zip(mlp, (False, True))]
    for x in flat:
        x.prepare()
        x.send()
    ortho, momentum_new, packed = run_gram(scale[None], sums[0] + sums[1], momentum_rows, loss)
    grams = ChipSum(ring, packed)
    grams.scatter_corners()
    for x in flat:
        x.add()
    together([grams] + flat)
    grams.sum_squares()
    for x in flat:
        x.prepare()
        x.send()
    for x in flat:
        x.add()
    together([grams] + flat)
    sum_flat = jnp.concatenate([sum(sum_squares(ring, x.terms[0], far)) for x, far in zip(flat, (False, True))])
    steps = 2
    ortho, gram, loss_total = run_newton_first(grams.gather_corners(), ortho, steps)
    lag = (devices_count - 1) * (each * LANES - flat_share)
    hops = -(-lag // (each * LANES))
    tail = min(each, -(-lag // (8 * LANES)) * 8)
    before = [
        lax.ppermute(sum_flat[each - tail :], AXES, [(i, i + h) for i in range(devices_count - h)])
        for h in range(hops, 0, -1)
    ]
    ortho = run_newton_last(sum_flat[each - 8 :], gram, ortho, steps)
    sum_flat = jnp.concatenate(before + [sum_flat])
    start = len(before) * tail * LANES - ring.me * (each * LANES - flat_share)
    if flat_share % LANES == 0:
        sum_flat = lax.dynamic_slice_in_dim(sum_flat, start // LANES, flat_rows, 0).reshape(-1)
    else:
        sum_flat = lax.dynamic_slice_in_dim(sum_flat.reshape(-1), start, flat_share, 0)
    sum_flat = sum_flat * scale
    first_new = 0.9 * flat_first + 0.1 * sum_flat
    second_new = 0.999 * flat_second + 0.001 * sum_flat * sum_flat
    first_hat = first_new / (1.0 - 0.9**STEP)
    second_hat = second_new / (1.0 - 0.999**STEP)
    params_new = flat_params - 0.02 * (
        first_hat / (jnp.sqrt(second_hat) + 1e-08) + 0.05 * flat_params
    )

    def to_owners(by_chip):
        parts = by_chip.reshape(2, share, C4)
        mine, theirs = pick(parts, ring.core, 0), ring.swap(pick(parts, 1 - ring.core, 0), 1)
        at_first = ring.core == 0
        return jnp.stack([jnp.where(at_first, mine, theirs), jnp.where(at_first, theirs, mine)])

    mats = mlp_weights.transpose(0, 2, 1)
    weights_new = mats * (1.0 - 0.1 * 0.05) - 0.1 * 0.2 * math.sqrt(HID) * to_owners(ortho)
    return (
        loss_total[0, 0],
        params_new,
        first_new,
        second_new,
        weights_new.transpose(0, 2, 1),
        to_owners(momentum_new).transpose(0, 2, 1),
    )


def solution(mesh):
    placed = (
        P(None, AXES, None, None, None),
        P(AXES),
        P(None, AXES),
        P(None, AXES),
        P(None, AXES),
        P(None, AXES),
        P(AXES),
        P(AXES),
        P(AXES),
        P(None, None, AXES),
        P(None, None, AXES),
    )
    devices_count = math.prod(mesh.shape[axis] for axis in AXES)
    return jax.shard_map(
        functools.partial(per_device, devices_count),
        mesh=mesh,
        in_specs=placed,
        out_specs=(
            P(),
            P(AXES),
            P(AXES),
            P(AXES),
            P(None, None, AXES),
            P(None, None, AXES),
        ),
        check_vma=False,
    )
```

```python
import functools
import math

import jax
import jax.numpy as jnp
import numpy as np
from jax import lax
from jax.experimental import pallas as pl
from jax.experimental.pallas import tpu as pltpu
from jax.sharding import PartitionSpec as P

C1 = 64
C2 = 128
C3 = 320
C4 = 512
HID = 2048
CLS = 1000
IN_CH = 3
RES_S = 96
RES_L = 160
RES_STEP = 32
MICRO = 2
NS_ITERS = 5
STEP = 10

AXES = ("fsdp", "ns")
LANES = 128
SIDE = 5
ROWS = 32
BOTH = MICRO * ROWS
C3P = 384
CLSP = 1024
K3P = 2944
TAPS = 9

f32 = jnp.float32
bf16 = jnp.bfloat16
norm_epsilon = 1e-05

NARROW = C1 * IN_CH * 49
ROW_B0 = NARROW // LANES
ROW_K1 = 74
ROW_B1 = 650
ROW_K2 = 651
ROW_B2 = 3531
ROW_K3 = 3533
ROW_B3 = 15053
REST = {"b3": 0, "block": 4, "fb1": 28, "fb2": 44, "final": 48, "head": 56, "hb": 4056, "end": 4064}
QUARTER = HID // 4
FACTOR_OTHER = (0, QUARTER + C4)
FACTOR_CHANNELS = QUARTER
FACTOR_OWN = (2 * QUARTER + C4, 3 * QUARTER + C4)
FACTOR_LOSS = HID + C4
FACTOR_ROWS = FACTOR_LOSS + 16
GROUP = 16
SPAN = GROUP * CLS // LANES
PAIRS = [(i, j) for i in range(4) for j in range(i, 4)]


def dot_nn(a, b):
    return lax.dot_general(a, b, (((1,), (0,)), ((), ())), preferred_element_type=f32)


def dot_nt(a, b):
    return lax.dot_general(a, b, (((1,), (1,)), ((), ())), preferred_element_type=f32)


def dot_tn(a, b):
    return lax.dot_general(a, b, (((0,), (0,)), ((), ())), preferred_element_type=f32)


def split2(x):
    hi = x.astype(bf16)
    return hi, (x - hi.astype(f32)).astype(bf16)


def split3(x):
    hi = x.astype(bf16)
    rest = x - hi.astype(f32)
    mid = rest.astype(bf16)
    return hi, mid, (rest - mid.astype(f32)).astype(bf16)


def stacked(dot, parts, other):
    rows = parts[0].shape[0]
    product = dot(jnp.concatenate(parts, axis=0), other)
    return functools.reduce(jnp.add, [product[k * rows : (k + 1) * rows] for k in range(len(parts))])


def two(dot, pair, other):
    return stacked(dot, pair, other)


def borrow(bits):
    out = list(bits)
    for at, bit in enumerate(out):
        if bit:
            out[at] = 0
            return tuple(out), 0
        out[at] = 1
    return tuple(out), 1


def tap_source(tap, row_bits, col_bits):
    r, c = divmod(tap, 3)
    src_r, down_r = (row_bits, 0) if r else borrow(row_bits)
    src_c, down_c = (col_bits, 0) if c else borrow(col_bits)
    return (int(r != 1), int(c != 1)), src_r, src_c, down_r, down_c


def plane_of(row_bits, col_bits):
    at = 0
    for r, c in zip(row_bits, col_bits):
        at = at * 4 + r * 2 + c
    return at


def stem_plane(quarter, row_bits, col_bits):
    row = quarter[0] + 2 * row_bits[0] + 4 * row_bits[1]
    return row * 8 + quarter[1] + 2 * col_bits[0] + 4 * col_bits[1]


def all_bits(pairs):
    for at in range(4**pairs):
        digits = [(at >> (2 * (pairs - 1 - k))) & 3 for k in range(pairs)]
        yield at, tuple(d >> 1 for d in digits), tuple(d & 1 for d in digits)


def moved(value, down_r, down_c, marks):
    if not (down_r or down_c):
        return value
    step = SIDE * down_r + down_c
    column = {(1, 0): 1, (0, 1): 2, (1, 1): 3}[(down_r, down_c)]
    return pltpu.roll(value, step, 0) * marks[:, column : column + 1]


def moved_back(value, down_r, down_c, marks):
    if not (down_r or down_c):
        return value
    step = SIDE * down_r + down_c
    column = {(1, 0): 1, (0, 1): 2, (1, 1): 3}[(down_r, down_c)]
    return pltpu.roll(value * marks[:, column : column + 1], BOTH - step, 0)


def erf(x):
    x = jnp.clip(x, -3.832506856900711, 3.832506856900711)
    s = x * x
    top = 2.2905065861350646e-4
    for coef in (3.4082910107109506e-3, 5.0955695062380861e-2, 1.8520832239976145e-1, 1.128379143519084):
        top = top * s + coef
    low = -1.1791602954361697e-7
    for coef in (
        2.3547966471313185e-5,
        1.0179625278914885e-3,
        1.4070470171167667e-2,
        1.1098505178285362e-1,
        4.9746925110067538e-1,
        1.0,
    ):
        low = low * s + coef
    return x * top / low


def total(x):
    return jnp.sum(jnp.sum(x, axis=1, keepdims=True), axis=0, keepdims=True)


def norm_images(value, mask, count):
    parts, scales = [], []
    for m in range(MICRO):
        v = value[m * ROWS : (m + 1) * ROWS]
        k = mask[m * ROWS : (m + 1) * ROWS]
        center = (v - total(v * k) / count) * k
        scale = lax.rsqrt(total(center * center) / count + norm_epsilon)
        parts.append(center * scale)
        scales.append(scale)
    return jnp.concatenate(parts, axis=0), scales


def norm_images_back(grad, hat, scales, gain, mask, count):
    parts = []
    for m in range(MICRO):
        at = slice(m * ROWS, (m + 1) * ROWS)
        g = grad[at] * gain
        h = hat[at]
        parts.append((g - total(g) / count - h * (total(g * h) / count)) * scales[m] * mask[at])
    return jnp.concatenate(parts, axis=0)


def rowsum(x):
    return jnp.sum(x, axis=0, keepdims=True)


def halves(low, high):
    lane = lax.broadcasted_iota(jnp.int32, low.shape, 1)
    return jnp.where(lane < LANES // 2, pltpu.roll(low, LANES // 2, 1), pltpu.roll(high, LANES // 2, 1))


def lanes_of(ref, row, count):
    return jnp.concatenate([ref[row + at : row + at + 1, :] for at in range(count)], axis=1)


def head_masks():
    row = lax.broadcasted_iota(jnp.int32, (C4 // GROUP, C4), 0)
    col = lax.broadcasted_iota(jnp.int32, (C4 // GROUP, C4), 1)
    return col // GROUP == row, col % GROUP == row // MICRO, row % MICRO == 0


class Copies:
    def __init__(self, sems):
        self.sems = sems
        self.count = 2

    def start_shared(self, source, target):
        pltpu.make_async_copy(source, target, self.sems.at[0]).start()

    def start_out(self, source, target):
        pltpu.make_async_copy(source, target, self.sems.at[1]).start()

    def out(self, source):
        return pltpu.make_async_copy(source, source, self.sems.at[1])

    def shared(self, target):
        return pltpu.make_async_copy(target, target, self.sems.at[0])

    def start(self, source, target):
        copy = self.make(source, target)
        copy.start()
        return copy

    def make(self, source, target):
        copy = pltpu.make_async_copy(source, target, self.sems.at[self.count])
        self.count += 1
        return copy


def pieces_of(gathered):
    for number, (unused_array, masks, base) in enumerate(gathered):
        for place in range(2 ** len(masks)):
            index, owner = [], base
            for k, mask in enumerate(masks):
                bit = (place >> k) & 1
                index.append(bit)
                owner ^= mask * bit
            yield number, tuple(index), owner


def conv_kernel(flat_share, gathered, *refs):
    if flat_share % LANES:
        conv_body(None, None, *refs)
    else:
        count = [len(side) for side in gathered]
        held = [refs[2 : 2 + count[0]], refs[2 + count[0] : 2 + sum(count)]]
        arrived = (refs[1], gathered, held)
        conv_body(flat_share, arrived, refs[0], refs[-1], *refs[2 + sum(count) : -1])


def conv_body(
    flat_share,
    arrived,
    whole_ref,
    flat_ref,
    unused_hbm,
    p0_hbm,
    tm_hbm,
    t64_hbm,
    pm_hbm,
    marks_ref,
    p1_hbm,
    p2_hbm,
    p3e_hbm,
    p3o_hbm,
    k1t_hbm,
    k2_hbm,
    k3e_hbm,
    k3o_hbm,
    stream_ref,
    rest_ref,
    wide_ref,
    hb_ref,
    count_ref,
    p0_ref,
    tm_ref,
    t64_ref,
    pm_ref,
    p1_ref,
    p2_ref,
    p3e_ref,
    p3o_ref,
    k1t_ref,
    k2_ref,
    k3e_ref,
    k3o_ref,
    s1_ref,
    s2_ref,
    s3_ref,
    t2_ref,
    t3_ref,
    w0_ref,
    k1f_ref,
    sems,
    *near_refs,
):
    copies = Copies(sems)
    if arrived is not None:
        near_ref = near_refs[0]
        got_hbm, gathered, held = arrived
        first = got_hbm.shape[1]
        copies.start_shared(got_hbm, near_ref.at[:, pl.ds(0, first), :] if gathered[0] else near_ref)
        more = (near_ref.shape[1] - first) // 2
        me = whole_ref[5]
        for side in range(2):
            for number, index, owner in pieces_of(gathered[side]):
                source = held[side][number].at[index]
                copies.start_shared(
                    source.at[pl.ds(source.shape[0] - more, more), :],
                    near_ref.at[me ^ owner, pl.ds(first + side * more, more), :],
                )
        flat_copy = copies.shared(near_ref)
    p0_copy = copies.start(p0_hbm, p0_ref)
    t64_copy = copies.start(t64_hbm, t64_ref)
    tm_copy = copies.start(tm_hbm, tm_ref)
    pm_copy = copies.start(pm_hbm, pm_ref)
    outward = []
    if arrived is not None:
        flat_copy.wait()
        flat_rows = flat_share // LANES
        counted = jnp.zeros((1, LANES), f32)
        for at in range(near_ref.shape[0]):
            flat_ref[pl.ds(at * flat_rows, flat_rows), :] = near_ref[at, pl.ds(0, flat_rows), :].astype(f32)
            counted = counted + near_ref[at, pl.ds(flat_rows, 1), :].astype(f32)
        count_ref[...] = jnp.broadcast_to(counted, (8, LANES))
    else:
        count_ref[...] = jnp.zeros((8, LANES), f32)
    marks = marks_ref[...]
    lane = lax.broadcasted_iota(jnp.int32, (BOTH, LANES), 1)
    lane1 = lax.broadcasted_iota(jnp.int32, (1, LANES), 1)
    depth = IN_CH * 49
    for at in range(C1):
        row, shift = divmod(depth * at, LANES)
        line = lanes_of(flat_ref, row, 3)
        if shift:
            line = pltpu.roll(line, 3 * LANES - shift, 1)
        w0_ref[at : at + 1, :] = line[:, : 2 * LANES]
    w0 = w0_ref[...].astype(bf16)
    w0 = jnp.concatenate([w0, w0], axis=0)
    b0 = flat_ref[ROW_B0 : ROW_B0 + 1, :]
    b0 = jnp.where(lane1 < C1, pltpu.roll(b0, C1, 1), b0)
    quarter = 16 * BOTH
    p0_copy.wait()
    for at in range(4):
        span = pl.ds(at * quarter, quarter)
        s1_ref[span, :] = (dot_nt(p0_ref[span, :], w0) + b0).astype(bf16).astype(f32)

    def tap_value(ref, pairs, tap, row_bits, col_bits, cols):
        q, src_r, src_c, down_r, down_c = tap_source(tap, row_bits, col_bits)
        if pairs == 2:
            at = stem_plane(q, src_r, src_c)
        else:
            at = (q[0] * 2 + q[1]) * 4**pairs + plane_of(src_r, src_c)
        return moved(ref[pl.ds(at * BOTH, BOTH), cols], down_r, down_c, marks)

    half = C2 // 2
    t64_copy.wait()
    for odd in range(2):
        block = jnp.concatenate(
            [flat_ref[pl.ds(ROW_K1 + 4 * odd + j, half, stride=9), :].astype(bf16) for j in range(5)], axis=1
        )
        block = dot_nn(block, t64_ref[pl.ds(C1 * (1 - odd), 5 * LANES), :])
        for j in range(5):
            k1f_ref[j, pl.ds(odd, half, stride=2), :] = block[:, j * LANES : (j + 1) * LANES]
    for j in range(5):
        k1t_ref[:, pl.ds(j * LANES, LANES)] = k1f_ref[j].astype(bf16)
    outward.append(copies.start(k1t_ref, k1t_hbm))
    everything = slice(None)
    for at, rb, cb in all_bits(2):
        for pair in range(5):
            left = tap_value(s1_ref, 2, 2 * pair, rb, cb, everything)
            if pair < 4:
                right = tap_value(s1_ref, 2, 2 * pair + 1, rb, cb, everything)
            else:
                right = jnp.zeros_like(left)
            p1_ref[pl.ds(at * BOTH, BOTH), pl.ds(pair * LANES, LANES)] = jnp.where(
                lane < C1, left, right
            ).astype(bf16)
    outward.append(copies.start(p1_ref, p1_hbm))
    b1 = flat_ref[ROW_B1 : ROW_B1 + 1, :]
    s2_ref[...] = (dot_nt(p1_ref[...], k1t_ref[...]) + b1).astype(bf16).astype(f32)
    for j in range(TAPS):
        k2_ref[pl.ds(0, C3), pl.ds(j * LANES, LANES)] = flat_ref[pl.ds(ROW_K2 + j, C3, stride=TAPS), :].astype(bf16)
    k2_ref[pl.ds(C3, C3P - C3), :] = jnp.zeros((C3P - C3, TAPS * LANES), bf16)
    outward.append(copies.start(k2_ref, k2_hbm))
    b2 = lanes_of(flat_ref, ROW_B2, 3)
    b2 = jnp.where(lax.broadcasted_iota(jnp.int32, b2.shape, 1) < C3, b2, 0.0)
    for at, rb, cb in all_bits(1):
        for tap in range(TAPS):
            t2_ref[pl.ds(at * BOTH, BOTH), pl.ds(tap * LANES, LANES)] = tap_value(
                s2_ref, 1, tap, rb, cb, everything
            ).astype(bf16)
    tm_copy.wait()
    p2_ref[...] = dot_nn(t2_ref[...], tm_ref[...]).astype(bf16)
    outward.append(copies.start(p2_ref, p2_hbm))
    s3_ref[...] = (dot_nt(p2_ref[...], k2_ref[...]) + b2).astype(bf16).astype(f32)
    for part in range(3):
        for tap in range(TAPS):
            t3_ref[pl.ds(part * BOTH, BOTH), pl.ds(tap * LANES, LANES)] = tap_value(
                s3_ref, 0, tap, (), (), pl.ds(part * LANES, LANES)
            ).astype(bf16)
    spread = dot_nn(t3_ref[...], tm_ref[...])
    spread = jnp.concatenate([spread[part * BOTH : (part + 1) * BOTH] for part in range(3)], axis=1)
    p3o_ref[...] = spread[:, :K3P].astype(bf16)
    p3e_ref[...] = pltpu.roll(spread, LANES // 2, 1)[:, :K3P].astype(bf16)
    for j in range(K3P // LANES):
        cols = pl.ds(j * LANES, LANES)
        k3e_ref[:, cols] = flat_ref[pl.ds(ROW_K3 + j, C4 // 2, stride=45), :].astype(bf16)
        k3o_ref[:, cols] = flat_ref[pl.ds(ROW_K3 + 23 + j, C4 // 2, stride=45), :].astype(bf16)
    for source, target in ((p3e_ref, p3e_hbm), (p3o_ref, p3o_hbm), (k3e_ref, k3e_hbm), (k3o_ref, k3o_hbm)):
        outward.append(copies.start(source, target))
    pm_copy.wait()
    apart = split3(
        jnp.concatenate([dot_nt(p3e_ref[...], k3e_ref[...]), dot_nt(p3o_ref[...], k3o_ref[...])], axis=1)
    )
    stream = stacked(dot_nn, apart, pm_ref[...])

    stream_ref[...] = stream

    amount = REST["head"]
    rest_ref[...] = halves(flat_ref[ROW_B3 : ROW_B3 + amount, :], flat_ref[ROW_B3 + 1 : ROW_B3 + 1 + amount, :])
    row_hb = ROW_B3 + REST["hb"]
    hb_ref[...] = halves(flat_ref[row_hb : row_hb + 8, :], flat_ref[row_hb + 1 : row_hb + 9, :])
    groups = C4 // GROUP
    row_head = ROW_B3 + REST["head"]
    low = pltpu.roll(flat_ref[pl.ds(row_head, groups, stride=SPAN), :], LANES // 2, 1)
    lane32 = lax.broadcasted_iota(jnp.int32, (groups, LANES), 1)
    for at in range(SPAN):
        high = pltpu.roll(flat_ref[pl.ds(row_head + at + 1, groups, stride=SPAN), :], LANES // 2, 1)
        wide_ref[:, pl.ds(at * LANES, LANES)] = jnp.where(lane32 < LANES // 2, low, high).astype(bf16)
        low = high
    wide_ref[:, pl.ds(SPAN * LANES, LANES)] = jnp.zeros((groups, LANES), bf16)
    for copy in outward:
        copy.wait()


def block_kernel(
    share,
    gathered,
    whole_ref,
    real_ref,
    *refs,
):
    count = [len(half) for half in gathered]
    held = [refs[: count[0]], refs[count[0] : sum(count)]]
    block_body(share, gathered, held, whole_ref, real_ref, *refs[sum(count) :])


def block_body(
    share,
    gathered,
    held,
    whole_ref,
    real_ref,
    stream_ref,
    rest_ref,
    wide_ref,
    hb_ref,
    marks_ref,
    near_ref,
    keep_hbm,
    send_hbm,
    dstream_ref,
    dblock_ref,
    dfb1_ref,
    small_ref,
    pooled_ref,
    dlog_ref,
    factor_ref,
    hid_ref,
    z_ref,
    per_ref,
    mats_ref,
    sems,
):
    copies = Copies(sems)
    me = whole_ref[5]
    for mat in range(2):
        for number, index, owner in pieces_of(gathered[mat]):
            source = held[mat][number].at[index]
            copies.start_shared(source.at[pl.ds(0, mats_ref.shape[2]), :], mats_ref.at[mat, me ^ owner])
    mats_copy = copies.shared(mats_ref)
    marks = marks_ref[...]
    stream = stream_ref[...]
    b3 = lanes_of(rest_ref, REST["b3"], 4)
    gain1, shift1, scale1, gain2, shift2, scale2 = (lanes_of(rest_ref, REST["block"] + 4 * k, 4) for k in range(6))
    fb1 = lanes_of(rest_ref, REST["fb1"], HID // LANES)
    fb2 = lanes_of(rest_ref, REST["fb2"], 4)
    gain3, shift3 = (lanes_of(rest_ref, REST["final"] + 4 * k, 4) for k in range(2))

    stream = stream + b3
    mask = marks[:, 0:1]
    per_count = marks[:, 4:5]
    cells = real_ref[4]
    count = real_ref[5]
    near = near_ref[...]
    hat1, rs1 = norm_images(stream, mask, count)
    u = (hat1 * gain1 + shift1) * mask
    u3 = split3(u)
    around = dot_nn(near, u3[0]) + (dot_nn(near, u3[1]) + dot_nn(near, u3[2]))
    pool = around * per_count - u
    stream1 = stream + scale1 * pool
    hat2, rs2 = norm_images(stream1, mask, count)
    normed = ((hat2 * gain2 + shift2) * mask).astype(bf16)
    mats_copy.wait()
    blocks = C4 // LANES

    def matrix(mat, part):
        return mats_ref[mat, :, pl.ds(part * share, share), :].reshape(HID, LANES)

    def lanes(x, part):
        return x[:, part * LANES : (part + 1) * LANES]

    hidden = fb1
    for part in range(blocks):
        hidden = hidden + dot_nt(lanes(normed, part), matrix(0, part))
    hid_ref[...] = hidden
    active = (hidden * (0.5 * (1.0 + erf(hidden * math.sqrt(0.5))))).astype(bf16)
    branch = jnp.concatenate([dot_nn(active, matrix(1, part)) for part in range(blocks)], axis=1) + fb2
    stream2 = stream1 + scale2 * branch
    hat3, rs3 = norm_images(stream2, mask, count)
    outs = (hat3 * gain3 + shift3) * mask
    row8 = lax.broadcasted_iota(jnp.int32, (8, 1), 0)
    first, second = row8 == 0, row8 == 1

    def by_row(a, b):
        return jnp.where(first, a, jnp.where(second, b, 0.0))

    pooled = (by_row(rowsum(outs[:ROWS]), rowsum(outs[ROWS:])) / cells).astype(bf16)
    pooled_f = pooled.astype(f32)
    pooled_ref[...] = pooled_f
    in_group, in_place, own_row = head_masks()
    picked = jnp.where(in_place, jnp.where(own_row, pooled_f[0:1, :], pooled_f[1:2, :]), 0.0).astype(bf16)
    by_place = dot_nt(picked, in_group.astype(bf16)).astype(bf16)
    z_ref[...] = dot_nn(by_place, wide_ref[...])
    column = lax.broadcasted_iota(jnp.int32, (8, CLSP), 1)
    hb = lanes_of(hb_ref, 0, 8)
    logits = jnp.zeros((MICRO, CLSP), f32)
    for place in range(GROUP):
        at, shift = divmod(CLS * place, LANES)
        window = z_ref[pl.ds(MICRO * place, MICRO), pl.ds(at * LANES, CLSP + LANES)]
        if shift:
            window = pltpu.roll(window, CLSP + LANES - shift, 1)
        logits = logits + window[:, :CLSP]
    logits = by_row(logits[0:1], logits[1:2]) + hb
    logits = jnp.where(column < CLS, logits, -1e30)
    top = jnp.max(logits, axis=1, keepdims=True)
    powers = jnp.exp(logits - top)
    mass = jnp.sum(powers, axis=1, keepdims=True)
    own = jnp.where(first, whole_ref[0], whole_ref[1])
    other = jnp.where(first, whole_ref[2], whole_ref[3])
    mix = by_row(real_ref[0], real_ref[1])
    target = jnp.where(column == own, mix, 0.0) + jnp.where(column == other, 1.0 - mix, 0.0)
    valid = by_row(real_ref[2], real_ref[3])
    logp = logits - top - jnp.log(mass)
    losses = -jnp.sum(target * logp, axis=1, keepdims=True) * valid
    loss = split3(jnp.broadcast_to(jnp.sum(losses, axis=0, keepdims=True), (1, LANES)))
    dlogits = (powers / mass * jnp.sum(target, axis=1, keepdims=True) - target) * valid
    dlog_ref[...] = dlogits
    padded = jnp.concatenate([dlogits, jnp.zeros((8, LANES), f32)], axis=1)
    for place in range(GROUP):
        at, shift = divmod(CLS * place, LANES)
        window = pltpu.roll(padded, shift, 1) if shift else padded
        per_group = two(dot_nt, split2(window), wide_ref[:, pl.ds(at * LANES, CLSP + LANES)])
        per_ref[pl.ds(MICRO * place, MICRO), :] = per_group[:MICRO]
    per3 = split3(per_ref[...])
    ones = in_group.astype(bf16)
    by_channel = dot_nn(per3[0], ones) + (dot_nn(per3[1], ones) + dot_nn(per3[2], ones))
    dpooled = by_row(
        rowsum(jnp.where(in_place & own_row, by_channel, 0.0)),
        rowsum(jnp.where(in_place & ~own_row, by_channel, 0.0)),
    )
    dpooled = dpooled / cells
    douts = jnp.concatenate(
        [
            jnp.broadcast_to(dpooled[0:1], (ROWS, C4)),
            jnp.broadcast_to(dpooled[1:2], (ROWS, C4)),
        ],
        axis=0,
    ) * mask
    row8w = lax.broadcasted_iota(jnp.int32, (8, C4), 0)

    def stack8(values):
        out = jnp.zeros((8, C4), f32)
        for at, v in enumerate(values):
            out = jnp.where(row8w == at, v, out)
        return out

    dgain3, dshift3 = rowsum(douts * hat3), rowsum(douts)
    dstream2 = norm_images_back(douts, hat3, rs3, gain3, mask, count)
    dscale2 = rowsum(dstream2 * branch)
    dbranch = dstream2 * scale2
    dfb2 = rowsum(dbranch)
    dbr = split2(dbranch)
    dactive = None
    for part in range(blocks):
        term = two(dot_nt, (lanes(dbr[0], part), lanes(dbr[1], part)), matrix(1, part))
        dactive = term if dactive is None else dactive + term
    hidden = hid_ref[...]
    slope = 0.5 * (1.0 + erf(hidden * math.sqrt(0.5))) + hidden * (
        jnp.exp(-0.5 * hidden * hidden) * (1.0 / math.sqrt(2.0 * math.pi))
    )
    dhidden = dactive * slope
    dfb1_ref[...] = jnp.broadcast_to(rowsum(dhidden), (8, HID))
    dhid = split2(dhidden)

    core, corner_high, corner_low = whole_ref[4], (me // 4) % 2, (me // 2) % 2
    active_f = active.astype(f32)
    sides = (
        (jnp.concatenate([d.astype(f32) for d in dhid], axis=0), jnp.concatenate([normed, normed], axis=0)),
        (jnp.concatenate([active_f, active_f], axis=0), jnp.concatenate(dbr, axis=0)),
    )
    each = 2 * share
    factor_ref[:, pl.ds(FACTOR_LOSS, FACTOR_ROWS - FACTOR_LOSS), :] = jnp.zeros(
        (2, FACTOR_ROWS - FACTOR_LOSS, LANES), bf16
    )
    for mat, (hidden_side, channel_side) in enumerate(sides):
        for at in range(HID // LANES):
            cols = slice(at * LANES, (at + 1) * LANES)
            factor_ref[mat, pl.ds(at * LANES, LANES), :] = hidden_side[:, cols].T.astype(bf16)
        for part in range(blocks):
            factor_ref[mat, pl.ds(HID + part * LANES, LANES), :] = lanes(channel_side, part)

        for k in range(3):
            factor_ref[mat, pl.ds(FACTOR_LOSS + k, 1), :] = loss[k]

        def send_out(mat, target):
            for chip in range(HID // each):
                square, high, low = chip // 4, (chip // 2) % 2, chip % 2
                for side, (bit, mine, place) in enumerate(((high, corner_high, low), (low, corner_low, high))):
                    begin = jnp.where(mine == bit, FACTOR_OWN[side], FACTOR_OTHER[side])
                    to = pl.multiple_of(begin + (square * 2 + place) * share, share)
                    source = factor_ref.at[mat, pl.ds(chip * each + side * share, share), :]
                    copies.start_out(source, target.at[pl.ds(to, share), :])
            copies.start_out(
                factor_ref.at[mat, pl.ds(HID, blocks * LANES), :], target.at[pl.ds(FACTOR_CHANNELS, blocks * LANES), :]
            )
            rest = pl.ds(FACTOR_LOSS, FACTOR_ROWS - FACTOR_LOSS)
            copies.start_out(factor_ref.at[mat, rest, :], target.at[rest, :])

        pl.when(core == mat)(functools.partial(send_out, mat, keep_hbm))
        pl.when(core != mat)(functools.partial(send_out, mat, send_hbm))
    dnormed = jnp.concatenate([two(dot_nn, dhid, matrix(0, part)) for part in range(blocks)], axis=1)
    dgain2, dshift2 = rowsum(dnormed * hat2), rowsum(dnormed * mask)
    dstream1 = dstream2 + norm_images_back(dnormed, hat2, rs2, gain2, mask, count)
    dscale1 = rowsum(dstream1 * pool)
    dpool = dstream1 * scale1
    back = split3(dpool * per_count)
    du = dot_nn(near, back[0]) + (dot_nn(near, back[1]) + dot_nn(near, back[2])) - dpool
    dgain1, dshift1 = rowsum(du * hat1), rowsum(du)
    dstream = dstream1 + norm_images_back(du, hat1, rs1, gain1, mask, count)
    dblock_ref[...] = stack8([dgain1, dshift1, dscale1, dgain2, dshift2, dscale2])
    small_ref[...] = stack8([rowsum(dstream), dfb2, dgain3, dshift3])
    dstream_ref[...] = dstream
    copies.out(factor_ref).wait()


def backward_kernel(
    unused_one_ref,
    unused_two_ref,
    dstream_ref,
    p0_ref,
    p1_ref,
    p2_ref,
    p3e_ref,
    p3o_ref,
    k1t_ref,
    k2_ref,
    k3e_ref,
    k3o_ref,
    tm_ref,
    t64_ref,
    pm_ref,
    marks_ref,
    dblock_ref,
    dfb1_ref,
    small_ref,
    pooled_ref,
    dlog_ref,
    whole_ref,
    keep_a_hbm,
    keep_b_hbm,
    send_a_hbm,
    send_b_hbm,
    out_ref,
    ds3_ref,
    ds2_ref,
    ds1_ref,
    dt_ref,
    dk1t_ref,
    rest_ref,
    sems,
):
    marks = marks_ref[...]
    lane = lax.broadcasted_iota(jnp.int32, (BOTH, LANES), 1)
    lane1 = lax.broadcasted_iota(jnp.int32, (1, LANES), 1)
    wide = TAPS * LANES
    grad3 = split3(dstream_ref[...])
    apart = stacked(dot_nt, grad3, pm_ref[...])
    half = C4 // 2
    even, odd = split2(apart[:, :half]), split2(apart[:, half:])
    tall_even, tall_odd = jnp.concatenate(even, axis=0), jnp.concatenate(odd, axis=0)

    def by_even(cols):
        return dot_tn(tall_even, jnp.concatenate([p3e_ref[:, cols]] * 2, axis=0))

    def by_odd(cols):
        return dot_tn(tall_odd, jnp.concatenate([p3o_ref[:, cols]] * 2, axis=0))

    last = K3P // LANES - 1
    for j in range(last):
        cols = pl.ds(j * LANES, LANES)
        out_ref[pl.ds(ROW_K3 + 23 + j, half, stride=45), :] = by_odd(cols)
        if j:
            out_ref[pl.ds(ROW_K3 + j, half, stride=45), :] = by_even(cols)
    cols = pl.ds(last * LANES, LANES)
    out_ref[pl.ds(ROW_K3 + last, half, stride=45), :] = by_even(cols)
    tail = by_odd(cols)
    begin = by_even(pl.ds(0, LANES))
    rows = lax.broadcasted_iota(jnp.int32, (half, LANES), 0)
    out_ref[pl.ds(ROW_K3, half, stride=45), :] = begin + jnp.where(rows == 0, 0.0, pltpu.roll(tail, 1, 0))
    tail = tail[half - 1 : half]
    ds3_ref[...] = jnp.zeros_like(ds3_ref)
    position = lax.broadcasted_iota(jnp.int32, (BOTH, K3P), 1)
    nat = jnp.where(position < LANES // 2, 0.0, two(dot_nn, even, k3e_ref[...]))
    nat = pltpu.roll(nat, K3P - LANES // 2, 1) + jnp.where(
        position < C3 * TAPS, two(dot_nn, odd, k3o_ref[...]), 0.0
    )
    for part in range(3):
        width = min(wide, K3P - part * wide)
        pieces = split2(nat[:, part * wide : part * wide + width])
        by_tap = dot_nt(pieces[0], tm_ref[:, pl.ds(0, width)]) + dot_nt(pieces[1], tm_ref[:, pl.ds(0, width)])
        for tap in range(TAPS):
            q, src_r, src_c, down_r, down_c = tap_source(tap, (), ())
            at = q[0] * 2 + q[1]
            ds3_ref[pl.ds(at * BOTH, BOTH), pl.ds(part * LANES, LANES)] += moved_back(
                by_tap[:, tap * LANES : (tap + 1) * LANES], down_r, down_c, marks
            )
    db2 = rowsum(ds3_ref[...])
    for k in range(2):
        out_ref[ROW_B2 + k : ROW_B2 + k + 1, :] = db2[:, k * LANES : (k + 1) * LANES]
    out_ref[ROW_K3 : ROW_K3 + 1, :] += jnp.where(lane1 < LANES // 2, db2[:, 2 * LANES :], 0.0)
    grad = split2(ds3_ref[...])
    grad_real = (grad[0][:, :C3], grad[1][:, :C3])
    for j in range(TAPS):
        cols = pl.ds(j * LANES, LANES)
        value = dot_tn(grad[0], p2_ref[:, cols]) + dot_tn(grad[1], p2_ref[:, cols])
        out_ref[pl.ds(ROW_K2 + j, C3, stride=TAPS), :] = value[:C3]
    pieces = split2(two(dot_nn, grad, k2_ref[...]))
    dt_ref[...] = two(dot_nt, pieces, tm_ref[...])
    ds2_ref[...] = jnp.zeros_like(ds2_ref)
    for at, rb, cb in all_bits(1):
        for tap in range(TAPS):
            q, src_r, src_c, down_r, down_c = tap_source(tap, rb, cb)
            to = (q[0] * 2 + q[1]) * 4 + plane_of(src_r, src_c)
            ds2_ref[pl.ds(to * BOTH, BOTH), :] += moved_back(
                dt_ref[pl.ds(at * BOTH, BOTH), pl.ds(tap * LANES, LANES)], down_r, down_c, marks
            )
    out_ref[ROW_B1 : ROW_B1 + 1, :] = rowsum(ds2_ref[...])
    grad = split2(ds2_ref[...])
    few = C2 // 2
    for j in range(5):
        cols = pl.ds(j * LANES, LANES)
        dk1t_ref[j] = dot_tn(grad[0], p1_ref[:, cols]) + dot_tn(grad[1], p1_ref[:, cols])
    evens, odds = (
        two(
            dot_nt,
            split2(jnp.concatenate([dk1t_ref[j, pl.ds(odd, few, stride=2), :] for j in range(5)], axis=1)),
            t64_ref[pl.ds(C1 * (1 - odd), 5 * LANES), :],
        )
        for odd in range(2)
    )
    for j in range(9):
        if j < 4:
            value = evens[:, j * LANES : (j + 1) * LANES]
        elif j == 4:
            value = evens[:, 4 * LANES :] + odds[:, :LANES]
        else:
            value = odds[:, (j - 4) * LANES : (j - 3) * LANES]
        out_ref[pl.ds(ROW_K1 + j, few, stride=9), :] = value
    ds1_ref[...] = jnp.zeros_like(ds1_ref)
    for pair in range(5):
        values = two(dot_nn, grad, k1t_ref[:, pl.ds(pair * LANES, LANES)])
        for at, rb, cb in all_bits(2):
            here = values[at * BOTH : (at + 1) * BOTH]
            for side in range(2):
                tap = 2 * pair + side
                if tap >= TAPS:
                    continue
                q, src_r, src_c, down_r, down_c = tap_source(tap, rb, cb)
                to = stem_plane(q, src_r, src_c)
                mine = (lane < C1) if side == 0 else (lane >= C1)
                ds1_ref[pl.ds(to * BOTH, BOTH), :] += moved_back(
                    jnp.where(mine, here, 0.0), down_r, down_c, marks
                )
    db0 = rowsum(ds1_ref[...])
    db0 = db0 + pltpu.roll(db0, LANES // 2, 1)
    stem = jnp.zeros((LANES, 2 * LANES), f32)
    for at in range(4):
        span = pl.ds(at * 16 * BOTH, 16 * BOTH)
        grad = split2(ds1_ref[span, :])
        stem = stem + (dot_tn(grad[0], p0_ref[span, :]) + dot_tn(grad[1], p0_ref[span, :]))
    stem = stem[:C1] + stem[C1:]
    depth = IN_CH * 49
    held = jnp.zeros((1, 3 * LANES), f32)
    done = 0
    for at in range(C1):
        row, shift = divmod(depth * at, LANES)
        line = jnp.concatenate([stem[at : at + 1], jnp.zeros((1, LANES), f32)], axis=1)
        if shift:
            line = pltpu.roll(line, shift, 1)
        while done < row:
            out_ref[done : done + 1, :] = held[:, :LANES]
            held = jnp.concatenate([held[:, LANES:], jnp.zeros((1, LANES), f32)], axis=1)
            done += 1
        held = held + line
    out_ref[done : done + 1, :] = held[:, :LANES]
    if done < ROW_B0:
        out_ref[ROW_B0 : ROW_B0 + 1, :] = held[:, LANES : 2 * LANES]
    out_ref[ROW_B0 : ROW_B0 + 1, :] += jnp.where(lane1 < LANES // 2, 0.0, db0)

    lead = 5

    def put(name, value):
        for k in range(value.shape[1] // LANES):
            at = lead + REST[name] + k
            rest_ref[at : at + 1, :] = value[:, k * LANES : (k + 1) * LANES]

    rest_ref[0:8, :] = jnp.zeros((8, LANES), f32)
    put("b3", small_ref[0:1, :])
    for k in range(6):
        at = lead + REST["block"] + 4 * k
        for i in range(4):
            rest_ref[at + i : at + i + 1, :] = dblock_ref[k : k + 1, i * LANES : (i + 1) * LANES]
    put("fb1", dfb1_ref[0:1, :])
    put("fb2", small_ref[1:2, :])
    put("final", jnp.concatenate([small_ref[2:3, :], small_ref[3:4, :]], axis=1))
    dlog = dlog_ref[...]
    put("hb", dlog[0:1] + dlog[1:2])
    rest_ref[lead + REST["end"] : lead + REST["end"] + 11, :] = jnp.zeros((11, LANES), f32)
    pooled = pooled_ref[...]
    in_group, in_place, own_row = head_masks()
    picked = jnp.where(in_place, jnp.where(own_row, pooled[0:1, :], pooled[1:2, :]), 0.0).astype(bf16)
    by_group = dot_nt(in_group.astype(bf16), picked)
    padded = jnp.concatenate([dlog, jnp.zeros((8, LANES), f32)], axis=1)
    groups = C4 // GROUP
    written = -1
    for place in range(GROUP):
        at, shift = divmod(CLS * place, LANES)
        window = pltpu.roll(padded, shift, 1) if shift else padded
        ours = by_group[:, MICRO * place : MICRO * place + 1]
        others = by_group[:, MICRO * place + 1 : MICRO * place + 2]
        for k in range(CLSP // LANES + 1):
            if (at + k) * LANES >= CLS * (place + 1):
                break
            block = slice(k * LANES, (k + 1) * LANES)
            value = ours * window[0:1, block] + others * window[1:2, block]
            target = pl.ds(lead + REST["head"] + at + k, groups, stride=SPAN)
            if at + k == written:
                rest_ref[target, :] += value
            else:
                rest_ref[target, :] = value
            written = at + k
    first = ROW_B3 + 3
    out_ref[ROW_B3 : first, :] = halves(rest_ref[lead - 1 : lead + 2, :], rest_ref[lead : lead + 3, :])
    out_ref[ROW_B3 : ROW_B3 + 1, :] += tail
    step = 508
    for at in range(0, REST["end"], step):
        out_ref[first + at : first + at + step, :] = halves(
            rest_ref[lead + 2 + at : lead + 2 + at + step, :], rest_ref[lead + 3 + at : lead + 3 + at + step, :]
        )
    end = first + REST["end"]
    out_ref[end : out_ref.shape[0], :] = jnp.zeros((out_ref.shape[0] - end, LANES), f32)
    chips, cut, unused_lanes = keep_a_hbm.shape
    each = cut + keep_b_hbm.shape[1]
    core = whole_ref[4]
    copies = Copies(sems)
    for chunk in range(2 * chips):
        for keep, send, at, rows in ((keep_a_hbm, send_a_hbm, 0, cut), (keep_b_hbm, send_b_hbm, cut, each - cut)):
            source = out_ref.at[pl.ds(chunk * each + at, rows), :]
            ours, theirs = (keep, send) if chunk % 2 == 0 else (send, keep)
            pl.when(core == 0)(functools.partial(copies.start_out, source, ours.at[chunk // 2]))
            pl.when(core != 0)(functools.partial(copies.start_out, source, theirs.at[chunk // 2]))
    copies.out(out_ref).wait()


def product_kernel(whole_ref, keep_ref, got_ref, far_a_ref, far_b_ref, keep_a_ref, send_a_ref, keep_b_ref, send_b_ref, loss_ref):
    me = whole_ref[5]
    loss = keep_ref[pl.ds(FACTOR_LOSS, 8), :].astype(f32) + got_ref[pl.ds(FACTOR_LOSS, 8), :].astype(f32)
    loss_ref[...] = jnp.broadcast_to(loss[0:1] + (loss[1:2] + loss[2:3]), (8, LANES))
    squares, share, unused_channels = keep_a_ref.shape
    blocks = C4 // LANES
    ways = (
        (0, far_a_ref, 0, QUARTER, (me // 2) % 2, keep_a_ref, send_a_ref),
        (1, far_b_ref, C4, 0, (me // 4) % 2, keep_b_ref, send_b_ref),
    )
    for way, far_ref, far_hidden, far_channels, mine, to_keep_ref, to_send_ref in ways:
        own = pl.ds(FACTOR_OWN[way], QUARTER)
        hidden = jnp.concatenate(
            [keep_ref[own, :], got_ref[own, :]] + [far_ref[k, pl.ds(far_hidden, QUARTER), :] for k in range(2)], axis=1
        )
        channels = [
            jnp.concatenate(
                [
                    keep_ref[pl.ds(FACTOR_CHANNELS + part * LANES, LANES), :],
                    got_ref[pl.ds(FACTOR_CHANNELS + part * LANES, LANES), :],
                ]
                + [far_ref[k, pl.ds(far_channels + part * LANES, LANES), :] for k in range(2)],
                axis=0,
            )
            for part in range(blocks)
        ]
        product = dot_nn(hidden, jnp.concatenate(channels, axis=1))
        for square in range(squares):
            first, second = (product[(2 * square + k) * share : (2 * square + k + 1) * share] for k in range(2))
            to_keep_ref[square] = jnp.where(mine == 0, first, second)
            to_send_ref[square] = jnp.where(mine == 0, second, first)


def passes(a, b, dot, many):
    pairs = [(0, 0), (0, 1), (1, 0)]
    if many:
        pairs += [(0, 2), (1, 1), (2, 0)]
    axis = 0 if dot is dot_tn else 1
    return dot(
        jnp.concatenate([a[i] for i, unused in pairs], axis=axis),
        jnp.concatenate([b[j] for unused, j in pairs], axis=0),
    )


def gram_kernel(scale_ref, terms, momentum_ref, loss_ref, ortho_ref, new_ref, packed_ref):
    grad = functools.reduce(jnp.add, [term[...] for term in terms]) * scale_ref[0]
    new = 0.95 * momentum_ref[...] + grad
    new_ref[...] = new
    ortho = grad + 0.95 * new
    ortho_ref[...] = ortho
    parts = split3(ortho)

    def cut(k):
        return tuple(p[:, k * LANES : (k + 1) * LANES] for p in parts)

    for at, (i, j) in enumerate(PAIRS):
        block = passes(cut(i), cut(j), dot_tn, True)
        if at == 0:
            row = lax.broadcasted_iota(jnp.int32, block.shape, 0)
            col = lax.broadcasted_iota(jnp.int32, block.shape, 1)
            block = jnp.where((row == LANES - 1) & (col == 0), loss_ref[0:1, 0:1], block)
        packed_ref[pl.ds(at * LANES, LANES), :] = block


def newton_steps(gram, ortho, steps, last):
    wide_row = lax.broadcasted_iota(jnp.int32, (C4, C4), 0)
    wide_col = lax.broadcasted_iota(jnp.int32, (C4, C4), 1)
    for iteration in steps:
        many = iteration == 0
        split = split3 if many else split2
        parts = split(gram)
        poly = jnp.where(wide_row == wide_col, 3.4445, 0.0) + (
            -4.775 * gram + 2.0315 * passes(parts, parts, dot_nn, many)
        )
        poly_parts = split(poly)
        ortho = passes(split(ortho), poly_parts, dot_nn, many)
        if iteration < last:
            gram = passes(split(passes(poly_parts, parts, dot_nn, many)), poly_parts, dot_nn, many)
    return gram, ortho


def newton_first_kernel(steps, packed_ref, ortho_ref, out_ref, gram_ref, loss_ref):
    row = lax.broadcasted_iota(jnp.int32, (LANES, LANES), 0)
    col = lax.broadcasted_iota(jnp.int32, (LANES, LANES), 1)
    trace = jnp.zeros((1, 1), f32)
    for at, (i, j) in enumerate(PAIRS):
        block = packed_ref[pl.ds(at * LANES, LANES), :]
        if at == 0:
            loss_ref[...] = jnp.broadcast_to(block[LANES - 1 : LANES, 0:1], (8, LANES))
            block = jnp.where((row == LANES - 1) & (col == 0), block.T, block)
        gram_ref[pl.ds(i * LANES, LANES), pl.ds(j * LANES, LANES)] = block
        if i == j:
            trace = trace + total(jnp.where(row == col, block, 0.0))
        else:
            gram_ref[pl.ds(j * LANES, LANES), pl.ds(i * LANES, LANES)] = block.T
    inverse = 1.0 / (jnp.sqrt(trace) + 1e-07)
    gram, ortho = newton_steps(
        gram_ref[...] * (inverse * inverse), ortho_ref[...] * inverse, range(steps), NS_ITERS - 1
    )
    gram_ref[...] = gram
    out_ref[...] = ortho


def newton_last_kernel(steps, unused_ref, gram_ref, ortho_ref, out_ref):
    unused_gram, ortho = newton_steps(gram_ref[...], ortho_ref[...], range(steps, NS_ITERS), NS_ITERS - 1)
    out_ref[...] = ortho


def shape(*dims, dtype=f32):
    return jax.ShapeDtypeStruct(dims, dtype)


def kernel_call(body, outs, scratch, smem, kept, count, micros, outs_kept=0, aliases=None):
    vmem = pl.BlockSpec(memory_space=pltpu.VMEM)
    scalar = pl.BlockSpec(memory_space=pltpu.SMEM)
    anywhere = pl.BlockSpec(memory_space=pl.ANY)
    if isinstance(kept, int):
        specs = [anywhere] * kept + [vmem] * (count - smem - kept)
    else:
        specs = [anywhere if k else vmem for k in kept[smem:]] + [vmem] * (count - len(kept))
    return pl.pallas_call(
        body,
        out_shape=outs,
        in_specs=[scalar] * smem + specs,
        out_specs=[anywhere] * outs_kept + [vmem] * (len(outs) - outs_kept),
        scratch_shapes=scratch,
        input_output_aliases=aliases or {},
        compiler_params=pltpu.CompilerParams(vmem_limit_bytes=60 * 1024 * 1024),
        cost_estimate=pl.CostEstimate(flops=10**6, bytes_accessed=micros * 3_000_000, transcendentals=0),
    )


def pack_kernel(valid_ref, mats_ref, flat_ref, one_ref, two_ref, out_ref):
    share = mats_ref.shape[1]
    rows = C4 // LANES * share
    first = out_ref.shape[0]
    more = one_ref.shape[0] - rows
    for mat, to_ref in enumerate((one_ref, two_ref)):
        for part in range(C4 // LANES):
            to_ref[pl.ds(part * share, share), :] = mats_ref[mat, :, pl.ds(part * LANES, LANES)].astype(bf16)
    count = flat_ref.shape[0]
    counted = (valid_ref[0] + valid_ref[1]).astype(f32)

    def fill(to_ref, at, begin, amount):
        held = min(amount, count - begin)
        to_ref[pl.ds(at, held), :] = flat_ref[pl.ds(begin, held), :].astype(bf16)
        if held < amount:
            to_ref[pl.ds(at + held, amount - held), :] = jnp.full((amount - held, LANES), counted, f32).astype(bf16)

    fill(out_ref, 0, 0, first)
    if more:
        fill(one_ref, rows, first, more)
        fill(two_ref, rows, first + more, more)


def run_pack(valid, mats, flat, split):
    rows = (flat.shape[0] // 16 + 1) * 16
    more = 0
    with_mats = shape(C4 // LANES * mats.shape[1] + more, LANES, dtype=bf16)
    outs = [with_mats, with_mats, shape(rows - 2 * more, LANES, dtype=bf16)]
    return kernel_call(pack_kernel, outs, [], 1, 0, 3, 2)(valid, mats, flat)


def run_conv(whole, flat, gathered, tie, moved, marks, flat_share):
    half = C4 // 2
    moved_outs = [
        shape(16 * BOTH, 5 * LANES, dtype=bf16),
        shape(4 * BOTH, TAPS * LANES, dtype=bf16),
        shape(BOTH, K3P, dtype=bf16),
        shape(BOTH, K3P, dtype=bf16),
        shape(C2, 5 * LANES, dtype=bf16),
        shape(C3P, TAPS * LANES, dtype=bf16),
        shape(half, K3P, dtype=bf16),
        shape(half, K3P, dtype=bf16),
    ]
    outs = moved_outs + [
        shape(BOTH, C4),
        shape(REST["head"], LANES),
        shape(C4 // GROUP, (SPAN + 1) * LANES, dtype=bf16),
        shape(8, LANES),
        shape(8, LANES),
    ]
    scratch = [pltpu.VMEM(a.shape, a.dtype) for a in moved + moved_outs]
    scratch += [
        pltpu.VMEM((64 * BOTH, LANES), f32),
        pltpu.VMEM((16 * BOTH, LANES), f32),
        pltpu.VMEM((4 * BOTH, C3P), f32),
        pltpu.VMEM((4 * BOTH, TAPS * LANES), bf16),
        pltpu.VMEM((3 * BOTH, TAPS * LANES), bf16),
        pltpu.VMEM((C1, 2 * LANES), f32),
        pltpu.VMEM((5, C2, LANES), f32),
        pltpu.SemaphoreType.DMA((16,)),
    ]
    if flat_share % LANES:
        args = [whole, flat, tie] + moved + [marks]
        kept = [False, False] + [True] * 5
    else:
        arrays = [array for side in gathered for array, *unused in side]
        args = [whole, flat] + arrays + [tie] + moved + [marks]
        kept = [False] + [True] * (len(arrays) + 6)
        devices_count = flat.shape[0]
        flat_rows = flat_share // LANES
        scratch += [
            pltpu.VMEM((devices_count, (flat_rows // 16 + 1) * 16, LANES), bf16),
            pltpu.VMEM((devices_count * flat_rows, LANES), f32),
        ]
    body = functools.partial(conv_kernel, flat_share, gathered)
    return kernel_call(body, outs, scratch, 1, kept, len(args), 12, 8)(*args)


def run_block(whole, real, gathered, made, marks, near, share):
    outs = [shape(FACTOR_ROWS, LANES, dtype=bf16)] * 2 + [
        shape(BOTH, C4),
        shape(8, C4),
        shape(8, HID),
        shape(8, C4),
        shape(8, C4),
        shape(8, CLSP),
    ]
    scratch = [
        pltpu.VMEM((2, FACTOR_ROWS, LANES), bf16),
        pltpu.VMEM((BOTH, HID), f32),
        pltpu.VMEM((C4 // GROUP, (SPAN + 1) * LANES), f32),
        pltpu.VMEM((MICRO * GROUP, C4 // GROUP), f32),
        pltpu.VMEM((2, HID // share, C4 // LANES * share, LANES), bf16),
        pltpu.SemaphoreType.DMA((2,)),
    ]
    arrays = [array for side in gathered for array, *unused in side]
    args = [whole, real] + arrays + list(made) + [marks, near]
    kept = [False] * 2 + [True] * len(arrays)
    body = functools.partial(block_kernel, share, gathered)
    return kernel_call(body, outs, scratch, 2, kept, len(args), 12, 2)(*args)


def run_backward(args, chips, each):
    scratch = [
        pltpu.VMEM((2 * chips * each, LANES), f32),
        pltpu.VMEM((4 * BOTH, C3P), f32),
        pltpu.VMEM((16 * BOTH, LANES), f32),
        pltpu.VMEM((64 * BOTH, LANES), f32),
        pltpu.VMEM((4 * BOTH, TAPS * LANES), f32),
        pltpu.VMEM((5, C2, LANES), f32),
        pltpu.VMEM((REST["end"] + 16, LANES), f32),
        pltpu.SemaphoreType.DMA((2,)),
    ]
    cut = -(-each // 16) * 8
    outs = [shape(chips, cut, LANES), shape(chips, each - cut, LANES)] * 2

    def body(*refs):
        backward_kernel(*refs[1 : len(args)], refs[0], *refs[len(args) :])

    return kernel_call(body, outs, scratch, 1, 2, len(args), 20, 4)(*args)


def run_product(whole, through, keep, got, far_a, far_b, squares, share):
    outs = [shape(*x.shape) for x in through] + [shape(squares, share, C4)] * 4 + [shape(8, LANES)]
    count = len(through)

    def body(*refs):
        product_kernel(refs[0], *refs[1 + count : 5 + count], *refs[5 + 2 * count :])

    return kernel_call(body, outs, [], 1, count, 5 + count, 3, count, {1 + k: k for k in range(count)})(
        whole, *through, keep, got, far_a, far_b
    )


def sum_kernel(whole_ref, keep_one_ref, got_one_ref, keep_two_ref, got_two_ref, *out_refs):
    square = whole_ref[5] // 8
    share = keep_one_ref.shape[1]
    for j, out_ref in enumerate(out_refs):
        entry = square ^ j
        out_ref[pl.ds(0, share), :] = keep_one_ref[entry] + got_one_ref[entry]
        out_ref[pl.ds(share, share), :] = keep_two_ref[entry] + got_two_ref[entry]


def run_sum(whole, tie, keep_one, got_one, keep_two, got_two):
    squares, share, unused_channels = keep_one.shape
    outs = [shape(2 * share, C4)] * squares

    def body(*refs):
        sum_kernel(refs[0], *refs[2:])

    return kernel_call(body, outs, [], 1, 1, 6, 2)(whole, tie, keep_one, got_one, keep_two, got_two)


def halve_kernel(whole_ref, tie_ref, keep_a, got_a, keep_b, got_b, sent_a, left_a, sent_b, left_b):
    me = whole_ref[5]
    high, low = (me // 4) % 2, (me // 2) % 2
    for place in range(2):
        first, second = (keep_a[0, k, place] + got_a[0, k, place] for k in range(2))
        sent_a[place, 0] = jnp.where(high == 0, second, first)
        left_a[place, 0] = jnp.where(high == 0, first, second)
        first, second = (keep_b[0, place, k] + got_b[0, place, k] for k in range(2))
        sent_b[place, 0] = jnp.where(low == 0, second, first)
        left_b[place, 0] = jnp.where(low == 0, first, second)


def run_halve(whole, tie, keep_a, got_a, keep_b, got_b):
    squares = keep_a.shape[0] // 4
    inputs = [x.reshape(squares, 2, 2, *x.shape[1:]) for x in (keep_a, got_a, keep_b, got_b)]
    rows = [x.shape[3] for x in inputs]
    outs = [shape(2, squares, rows[0], LANES)] * 2 + [shape(2, squares, rows[2], LANES)] * 2
    return pl.pallas_call(
        halve_kernel,
        grid=(squares,),
        out_shape=outs,
        in_specs=[pl.BlockSpec(memory_space=pltpu.SMEM), pl.BlockSpec(memory_space=pl.ANY)]
        + [pl.BlockSpec((1, 2, 2, r, LANES), lambda i: (i, 0, 0, 0, 0)) for r in rows],
        out_specs=[pl.BlockSpec((2, 1, x.shape[2], LANES), lambda i: (0, i, 0, 0)) for x in outs],
        compiler_params=pltpu.CompilerParams(vmem_limit_bytes=60 * 1024 * 1024),
        cost_estimate=pl.CostEstimate(flops=10**6, bytes_accessed=15_000_000, transcendentals=0),
    )(whole, tie, *inputs)


def run_gram(scale, terms, momentum, loss):
    rows, count = momentum.shape[0], len(terms)
    outs = [shape(rows, C4), shape(rows, C4), shape(len(PAIRS) * LANES, LANES)]

    def body(*refs):
        gram_kernel(refs[0], refs[1 : 1 + count], *refs[1 + count :])

    return kernel_call(body, outs, [], 1, 0, 3 + count, 4)(scale, *terms, momentum, loss)


def run_newton_first(packed, ortho, steps):
    outs = [shape(*ortho.shape), shape(C4, C4), shape(8, LANES)]
    return kernel_call(functools.partial(newton_first_kernel, steps), outs, [], 0, 0, 2, 12)(packed, ortho)


def run_newton_last(tie, gram, ortho, steps):
    outs = [shape(*ortho.shape)]
    return kernel_call(functools.partial(newton_last_kernel, steps), outs, [], 0, 1, 3, 8)(tie, gram, ortho)[0]


def patches(images, resolution, partner_col, mix_col):
    pictures = images[:, 0].astype(f32)
    dims = (1, 1, RES_L, RES_L)
    inside = (lax.broadcasted_iota(jnp.int32, dims, 2) < resolution) & (
        lax.broadcasted_iota(jnp.int32, dims, 3) < resolution
    )
    mixing = mix_col[:, None, None, None]
    other = jnp.where(partner_col[:, None, None, None] == 0, pictures[0][None], pictures[1][None])
    pixels = jnp.where(inside, mixing * pictures + (1.0 - mixing) * other, 0.0).astype(bf16)
    padded = jnp.pad(pixels, ((0, 0), (0, 0), (2, 1), (2, 1)))
    size = RES_STEP + 3
    blocks = [
        padded[:, :, RES_STEP * i : RES_STEP * i + size, RES_STEP * j : RES_STEP * j + size]
        for i in range(SIDE)
        for j in range(SIDE)
    ]
    blocks = jnp.stack(blocks, axis=1).reshape(MICRO * SIDE * SIDE, IN_CH, size, size)
    depth = IN_CH * 49
    choose = jnp.eye(depth, dtype=bf16).reshape(IN_CH, 7, 7, depth).transpose(1, 2, 0, 3)
    columns = lax.conv_general_dilated(
        blocks,
        choose,
        (4, 4),
        ((0, 0), (0, 0)),
        dimension_numbers=("NCHW", "HWIO", "HWNC"),
        preferred_element_type=f32,
    ).astype(bf16)
    columns = columns.reshape(64, MICRO, SIDE * SIDE, depth)
    columns = jnp.pad(columns, ((0, 0), (0, 0), (0, ROWS - SIDE * SIDE), (0, 2 * LANES - depth)))
    return columns.reshape(64 * BOTH, 2 * LANES)


def tap_orders(zero):
    row = lax.broadcasted_iota(jnp.int32, (TAPS * LANES, TAPS * LANES), 0) + zero
    col = lax.broadcasted_iota(jnp.int32, (TAPS * LANES, TAPS * LANES), 1)
    forth = ((row % LANES) * TAPS + row // LANES == col).astype(bf16)
    dims = (5 * LANES + C1, 5 * LANES)
    row = lax.broadcasted_iota(jnp.int32, dims, 0) - C1 + zero
    col = lax.broadcasted_iota(jnp.int32, dims, 1)
    real = (row >= 0) & (row < TAPS * C1)
    row = jnp.maximum(row, 0)
    back = (real & ((row % TAPS) * C1 + row // TAPS == col)).astype(bf16)
    row = lax.broadcasted_iota(jnp.int32, (C4, C4), 0) + zero
    col = lax.broadcasted_iota(jnp.int32, (C4, C4), 1)
    merge = ((row % (C4 // 2)) * 2 + row // (C4 // 2) == col).astype(bf16)
    return forth, back, merge


def grid_marks(side):
    row = np.arange(BOTH)
    image, q = row // ROWS, row % ROWS
    y, x = q // SIDE, q % SIDE
    real = q < SIDE * SIDE
    fixed = np.stack([real & (y > 0), real & (x > 0), real & (y > 0) & (x > 0)], 1).astype(np.float32)
    close = (
        (image[:, None] == image[None])
        & (abs(y[:, None] - y[None]) <= 1)
        & (abs(x[:, None] - x[None]) <= 1)
        & real[:, None]
        & real[None]
    )
    inside = jnp.asarray(real) & (jnp.asarray(y) < side) & (jnp.asarray(x) < side)
    near = jnp.where(jnp.asarray(close) & inside[:, None] & inside[None], 1.0, 0.0)
    cells = jnp.maximum(jnp.sum(near, axis=1), 1.0)
    marks = jnp.concatenate(
        [inside.astype(f32)[:, None], jnp.asarray(fixed), (1.0 / cells)[:, None]], axis=1
    )
    return jnp.pad(marks, ((0, 0), (0, LANES - marks.shape[1]))), near.astype(bf16)


def local_inputs(images, group, label_col, partner_col, mix_col, valid_col, me):
    side = RES_S // RES_STEP + group
    columns = patches(images, side * RES_STEP, partner_col, mix_col)
    orders = tap_orders(jnp.minimum(group, 0))
    marks, near = grid_marks(side)
    other = jnp.where(partner_col == 0, label_col[0], label_col[1])
    whole = jnp.concatenate([label_col, other, jnp.stack([me % 2, me]).astype(jnp.int32)])
    cells = (side * side).astype(f32)
    real = jnp.concatenate([mix_col, valid_col.astype(f32), jnp.stack([cells, cells * C4])])
    return whole, real, columns, orders, marks, near


def second_half(prepared, convs, made, chips, each, ties):
    columns, (forth, back, merge), marks = prepared[2], prepared[3], prepared[4]
    p1, p2, p3e, p3o, k1t, k2, k3e, k3o = convs[:8]
    args = [made[2], columns, p1, p2, p3e, p3o, k1t, k2, k3e, k3o, forth, back, merge, marks]
    return run_backward([prepared[0]] + list(ties) + args + list(made[3:8]), chips, each)


class Ring:
    def __init__(self, count):
        self.count = count
        self.squares = count // 8
        me = lax.axis_index(AXES)
        self.me = me
        self.core = me % 2
        self.low = (me // 2) % 2
        self.high = (me // 4) % 2
        self.corner = (me // 2) % 4
        self.square = me // 8

    def swap(self, value, bits):
        return lax.ppermute(value, AXES, [(i, i ^ bits) for i in range(self.count)])


def pick(value, at, axis):
    return lax.dynamic_index_in_dim(value, at, axis, keepdims=False)


class Scatter:
    def __init__(self, ring, terms, mine, bits):
        self.ring = ring
        self.terms = terms
        self.mine = mine
        self.bits = bits

    def exchange(self):
        sent = functools.reduce(jnp.add, [pick(x, 1 - self.mine, 0) for x in self.terms])
        self.terms = [pick(x, self.mine, 0) for x in self.terms] + [self.ring.swap(sent, self.bits)]

    def add(self):
        self.terms = [functools.reduce(jnp.add, self.terms)]


def sum_squares(ring, value, far_first):
    bits = ring.squares.bit_length() - 1
    order = list(range(bits))
    if far_first:
        order.reverse()
    held = order.copy()
    value = value.reshape((2,) * bits + value.shape[1:])
    got = None
    for bit in order:
        axis = len(held) - 1 - sorted(held).index(bit)
        held.remove(bit)
        mine = (ring.square >> bit) & 1
        if got is not None:
            value = value + got
        got = ring.swap(pick(value, 1 - mine, axis), 8 << bit)
        value = pick(value, mine, axis)
    return value, got


class Gather:
    def __init__(self, ring, value, far_first, high_first):
        self.ring = ring
        self.value = value
        self.masks = []
        bits = list(range(ring.squares.bit_length() - 1))
        self.squares = [8 << bit for bit in (reversed(bits) if far_first else bits)]
        self.corners = (4, 2) if high_first else (2, 4)
        self.pieces = []

    def exchange(self, mask):
        self.value = jnp.stack([self.value, self.ring.swap(self.value, mask)])
        self.masks = [mask] + self.masks

    def between_squares(self):
        for mask in self.squares:
            self.exchange(mask)

    def first_corner(self):
        self.exchange(self.corners[0])

    def second_corner(self):
        got = self.ring.swap(self.value, self.corners[1])
        self.pieces = [(self.value, self.masks, 0), (got, self.masks, self.corners[1])]

    def between_cores(self):
        self.pieces += [(self.ring.swap(array, 1), masks, base | 1) for array, masks, base in self.pieces]


def together(scatters, *others):
    counts = [len(x.terms) for x in scatters]
    values = lax.optimization_barrier(tuple(t for x in scatters for t in x.terms) + tuple(others))
    at = 0
    for x, count in zip(scatters, counts):
        x.terms = list(values[at : at + count])
        at += count
    return values[at:]


class ChipSum:
    def __init__(self, ring, value):
        self.ring = ring
        self.shape = value.shape
        self.terms = [value.reshape(4, value.shape[0] // 4, value.shape[1])]

    def scatter_corners(self):
        ring = self.ring
        got = [ring.swap(pick(self.terms[0], ring.corner ^ j, 0), 2 * j) for j in range(1, 4)]
        self.terms = [functools.reduce(jnp.add, got, pick(self.terms[0], ring.corner, 0))]

    def sum_squares(self):
        ring = self.ring
        got = [ring.swap(self.terms[0], 8 * j) for j in range(1, ring.squares)]
        self.terms = [functools.reduce(jnp.add, got, self.terms[0])]


    def gather_corners(self):
        ring = self.ring
        held = jnp.stack([self.terms[0]] + [ring.swap(self.terms[0], 2 * j) for j in range(1, 4)])
        return jnp.stack([pick(held, ring.corner ^ j, 0) for j in range(4)]).reshape(self.shape)


def per_device(
    devices_count,
    images,
    group_ids,
    labels,
    partners,
    mix_weights,
    valid,
    flat_params,
    flat_first,
    flat_second,
    mlp_weights,
    mlp_momentum,
):
    ring = Ring(devices_count)
    chips = devices_count // 2
    share = mlp_weights.shape[2]
    flat_share = flat_params.shape[0]
    flat_rows = -(-flat_share // LANES)
    spare = flat_rows * LANES - flat_share
    mine = jnp.pad(flat_params, (0, spare)) if spare else flat_params
    mats_one, mats_two, sent = run_pack(
        valid.reshape(MICRO),
        mlp_weights.transpose(0, 2, 1),
        mine.reshape(flat_rows, LANES),
        flat_share % LANES == 0,
    )
    mats = [Gather(ring, mats_one, False, True), Gather(ring, mats_two, True, False)]
    for x in mats:
        x.between_squares()
    for x in mats:
        x.first_corner()
    group, images, mats[0].value, mats[1].value = lax.optimization_barrier(
        (group_ids[0], images, mats[0].value, mats[1].value)
    )
    prepared = local_inputs(
        images, group, labels[:, 0], partners[:, 0], mix_weights[:, 0], valid[:, 0], ring.me
    )
    whole, real, columns, orders, marks, near = prepared
    momentum = mlp_momentum.transpose(0, 2, 1)

    def of_both_cores(mine, theirs):
        at_first = ring.core == 0
        return jnp.concatenate([jnp.where(at_first, mine, theirs), jnp.where(at_first, theirs, mine)])

    momentum_rows = of_both_cores(
        pick(momentum, ring.core, 0), ring.swap(pick(momentum, 1 - ring.core, 0), 1)
    )
    got = lax.all_gather(sent, AXES, axis=0, tiled=False)
    for x in mats:
        x.second_corner()
    for x in mats:
        x.between_cores()
    moved = [columns, *orders]
    if flat_share % LANES:
        whole_flat = (
            got[:, :flat_rows]
            .astype(f32)
            .reshape(devices_count, flat_rows * LANES)[:, :flat_share]
            .reshape(devices_count * flat_share // LANES, LANES)
        )
        convs = run_conv(whole, whole_flat, None, momentum_rows, moved, marks, flat_share)
        counted = jnp.sum(got[:, flat_rows, 0].astype(f32))
    else:
        convs = run_conv(whole, got, [[], []], momentum_rows, moved, marks, flat_share)
        counted = convs[12][0, 0]
    scale = 1.0 / jnp.maximum(counted, 1.0)
    made = run_block(whole, real, [x.pieces for x in mats], convs[8:12], marks, near, share)
    keep, send = made[:2]
    got_factors = ring.swap(send, 1)
    ahead = [
        jnp.stack([x[begin : begin + QUARTER + C4] for x in (keep, got_factors)]) for begin in (0, FACTOR_CHANNELS)
    ]
    far_a, far_b = ring.swap(ahead[0], 4), ring.swap(ahead[1], 2)

    each = -(-(devices_count * flat_share) // (devices_count * LANES * 8)) * 8
    ties = [x[1, :16] for x in ahead]
    keep_a, keep_b, send_a, send_b = second_half(prepared, convs, made, chips, each, ties)
    send_a, send_b, keep_one, send_one, keep_two, send_two, loss = run_product(
        whole, [send_a, send_b], keep, got_factors, far_a, far_b, ring.squares, share
    )
    got_one, got_two = ring.swap(send_one, 2), ring.swap(send_two, 4)
    got_a, got_b = ring.swap(send_a, 1), ring.swap(send_b, 1)
    sent_a, left_a, sent_b, left_b = run_halve(whole, keep_one[0, :8, :LANES], keep_a, got_a, keep_b, got_b)
    entries = run_sum(whole, sent_a[0, 0, :8], keep_one, got_one, keep_two, got_two)
    terms = [entries[0]] + [ring.swap(entries[j], 8 * j) for j in range(1, ring.squares)]
    flat = [
        Scatter(ring, [left_a, ring.swap(sent_a, 4)], ring.low, 2),
        Scatter(ring, [left_b, ring.swap(sent_b, 2)], ring.high, 4),
    ]
    ortho, momentum_new, packed = run_gram(scale[None], terms, momentum_rows, loss)
    grams = ChipSum(ring, packed)
    grams.scatter_corners()
    grams.sum_squares()
    for x in flat:
        x.exchange()
        x.add()
    together([grams] + flat)
    sum_flat = jnp.concatenate([sum(sum_squares(ring, x.terms[0], far)) for x, far in zip(flat, (False, True))])
    steps = 2
    ortho, gram, loss_total = run_newton_first(grams.gather_corners(), ortho, steps)
    lag = (devices_count - 1) * (each * LANES - flat_share)
    hops = -(-lag // (each * LANES))
    tail = min(each, -(-lag // (8 * LANES)) * 8)
    before = [
        lax.ppermute(sum_flat[each - tail :], AXES, [(i, i + h) for i in range(devices_count - h)])
        for h in range(hops, 0, -1)
    ]
    ortho = run_newton_last(sum_flat[each - 8 :], gram, ortho, steps)
    sum_flat = jnp.concatenate(before + [sum_flat])
    start = len(before) * tail * LANES - ring.me * (each * LANES - flat_share)
    if flat_share % LANES == 0:
        sum_flat = lax.dynamic_slice_in_dim(sum_flat, start // LANES, flat_rows, 0).reshape(-1)
    else:
        sum_flat = lax.dynamic_slice_in_dim(sum_flat.reshape(-1), start, flat_share, 0)
    sum_flat = sum_flat * scale
    first_new = 0.9 * flat_first + 0.1 * sum_flat
    second_new = 0.999 * flat_second + 0.001 * sum_flat * sum_flat
    first_hat = first_new / (1.0 - 0.9**STEP)
    second_hat = second_new / (1.0 - 0.999**STEP)
    params_new = flat_params - 0.02 * (
        first_hat / (jnp.sqrt(second_hat) + 1e-08) + 0.05 * flat_params
    )

    def to_owners(by_chip):
        parts = by_chip.reshape(2, share, C4)
        mine, theirs = pick(parts, ring.core, 0), ring.swap(pick(parts, 1 - ring.core, 0), 1)
        at_first = ring.core == 0
        return jnp.stack([jnp.where(at_first, mine, theirs), jnp.where(at_first, theirs, mine)])

    mats = mlp_weights.transpose(0, 2, 1)
    weights_new = mats * (1.0 - 0.1 * 0.05) - 0.1 * 0.2 * math.sqrt(HID) * to_owners(ortho)
    return (
        loss_total[0, 0],
        params_new,
        first_new,
        second_new,
        weights_new.transpose(0, 2, 1),
        to_owners(momentum_new).transpose(0, 2, 1),
    )


def solution(mesh):
    placed = (
        P(None, AXES, None, None, None),
        P(AXES),
        P(None, AXES),
        P(None, AXES),
        P(None, AXES),
        P(None, AXES),
        P(AXES),
        P(AXES),
        P(AXES),
        P(None, None, AXES),
        P(None, None, AXES),
    )
    devices_count = math.prod(mesh.shape[axis] for axis in AXES)
    return jax.shard_map(
        functools.partial(per_device, devices_count),
        mesh=mesh,
        in_specs=placed,
        out_specs=(
            P(),
            P(AXES),
            P(AXES),
            P(AXES),
            P(None, None, AXES),
            P(None, None, AXES),
        ),
        check_vma=False,
    )
```

```python
import functools
import math

import jax
import jax.numpy as jnp
import numpy as np
from jax import lax
from jax.experimental import pallas as pl
from jax.experimental.pallas import tpu as pltpu
from jax.sharding import PartitionSpec as P

C1 = 64
C2 = 128
C3 = 320
C4 = 512
HID = 2048
CLS = 1000
IN_CH = 3
RES_S = 96
RES_L = 160
RES_STEP = 32
MICRO = 2
NS_ITERS = 5
STEP = 10

AXES = ("fsdp", "ns")
LANES = 128
SIDE = 5
ROWS = 32
BOTH = MICRO * ROWS
C3P = 384
CLSP = 1024
K3P = 2944
TAPS = 9

f32 = jnp.float32
bf16 = jnp.bfloat16
norm_epsilon = 1e-05

NARROW = C1 * IN_CH * 49
ROW_B0 = NARROW // LANES
ROW_K1 = 74
ROW_B1 = 650
ROW_K2 = 651
ROW_B2 = 3531
ROW_K3 = 3533
ROW_B3 = 15053
REST = {"b3": 0, "block": 4, "fb1": 28, "fb2": 44, "final": 48, "head": 56, "hb": 4056, "end": 4064}
QUARTER = HID // 4
FACTOR_OTHER = (0, QUARTER + C4)
FACTOR_CHANNELS = QUARTER
FACTOR_OWN = (2 * QUARTER + C4, 3 * QUARTER + C4)
FACTOR_LOSS = HID + C4
FACTOR_ROWS = FACTOR_LOSS + 16
GROUP = 16
SPAN = GROUP * CLS // LANES
PAIRS = [(i, j) for i in range(4) for j in range(i, 4)]


def dot_nn(a, b):
    return lax.dot_general(a, b, (((1,), (0,)), ((), ())), preferred_element_type=f32)


def dot_nt(a, b):
    return lax.dot_general(a, b, (((1,), (1,)), ((), ())), preferred_element_type=f32)


def dot_tn(a, b):
    return lax.dot_general(a, b, (((0,), (0,)), ((), ())), preferred_element_type=f32)


def split2(x):
    hi = x.astype(bf16)
    return hi, (x - hi.astype(f32)).astype(bf16)


def split3(x):
    hi = x.astype(bf16)
    rest = x - hi.astype(f32)
    mid = rest.astype(bf16)
    return hi, mid, (rest - mid.astype(f32)).astype(bf16)


def stacked(dot, parts, other):
    rows = parts[0].shape[0]
    product = dot(jnp.concatenate(parts, axis=0), other)
    return functools.reduce(jnp.add, [product[k * rows : (k + 1) * rows] for k in range(len(parts))])


def two(dot, pair, other):
    return stacked(dot, pair, other)


def borrow(bits):
    out = list(bits)
    for at, bit in enumerate(out):
        if bit:
            out[at] = 0
            return tuple(out), 0
        out[at] = 1
    return tuple(out), 1


def tap_source(tap, row_bits, col_bits):
    r, c = divmod(tap, 3)
    src_r, down_r = (row_bits, 0) if r else borrow(row_bits)
    src_c, down_c = (col_bits, 0) if c else borrow(col_bits)
    return (int(r != 1), int(c != 1)), src_r, src_c, down_r, down_c


def plane_of(row_bits, col_bits):
    at = 0
    for r, c in zip(row_bits, col_bits):
        at = at * 4 + r * 2 + c
    return at


def stem_plane(quarter, row_bits, col_bits):
    row = quarter[0] + 2 * row_bits[0] + 4 * row_bits[1]
    return row * 8 + quarter[1] + 2 * col_bits[0] + 4 * col_bits[1]


def all_bits(pairs):
    for at in range(4**pairs):
        digits = [(at >> (2 * (pairs - 1 - k))) & 3 for k in range(pairs)]
        yield at, tuple(d >> 1 for d in digits), tuple(d & 1 for d in digits)


def moved(value, down_r, down_c, marks):
    if not (down_r or down_c):
        return value
    step = SIDE * down_r + down_c
    column = {(1, 0): 1, (0, 1): 2, (1, 1): 3}[(down_r, down_c)]
    return pltpu.roll(value, step, 0) * marks[:, column : column + 1]


def moved_back(value, down_r, down_c, marks):
    if not (down_r or down_c):
        return value
    step = SIDE * down_r + down_c
    column = {(1, 0): 1, (0, 1): 2, (1, 1): 3}[(down_r, down_c)]
    return pltpu.roll(value * marks[:, column : column + 1], BOTH - step, 0)


def erf(x):
    x = jnp.clip(x, -3.832506856900711, 3.832506856900711)
    s = x * x
    top = 2.2905065861350646e-4
    for coef in (3.4082910107109506e-3, 5.0955695062380861e-2, 1.8520832239976145e-1, 1.128379143519084):
        top = top * s + coef
    low = -1.1791602954361697e-7
    for coef in (
        2.3547966471313185e-5,
        1.0179625278914885e-3,
        1.4070470171167667e-2,
        1.1098505178285362e-1,
        4.9746925110067538e-1,
        1.0,
    ):
        low = low * s + coef
    return x * top / low


def total(x):
    return jnp.sum(jnp.sum(x, axis=1, keepdims=True), axis=0, keepdims=True)


def norm_images(value, mask, count):
    parts, scales = [], []
    for m in range(MICRO):
        v = value[m * ROWS : (m + 1) * ROWS]
        k = mask[m * ROWS : (m + 1) * ROWS]
        center = (v - total(v * k) / count) * k
        scale = lax.rsqrt(total(center * center) / count + norm_epsilon)
        parts.append(center * scale)
        scales.append(scale)
    return jnp.concatenate(parts, axis=0), scales


def norm_images_back(grad, hat, scales, gain, mask, count):
    parts = []
    for m in range(MICRO):
        at = slice(m * ROWS, (m + 1) * ROWS)
        g = grad[at] * gain
        h = hat[at]
        parts.append((g - total(g) / count - h * (total(g * h) / count)) * scales[m] * mask[at])
    return jnp.concatenate(parts, axis=0)


def rowsum(x):
    return jnp.sum(x, axis=0, keepdims=True)


def halves(low, high):
    lane = lax.broadcasted_iota(jnp.int32, low.shape, 1)
    return jnp.where(lane < LANES // 2, pltpu.roll(low, LANES // 2, 1), pltpu.roll(high, LANES // 2, 1))


def lanes_of(ref, row, count):
    return jnp.concatenate([ref[row + at : row + at + 1, :] for at in range(count)], axis=1)


def head_masks():
    row = lax.broadcasted_iota(jnp.int32, (C4 // GROUP, C4), 0)
    col = lax.broadcasted_iota(jnp.int32, (C4 // GROUP, C4), 1)
    return col // GROUP == row, col % GROUP == row // MICRO, row % MICRO == 0


class Copies:
    def __init__(self, sems):
        self.sems = sems
        self.count = 2

    def start_shared(self, source, target):
        pltpu.make_async_copy(source, target, self.sems.at[0]).start()

    def start_out(self, source, target):
        pltpu.make_async_copy(source, target, self.sems.at[1]).start()

    def out(self, source):
        return pltpu.make_async_copy(source, source, self.sems.at[1])

    def shared(self, target):
        return pltpu.make_async_copy(target, target, self.sems.at[0])

    def start(self, source, target):
        copy = self.make(source, target)
        copy.start()
        return copy

    def make(self, source, target):
        copy = pltpu.make_async_copy(source, target, self.sems.at[self.count])
        self.count += 1
        return copy


def pieces_of(gathered):
    for number, (unused_array, masks, base) in enumerate(gathered):
        for place in range(2 ** len(masks)):
            index, owner = [], base
            for k, mask in enumerate(masks):
                bit = (place >> k) & 1
                index.append(bit)
                owner ^= mask * bit
            yield number, tuple(index), owner


def conv_kernel(flat_share, gathered, *refs):
    if flat_share % LANES:
        conv_body(None, None, *refs)
    else:
        count = [len(side) for side in gathered]
        held = [refs[1 : 1 + count[0]], refs[1 + count[0] : 1 + sum(count)]]
        conv_body(flat_share, (gathered, held), refs[0], refs[-1], *refs[1 + sum(count) : -1])


def conv_body(
    flat_share,
    arrived,
    whole_ref,
    flat_ref,
    unused_hbm,
    p0_hbm,
    tm_hbm,
    t64_hbm,
    pm_hbm,
    marks_ref,
    p1_hbm,
    p2_hbm,
    p3e_hbm,
    p3o_hbm,
    k1t_hbm,
    k2_hbm,
    k3e_hbm,
    k3o_hbm,
    stream_ref,
    rest_ref,
    wide_ref,
    hb_ref,
    count_ref,
    p0_ref,
    tm_ref,
    t64_ref,
    pm_ref,
    p1_ref,
    p2_ref,
    p3e_ref,
    p3o_ref,
    k1t_ref,
    k2_ref,
    k3e_ref,
    k3o_ref,
    s1_ref,
    s2_ref,
    s3_ref,
    t2_ref,
    t3_ref,
    w0_ref,
    k1f_ref,
    sems,
    *near_refs,
):
    copies = Copies(sems)
    if arrived is not None:
        near_ref = near_refs[0]
        gathered, held = arrived
        half_rows = near_ref.shape[1] // 2
        me = whole_ref[5]
        for side in range(2):
            for number, index, owner in pieces_of(gathered[side]):
                copies.start_shared(
                    held[side][number].at[index], near_ref.at[me ^ owner, pl.ds(side * half_rows, half_rows), :]
                )
        flat_copy = copies.shared(near_ref)
    p0_copy = copies.start(p0_hbm, p0_ref)
    t64_copy = copies.start(t64_hbm, t64_ref)
    tm_copy = copies.start(tm_hbm, tm_ref)
    pm_copy = copies.start(pm_hbm, pm_ref)
    outward = []
    if arrived is not None:
        flat_copy.wait()
        flat_rows = flat_share // LANES
        counted = jnp.zeros((1, LANES), f32)
        for at in range(near_ref.shape[0]):
            flat_ref[pl.ds(at * flat_rows, flat_rows), :] = near_ref[at, pl.ds(0, flat_rows), :].astype(f32)
            counted = counted + near_ref[at, pl.ds(flat_rows, 1), :].astype(f32)
        count_ref[...] = jnp.broadcast_to(counted, (8, LANES))
    else:
        count_ref[...] = jnp.zeros((8, LANES), f32)
    marks = marks_ref[...]
    lane = lax.broadcasted_iota(jnp.int32, (BOTH, LANES), 1)
    lane1 = lax.broadcasted_iota(jnp.int32, (1, LANES), 1)
    depth = IN_CH * 49
    for at in range(C1):
        row, shift = divmod(depth * at, LANES)
        line = lanes_of(flat_ref, row, 3)
        if shift:
            line = pltpu.roll(line, 3 * LANES - shift, 1)
        w0_ref[at : at + 1, :] = line[:, : 2 * LANES]
    w0 = w0_ref[...].astype(bf16)
    w0 = jnp.concatenate([w0, w0], axis=0)
    b0 = flat_ref[ROW_B0 : ROW_B0 + 1, :]
    b0 = jnp.where(lane1 < C1, pltpu.roll(b0, C1, 1), b0)
    quarter = 16 * BOTH
    p0_copy.wait()
    for at in range(4):
        span = pl.ds(at * quarter, quarter)
        s1_ref[span, :] = (dot_nt(p0_ref[span, :], w0) + b0).astype(bf16).astype(f32)

    def tap_value(ref, pairs, tap, row_bits, col_bits, cols):
        q, src_r, src_c, down_r, down_c = tap_source(tap, row_bits, col_bits)
        if pairs == 2:
            at = stem_plane(q, src_r, src_c)
        else:
            at = (q[0] * 2 + q[1]) * 4**pairs + plane_of(src_r, src_c)
        return moved(ref[pl.ds(at * BOTH, BOTH), cols], down_r, down_c, marks)

    half = C2 // 2
    t64_copy.wait()
    for odd in range(2):
        block = jnp.concatenate(
            [flat_ref[pl.ds(ROW_K1 + 4 * odd + j, half, stride=9), :].astype(bf16) for j in range(5)], axis=1
        )
        block = dot_nn(block, t64_ref[pl.ds(C1 * (1 - odd), 5 * LANES), :])
        for j in range(5):
            k1f_ref[j, pl.ds(odd, half, stride=2), :] = block[:, j * LANES : (j + 1) * LANES]
    for j in range(5):
        k1t_ref[:, pl.ds(j * LANES, LANES)] = k1f_ref[j].astype(bf16)
    outward.append(copies.start(k1t_ref, k1t_hbm))
    everything = slice(None)
    for at, rb, cb in all_bits(2):
        for pair in range(5):
            left = tap_value(s1_ref, 2, 2 * pair, rb, cb, everything)
            if pair < 4:
                right = tap_value(s1_ref, 2, 2 * pair + 1, rb, cb, everything)
            else:
                right = jnp.zeros_like(left)
            p1_ref[pl.ds(at * BOTH, BOTH), pl.ds(pair * LANES, LANES)] = jnp.where(
                lane < C1, left, right
            ).astype(bf16)
    outward.append(copies.start(p1_ref, p1_hbm))
    b1 = flat_ref[ROW_B1 : ROW_B1 + 1, :]
    s2_ref[...] = (dot_nt(p1_ref[...], k1t_ref[...]) + b1).astype(bf16).astype(f32)
    for j in range(TAPS):
        k2_ref[pl.ds(0, C3), pl.ds(j * LANES, LANES)] = flat_ref[pl.ds(ROW_K2 + j, C3, stride=TAPS), :].astype(bf16)
    k2_ref[pl.ds(C3, C3P - C3), :] = jnp.zeros((C3P - C3, TAPS * LANES), bf16)
    outward.append(copies.start(k2_ref, k2_hbm))
    b2 = lanes_of(flat_ref, ROW_B2, 3)
    b2 = jnp.where(lax.broadcasted_iota(jnp.int32, b2.shape, 1) < C3, b2, 0.0)
    for at, rb, cb in all_bits(1):
        for tap in range(TAPS):
            t2_ref[pl.ds(at * BOTH, BOTH), pl.ds(tap * LANES, LANES)] = tap_value(
                s2_ref, 1, tap, rb, cb, everything
            ).astype(bf16)
    tm_copy.wait()
    p2_ref[...] = dot_nn(t2_ref[...], tm_ref[...]).astype(bf16)
    outward.append(copies.start(p2_ref, p2_hbm))
    s3_ref[...] = (dot_nt(p2_ref[...], k2_ref[...]) + b2).astype(bf16).astype(f32)
    for part in range(3):
        for tap in range(TAPS):
            t3_ref[pl.ds(part * BOTH, BOTH), pl.ds(tap * LANES, LANES)] = tap_value(
                s3_ref, 0, tap, (), (), pl.ds(part * LANES, LANES)
            ).astype(bf16)
    spread = dot_nn(t3_ref[...], tm_ref[...])
    spread = jnp.concatenate([spread[part * BOTH : (part + 1) * BOTH] for part in range(3)], axis=1)
    p3o_ref[...] = spread[:, :K3P].astype(bf16)
    p3e_ref[...] = pltpu.roll(spread, LANES // 2, 1)[:, :K3P].astype(bf16)
    for j in range(K3P // LANES):
        cols = pl.ds(j * LANES, LANES)
        k3e_ref[:, cols] = flat_ref[pl.ds(ROW_K3 + j, C4 // 2, stride=45), :].astype(bf16)
        k3o_ref[:, cols] = flat_ref[pl.ds(ROW_K3 + 23 + j, C4 // 2, stride=45), :].astype(bf16)
    for source, target in ((p3e_ref, p3e_hbm), (p3o_ref, p3o_hbm), (k3e_ref, k3e_hbm), (k3o_ref, k3o_hbm)):
        outward.append(copies.start(source, target))
    pm_copy.wait()
    apart = split3(
        jnp.concatenate([dot_nt(p3e_ref[...], k3e_ref[...]), dot_nt(p3o_ref[...], k3o_ref[...])], axis=1)
    )
    stream = stacked(dot_nn, apart, pm_ref[...])

    stream_ref[...] = stream

    amount = REST["head"]
    rest_ref[...] = halves(flat_ref[ROW_B3 : ROW_B3 + amount, :], flat_ref[ROW_B3 + 1 : ROW_B3 + 1 + amount, :])
    row_hb = ROW_B3 + REST["hb"]
    hb_ref[...] = halves(flat_ref[row_hb : row_hb + 8, :], flat_ref[row_hb + 1 : row_hb + 9, :])
    groups = C4 // GROUP
    row_head = ROW_B3 + REST["head"]
    low = pltpu.roll(flat_ref[pl.ds(row_head, groups, stride=SPAN), :], LANES // 2, 1)
    lane32 = lax.broadcasted_iota(jnp.int32, (groups, LANES), 1)
    for at in range(SPAN):
        high = pltpu.roll(flat_ref[pl.ds(row_head + at + 1, groups, stride=SPAN), :], LANES // 2, 1)
        wide_ref[:, pl.ds(at * LANES, LANES)] = jnp.where(lane32 < LANES // 2, low, high).astype(bf16)
        low = high
    wide_ref[:, pl.ds(SPAN * LANES, LANES)] = jnp.zeros((groups, LANES), bf16)
    for copy in outward:
        copy.wait()


def block_kernel(
    share,
    whole_ref,
    real_ref,
    got_hbm,
    stream_ref,
    rest_ref,
    wide_ref,
    hb_ref,
    marks_ref,
    near_ref,
    keep_hbm,
    send_hbm,
    dstream_ref,
    dblock_ref,
    dfb1_ref,
    small_ref,
    pooled_ref,
    dlog_ref,
    factor_ref,
    hid_ref,
    z_ref,
    per_ref,
    mats_ref,
    sems,
):
    copies = Copies(sems)
    me = whole_ref[5]
    for mat in range(2):
        rows = mats_ref.shape[2]
        copies.start_shared(got_hbm.at[:, pl.ds(mat * rows, rows), :], mats_ref.at[mat])
    mats_copy = copies.shared(mats_ref)
    marks = marks_ref[...]
    stream = stream_ref[...]
    b3 = lanes_of(rest_ref, REST["b3"], 4)
    gain1, shift1, scale1, gain2, shift2, scale2 = (lanes_of(rest_ref, REST["block"] + 4 * k, 4) for k in range(6))
    fb1 = lanes_of(rest_ref, REST["fb1"], HID // LANES)
    fb2 = lanes_of(rest_ref, REST["fb2"], 4)
    gain3, shift3 = (lanes_of(rest_ref, REST["final"] + 4 * k, 4) for k in range(2))

    stream = stream + b3
    mask = marks[:, 0:1]
    per_count = marks[:, 4:5]
    cells = real_ref[4]
    count = real_ref[5]
    near = near_ref[...]
    hat1, rs1 = norm_images(stream, mask, count)
    u = (hat1 * gain1 + shift1) * mask
    u3 = split3(u)
    around = dot_nn(near, u3[0]) + (dot_nn(near, u3[1]) + dot_nn(near, u3[2]))
    pool = around * per_count - u
    stream1 = stream + scale1 * pool
    hat2, rs2 = norm_images(stream1, mask, count)
    normed = ((hat2 * gain2 + shift2) * mask).astype(bf16)
    mats_copy.wait()
    blocks = C4 // LANES

    def matrix(mat, part):
        return mats_ref[mat, :, pl.ds(part * share, share), :].reshape(HID, LANES)

    def lanes(x, part):
        return x[:, part * LANES : (part + 1) * LANES]

    hidden = fb1
    for part in range(blocks):
        hidden = hidden + dot_nt(lanes(normed, part), matrix(0, part))
    hid_ref[...] = hidden
    active = (hidden * (0.5 * (1.0 + erf(hidden * math.sqrt(0.5))))).astype(bf16)
    branch = jnp.concatenate([dot_nn(active, matrix(1, part)) for part in range(blocks)], axis=1) + fb2
    stream2 = stream1 + scale2 * branch
    hat3, rs3 = norm_images(stream2, mask, count)
    outs = (hat3 * gain3 + shift3) * mask
    row8 = lax.broadcasted_iota(jnp.int32, (8, 1), 0)
    first, second = row8 == 0, row8 == 1

    def by_row(a, b):
        return jnp.where(first, a, jnp.where(second, b, 0.0))

    pooled = (by_row(rowsum(outs[:ROWS]), rowsum(outs[ROWS:])) / cells).astype(bf16)
    pooled_f = pooled.astype(f32)
    pooled_ref[...] = pooled_f
    in_group, in_place, own_row = head_masks()
    picked = jnp.where(in_place, jnp.where(own_row, pooled_f[0:1, :], pooled_f[1:2, :]), 0.0).astype(bf16)
    by_place = dot_nt(picked, in_group.astype(bf16)).astype(bf16)
    z_ref[...] = dot_nn(by_place, wide_ref[...])
    column = lax.broadcasted_iota(jnp.int32, (8, CLSP), 1)
    hb = lanes_of(hb_ref, 0, 8)
    logits = jnp.zeros((MICRO, CLSP), f32)
    for place in range(GROUP):
        at, shift = divmod(CLS * place, LANES)
        window = z_ref[pl.ds(MICRO * place, MICRO), pl.ds(at * LANES, CLSP + LANES)]
        if shift:
            window = pltpu.roll(window, CLSP + LANES - shift, 1)
        logits = logits + window[:, :CLSP]
    logits = by_row(logits[0:1], logits[1:2]) + hb
    logits = jnp.where(column < CLS, logits, -1e30)
    top = jnp.max(logits, axis=1, keepdims=True)
    powers = jnp.exp(logits - top)
    mass = jnp.sum(powers, axis=1, keepdims=True)
    own = jnp.where(first, whole_ref[0], whole_ref[1])
    other = jnp.where(first, whole_ref[2], whole_ref[3])
    mix = by_row(real_ref[0], real_ref[1])
    target = jnp.where(column == own, mix, 0.0) + jnp.where(column == other, 1.0 - mix, 0.0)
    valid = by_row(real_ref[2], real_ref[3])
    logp = logits - top - jnp.log(mass)
    losses = -jnp.sum(target * logp, axis=1, keepdims=True) * valid
    loss = split3(jnp.broadcast_to(jnp.sum(losses, axis=0, keepdims=True), (1, LANES)))
    dlogits = (powers / mass * jnp.sum(target, axis=1, keepdims=True) - target) * valid
    dlog_ref[...] = dlogits
    padded = jnp.concatenate([dlogits, jnp.zeros((8, LANES), f32)], axis=1)
    for place in range(GROUP):
        at, shift = divmod(CLS * place, LANES)
        window = pltpu.roll(padded, shift, 1) if shift else padded
        per_group = two(dot_nt, split2(window), wide_ref[:, pl.ds(at * LANES, CLSP + LANES)])
        per_ref[pl.ds(MICRO * place, MICRO), :] = per_group[:MICRO]
    per3 = split3(per_ref[...])
    ones = in_group.astype(bf16)
    by_channel = dot_nn(per3[0], ones) + (dot_nn(per3[1], ones) + dot_nn(per3[2], ones))
    dpooled = by_row(
        rowsum(jnp.where(in_place & own_row, by_channel, 0.0)),
        rowsum(jnp.where(in_place & ~own_row, by_channel, 0.0)),
    )
    dpooled = dpooled / cells
    douts = jnp.concatenate(
        [
            jnp.broadcast_to(dpooled[0:1], (ROWS, C4)),
            jnp.broadcast_to(dpooled[1:2], (ROWS, C4)),
        ],
        axis=0,
    ) * mask
    row8w = lax.broadcasted_iota(jnp.int32, (8, C4), 0)

    def stack8(values):
        out = jnp.zeros((8, C4), f32)
        for at, v in enumerate(values):
            out = jnp.where(row8w == at, v, out)
        return out

    dgain3, dshift3 = rowsum(douts * hat3), rowsum(douts)
    dstream2 = norm_images_back(douts, hat3, rs3, gain3, mask, count)
    dscale2 = rowsum(dstream2 * branch)
    dbranch = dstream2 * scale2
    dfb2 = rowsum(dbranch)
    dbr = split2(dbranch)
    dactive = None
    for part in range(blocks):
        term = two(dot_nt, (lanes(dbr[0], part), lanes(dbr[1], part)), matrix(1, part))
        dactive = term if dactive is None else dactive + term
    hidden = hid_ref[...]
    slope = 0.5 * (1.0 + erf(hidden * math.sqrt(0.5))) + hidden * (
        jnp.exp(-0.5 * hidden * hidden) * (1.0 / math.sqrt(2.0 * math.pi))
    )
    dhidden = dactive * slope
    dfb1_ref[...] = jnp.broadcast_to(rowsum(dhidden), (8, HID))
    dhid = split2(dhidden)

    core, corner_high, corner_low = whole_ref[4], (me // 4) % 2, (me // 2) % 2
    active_f = active.astype(f32)
    sides = (
        (jnp.concatenate([d.astype(f32) for d in dhid], axis=0), jnp.concatenate([normed, normed], axis=0)),
        (jnp.concatenate([active_f, active_f], axis=0), jnp.concatenate(dbr, axis=0)),
    )
    each = 2 * share
    factor_ref[:, pl.ds(FACTOR_LOSS, FACTOR_ROWS - FACTOR_LOSS), :] = jnp.zeros(
        (2, FACTOR_ROWS - FACTOR_LOSS, LANES), bf16
    )
    for mat, (hidden_side, channel_side) in enumerate(sides):
        for at in range(HID // LANES):
            cols = slice(at * LANES, (at + 1) * LANES)
            factor_ref[mat, pl.ds(at * LANES, LANES), :] = hidden_side[:, cols].T.astype(bf16)
        for part in range(blocks):
            factor_ref[mat, pl.ds(HID + part * LANES, LANES), :] = lanes(channel_side, part)

        for k in range(3):
            factor_ref[mat, pl.ds(FACTOR_LOSS + k, 1), :] = loss[k]

        def send_out(mat, target):
            for chip in range(HID // each):
                square, high, low = chip // 4, (chip // 2) % 2, chip % 2
                for side, (bit, mine, place) in enumerate(((high, corner_high, low), (low, corner_low, high))):
                    begin = jnp.where(mine == bit, FACTOR_OWN[side], FACTOR_OTHER[side])
                    to = pl.multiple_of(begin + (square * 2 + place) * share, share)
                    source = factor_ref.at[mat, pl.ds(chip * each + side * share, share), :]
                    copies.start_out(source, target.at[pl.ds(to, share), :])
            copies.start_out(
                factor_ref.at[mat, pl.ds(HID, blocks * LANES), :], target.at[pl.ds(FACTOR_CHANNELS, blocks * LANES), :]
            )
            rest = pl.ds(FACTOR_LOSS, FACTOR_ROWS - FACTOR_LOSS)
            copies.start_out(factor_ref.at[mat, rest, :], target.at[rest, :])

        pl.when(core == mat)(functools.partial(send_out, mat, keep_hbm))
        pl.when(core != mat)(functools.partial(send_out, mat, send_hbm))
    dnormed = jnp.concatenate([two(dot_nn, dhid, matrix(0, part)) for part in range(blocks)], axis=1)
    dgain2, dshift2 = rowsum(dnormed * hat2), rowsum(dnormed * mask)
    dstream1 = dstream2 + norm_images_back(dnormed, hat2, rs2, gain2, mask, count)
    dscale1 = rowsum(dstream1 * pool)
    dpool = dstream1 * scale1
    back = split3(dpool * per_count)
    du = dot_nn(near, back[0]) + (dot_nn(near, back[1]) + dot_nn(near, back[2])) - dpool
    dgain1, dshift1 = rowsum(du * hat1), rowsum(du)
    dstream = dstream1 + norm_images_back(du, hat1, rs1, gain1, mask, count)
    dblock_ref[...] = stack8([dgain1, dshift1, dscale1, dgain2, dshift2, dscale2])
    small_ref[...] = stack8([rowsum(dstream), dfb2, dgain3, dshift3])
    dstream_ref[...] = dstream
    copies.out(factor_ref).wait()


def backward_kernel(
    unused_one_ref,
    unused_two_ref,
    dstream_ref,
    p0_ref,
    p1_ref,
    p2_ref,
    p3e_ref,
    p3o_ref,
    k1t_ref,
    k2_ref,
    k3e_ref,
    k3o_ref,
    tm_ref,
    t64_ref,
    pm_ref,
    marks_ref,
    dblock_ref,
    dfb1_ref,
    small_ref,
    pooled_ref,
    dlog_ref,
    whole_ref,
    keep_a_hbm,
    keep_b_hbm,
    send_a_hbm,
    send_b_hbm,
    out_ref,
    ds3_ref,
    ds2_ref,
    ds1_ref,
    dt_ref,
    dk1t_ref,
    rest_ref,
    sems,
):
    marks = marks_ref[...]
    lane = lax.broadcasted_iota(jnp.int32, (BOTH, LANES), 1)
    lane1 = lax.broadcasted_iota(jnp.int32, (1, LANES), 1)
    wide = TAPS * LANES
    grad3 = split3(dstream_ref[...])
    apart = stacked(dot_nt, grad3, pm_ref[...])
    half = C4 // 2
    even, odd = split2(apart[:, :half]), split2(apart[:, half:])
    tall_even, tall_odd = jnp.concatenate(even, axis=0), jnp.concatenate(odd, axis=0)

    def by_even(cols):
        return dot_tn(tall_even, jnp.concatenate([p3e_ref[:, cols]] * 2, axis=0))

    def by_odd(cols):
        return dot_tn(tall_odd, jnp.concatenate([p3o_ref[:, cols]] * 2, axis=0))

    last = K3P // LANES - 1
    for j in range(last):
        cols = pl.ds(j * LANES, LANES)
        out_ref[pl.ds(ROW_K3 + 23 + j, half, stride=45), :] = by_odd(cols)
        if j:
            out_ref[pl.ds(ROW_K3 + j, half, stride=45), :] = by_even(cols)
    cols = pl.ds(last * LANES, LANES)
    out_ref[pl.ds(ROW_K3 + last, half, stride=45), :] = by_even(cols)
    tail = by_odd(cols)
    begin = by_even(pl.ds(0, LANES))
    rows = lax.broadcasted_iota(jnp.int32, (half, LANES), 0)
    out_ref[pl.ds(ROW_K3, half, stride=45), :] = begin + jnp.where(rows == 0, 0.0, pltpu.roll(tail, 1, 0))
    tail = tail[half - 1 : half]
    ds3_ref[...] = jnp.zeros_like(ds3_ref)
    position = lax.broadcasted_iota(jnp.int32, (BOTH, K3P), 1)
    nat = jnp.where(position < LANES // 2, 0.0, two(dot_nn, even, k3e_ref[...]))
    nat = pltpu.roll(nat, K3P - LANES // 2, 1) + jnp.where(
        position < C3 * TAPS, two(dot_nn, odd, k3o_ref[...]), 0.0
    )
    for part in range(3):
        width = min(wide, K3P - part * wide)
        pieces = split2(nat[:, part * wide : part * wide + width])
        by_tap = dot_nt(pieces[0], tm_ref[:, pl.ds(0, width)]) + dot_nt(pieces[1], tm_ref[:, pl.ds(0, width)])
        for tap in range(TAPS):
            q, src_r, src_c, down_r, down_c = tap_source(tap, (), ())
            at = q[0] * 2 + q[1]
            ds3_ref[pl.ds(at * BOTH, BOTH), pl.ds(part * LANES, LANES)] += moved_back(
                by_tap[:, tap * LANES : (tap + 1) * LANES], down_r, down_c, marks
            )
    db2 = rowsum(ds3_ref[...])
    for k in range(2):
        out_ref[ROW_B2 + k : ROW_B2 + k + 1, :] = db2[:, k * LANES : (k + 1) * LANES]
    out_ref[ROW_K3 : ROW_K3 + 1, :] += jnp.where(lane1 < LANES // 2, db2[:, 2 * LANES :], 0.0)
    grad = split2(ds3_ref[...])
    grad_real = (grad[0][:, :C3], grad[1][:, :C3])
    for j in range(TAPS):
        cols = pl.ds(j * LANES, LANES)
        value = dot_tn(grad[0], p2_ref[:, cols]) + dot_tn(grad[1], p2_ref[:, cols])
        out_ref[pl.ds(ROW_K2 + j, C3, stride=TAPS), :] = value[:C3]
    pieces = split2(two(dot_nn, grad, k2_ref[...]))
    dt_ref[...] = two(dot_nt, pieces, tm_ref[...])
    ds2_ref[...] = jnp.zeros_like(ds2_ref)
    for at, rb, cb in all_bits(1):
        for tap in range(TAPS):
            q, src_r, src_c, down_r, down_c = tap_source(tap, rb, cb)
            to = (q[0] * 2 + q[1]) * 4 + plane_of(src_r, src_c)
            ds2_ref[pl.ds(to * BOTH, BOTH), :] += moved_back(
                dt_ref[pl.ds(at * BOTH, BOTH), pl.ds(tap * LANES, LANES)], down_r, down_c, marks
            )
    out_ref[ROW_B1 : ROW_B1 + 1, :] = rowsum(ds2_ref[...])
    grad = split2(ds2_ref[...])
    few = C2 // 2
    for j in range(5):
        cols = pl.ds(j * LANES, LANES)
        dk1t_ref[j] = dot_tn(grad[0], p1_ref[:, cols]) + dot_tn(grad[1], p1_ref[:, cols])
    evens, odds = (
        two(
            dot_nt,
            split2(jnp.concatenate([dk1t_ref[j, pl.ds(odd, few, stride=2), :] for j in range(5)], axis=1)),
            t64_ref[pl.ds(C1 * (1 - odd), 5 * LANES), :],
        )
        for odd in range(2)
    )
    for j in range(9):
        if j < 4:
            value = evens[:, j * LANES : (j + 1) * LANES]
        elif j == 4:
            value = evens[:, 4 * LANES :] + odds[:, :LANES]
        else:
            value = odds[:, (j - 4) * LANES : (j - 3) * LANES]
        out_ref[pl.ds(ROW_K1 + j, few, stride=9), :] = value
    ds1_ref[...] = jnp.zeros_like(ds1_ref)
    for pair in range(5):
        values = two(dot_nn, grad, k1t_ref[:, pl.ds(pair * LANES, LANES)])
        for at, rb, cb in all_bits(2):
            here = values[at * BOTH : (at + 1) * BOTH]
            for side in range(2):
                tap = 2 * pair + side
                if tap >= TAPS:
                    continue
                q, src_r, src_c, down_r, down_c = tap_source(tap, rb, cb)
                to = stem_plane(q, src_r, src_c)
                mine = (lane < C1) if side == 0 else (lane >= C1)
                ds1_ref[pl.ds(to * BOTH, BOTH), :] += moved_back(
                    jnp.where(mine, here, 0.0), down_r, down_c, marks
                )
    db0 = rowsum(ds1_ref[...])
    db0 = db0 + pltpu.roll(db0, LANES // 2, 1)
    stem = jnp.zeros((LANES, 2 * LANES), f32)
    for at in range(4):
        span = pl.ds(at * 16 * BOTH, 16 * BOTH)
        grad = split2(ds1_ref[span, :])
        stem = stem + (dot_tn(grad[0], p0_ref[span, :]) + dot_tn(grad[1], p0_ref[span, :]))
    stem = stem[:C1] + stem[C1:]
    depth = IN_CH * 49
    held = jnp.zeros((1, 3 * LANES), f32)
    done = 0
    for at in range(C1):
        row, shift = divmod(depth * at, LANES)
        line = jnp.concatenate([stem[at : at + 1], jnp.zeros((1, LANES), f32)], axis=1)
        if shift:
            line = pltpu.roll(line, shift, 1)
        while done < row:
            out_ref[done : done + 1, :] = held[:, :LANES]
            held = jnp.concatenate([held[:, LANES:], jnp.zeros((1, LANES), f32)], axis=1)
            done += 1
        held = held + line
    out_ref[done : done + 1, :] = held[:, :LANES]
    if done < ROW_B0:
        out_ref[ROW_B0 : ROW_B0 + 1, :] = held[:, LANES : 2 * LANES]
    out_ref[ROW_B0 : ROW_B0 + 1, :] += jnp.where(lane1 < LANES // 2, 0.0, db0)

    lead = 5

    def put(name, value):
        for k in range(value.shape[1] // LANES):
            at = lead + REST[name] + k
            rest_ref[at : at + 1, :] = value[:, k * LANES : (k + 1) * LANES]

    rest_ref[0:8, :] = jnp.zeros((8, LANES), f32)
    put("b3", small_ref[0:1, :])
    for k in range(6):
        at = lead + REST["block"] + 4 * k
        for i in range(4):
            rest_ref[at + i : at + i + 1, :] = dblock_ref[k : k + 1, i * LANES : (i + 1) * LANES]
    put("fb1", dfb1_ref[0:1, :])
    put("fb2", small_ref[1:2, :])
    put("final", jnp.concatenate([small_ref[2:3, :], small_ref[3:4, :]], axis=1))
    dlog = dlog_ref[...]
    put("hb", dlog[0:1] + dlog[1:2])
    rest_ref[lead + REST["end"] : lead + REST["end"] + 11, :] = jnp.zeros((11, LANES), f32)
    pooled = pooled_ref[...]
    in_group, in_place, own_row = head_masks()
    picked = jnp.where(in_place, jnp.where(own_row, pooled[0:1, :], pooled[1:2, :]), 0.0).astype(bf16)
    by_group = dot_nt(in_group.astype(bf16), picked)
    padded = jnp.concatenate([dlog, jnp.zeros((8, LANES), f32)], axis=1)
    groups = C4 // GROUP
    written = -1
    for place in range(GROUP):
        at, shift = divmod(CLS * place, LANES)
        window = pltpu.roll(padded, shift, 1) if shift else padded
        ours = by_group[:, MICRO * place : MICRO * place + 1]
        others = by_group[:, MICRO * place + 1 : MICRO * place + 2]
        for k in range(CLSP // LANES + 1):
            if (at + k) * LANES >= CLS * (place + 1):
                break
            block = slice(k * LANES, (k + 1) * LANES)
            value = ours * window[0:1, block] + others * window[1:2, block]
            target = pl.ds(lead + REST["head"] + at + k, groups, stride=SPAN)
            if at + k == written:
                rest_ref[target, :] += value
            else:
                rest_ref[target, :] = value
            written = at + k
    first = ROW_B3 + 3
    out_ref[ROW_B3 : first, :] = halves(rest_ref[lead - 1 : lead + 2, :], rest_ref[lead : lead + 3, :])
    out_ref[ROW_B3 : ROW_B3 + 1, :] += tail
    step = 508
    for at in range(0, REST["end"], step):
        out_ref[first + at : first + at + step, :] = halves(
            rest_ref[lead + 2 + at : lead + 2 + at + step, :], rest_ref[lead + 3 + at : lead + 3 + at + step, :]
        )
    end = first + REST["end"]
    out_ref[end : out_ref.shape[0], :] = jnp.zeros((out_ref.shape[0] - end, LANES), f32)
    chips, cut, unused_lanes = keep_a_hbm.shape
    each = cut + keep_b_hbm.shape[1]
    core = whole_ref[4]
    copies = Copies(sems)
    for chunk in range(2 * chips):
        for keep, send, at, rows in ((keep_a_hbm, send_a_hbm, 0, cut), (keep_b_hbm, send_b_hbm, cut, each - cut)):
            source = out_ref.at[pl.ds(chunk * each + at, rows), :]
            ours, theirs = (keep, send) if chunk % 2 == 0 else (send, keep)
            pl.when(core == 0)(functools.partial(copies.start_out, source, ours.at[chunk // 2]))
            pl.when(core != 0)(functools.partial(copies.start_out, source, theirs.at[chunk // 2]))
    copies.out(out_ref).wait()


def product_kernel(whole_ref, keep_ref, got_ref, far_a_ref, far_b_ref, keep_a_ref, send_a_ref, keep_b_ref, send_b_ref, loss_ref):
    me = whole_ref[5]
    loss = keep_ref[pl.ds(FACTOR_LOSS, 8), :].astype(f32) + got_ref[pl.ds(FACTOR_LOSS, 8), :].astype(f32)
    loss_ref[...] = jnp.broadcast_to(loss[0:1] + (loss[1:2] + loss[2:3]), (8, LANES))
    squares, share, unused_channels = keep_a_ref.shape
    blocks = C4 // LANES
    ways = (
        (0, far_a_ref, 0, QUARTER, (me // 2) % 2, keep_a_ref, send_a_ref),
        (1, far_b_ref, C4, 0, (me // 4) % 2, keep_b_ref, send_b_ref),
    )
    for way, far_ref, far_hidden, far_channels, mine, to_keep_ref, to_send_ref in ways:
        own = pl.ds(FACTOR_OWN[way], QUARTER)
        hidden = jnp.concatenate(
            [keep_ref[own, :], got_ref[own, :]] + [far_ref[k, pl.ds(far_hidden, QUARTER), :] for k in range(2)], axis=1
        )
        channels = [
            jnp.concatenate(
                [
                    keep_ref[pl.ds(FACTOR_CHANNELS + part * LANES, LANES), :],
                    got_ref[pl.ds(FACTOR_CHANNELS + part * LANES, LANES), :],
                ]
                + [far_ref[k, pl.ds(far_channels + part * LANES, LANES), :] for k in range(2)],
                axis=0,
            )
            for part in range(blocks)
        ]
        product = dot_nn(hidden, jnp.concatenate(channels, axis=1))
        for square in range(squares):
            first, second = (product[(2 * square + k) * share : (2 * square + k + 1) * share] for k in range(2))
            to_keep_ref[square] = jnp.where(mine == 0, first, second)
            to_send_ref[square] = jnp.where(mine == 0, second, first)


def passes(a, b, dot, many):
    pairs = [(0, 0), (0, 1), (1, 0)]
    if many:
        pairs += [(0, 2), (1, 1), (2, 0)]
    axis = 0 if dot is dot_tn else 1
    return dot(
        jnp.concatenate([a[i] for i, unused in pairs], axis=axis),
        jnp.concatenate([b[j] for unused, j in pairs], axis=0),
    )


def gram_kernel(scale_ref, terms, momentum_ref, loss_ref, ortho_ref, new_ref, packed_ref):
    grad = functools.reduce(jnp.add, [term[...] for term in terms]) * scale_ref[0]
    new = 0.95 * momentum_ref[...] + grad
    new_ref[...] = new
    ortho = grad + 0.95 * new
    ortho_ref[...] = ortho
    parts = split3(ortho)

    def cut(k):
        return tuple(p[:, k * LANES : (k + 1) * LANES] for p in parts)

    for at, (i, j) in enumerate(PAIRS):
        block = passes(cut(i), cut(j), dot_tn, True)
        if at == 0:
            row = lax.broadcasted_iota(jnp.int32, block.shape, 0)
            col = lax.broadcasted_iota(jnp.int32, block.shape, 1)
            block = jnp.where((row == LANES - 1) & (col == 0), loss_ref[0:1, 0:1], block)
        packed_ref[pl.ds(at * LANES, LANES), :] = block


def newton_steps(gram, ortho, steps, last):
    wide_row = lax.broadcasted_iota(jnp.int32, (C4, C4), 0)
    wide_col = lax.broadcasted_iota(jnp.int32, (C4, C4), 1)
    for iteration in steps:
        many = iteration == 0
        split = split3 if many else split2
        parts = split(gram)
        poly = jnp.where(wide_row == wide_col, 3.4445, 0.0) + (
            -4.775 * gram + 2.0315 * passes(parts, parts, dot_nn, many)
        )
        poly_parts = split(poly)
        ortho = passes(split(ortho), poly_parts, dot_nn, many)
        if iteration < last:
            gram = passes(split(passes(poly_parts, parts, dot_nn, many)), poly_parts, dot_nn, many)
    return gram, ortho


def newton_first_kernel(steps, packed_ref, ortho_ref, out_ref, gram_ref, loss_ref):
    row = lax.broadcasted_iota(jnp.int32, (LANES, LANES), 0)
    col = lax.broadcasted_iota(jnp.int32, (LANES, LANES), 1)
    trace = jnp.zeros((1, 1), f32)
    for at, (i, j) in enumerate(PAIRS):
        block = packed_ref[pl.ds(at * LANES, LANES), :]
        if at == 0:
            loss_ref[...] = jnp.broadcast_to(block[LANES - 1 : LANES, 0:1], (8, LANES))
            block = jnp.where((row == LANES - 1) & (col == 0), block.T, block)
        gram_ref[pl.ds(i * LANES, LANES), pl.ds(j * LANES, LANES)] = block
        if i == j:
            trace = trace + total(jnp.where(row == col, block, 0.0))
        else:
            gram_ref[pl.ds(j * LANES, LANES), pl.ds(i * LANES, LANES)] = block.T
    inverse = 1.0 / (jnp.sqrt(trace) + 1e-07)
    gram, ortho = newton_steps(
        gram_ref[...] * (inverse * inverse), ortho_ref[...] * inverse, range(steps), NS_ITERS - 1
    )
    gram_ref[...] = gram
    out_ref[...] = ortho


def newton_last_kernel(steps, unused_ref, gram_ref, ortho_ref, out_ref):
    unused_gram, ortho = newton_steps(gram_ref[...], ortho_ref[...], range(steps, NS_ITERS), NS_ITERS - 1)
    out_ref[...] = ortho


def shape(*dims, dtype=f32):
    return jax.ShapeDtypeStruct(dims, dtype)


def kernel_call(body, outs, scratch, smem, kept, count, micros, outs_kept=0, aliases=None):
    vmem = pl.BlockSpec(memory_space=pltpu.VMEM)
    scalar = pl.BlockSpec(memory_space=pltpu.SMEM)
    anywhere = pl.BlockSpec(memory_space=pl.ANY)
    if isinstance(kept, int):
        specs = [anywhere] * kept + [vmem] * (count - smem - kept)
    else:
        specs = [anywhere if k else vmem for k in kept[smem:]] + [vmem] * (count - len(kept))
    return pl.pallas_call(
        body,
        out_shape=outs,
        in_specs=[scalar] * smem + specs,
        out_specs=[anywhere] * outs_kept + [vmem] * (len(outs) - outs_kept),
        scratch_shapes=scratch,
        input_output_aliases=aliases or {},
        compiler_params=pltpu.CompilerParams(vmem_limit_bytes=60 * 1024 * 1024),
        cost_estimate=pl.CostEstimate(flops=10**6, bytes_accessed=micros * 3_000_000, transcendentals=0),
    )


def pack_kernel(valid_ref, mats_ref, flat_ref, out_ref, low_ref, high_ref):
    share = mats_ref.shape[1]
    blocks = C4 // LANES
    for mat in range(2):
        for part in range(blocks):
            at = (mat * blocks + part) * share
            out_ref[pl.ds(at, share), :] = mats_ref[mat, :, pl.ds(part * LANES, LANES)].astype(bf16)
    half, count = low_ref.shape[0], flat_ref.shape[0]
    low_ref[...] = flat_ref[pl.ds(0, half), :].astype(bf16)
    high_ref[pl.ds(0, count - half), :] = flat_ref[pl.ds(half, count - half), :].astype(bf16)
    left = 2 * half - count
    counted = (valid_ref[0] + valid_ref[1]).astype(f32)
    high_ref[pl.ds(count - half, left), :] = jnp.full((left, LANES), counted, f32).astype(bf16)


def run_pack(valid, mats, flat):
    half = (flat.shape[0] // 32 + 1) * 16
    outs = [shape(2 * C4 // LANES * mats.shape[1], LANES, dtype=bf16)] + [shape(half, LANES, dtype=bf16)] * 2
    return kernel_call(pack_kernel, outs, [], 1, 0, 3, 2)(valid, mats, flat)


def late_kernel(group_ref, unused_ref, out_ref):
    out_ref[0] = group_ref[0]


def run_late(group, tie):
    return pl.pallas_call(
        late_kernel,
        out_shape=shape(1, dtype=jnp.int32),
        in_specs=[pl.BlockSpec(memory_space=pltpu.SMEM), pl.BlockSpec(memory_space=pl.ANY)],
        out_specs=pl.BlockSpec(memory_space=pltpu.SMEM),
    )(group, tie)[0]


def run_conv(whole, flat, gathered, tie, moved, marks, flat_share, devices_count):
    half = C4 // 2
    moved_outs = [
        shape(16 * BOTH, 5 * LANES, dtype=bf16),
        shape(4 * BOTH, TAPS * LANES, dtype=bf16),
        shape(BOTH, K3P, dtype=bf16),
        shape(BOTH, K3P, dtype=bf16),
        shape(C2, 5 * LANES, dtype=bf16),
        shape(C3P, TAPS * LANES, dtype=bf16),
        shape(half, K3P, dtype=bf16),
        shape(half, K3P, dtype=bf16),
    ]
    outs = moved_outs + [
        shape(BOTH, C4),
        shape(REST["head"], LANES),
        shape(C4 // GROUP, (SPAN + 1) * LANES, dtype=bf16),
        shape(8, LANES),
        shape(8, LANES),
    ]
    scratch = [pltpu.VMEM(a.shape, a.dtype) for a in moved + moved_outs]
    scratch += [
        pltpu.VMEM((64 * BOTH, LANES), f32),
        pltpu.VMEM((16 * BOTH, LANES), f32),
        pltpu.VMEM((4 * BOTH, C3P), f32),
        pltpu.VMEM((4 * BOTH, TAPS * LANES), bf16),
        pltpu.VMEM((3 * BOTH, TAPS * LANES), bf16),
        pltpu.VMEM((C1, 2 * LANES), f32),
        pltpu.VMEM((5, C2, LANES), f32),
        pltpu.SemaphoreType.DMA((16,)),
    ]
    if flat_share % LANES:
        args = [whole, flat, tie] + moved + [marks]
        kept = [False, False] + [True] * 5
    else:
        arrays = [array for side in gathered for array, *unused in side]
        args = [whole] + arrays + [tie] + moved + [marks]
        kept = [False] + [True] * (len(arrays) + 5)
        scratch += [
            pltpu.VMEM((devices_count, 2 * arrays[0].shape[-2], LANES), bf16),
            pltpu.VMEM((devices_count * flat_share // LANES, LANES), f32),
        ]
    body = functools.partial(conv_kernel, flat_share, gathered)
    return kernel_call(body, outs, scratch, 1, kept, len(args), 12, 8)(*args)


def run_block(whole, real, got, made, marks, near, share):
    outs = [shape(FACTOR_ROWS, LANES, dtype=bf16)] * 2 + [
        shape(BOTH, C4),
        shape(8, C4),
        shape(8, HID),
        shape(8, C4),
        shape(8, C4),
        shape(8, CLSP),
    ]
    scratch = [
        pltpu.VMEM((2, FACTOR_ROWS, LANES), bf16),
        pltpu.VMEM((BOTH, HID), f32),
        pltpu.VMEM((C4 // GROUP, (SPAN + 1) * LANES), f32),
        pltpu.VMEM((MICRO * GROUP, C4 // GROUP), f32),
        pltpu.VMEM((2, HID // share, C4 // LANES * share, LANES), bf16),
        pltpu.SemaphoreType.DMA((2,)),
    ]
    args = [whole, real, got] + list(made) + [marks, near]
    body = functools.partial(block_kernel, share)
    return kernel_call(body, outs, scratch, 2, 1, len(args), 12, 2)(*args)


def run_backward(args, chips, each):
    scratch = [
        pltpu.VMEM((2 * chips * each, LANES), f32),
        pltpu.VMEM((4 * BOTH, C3P), f32),
        pltpu.VMEM((16 * BOTH, LANES), f32),
        pltpu.VMEM((64 * BOTH, LANES), f32),
        pltpu.VMEM((4 * BOTH, TAPS * LANES), f32),
        pltpu.VMEM((5, C2, LANES), f32),
        pltpu.VMEM((REST["end"] + 16, LANES), f32),
        pltpu.SemaphoreType.DMA((2,)),
    ]
    cut = -(-each // 16) * 8
    outs = [shape(chips, cut, LANES), shape(chips, each - cut, LANES)] * 2

    def body(*refs):
        backward_kernel(*refs[1 : len(args)], refs[0], *refs[len(args) :])

    return kernel_call(body, outs, scratch, 1, 2, len(args), 20, 4)(*args)


def run_product(whole, through, keep, got, far_a, far_b, squares, share):
    outs = [shape(*x.shape) for x in through] + [shape(squares, share, C4)] * 4 + [shape(8, LANES)]
    count = len(through)

    def body(*refs):
        product_kernel(refs[0], *refs[1 + count : 5 + count], *refs[5 + 2 * count :])

    return kernel_call(body, outs, [], 1, count, 5 + count, 3, count, {1 + k: k for k in range(count)})(
        whole, *through, keep, got, far_a, far_b
    )


def sum_kernel(whole_ref, keep_one_ref, got_one_ref, keep_two_ref, got_two_ref, *out_refs):
    square = whole_ref[5] // 8
    share = keep_one_ref.shape[1]
    for j, out_ref in enumerate(out_refs):
        entry = square ^ j
        out_ref[pl.ds(0, share), :] = keep_one_ref[entry] + got_one_ref[entry]
        out_ref[pl.ds(share, share), :] = keep_two_ref[entry] + got_two_ref[entry]


def run_sum(whole, tie, keep_one, got_one, keep_two, got_two):
    squares, share, unused_channels = keep_one.shape
    outs = [shape(2 * share, C4)] * squares

    def body(*refs):
        sum_kernel(refs[0], *refs[2:])

    return kernel_call(body, outs, [], 1, 1, 6, 2)(whole, tie, keep_one, got_one, keep_two, got_two)


def halve_kernel(whole_ref, tie_ref, keep_a, got_a, keep_b, got_b, sent_a, left_a, sent_b, left_b):
    me = whole_ref[5]
    high, low = (me // 4) % 2, (me // 2) % 2
    for place in range(2):
        first, second = (keep_a[0, k, place] + got_a[0, k, place] for k in range(2))
        sent_a[place, 0] = jnp.where(high == 0, second, first)
        left_a[place, 0] = jnp.where(high == 0, first, second)
        first, second = (keep_b[0, place, k] + got_b[0, place, k] for k in range(2))
        sent_b[place, 0] = jnp.where(low == 0, second, first)
        left_b[place, 0] = jnp.where(low == 0, first, second)


def run_halve(whole, tie, keep_a, got_a, keep_b, got_b):
    squares = keep_a.shape[0] // 4
    inputs = [x.reshape(squares, 2, 2, *x.shape[1:]) for x in (keep_a, got_a, keep_b, got_b)]
    rows = [x.shape[3] for x in inputs]
    outs = [shape(2, squares, rows[0], LANES)] * 2 + [shape(2, squares, rows[2], LANES)] * 2
    return pl.pallas_call(
        halve_kernel,
        grid=(squares,),
        out_shape=outs,
        in_specs=[pl.BlockSpec(memory_space=pltpu.SMEM), pl.BlockSpec(memory_space=pl.ANY)]
        + [pl.BlockSpec((1, 2, 2, r, LANES), lambda i: (i, 0, 0, 0, 0)) for r in rows],
        out_specs=[pl.BlockSpec((2, 1, x.shape[2], LANES), lambda i: (0, i, 0, 0)) for x in outs],
        compiler_params=pltpu.CompilerParams(vmem_limit_bytes=60 * 1024 * 1024),
        cost_estimate=pl.CostEstimate(flops=10**6, bytes_accessed=15_000_000, transcendentals=0),
    )(whole, tie, *inputs)


def run_gram(scale, terms, momentum, loss):
    rows, count = momentum.shape[0], len(terms)
    outs = [shape(rows, C4), shape(rows, C4), shape(len(PAIRS) * LANES, LANES)]

    def body(*refs):
        gram_kernel(refs[0], refs[1 : 1 + count], *refs[1 + count :])

    return kernel_call(body, outs, [], 1, 0, 3 + count, 4)(scale, *terms, momentum, loss)


def run_newton_first(packed, ortho, steps):
    outs = [shape(*ortho.shape), shape(C4, C4), shape(8, LANES)]
    return kernel_call(functools.partial(newton_first_kernel, steps), outs, [], 0, 0, 2, 12)(packed, ortho)


def run_newton_last(tie, gram, ortho, steps):
    outs = [shape(*ortho.shape)]
    return kernel_call(functools.partial(newton_last_kernel, steps), outs, [], 0, 1, 3, 8)(tie, gram, ortho)[0]


def patches(images, resolution, partner_col, mix_col):
    pictures = images[:, 0].astype(f32)
    dims = (1, 1, RES_L, RES_L)
    inside = (lax.broadcasted_iota(jnp.int32, dims, 2) < resolution) & (
        lax.broadcasted_iota(jnp.int32, dims, 3) < resolution
    )
    mixing = mix_col[:, None, None, None]
    other = jnp.where(partner_col[:, None, None, None] == 0, pictures[0][None], pictures[1][None])
    pixels = jnp.where(inside, mixing * pictures + (1.0 - mixing) * other, 0.0).astype(bf16)
    padded = jnp.pad(pixels, ((0, 0), (0, 0), (2, 1), (2, 1)))
    size = RES_STEP + 3
    blocks = [
        padded[:, :, RES_STEP * i : RES_STEP * i + size, RES_STEP * j : RES_STEP * j + size]
        for i in range(SIDE)
        for j in range(SIDE)
    ]
    blocks = jnp.stack(blocks, axis=1).reshape(MICRO * SIDE * SIDE, IN_CH, size, size)
    depth = IN_CH * 49
    choose = jnp.eye(depth, dtype=bf16).reshape(IN_CH, 7, 7, depth).transpose(1, 2, 0, 3)
    columns = lax.conv_general_dilated(
        blocks,
        choose,
        (4, 4),
        ((0, 0), (0, 0)),
        dimension_numbers=("NCHW", "HWIO", "HWNC"),
        preferred_element_type=f32,
    ).astype(bf16)
    columns = columns.reshape(64, MICRO, SIDE * SIDE, depth)
    columns = jnp.pad(columns, ((0, 0), (0, 0), (0, ROWS - SIDE * SIDE), (0, 2 * LANES - depth)))
    return columns.reshape(64 * BOTH, 2 * LANES)


def tap_orders(zero):
    row = lax.broadcasted_iota(jnp.int32, (TAPS * LANES, TAPS * LANES), 0) + zero
    col = lax.broadcasted_iota(jnp.int32, (TAPS * LANES, TAPS * LANES), 1)
    forth = ((row % LANES) * TAPS + row // LANES == col).astype(bf16)
    dims = (5 * LANES + C1, 5 * LANES)
    row = lax.broadcasted_iota(jnp.int32, dims, 0) - C1 + zero
    col = lax.broadcasted_iota(jnp.int32, dims, 1)
    real = (row >= 0) & (row < TAPS * C1)
    row = jnp.maximum(row, 0)
    back = (real & ((row % TAPS) * C1 + row // TAPS == col)).astype(bf16)
    row = lax.broadcasted_iota(jnp.int32, (C4, C4), 0) + zero
    col = lax.broadcasted_iota(jnp.int32, (C4, C4), 1)
    merge = ((row % (C4 // 2)) * 2 + row // (C4 // 2) == col).astype(bf16)
    return forth, back, merge


def grid_marks(side):
    row = np.arange(BOTH)
    image, q = row // ROWS, row % ROWS
    y, x = q // SIDE, q % SIDE
    real = q < SIDE * SIDE
    fixed = np.stack([real & (y > 0), real & (x > 0), real & (y > 0) & (x > 0)], 1).astype(np.float32)
    close = (
        (image[:, None] == image[None])
        & (abs(y[:, None] - y[None]) <= 1)
        & (abs(x[:, None] - x[None]) <= 1)
        & real[:, None]
        & real[None]
    )
    inside = jnp.asarray(real) & (jnp.asarray(y) < side) & (jnp.asarray(x) < side)
    near = jnp.where(jnp.asarray(close) & inside[:, None] & inside[None], 1.0, 0.0)
    cells = jnp.maximum(jnp.sum(near, axis=1), 1.0)
    marks = jnp.concatenate(
        [inside.astype(f32)[:, None], jnp.asarray(fixed), (1.0 / cells)[:, None]], axis=1
    )
    return jnp.pad(marks, ((0, 0), (0, LANES - marks.shape[1]))), near.astype(bf16)


def local_inputs(images, group, label_col, partner_col, mix_col, valid_col, me):
    side = RES_S // RES_STEP + group
    columns = patches(images, side * RES_STEP, partner_col, mix_col)
    orders = tap_orders(jnp.minimum(group, 0))
    marks, near = grid_marks(side)
    other = jnp.where(partner_col == 0, label_col[0], label_col[1])
    whole = jnp.concatenate([label_col, other, jnp.stack([me % 2, me]).astype(jnp.int32)])
    cells = (side * side).astype(f32)
    real = jnp.concatenate([mix_col, valid_col.astype(f32), jnp.stack([cells, cells * C4])])
    return whole, real, columns, orders, marks, near


def second_half(prepared, convs, made, chips, each, ties):
    columns, (forth, back, merge), marks = prepared[2], prepared[3], prepared[4]
    p1, p2, p3e, p3o, k1t, k2, k3e, k3o = convs[:8]
    args = [made[2], columns, p1, p2, p3e, p3o, k1t, k2, k3e, k3o, forth, back, merge, marks]
    return run_backward([prepared[0]] + list(ties) + args + list(made[3:8]), chips, each)


class Ring:
    def __init__(self, count):
        self.count = count
        self.squares = count // 8
        me = lax.axis_index(AXES)
        self.me = me
        self.core = me % 2
        self.low = (me // 2) % 2
        self.high = (me // 4) % 2
        self.corner = (me // 2) % 4
        self.square = me // 8

    def swap(self, value, bits):
        return lax.ppermute(value, AXES, [(i, i ^ bits) for i in range(self.count)])


def pick(value, at, axis):
    return lax.dynamic_index_in_dim(value, at, axis, keepdims=False)


class Scatter:
    def __init__(self, ring, terms, mine, bits):
        self.ring = ring
        self.terms = terms
        self.mine = mine
        self.bits = bits

    def exchange(self):
        sent = functools.reduce(jnp.add, [pick(x, 1 - self.mine, 0) for x in self.terms])
        self.terms = [pick(x, self.mine, 0) for x in self.terms] + [self.ring.swap(sent, self.bits)]

    def add(self):
        self.terms = [functools.reduce(jnp.add, self.terms)]


def sum_squares(ring, value, far_first):
    bits = ring.squares.bit_length() - 1
    order = list(range(bits))
    if far_first:
        order.reverse()
    held = order.copy()
    value = value.reshape((2,) * bits + value.shape[1:])
    got = None
    for bit in order:
        axis = len(held) - 1 - sorted(held).index(bit)
        held.remove(bit)
        mine = (ring.square >> bit) & 1
        if got is not None:
            value = value + got
        got = ring.swap(pick(value, 1 - mine, axis), 8 << bit)
        value = pick(value, mine, axis)
    return value, got


class Gather:
    def __init__(self, ring, value, far_first, high_first):
        self.ring = ring
        self.value = value
        self.masks = []
        bits = list(range(ring.squares.bit_length() - 1))
        self.squares = [8 << bit for bit in (reversed(bits) if far_first else bits)]
        self.corners = (4, 2) if high_first else (2, 4)
        self.pieces = []

    def exchange(self, mask):
        self.value = jnp.stack([self.value, self.ring.swap(self.value, mask)])
        self.masks = [mask] + self.masks

    def between_squares(self):
        for mask in self.squares:
            self.exchange(mask)

    def first_corner(self):
        self.exchange(self.corners[0])

    def second_corner(self):
        got = self.ring.swap(self.value, self.corners[1])
        self.pieces = [(self.value, self.masks, 0), (got, self.masks, self.corners[1])]

    def between_cores(self):
        self.pieces += [(self.ring.swap(array, 1), masks, base | 1) for array, masks, base in self.pieces]


def together(scatters, *others):
    counts = [len(x.terms) for x in scatters]
    values = lax.optimization_barrier(tuple(t for x in scatters for t in x.terms) + tuple(others))
    at = 0
    for x, count in zip(scatters, counts):
        x.terms = list(values[at : at + count])
        at += count
    return values[at:]


class ChipSum:
    def __init__(self, ring, value):
        self.ring = ring
        self.shape = value.shape
        self.terms = [value.reshape(4, value.shape[0] // 4, value.shape[1])]

    def scatter_corners(self):
        ring = self.ring
        got = [ring.swap(pick(self.terms[0], ring.corner ^ j, 0), 2 * j) for j in range(1, 4)]
        self.terms = [functools.reduce(jnp.add, got, pick(self.terms[0], ring.corner, 0))]

    def sum_squares(self):
        ring = self.ring
        got = [ring.swap(self.terms[0], 8 * j) for j in range(1, ring.squares)]
        self.terms = [functools.reduce(jnp.add, got, self.terms[0])]


    def gather_corners(self):
        ring = self.ring
        held = jnp.stack([self.terms[0]] + [ring.swap(self.terms[0], 2 * j) for j in range(1, 4)])
        return jnp.stack([pick(held, ring.corner ^ j, 0) for j in range(4)]).reshape(self.shape)


def per_device(
    devices_count,
    images,
    group_ids,
    labels,
    partners,
    mix_weights,
    valid,
    flat_params,
    flat_first,
    flat_second,
    mlp_weights,
    mlp_momentum,
):
    ring = Ring(devices_count)
    chips = devices_count // 2
    share = mlp_weights.shape[2]
    flat_share = flat_params.shape[0]
    flat_rows = -(-flat_share // LANES)
    spare = flat_rows * LANES - flat_share
    mine = jnp.pad(flat_params, (0, spare)) if spare else flat_params
    sent, flat_low, flat_high = run_pack(
        valid.reshape(MICRO), mlp_weights.transpose(0, 2, 1), mine.reshape(flat_rows, LANES)
    )
    got = lax.all_gather(sent, AXES, axis=0, tiled=False)
    aligned = flat_share % LANES == 0
    pieces = [Gather(ring, flat_low, False, True), Gather(ring, flat_high, True, False)]
    group = group_ids
    if aligned:
        for x in pieces:
            x.between_squares()
        for x in pieces:
            x.first_corner()
        group = run_late(group, pieces[1].value)
    else:
        group = group[0]
    prepared = local_inputs(
        images, group, labels[:, 0], partners[:, 0], mix_weights[:, 0], valid[:, 0], ring.me
    )
    whole, real, columns, orders, marks, near = prepared
    momentum = mlp_momentum.transpose(0, 2, 1)

    def of_both_cores(mine, theirs):
        at_first = ring.core == 0
        return jnp.concatenate([jnp.where(at_first, mine, theirs), jnp.where(at_first, theirs, mine)])

    momentum_rows = of_both_cores(
        pick(momentum, ring.core, 0), ring.swap(pick(momentum, 1 - ring.core, 0), 1)
    )
    moved = [columns, *orders]
    if aligned:
        for x in pieces:
            x.second_corner()
        for x in pieces:
            x.between_cores()
        convs = run_conv(
            whole, None, [x.pieces for x in pieces], momentum_rows, moved, marks, flat_share, devices_count
        )
        counted = convs[12][0, 0]
    else:
        rows = lax.all_gather(jnp.concatenate([flat_low, flat_high]), AXES, axis=0, tiled=False)
        whole_flat = (
            rows[:, :flat_rows]
            .astype(f32)
            .reshape(devices_count, flat_rows * LANES)[:, :flat_share]
            .reshape(devices_count * flat_share // LANES, LANES)
        )
        convs = run_conv(whole, whole_flat, None, momentum_rows, moved, marks, flat_share, devices_count)
        counted = jnp.sum(rows[:, flat_rows, 0].astype(f32))
    scale = 1.0 / jnp.maximum(counted, 1.0)
    made = run_block(whole, real, got, convs[8:12], marks, near, share)
    keep, send = made[:2]
    got_factors = ring.swap(send, 1)
    ahead = [
        jnp.stack([x[begin : begin + QUARTER + C4] for x in (keep, got_factors)]) for begin in (0, FACTOR_CHANNELS)
    ]
    far_a, far_b = ring.swap(ahead[0], 4), ring.swap(ahead[1], 2)

    each = -(-(devices_count * flat_share) // (devices_count * LANES * 8)) * 8
    ties = ahead
    keep_a, keep_b, send_a, send_b = second_half(prepared, convs, made, chips, each, ties)
    send_a, send_b, keep_one, send_one, keep_two, send_two, loss = run_product(
        whole, [send_a, send_b], keep, got_factors, far_a, far_b, ring.squares, share
    )
    got_one, got_two = ring.swap(send_one, 2), ring.swap(send_two, 4)
    got_a, got_b = ring.swap(send_a, 1), ring.swap(send_b, 1)
    sent_a, left_a, sent_b, left_b = run_halve(whole, keep_one, keep_a, got_a, keep_b, got_b)
    entries = run_sum(whole, sent_a, keep_one, got_one, keep_two, got_two)
    terms = [entries[0]] + [ring.swap(entries[j], 8 * j) for j in range(1, ring.squares)]
    flat = [
        Scatter(ring, [left_a, ring.swap(sent_a, 4)], ring.low, 2),
        Scatter(ring, [left_b, ring.swap(sent_b, 2)], ring.high, 4),
    ]
    ortho, momentum_new, packed = run_gram(scale[None], terms, momentum_rows, loss)
    grams = ChipSum(ring, packed)
    grams.scatter_corners()
    grams.sum_squares()
    for x in flat:
        x.exchange()
        x.add()
    together([grams] + flat)
    sum_flat = jnp.concatenate([sum(sum_squares(ring, x.terms[0], far)) for x, far in zip(flat, (False, True))])
    steps = 2
    ortho, gram, loss_total = run_newton_first(grams.gather_corners(), ortho, steps)
    lag = (devices_count - 1) * (each * LANES - flat_share)
    hops = -(-lag // (each * LANES))
    tail = min(each, -(-lag // (8 * LANES)) * 8)
    before = [
        lax.ppermute(sum_flat[each - tail :], AXES, [(i, i + h) for i in range(devices_count - h)])
        for h in range(hops, 0, -1)
    ]
    ortho = run_newton_last(sum_flat[each - 8 :], gram, ortho, steps)
    sum_flat = jnp.concatenate(before + [sum_flat])
    start = len(before) * tail * LANES - ring.me * (each * LANES - flat_share)
    if flat_share % LANES == 0:
        sum_flat = lax.dynamic_slice_in_dim(sum_flat, start // LANES, flat_rows, 0).reshape(-1)
    else:
        sum_flat = lax.dynamic_slice_in_dim(sum_flat.reshape(-1), start, flat_share, 0)
    sum_flat = sum_flat * scale
    first_new = 0.9 * flat_first + 0.1 * sum_flat
    second_new = 0.999 * flat_second + 0.001 * sum_flat * sum_flat
    first_hat = first_new / (1.0 - 0.9**STEP)
    second_hat = second_new / (1.0 - 0.999**STEP)
    params_new = flat_params - 0.02 * (
        first_hat / (jnp.sqrt(second_hat) + 1e-08) + 0.05 * flat_params
    )

    def to_owners(by_chip):
        parts = by_chip.reshape(2, share, C4)
        mine, theirs = pick(parts, ring.core, 0), ring.swap(pick(parts, 1 - ring.core, 0), 1)
        at_first = ring.core == 0
        return jnp.stack([jnp.where(at_first, mine, theirs), jnp.where(at_first, theirs, mine)])

    mats = mlp_weights.transpose(0, 2, 1)
    weights_new = mats * (1.0 - 0.1 * 0.05) - 0.1 * 0.2 * math.sqrt(HID) * to_owners(ortho)
    return (
        loss_total[0, 0],
        params_new,
        first_new,
        second_new,
        weights_new.transpose(0, 2, 1),
        to_owners(momentum_new).transpose(0, 2, 1),
    )


def solution(mesh):
    placed = (
        P(None, AXES, None, None, None),
        P(AXES),
        P(None, AXES),
        P(None, AXES),
        P(None, AXES),
        P(None, AXES),
        P(AXES),
        P(AXES),
        P(AXES),
        P(None, None, AXES),
        P(None, None, AXES),
    )
    devices_count = math.prod(mesh.shape[axis] for axis in AXES)
    return jax.shard_map(
        functools.partial(per_device, devices_count),
        mesh=mesh,
        in_specs=placed,
        out_specs=(
            P(),
            P(AXES),
            P(AXES),
            P(AXES),
            P(None, None, AXES),
            P(None, None, AXES),
        ),
        check_vma=False,
    )
```

```python
import functools
import math

import jax
import jax.numpy as jnp
import numpy as np
from jax import lax
from jax.experimental import pallas as pl
from jax.experimental.pallas import tpu as pltpu
from jax.sharding import PartitionSpec as P

C1 = 64
C2 = 128
C3 = 320
C4 = 512
HID = 2048
CLS = 1000
IN_CH = 3
RES_S = 96
RES_L = 160
RES_STEP = 32
MICRO = 2
NS_ITERS = 5
STEP = 10

AXES = ("fsdp", "ns")
LANES = 128
SIDE = 5
ROWS = 32
BOTH = MICRO * ROWS
C3P = 384
CLSP = 1024
K3P = 2944
TAPS = 9

f32 = jnp.float32
bf16 = jnp.bfloat16
norm_epsilon = 1e-05

NARROW = C1 * IN_CH * 49
ROW_B0 = NARROW // LANES
ROW_K1 = 74
ROW_B1 = 650
ROW_K2 = 651
ROW_B2 = 3531
ROW_K3 = 3533
ROW_B3 = 15053
REST = {"b3": 0, "block": 4, "fb1": 28, "fb2": 44, "final": 48, "head": 56, "hb": 4056, "end": 4064}
QUARTER = HID // 4
FACTOR_OTHER = (0, QUARTER + C4)
FACTOR_CHANNELS = QUARTER
FACTOR_OWN = (2 * QUARTER + C4, 3 * QUARTER + C4)
FACTOR_LOSS = HID + C4
FACTOR_ROWS = FACTOR_LOSS + 16
GROUP = 16
SPAN = GROUP * CLS // LANES
PAIRS = [(i, j) for i in range(4) for j in range(i, 4)]


def dot_nn(a, b):
    return lax.dot_general(a, b, (((1,), (0,)), ((), ())), preferred_element_type=f32)


def dot_nt(a, b):
    return lax.dot_general(a, b, (((1,), (1,)), ((), ())), preferred_element_type=f32)


def dot_tn(a, b):
    return lax.dot_general(a, b, (((0,), (0,)), ((), ())), preferred_element_type=f32)


def split2(x):
    hi = x.astype(bf16)
    return hi, (x - hi.astype(f32)).astype(bf16)


def split3(x):
    hi = x.astype(bf16)
    rest = x - hi.astype(f32)
    mid = rest.astype(bf16)
    return hi, mid, (rest - mid.astype(f32)).astype(bf16)


def stacked(dot, parts, other):
    rows = parts[0].shape[0]
    product = dot(jnp.concatenate(parts, axis=0), other)
    return functools.reduce(jnp.add, [product[k * rows : (k + 1) * rows] for k in range(len(parts))])


def two(dot, pair, other):
    return stacked(dot, pair, other)


def borrow(bits):
    out = list(bits)
    for at, bit in enumerate(out):
        if bit:
            out[at] = 0
            return tuple(out), 0
        out[at] = 1
    return tuple(out), 1


def tap_source(tap, row_bits, col_bits):
    r, c = divmod(tap, 3)
    src_r, down_r = (row_bits, 0) if r else borrow(row_bits)
    src_c, down_c = (col_bits, 0) if c else borrow(col_bits)
    return (int(r != 1), int(c != 1)), src_r, src_c, down_r, down_c


def plane_of(row_bits, col_bits):
    at = 0
    for r, c in zip(row_bits, col_bits):
        at = at * 4 + r * 2 + c
    return at


def stem_plane(quarter, row_bits, col_bits):
    row = quarter[0] + 2 * row_bits[0] + 4 * row_bits[1]
    return row * 8 + quarter[1] + 2 * col_bits[0] + 4 * col_bits[1]


def all_bits(pairs):
    for at in range(4**pairs):
        digits = [(at >> (2 * (pairs - 1 - k))) & 3 for k in range(pairs)]
        yield at, tuple(d >> 1 for d in digits), tuple(d & 1 for d in digits)


def moved(value, down_r, down_c, marks):
    if not (down_r or down_c):
        return value
    step = SIDE * down_r + down_c
    column = {(1, 0): 1, (0, 1): 2, (1, 1): 3}[(down_r, down_c)]
    return pltpu.roll(value, step, 0) * marks[:, column : column + 1]


def moved_back(value, down_r, down_c, marks):
    if not (down_r or down_c):
        return value
    step = SIDE * down_r + down_c
    column = {(1, 0): 1, (0, 1): 2, (1, 1): 3}[(down_r, down_c)]
    return pltpu.roll(value * marks[:, column : column + 1], BOTH - step, 0)


def erf(x):
    x = jnp.clip(x, -3.832506856900711, 3.832506856900711)
    s = x * x
    top = 2.2905065861350646e-4
    for coef in (3.4082910107109506e-3, 5.0955695062380861e-2, 1.8520832239976145e-1, 1.128379143519084):
        top = top * s + coef
    low = -1.1791602954361697e-7
    for coef in (
        2.3547966471313185e-5,
        1.0179625278914885e-3,
        1.4070470171167667e-2,
        1.1098505178285362e-1,
        4.9746925110067538e-1,
        1.0,
    ):
        low = low * s + coef
    return x * top / low


def total(x):
    return jnp.sum(jnp.sum(x, axis=1, keepdims=True), axis=0, keepdims=True)


def norm_images(value, mask, count):
    parts, scales = [], []
    for m in range(MICRO):
        v = value[m * ROWS : (m + 1) * ROWS]
        k = mask[m * ROWS : (m + 1) * ROWS]
        center = (v - total(v * k) / count) * k
        scale = lax.rsqrt(total(center * center) / count + norm_epsilon)
        parts.append(center * scale)
        scales.append(scale)
    return jnp.concatenate(parts, axis=0), scales


def norm_images_back(grad, hat, scales, gain, mask, count):
    parts = []
    for m in range(MICRO):
        at = slice(m * ROWS, (m + 1) * ROWS)
        g = grad[at] * gain
        h = hat[at]
        parts.append((g - total(g) / count - h * (total(g * h) / count)) * scales[m] * mask[at])
    return jnp.concatenate(parts, axis=0)


def rowsum(x):
    return jnp.sum(x, axis=0, keepdims=True)


def halves(low, high):
    lane = lax.broadcasted_iota(jnp.int32, low.shape, 1)
    return jnp.where(lane < LANES // 2, pltpu.roll(low, LANES // 2, 1), pltpu.roll(high, LANES // 2, 1))


def lanes_of(ref, row, count):
    return jnp.concatenate([ref[row + at : row + at + 1, :] for at in range(count)], axis=1)


def head_masks():
    row = lax.broadcasted_iota(jnp.int32, (C4 // GROUP, C4), 0)
    col = lax.broadcasted_iota(jnp.int32, (C4 // GROUP, C4), 1)
    return col // GROUP == row, col % GROUP == row // MICRO, row % MICRO == 0


class Copies:
    def __init__(self, sems):
        self.sems = sems
        self.count = 2

    def start_shared(self, source, target):
        pltpu.make_async_copy(source, target, self.sems.at[0]).start()

    def start_out(self, source, target):
        pltpu.make_async_copy(source, target, self.sems.at[1]).start()

    def out(self, source):
        return pltpu.make_async_copy(source, source, self.sems.at[1])

    def shared(self, target):
        return pltpu.make_async_copy(target, target, self.sems.at[0])

    def start(self, source, target):
        copy = self.make(source, target)
        copy.start()
        return copy

    def make(self, source, target):
        copy = pltpu.make_async_copy(source, target, self.sems.at[self.count])
        self.count += 1
        return copy


def pieces_of(gathered):
    for number, (unused_array, masks, base) in enumerate(gathered):
        for place in range(2 ** len(masks)):
            index, owner = [], base
            for k, mask in enumerate(masks):
                bit = (place >> k) & 1
                index.append(bit)
                owner ^= mask * bit
            yield number, tuple(index), owner


def conv_kernel(flat_share, gathered, *refs):
    if flat_share % LANES:
        conv_body(None, None, *refs)
    else:
        count = [len(side) for side in gathered]
        held = [refs[1 : 1 + count[0]], refs[1 + count[0] : 1 + sum(count)]]
        conv_body(flat_share, (gathered, held), refs[0], refs[-1], *refs[1 + sum(count) : -1])


def conv_body(
    flat_share,
    arrived,
    whole_ref,
    flat_ref,
    unused_hbm,
    p0_hbm,
    tm_hbm,
    t64_hbm,
    pm_hbm,
    marks_ref,
    p1_hbm,
    p2_hbm,
    p3e_hbm,
    p3o_hbm,
    k1t_hbm,
    k2_hbm,
    k3e_hbm,
    k3o_hbm,
    stream_ref,
    rest_ref,
    wide_ref,
    hb_ref,
    count_ref,
    p0_ref,
    tm_ref,
    t64_ref,
    pm_ref,
    p1_ref,
    p2_ref,
    p3e_ref,
    p3o_ref,
    k1t_ref,
    k2_ref,
    k3e_ref,
    k3o_ref,
    s1_ref,
    s2_ref,
    s3_ref,
    t2_ref,
    t3_ref,
    w0_ref,
    k1f_ref,
    sems,
    *near_refs,
):
    copies = Copies(sems)
    if arrived is not None:
        near_ref = near_refs[0]
        gathered, held = arrived
        half_rows = near_ref.shape[1] // 2
        me = whole_ref[5]
        for side in range(2):
            for number, index, owner in pieces_of(gathered[side]):
                copies.start_shared(
                    held[side][number].at[index], near_ref.at[me ^ owner, pl.ds(side * half_rows, half_rows), :]
                )
        flat_copy = copies.shared(near_ref)
    p0_copy = copies.start(p0_hbm, p0_ref)
    t64_copy = copies.start(t64_hbm, t64_ref)
    tm_copy = copies.start(tm_hbm, tm_ref)
    pm_copy = copies.start(pm_hbm, pm_ref)
    outward = []
    if arrived is not None:
        flat_copy.wait()
        flat_rows = flat_share // LANES
        counted = jnp.zeros((1, LANES), f32)
        for at in range(near_ref.shape[0]):
            flat_ref[pl.ds(at * flat_rows, flat_rows), :] = near_ref[at, pl.ds(0, flat_rows), :].astype(f32)
            counted = counted + near_ref[at, pl.ds(flat_rows, 1), :].astype(f32)
        count_ref[...] = jnp.broadcast_to(counted, (8, LANES))
    else:
        count_ref[...] = jnp.zeros((8, LANES), f32)
    marks = marks_ref[...]
    lane = lax.broadcasted_iota(jnp.int32, (BOTH, LANES), 1)
    lane1 = lax.broadcasted_iota(jnp.int32, (1, LANES), 1)
    depth = IN_CH * 49
    for at in range(C1):
        row, shift = divmod(depth * at, LANES)
        line = lanes_of(flat_ref, row, 3)
        if shift:
            line = pltpu.roll(line, 3 * LANES - shift, 1)
        w0_ref[at : at + 1, :] = line[:, : 2 * LANES]
    w0 = w0_ref[...].astype(bf16)
    w0 = jnp.concatenate([w0, w0], axis=0)
    b0 = flat_ref[ROW_B0 : ROW_B0 + 1, :]
    b0 = jnp.where(lane1 < C1, pltpu.roll(b0, C1, 1), b0)
    quarter = 16 * BOTH
    p0_copy.wait()
    for at in range(4):
        span = pl.ds(at * quarter, quarter)
        s1_ref[span, :] = (dot_nt(p0_ref[span, :], w0) + b0).astype(bf16).astype(f32)

    def tap_value(ref, pairs, tap, row_bits, col_bits, cols):
        q, src_r, src_c, down_r, down_c = tap_source(tap, row_bits, col_bits)
        if pairs == 2:
            at = stem_plane(q, src_r, src_c)
        else:
            at = (q[0] * 2 + q[1]) * 4**pairs + plane_of(src_r, src_c)
        return moved(ref[pl.ds(at * BOTH, BOTH), cols], down_r, down_c, marks)

    half = C2 // 2
    t64_copy.wait()
    for odd in range(2):
        block = jnp.concatenate(
            [flat_ref[pl.ds(ROW_K1 + 4 * odd + j, half, stride=9), :].astype(bf16) for j in range(5)], axis=1
        )
        block = dot_nn(block, t64_ref[pl.ds(C1 * (1 - odd), 5 * LANES), :])
        for j in range(5):
            k1f_ref[j, pl.ds(odd, half, stride=2), :] = block[:, j * LANES : (j + 1) * LANES]
    for j in range(5):
        k1t_ref[:, pl.ds(j * LANES, LANES)] = k1f_ref[j].astype(bf16)
    outward.append(copies.start(k1t_ref, k1t_hbm))
    everything = slice(None)
    for at, rb, cb in all_bits(2):
        for pair in range(5):
            left = tap_value(s1_ref, 2, 2 * pair, rb, cb, everything)
            if pair < 4:
                right = tap_value(s1_ref, 2, 2 * pair + 1, rb, cb, everything)
            else:
                right = jnp.zeros_like(left)
            p1_ref[pl.ds(at * BOTH, BOTH), pl.ds(pair * LANES, LANES)] = jnp.where(
                lane < C1, left, right
            ).astype(bf16)
    outward.append(copies.start(p1_ref, p1_hbm))
    b1 = flat_ref[ROW_B1 : ROW_B1 + 1, :]
    s2_ref[...] = (dot_nt(p1_ref[...], k1t_ref[...]) + b1).astype(bf16).astype(f32)
    for j in range(TAPS):
        k2_ref[pl.ds(0, C3), pl.ds(j * LANES, LANES)] = flat_ref[pl.ds(ROW_K2 + j, C3, stride=TAPS), :].astype(bf16)
    k2_ref[pl.ds(C3, C3P - C3), :] = jnp.zeros((C3P - C3, TAPS * LANES), bf16)
    outward.append(copies.start(k2_ref, k2_hbm))
    b2 = lanes_of(flat_ref, ROW_B2, 3)
    b2 = jnp.where(lax.broadcasted_iota(jnp.int32, b2.shape, 1) < C3, b2, 0.0)
    for at, rb, cb in all_bits(1):
        for tap in range(TAPS):
            t2_ref[pl.ds(at * BOTH, BOTH), pl.ds(tap * LANES, LANES)] = tap_value(
                s2_ref, 1, tap, rb, cb, everything
            ).astype(bf16)
    tm_copy.wait()
    p2_ref[...] = dot_nn(t2_ref[...], tm_ref[...]).astype(bf16)
    outward.append(copies.start(p2_ref, p2_hbm))
    s3_ref[...] = (dot_nt(p2_ref[...], k2_ref[...]) + b2).astype(bf16).astype(f32)
    for part in range(3):
        for tap in range(TAPS):
            t3_ref[pl.ds(part * BOTH, BOTH), pl.ds(tap * LANES, LANES)] = tap_value(
                s3_ref, 0, tap, (), (), pl.ds(part * LANES, LANES)
            ).astype(bf16)
    spread = dot_nn(t3_ref[...], tm_ref[...])
    spread = jnp.concatenate([spread[part * BOTH : (part + 1) * BOTH] for part in range(3)], axis=1)
    p3o_ref[...] = spread[:, :K3P].astype(bf16)
    p3e_ref[...] = pltpu.roll(spread, LANES // 2, 1)[:, :K3P].astype(bf16)
    for j in range(K3P // LANES):
        cols = pl.ds(j * LANES, LANES)
        k3e_ref[:, cols] = flat_ref[pl.ds(ROW_K3 + j, C4 // 2, stride=45), :].astype(bf16)
        k3o_ref[:, cols] = flat_ref[pl.ds(ROW_K3 + 23 + j, C4 // 2, stride=45), :].astype(bf16)
    for source, target in ((p3e_ref, p3e_hbm), (p3o_ref, p3o_hbm), (k3e_ref, k3e_hbm), (k3o_ref, k3o_hbm)):
        outward.append(copies.start(source, target))
    pm_copy.wait()
    apart = split3(
        jnp.concatenate([dot_nt(p3e_ref[...], k3e_ref[...]), dot_nt(p3o_ref[...], k3o_ref[...])], axis=1)
    )
    stream = stacked(dot_nn, apart, pm_ref[...])

    stream_ref[...] = stream

    amount = REST["head"]
    rest_ref[...] = halves(flat_ref[ROW_B3 : ROW_B3 + amount, :], flat_ref[ROW_B3 + 1 : ROW_B3 + 1 + amount, :])
    row_hb = ROW_B3 + REST["hb"]
    hb_ref[...] = halves(flat_ref[row_hb : row_hb + 8, :], flat_ref[row_hb + 1 : row_hb + 9, :])
    groups = C4 // GROUP
    row_head = ROW_B3 + REST["head"]
    low = pltpu.roll(flat_ref[pl.ds(row_head, groups, stride=SPAN), :], LANES // 2, 1)
    lane32 = lax.broadcasted_iota(jnp.int32, (groups, LANES), 1)
    for at in range(SPAN):
        high = pltpu.roll(flat_ref[pl.ds(row_head + at + 1, groups, stride=SPAN), :], LANES // 2, 1)
        wide_ref[:, pl.ds(at * LANES, LANES)] = jnp.where(lane32 < LANES // 2, low, high).astype(bf16)
        low = high
    wide_ref[:, pl.ds(SPAN * LANES, LANES)] = jnp.zeros((groups, LANES), bf16)
    for copy in outward:
        copy.wait()


def block_kernel(
    share,
    whole_ref,
    real_ref,
    got_hbm,
    stream_ref,
    rest_ref,
    wide_ref,
    hb_ref,
    marks_ref,
    near_ref,
    keep_hbm,
    send_hbm,
    dstream_ref,
    dblock_ref,
    dfb1_ref,
    small_ref,
    pooled_ref,
    dlog_ref,
    factor_ref,
    hid_ref,
    z_ref,
    per_ref,
    mats_ref,
    sems,
):
    copies = Copies(sems)
    me = whole_ref[5]
    for mat in range(2):
        rows = mats_ref.shape[2]
        copies.start_shared(got_hbm.at[:, pl.ds(mat * rows, rows), :], mats_ref.at[mat])
    mats_copy = copies.shared(mats_ref)
    marks = marks_ref[...]
    stream = stream_ref[...]
    b3 = lanes_of(rest_ref, REST["b3"], 4)
    gain1, shift1, scale1, gain2, shift2, scale2 = (lanes_of(rest_ref, REST["block"] + 4 * k, 4) for k in range(6))
    fb1 = lanes_of(rest_ref, REST["fb1"], HID // LANES)
    fb2 = lanes_of(rest_ref, REST["fb2"], 4)
    gain3, shift3 = (lanes_of(rest_ref, REST["final"] + 4 * k, 4) for k in range(2))

    stream = stream + b3
    mask = marks[:, 0:1]
    per_count = marks[:, 4:5]
    cells = real_ref[4]
    count = real_ref[5]
    near = near_ref[...]
    hat1, rs1 = norm_images(stream, mask, count)
    u = (hat1 * gain1 + shift1) * mask
    u3 = split3(u)
    around = dot_nn(near, u3[0]) + (dot_nn(near, u3[1]) + dot_nn(near, u3[2]))
    pool = around * per_count - u
    stream1 = stream + scale1 * pool
    hat2, rs2 = norm_images(stream1, mask, count)
    normed = ((hat2 * gain2 + shift2) * mask).astype(bf16)
    mats_copy.wait()
    blocks = C4 // LANES

    def matrix(mat, part):
        return mats_ref[mat, :, pl.ds(part * share, share), :].reshape(HID, LANES)

    def lanes(x, part):
        return x[:, part * LANES : (part + 1) * LANES]

    hidden = fb1
    for part in range(blocks):
        hidden = hidden + dot_nt(lanes(normed, part), matrix(0, part))
    hid_ref[...] = hidden
    active = (hidden * (0.5 * (1.0 + erf(hidden * math.sqrt(0.5))))).astype(bf16)
    branch = jnp.concatenate([dot_nn(active, matrix(1, part)) for part in range(blocks)], axis=1) + fb2
    stream2 = stream1 + scale2 * branch
    hat3, rs3 = norm_images(stream2, mask, count)
    outs = (hat3 * gain3 + shift3) * mask
    row8 = lax.broadcasted_iota(jnp.int32, (8, 1), 0)
    first, second = row8 == 0, row8 == 1

    def by_row(a, b):
        return jnp.where(first, a, jnp.where(second, b, 0.0))

    pooled = (by_row(rowsum(outs[:ROWS]), rowsum(outs[ROWS:])) / cells).astype(bf16)
    pooled_f = pooled.astype(f32)
    pooled_ref[...] = pooled_f
    in_group, in_place, own_row = head_masks()
    picked = jnp.where(in_place, jnp.where(own_row, pooled_f[0:1, :], pooled_f[1:2, :]), 0.0).astype(bf16)
    by_place = dot_nt(picked, in_group.astype(bf16)).astype(bf16)
    z_ref[...] = dot_nn(by_place, wide_ref[...])
    column = lax.broadcasted_iota(jnp.int32, (8, CLSP), 1)
    hb = lanes_of(hb_ref, 0, 8)
    logits = jnp.zeros((MICRO, CLSP), f32)
    for place in range(GROUP):
        at, shift = divmod(CLS * place, LANES)
        window = z_ref[pl.ds(MICRO * place, MICRO), pl.ds(at * LANES, CLSP + LANES)]
        if shift:
            window = pltpu.roll(window, CLSP + LANES - shift, 1)
        logits = logits + window[:, :CLSP]
    logits = by_row(logits[0:1], logits[1:2]) + hb
    logits = jnp.where(column < CLS, logits, -1e30)
    top = jnp.max(logits, axis=1, keepdims=True)
    powers = jnp.exp(logits - top)
    mass = jnp.sum(powers, axis=1, keepdims=True)
    own = jnp.where(first, whole_ref[0], whole_ref[1])
    other = jnp.where(first, whole_ref[2], whole_ref[3])
    mix = by_row(real_ref[0], real_ref[1])
    target = jnp.where(column == own, mix, 0.0) + jnp.where(column == other, 1.0 - mix, 0.0)
    valid = by_row(real_ref[2], real_ref[3])
    logp = logits - top - jnp.log(mass)
    losses = -jnp.sum(target * logp, axis=1, keepdims=True) * valid
    loss = split3(jnp.broadcast_to(jnp.sum(losses, axis=0, keepdims=True), (1, LANES)))
    dlogits = (powers / mass * jnp.sum(target, axis=1, keepdims=True) - target) * valid
    dlog_ref[...] = dlogits
    padded = jnp.concatenate([dlogits, jnp.zeros((8, LANES), f32)], axis=1)
    for place in range(GROUP):
        at, shift = divmod(CLS * place, LANES)
        window = pltpu.roll(padded, shift, 1) if shift else padded
        per_group = two(dot_nt, split2(window), wide_ref[:, pl.ds(at * LANES, CLSP + LANES)])
        per_ref[pl.ds(MICRO * place, MICRO), :] = per_group[:MICRO]
    per3 = split3(per_ref[...])
    ones = in_group.astype(bf16)
    by_channel = dot_nn(per3[0], ones) + (dot_nn(per3[1], ones) + dot_nn(per3[2], ones))
    dpooled = by_row(
        rowsum(jnp.where(in_place & own_row, by_channel, 0.0)),
        rowsum(jnp.where(in_place & ~own_row, by_channel, 0.0)),
    )
    dpooled = dpooled / cells
    douts = jnp.concatenate(
        [
            jnp.broadcast_to(dpooled[0:1], (ROWS, C4)),
            jnp.broadcast_to(dpooled[1:2], (ROWS, C4)),
        ],
        axis=0,
    ) * mask
    row8w = lax.broadcasted_iota(jnp.int32, (8, C4), 0)

    def stack8(values):
        out = jnp.zeros((8, C4), f32)
        for at, v in enumerate(values):
            out = jnp.where(row8w == at, v, out)
        return out

    dgain3, dshift3 = rowsum(douts * hat3), rowsum(douts)
    dstream2 = norm_images_back(douts, hat3, rs3, gain3, mask, count)
    dscale2 = rowsum(dstream2 * branch)
    dbranch = dstream2 * scale2
    dfb2 = rowsum(dbranch)
    dbr = split2(dbranch)
    dactive = None
    for part in range(blocks):
        term = two(dot_nt, (lanes(dbr[0], part), lanes(dbr[1], part)), matrix(1, part))
        dactive = term if dactive is None else dactive + term
    hidden = hid_ref[...]
    slope = 0.5 * (1.0 + erf(hidden * math.sqrt(0.5))) + hidden * (
        jnp.exp(-0.5 * hidden * hidden) * (1.0 / math.sqrt(2.0 * math.pi))
    )
    dhidden = dactive * slope
    dfb1_ref[...] = jnp.broadcast_to(rowsum(dhidden), (8, HID))
    dhid = split2(dhidden)

    core, corner_high, corner_low = whole_ref[4], (me // 4) % 2, (me // 2) % 2
    active_f = active.astype(f32)
    sides = (
        (jnp.concatenate([d.astype(f32) for d in dhid], axis=0), jnp.concatenate([normed, normed], axis=0)),
        (jnp.concatenate([active_f, active_f], axis=0), jnp.concatenate(dbr, axis=0)),
    )
    each = 2 * share
    factor_ref[:, pl.ds(FACTOR_LOSS, FACTOR_ROWS - FACTOR_LOSS), :] = jnp.zeros(
        (2, FACTOR_ROWS - FACTOR_LOSS, LANES), bf16
    )
    for mat, (hidden_side, channel_side) in enumerate(sides):
        for at in range(HID // LANES):
            cols = slice(at * LANES, (at + 1) * LANES)
            factor_ref[mat, pl.ds(at * LANES, LANES), :] = hidden_side[:, cols].T.astype(bf16)
        for part in range(blocks):
            factor_ref[mat, pl.ds(HID + part * LANES, LANES), :] = lanes(channel_side, part)

        for k in range(3):
            factor_ref[mat, pl.ds(FACTOR_LOSS + k, 1), :] = loss[k]

        def send_out(mat, target):
            for chip in range(HID // each):
                square, high, low = chip // 4, (chip // 2) % 2, chip % 2
                for side, (bit, mine, place) in enumerate(((high, corner_high, low), (low, corner_low, high))):
                    begin = jnp.where(mine == bit, FACTOR_OWN[side], FACTOR_OTHER[side])
                    to = pl.multiple_of(begin + (square * 2 + place) * share, share)
                    source = factor_ref.at[mat, pl.ds(chip * each + side * share, share), :]
                    copies.start_out(source, target.at[pl.ds(to, share), :])
            copies.start_out(
                factor_ref.at[mat, pl.ds(HID, blocks * LANES), :], target.at[pl.ds(FACTOR_CHANNELS, blocks * LANES), :]
            )
            rest = pl.ds(FACTOR_LOSS, FACTOR_ROWS - FACTOR_LOSS)
            copies.start_out(factor_ref.at[mat, rest, :], target.at[rest, :])

        pl.when(core == mat)(functools.partial(send_out, mat, keep_hbm))
        pl.when(core != mat)(functools.partial(send_out, mat, send_hbm))
    dnormed = jnp.concatenate([two(dot_nn, dhid, matrix(0, part)) for part in range(blocks)], axis=1)
    dgain2, dshift2 = rowsum(dnormed * hat2), rowsum(dnormed * mask)
    dstream1 = dstream2 + norm_images_back(dnormed, hat2, rs2, gain2, mask, count)
    dscale1 = rowsum(dstream1 * pool)
    dpool = dstream1 * scale1
    back = split3(dpool * per_count)
    du = dot_nn(near, back[0]) + (dot_nn(near, back[1]) + dot_nn(near, back[2])) - dpool
    dgain1, dshift1 = rowsum(du * hat1), rowsum(du)
    dstream = dstream1 + norm_images_back(du, hat1, rs1, gain1, mask, count)
    dblock_ref[...] = stack8([dgain1, dshift1, dscale1, dgain2, dshift2, dscale2])
    small_ref[...] = stack8([rowsum(dstream), dfb2, dgain3, dshift3])
    dstream_ref[...] = dstream
    copies.out(factor_ref).wait()


def backward_kernel(
    unused_one_ref,
    unused_two_ref,
    dstream_ref,
    p0_hbm,
    p1_hbm,
    p2_hbm,
    p3e_ref,
    p3o_ref,
    k1t_hbm,
    k2_hbm,
    k3e_hbm,
    k3o_hbm,
    tm_hbm,
    t64_hbm,
    pm_ref,
    marks_ref,
    dblock_ref,
    dfb1_ref,
    small_ref,
    pooled_ref,
    dlog_ref,
    whole_ref,
    keep_a_hbm,
    keep_b_hbm,
    send_a_hbm,
    send_b_hbm,
    out_ref,
    ds3_ref,
    ds2_ref,
    ds1_ref,
    dt_ref,
    dk1t_ref,
    rest_ref,
    p0_ref,
    p1_ref,
    p2_ref,
    k1t_ref,
    k2_ref,
    k3e_ref,
    k3o_ref,
    tm_ref,
    t64_ref,
    sems,
):
    copies = Copies(sems)
    third_copies = [copies.start(*x) for x in ((k3e_hbm, k3e_ref), (k3o_hbm, k3o_ref), (tm_hbm, tm_ref))]
    early_copies = [
        copies.start(*x)
        for x in (
            (p2_hbm, p2_ref),
            (k2_hbm, k2_ref),
            (p1_hbm, p1_ref),
            (k1t_hbm, k1t_ref),
            (t64_hbm, t64_ref),
            (p0_hbm, p0_ref),
        )
    ]
    marks = marks_ref[...]
    lane = lax.broadcasted_iota(jnp.int32, (BOTH, LANES), 1)
    lane1 = lax.broadcasted_iota(jnp.int32, (1, LANES), 1)
    wide = TAPS * LANES
    grad3 = split3(dstream_ref[...])
    apart = stacked(dot_nt, grad3, pm_ref[...])
    half = C4 // 2
    even, odd = split2(apart[:, :half]), split2(apart[:, half:])
    tall_even, tall_odd = jnp.concatenate(even, axis=0), jnp.concatenate(odd, axis=0)

    def by_even(cols):
        return dot_tn(tall_even, jnp.concatenate([p3e_ref[:, cols]] * 2, axis=0))

    def by_odd(cols):
        return dot_tn(tall_odd, jnp.concatenate([p3o_ref[:, cols]] * 2, axis=0))

    last = K3P // LANES - 1
    for j in range(last):
        cols = pl.ds(j * LANES, LANES)
        out_ref[pl.ds(ROW_K3 + 23 + j, half, stride=45), :] = by_odd(cols)
        if j:
            out_ref[pl.ds(ROW_K3 + j, half, stride=45), :] = by_even(cols)
    cols = pl.ds(last * LANES, LANES)
    out_ref[pl.ds(ROW_K3 + last, half, stride=45), :] = by_even(cols)
    tail = by_odd(cols)
    begin = by_even(pl.ds(0, LANES))
    rows = lax.broadcasted_iota(jnp.int32, (half, LANES), 0)
    out_ref[pl.ds(ROW_K3, half, stride=45), :] = begin + jnp.where(rows == 0, 0.0, pltpu.roll(tail, 1, 0))
    tail = tail[half - 1 : half]
    ds3_ref[...] = jnp.zeros_like(ds3_ref)
    position = lax.broadcasted_iota(jnp.int32, (BOTH, K3P), 1)
    for copy in third_copies:
        copy.wait()
    nat = jnp.where(position < LANES // 2, 0.0, two(dot_nn, even, k3e_ref[...]))
    nat = pltpu.roll(nat, K3P - LANES // 2, 1) + jnp.where(
        position < C3 * TAPS, two(dot_nn, odd, k3o_ref[...]), 0.0
    )
    for part in range(3):
        width = min(wide, K3P - part * wide)
        pieces = split2(nat[:, part * wide : part * wide + width])
        by_tap = dot_nt(pieces[0], tm_ref[:, pl.ds(0, width)]) + dot_nt(pieces[1], tm_ref[:, pl.ds(0, width)])
        for tap in range(TAPS):
            q, src_r, src_c, down_r, down_c = tap_source(tap, (), ())
            at = q[0] * 2 + q[1]
            ds3_ref[pl.ds(at * BOTH, BOTH), pl.ds(part * LANES, LANES)] += moved_back(
                by_tap[:, tap * LANES : (tap + 1) * LANES], down_r, down_c, marks
            )
    lead = 5

    def put(name, value):
        for k in range(value.shape[1] // LANES):
            at = lead + REST[name] + k
            rest_ref[at : at + 1, :] = value[:, k * LANES : (k + 1) * LANES]

    rest_ref[0:8, :] = jnp.zeros((8, LANES), f32)
    put("b3", small_ref[0:1, :])
    for k in range(6):
        at = lead + REST["block"] + 4 * k
        for i in range(4):
            rest_ref[at + i : at + i + 1, :] = dblock_ref[k : k + 1, i * LANES : (i + 1) * LANES]
    put("fb1", dfb1_ref[0:1, :])
    put("fb2", small_ref[1:2, :])
    put("final", jnp.concatenate([small_ref[2:3, :], small_ref[3:4, :]], axis=1))
    dlog = dlog_ref[...]
    put("hb", dlog[0:1] + dlog[1:2])
    rest_ref[lead + REST["end"] : lead + REST["end"] + 11, :] = jnp.zeros((11, LANES), f32)
    pooled = pooled_ref[...]
    in_group, in_place, own_row = head_masks()
    picked = jnp.where(in_place, jnp.where(own_row, pooled[0:1, :], pooled[1:2, :]), 0.0).astype(bf16)
    by_group = dot_nt(in_group.astype(bf16), picked)
    padded = jnp.concatenate([dlog, jnp.zeros((8, LANES), f32)], axis=1)
    groups = C4 // GROUP
    written = -1
    for place in range(GROUP):
        at, shift = divmod(CLS * place, LANES)
        window = pltpu.roll(padded, shift, 1) if shift else padded
        ours = by_group[:, MICRO * place : MICRO * place + 1]
        others = by_group[:, MICRO * place + 1 : MICRO * place + 2]
        for k in range(CLSP // LANES + 1):
            if (at + k) * LANES >= CLS * (place + 1):
                break
            block = slice(k * LANES, (k + 1) * LANES)
            value = ours * window[0:1, block] + others * window[1:2, block]
            target = pl.ds(lead + REST["head"] + at + k, groups, stride=SPAN)
            if at + k == written:
                rest_ref[target, :] += value
            else:
                rest_ref[target, :] = value
            written = at + k
    first = ROW_B3 + 3
    out_ref[ROW_B3 : first, :] = halves(rest_ref[lead - 1 : lead + 2, :], rest_ref[lead : lead + 3, :])
    out_ref[ROW_B3 : ROW_B3 + 1, :] += tail
    step = 508
    for at in range(0, REST["end"], step):
        out_ref[first + at : first + at + step, :] = halves(
            rest_ref[lead + 2 + at : lead + 2 + at + step, :], rest_ref[lead + 3 + at : lead + 3 + at + step, :]
        )
    end = first + REST["end"]
    out_ref[end : out_ref.shape[0], :] = jnp.zeros((out_ref.shape[0] - end, LANES), f32)
    chips, cut, unused_lanes = keep_a_hbm.shape
    each = cut + keep_b_hbm.shape[1]
    core = whole_ref[4]

    def send_chunks(chunks):
        for chunk in chunks:
            for keep, send, at, rows in ((keep_a_hbm, send_a_hbm, 0, cut), (keep_b_hbm, send_b_hbm, cut, each - cut)):
                source = out_ref.at[pl.ds(chunk * each + at, rows), :]
                ours, theirs = (keep, send) if chunk % 2 == 0 else (send, keep)
                pl.when(core == 0)(functools.partial(copies.start_out, source, ours.at[chunk // 2]))
                pl.when(core != 0)(functools.partial(copies.start_out, source, theirs.at[chunk // 2]))

    bound = -(-(ROW_K3 + 1) // each)
    send_chunks(range(bound, 2 * chips))
    for copy in early_copies:
        copy.wait()
    db2 = rowsum(ds3_ref[...])
    for k in range(2):
        out_ref[ROW_B2 + k : ROW_B2 + k + 1, :] = db2[:, k * LANES : (k + 1) * LANES]
    out_ref[ROW_K3 : ROW_K3 + 1, :] += jnp.where(lane1 < LANES // 2, db2[:, 2 * LANES :], 0.0)
    grad = split2(ds3_ref[...])
    grad_real = (grad[0][:, :C3], grad[1][:, :C3])
    for j in range(TAPS):
        cols = pl.ds(j * LANES, LANES)
        value = dot_tn(grad[0], p2_ref[:, cols]) + dot_tn(grad[1], p2_ref[:, cols])
        out_ref[pl.ds(ROW_K2 + j, C3, stride=TAPS), :] = value[:C3]
    pieces = split2(two(dot_nn, grad, k2_ref[...]))
    dt_ref[...] = two(dot_nt, pieces, tm_ref[...])
    ds2_ref[...] = jnp.zeros_like(ds2_ref)
    for at, rb, cb in all_bits(1):
        for tap in range(TAPS):
            q, src_r, src_c, down_r, down_c = tap_source(tap, rb, cb)
            to = (q[0] * 2 + q[1]) * 4 + plane_of(src_r, src_c)
            ds2_ref[pl.ds(to * BOTH, BOTH), :] += moved_back(
                dt_ref[pl.ds(at * BOTH, BOTH), pl.ds(tap * LANES, LANES)], down_r, down_c, marks
            )
    out_ref[ROW_B1 : ROW_B1 + 1, :] = rowsum(ds2_ref[...])
    grad = split2(ds2_ref[...])
    few = C2 // 2
    for j in range(5):
        cols = pl.ds(j * LANES, LANES)
        dk1t_ref[j] = dot_tn(grad[0], p1_ref[:, cols]) + dot_tn(grad[1], p1_ref[:, cols])
    evens, odds = (
        two(
            dot_nt,
            split2(jnp.concatenate([dk1t_ref[j, pl.ds(odd, few, stride=2), :] for j in range(5)], axis=1)),
            t64_ref[pl.ds(C1 * (1 - odd), 5 * LANES), :],
        )
        for odd in range(2)
    )
    for j in range(9):
        if j < 4:
            value = evens[:, j * LANES : (j + 1) * LANES]
        elif j == 4:
            value = evens[:, 4 * LANES :] + odds[:, :LANES]
        else:
            value = odds[:, (j - 4) * LANES : (j - 3) * LANES]
        out_ref[pl.ds(ROW_K1 + j, few, stride=9), :] = value
    ds1_ref[...] = jnp.zeros_like(ds1_ref)
    for pair in range(5):
        values = two(dot_nn, grad, k1t_ref[:, pl.ds(pair * LANES, LANES)])
        for at, rb, cb in all_bits(2):
            here = values[at * BOTH : (at + 1) * BOTH]
            for side in range(2):
                tap = 2 * pair + side
                if tap >= TAPS:
                    continue
                q, src_r, src_c, down_r, down_c = tap_source(tap, rb, cb)
                to = stem_plane(q, src_r, src_c)
                mine = (lane < C1) if side == 0 else (lane >= C1)
                ds1_ref[pl.ds(to * BOTH, BOTH), :] += moved_back(
                    jnp.where(mine, here, 0.0), down_r, down_c, marks
                )
    db0 = rowsum(ds1_ref[...])
    db0 = db0 + pltpu.roll(db0, LANES // 2, 1)
    stem = jnp.zeros((LANES, 2 * LANES), f32)
    for at in range(4):
        span = pl.ds(at * 16 * BOTH, 16 * BOTH)
        grad = split2(ds1_ref[span, :])
        stem = stem + (dot_tn(grad[0], p0_ref[span, :]) + dot_tn(grad[1], p0_ref[span, :]))
    stem = stem[:C1] + stem[C1:]
    depth = IN_CH * 49
    held = jnp.zeros((1, 3 * LANES), f32)
    done = 0
    for at in range(C1):
        row, shift = divmod(depth * at, LANES)
        line = jnp.concatenate([stem[at : at + 1], jnp.zeros((1, LANES), f32)], axis=1)
        if shift:
            line = pltpu.roll(line, shift, 1)
        while done < row:
            out_ref[done : done + 1, :] = held[:, :LANES]
            held = jnp.concatenate([held[:, LANES:], jnp.zeros((1, LANES), f32)], axis=1)
            done += 1
        held = held + line
    out_ref[done : done + 1, :] = held[:, :LANES]
    if done < ROW_B0:
        out_ref[ROW_B0 : ROW_B0 + 1, :] = held[:, LANES : 2 * LANES]
    out_ref[ROW_B0 : ROW_B0 + 1, :] += jnp.where(lane1 < LANES // 2, 0.0, db0)

    send_chunks(range(bound))
    copies.out(out_ref).wait()


def product_kernel(whole_ref, keep_ref, got_ref, far_a_ref, far_b_ref, keep_a_ref, send_a_ref, keep_b_ref, send_b_ref, loss_ref):
    me = whole_ref[5]
    loss = keep_ref[pl.ds(FACTOR_LOSS, 8), :].astype(f32) + got_ref[pl.ds(FACTOR_LOSS, 8), :].astype(f32)
    loss_ref[...] = jnp.broadcast_to(loss[0:1] + (loss[1:2] + loss[2:3]), (8, LANES))
    squares, share, unused_channels = keep_a_ref.shape
    blocks = C4 // LANES
    ways = (
        (0, far_a_ref, 0, QUARTER, (me // 2) % 2, keep_a_ref, send_a_ref),
        (1, far_b_ref, C4, 0, (me // 4) % 2, keep_b_ref, send_b_ref),
    )
    for way, far_ref, far_hidden, far_channels, mine, to_keep_ref, to_send_ref in ways:
        own = pl.ds(FACTOR_OWN[way], QUARTER)
        hidden = jnp.concatenate(
            [keep_ref[own, :], got_ref[own, :]] + [far_ref[k, pl.ds(far_hidden, QUARTER), :] for k in range(2)], axis=1
        )
        channels = [
            jnp.concatenate(
                [
                    keep_ref[pl.ds(FACTOR_CHANNELS + part * LANES, LANES), :],
                    got_ref[pl.ds(FACTOR_CHANNELS + part * LANES, LANES), :],
                ]
                + [far_ref[k, pl.ds(far_channels + part * LANES, LANES), :] for k in range(2)],
                axis=0,
            )
            for part in range(blocks)
        ]
        product = dot_nn(hidden, jnp.concatenate(channels, axis=1))
        for square in range(squares):
            first, second = (product[(2 * square + k) * share : (2 * square + k + 1) * share] for k in range(2))
            to_keep_ref[square] = jnp.where(mine == 0, first, second)
            to_send_ref[square] = jnp.where(mine == 0, second, first)


def passes(a, b, dot, many):
    pairs = [(0, 0), (0, 1), (1, 0)]
    if many:
        pairs += [(0, 2), (1, 1), (2, 0)]
    axis = 0 if dot is dot_tn else 1
    return dot(
        jnp.concatenate([a[i] for i, unused in pairs], axis=axis),
        jnp.concatenate([b[j] for unused, j in pairs], axis=0),
    )


def gram_kernel(scale_ref, terms, momentum_ref, loss_ref, ortho_ref, new_ref, packed_ref):
    grad = functools.reduce(jnp.add, [term[...] for term in terms]) * scale_ref[0]
    new = 0.95 * momentum_ref[...] + grad
    new_ref[...] = new
    ortho = grad + 0.95 * new
    ortho_ref[...] = ortho
    parts = split3(ortho)

    def cut(k):
        return tuple(p[:, k * LANES : (k + 1) * LANES] for p in parts)

    for at, (i, j) in enumerate(PAIRS):
        block = passes(cut(i), cut(j), dot_tn, True)
        if at == 0:
            row = lax.broadcasted_iota(jnp.int32, block.shape, 0)
            col = lax.broadcasted_iota(jnp.int32, block.shape, 1)
            block = jnp.where((row == LANES - 1) & (col == 0), loss_ref[0:1, 0:1], block)
        packed_ref[pl.ds(at * LANES, LANES), :] = block


def newton_steps(gram, ortho, steps, last):
    wide_row = lax.broadcasted_iota(jnp.int32, (C4, C4), 0)
    wide_col = lax.broadcasted_iota(jnp.int32, (C4, C4), 1)
    for iteration in steps:
        many = iteration == 0
        split = split3 if many else split2
        parts = split(gram)
        poly = jnp.where(wide_row == wide_col, 3.4445, 0.0) + (
            -4.775 * gram + 2.0315 * passes(parts, parts, dot_nn, many)
        )
        poly_parts = split(poly)
        ortho = passes(split(ortho), poly_parts, dot_nn, many)
        if iteration < last:
            gram = passes(split(passes(poly_parts, parts, dot_nn, many)), poly_parts, dot_nn, many)
    return gram, ortho


def newton_first_kernel(steps, packed_ref, ortho_ref, out_ref, gram_ref, loss_ref):
    row = lax.broadcasted_iota(jnp.int32, (LANES, LANES), 0)
    col = lax.broadcasted_iota(jnp.int32, (LANES, LANES), 1)
    trace = jnp.zeros((1, 1), f32)
    for at, (i, j) in enumerate(PAIRS):
        block = packed_ref[pl.ds(at * LANES, LANES), :]
        if at == 0:
            loss_ref[...] = jnp.broadcast_to(block[LANES - 1 : LANES, 0:1], (8, LANES))
            block = jnp.where((row == LANES - 1) & (col == 0), block.T, block)
        gram_ref[pl.ds(i * LANES, LANES), pl.ds(j * LANES, LANES)] = block
        if i == j:
            trace = trace + total(jnp.where(row == col, block, 0.0))
        else:
            gram_ref[pl.ds(j * LANES, LANES), pl.ds(i * LANES, LANES)] = block.T
    inverse = 1.0 / (jnp.sqrt(trace) + 1e-07)
    gram, ortho = newton_steps(
        gram_ref[...] * (inverse * inverse), ortho_ref[...] * inverse, range(steps), NS_ITERS - 1
    )
    gram_ref[...] = gram
    out_ref[...] = ortho


def newton_last_kernel(steps, gram_ref, ortho_ref, out_ref):
    unused_gram, ortho = newton_steps(gram_ref[...], ortho_ref[...], range(steps, NS_ITERS), NS_ITERS - 1)
    out_ref[...] = ortho


def shape(*dims, dtype=f32):
    return jax.ShapeDtypeStruct(dims, dtype)


def kernel_call(body, outs, scratch, smem, kept, count, micros, outs_kept=0, aliases=None):
    vmem = pl.BlockSpec(memory_space=pltpu.VMEM)
    scalar = pl.BlockSpec(memory_space=pltpu.SMEM)
    anywhere = pl.BlockSpec(memory_space=pl.ANY)
    if isinstance(kept, int):
        specs = [anywhere] * kept + [vmem] * (count - smem - kept)
    else:
        specs = [anywhere if k else vmem for k in kept[smem:]] + [vmem] * (count - len(kept))
    return pl.pallas_call(
        body,
        out_shape=outs,
        in_specs=[scalar] * smem + specs,
        out_specs=[anywhere] * outs_kept + [vmem] * (len(outs) - outs_kept),
        scratch_shapes=scratch,
        input_output_aliases=aliases or {},
        compiler_params=pltpu.CompilerParams(vmem_limit_bytes=60 * 1024 * 1024),
        cost_estimate=pl.CostEstimate(flops=10**6, bytes_accessed=micros * 3_000_000, transcendentals=0),
    )


def pack_kernel(valid_ref, mats_ref, flat_ref, out_ref, low_ref, high_ref):
    share = mats_ref.shape[1]
    blocks = C4 // LANES
    for mat in range(2):
        for part in range(blocks):
            at = (mat * blocks + part) * share
            out_ref[pl.ds(at, share), :] = mats_ref[mat, :, pl.ds(part * LANES, LANES)].astype(bf16)
    half, count = low_ref.shape[0], flat_ref.shape[0]
    low_ref[...] = flat_ref[pl.ds(0, half), :].astype(bf16)
    high_ref[pl.ds(0, count - half), :] = flat_ref[pl.ds(half, count - half), :].astype(bf16)
    left = 2 * half - count
    counted = (valid_ref[0] + valid_ref[1]).astype(f32)
    high_ref[pl.ds(count - half, left), :] = jnp.full((left, LANES), counted, f32).astype(bf16)


def run_pack(valid, mats, flat):
    half = (flat.shape[0] // 32 + 1) * 16
    outs = [shape(2 * C4 // LANES * mats.shape[1], LANES, dtype=bf16)] + [shape(half, LANES, dtype=bf16)] * 2
    return kernel_call(pack_kernel, outs, [], 1, 0, 3, 2)(valid, mats, flat)


def late_kernel(group_ref, unused_ref, out_ref):
    out_ref[0] = group_ref[0]


def run_late(group, tie):
    return pl.pallas_call(
        late_kernel,
        out_shape=shape(1, dtype=jnp.int32),
        in_specs=[pl.BlockSpec(memory_space=pltpu.SMEM), pl.BlockSpec(memory_space=pl.ANY)],
        out_specs=pl.BlockSpec(memory_space=pltpu.SMEM),
    )(group, tie)[0]


def run_conv(whole, flat, gathered, tie, moved, marks, flat_share, devices_count):
    half = C4 // 2
    moved_outs = [
        shape(16 * BOTH, 5 * LANES, dtype=bf16),
        shape(4 * BOTH, TAPS * LANES, dtype=bf16),
        shape(BOTH, K3P, dtype=bf16),
        shape(BOTH, K3P, dtype=bf16),
        shape(C2, 5 * LANES, dtype=bf16),
        shape(C3P, TAPS * LANES, dtype=bf16),
        shape(half, K3P, dtype=bf16),
        shape(half, K3P, dtype=bf16),
    ]
    outs = moved_outs + [
        shape(BOTH, C4),
        shape(REST["head"], LANES),
        shape(C4 // GROUP, (SPAN + 1) * LANES, dtype=bf16),
        shape(8, LANES),
        shape(8, LANES),
    ]
    scratch = [pltpu.VMEM(a.shape, a.dtype) for a in moved + moved_outs]
    scratch += [
        pltpu.VMEM((64 * BOTH, LANES), f32),
        pltpu.VMEM((16 * BOTH, LANES), f32),
        pltpu.VMEM((4 * BOTH, C3P), f32),
        pltpu.VMEM((4 * BOTH, TAPS * LANES), bf16),
        pltpu.VMEM((3 * BOTH, TAPS * LANES), bf16),
        pltpu.VMEM((C1, 2 * LANES), f32),
        pltpu.VMEM((5, C2, LANES), f32),
        pltpu.SemaphoreType.DMA((16,)),
    ]
    if flat_share % LANES:
        args = [whole, flat, tie] + moved + [marks]
        kept = [False, False] + [True] * 5
    else:
        arrays = [array for side in gathered for array, *unused in side]
        args = [whole] + arrays + [tie] + moved + [marks]
        kept = [False] + [True] * (len(arrays) + 5)
        scratch += [
            pltpu.VMEM((devices_count, 2 * arrays[0].shape[-2], LANES), bf16),
            pltpu.VMEM((devices_count * flat_share // LANES, LANES), f32),
        ]
    body = functools.partial(conv_kernel, flat_share, gathered)
    return kernel_call(body, outs, scratch, 1, kept, len(args), 12, 8)(*args)


def run_block(whole, real, got, made, marks, near, share):
    outs = [shape(FACTOR_ROWS, LANES, dtype=bf16)] * 2 + [
        shape(BOTH, C4),
        shape(8, C4),
        shape(8, HID),
        shape(8, C4),
        shape(8, C4),
        shape(8, CLSP),
    ]
    scratch = [
        pltpu.VMEM((2, FACTOR_ROWS, LANES), bf16),
        pltpu.VMEM((BOTH, HID), f32),
        pltpu.VMEM((C4 // GROUP, (SPAN + 1) * LANES), f32),
        pltpu.VMEM((MICRO * GROUP, C4 // GROUP), f32),
        pltpu.VMEM((2, HID // share, C4 // LANES * share, LANES), bf16),
        pltpu.SemaphoreType.DMA((2,)),
    ]
    args = [whole, real, got] + list(made) + [marks, near]
    body = functools.partial(block_kernel, share)
    return kernel_call(body, outs, scratch, 2, 1, len(args), 12, 2)(*args)


def run_backward(args, chips, each):
    scratch = [
        pltpu.VMEM((2 * chips * each, LANES), f32),
        pltpu.VMEM((4 * BOTH, C3P), f32),
        pltpu.VMEM((16 * BOTH, LANES), f32),
        pltpu.VMEM((64 * BOTH, LANES), f32),
        pltpu.VMEM((4 * BOTH, TAPS * LANES), f32),
        pltpu.VMEM((5, C2, LANES), f32),
        pltpu.VMEM((REST["end"] + 16, LANES), f32),
    ]
    moved = args[4:7] + args[9:15]
    scratch += [pltpu.VMEM(x.shape, x.dtype) for x in moved] + [pltpu.SemaphoreType.DMA((2 + len(moved),))]
    kept = [False] + [True] * 2 + [False] + [True] * 3 + [False] * 2 + [True] * 6
    cut = -(-each // 16) * 8
    outs = [shape(chips, cut, LANES), shape(chips, each - cut, LANES)] * 2

    def body(*refs):
        backward_kernel(*refs[1 : len(args)], refs[0], *refs[len(args) :])

    return kernel_call(body, outs, scratch, 1, kept, len(args), 20, 4)(*args)


def run_product(whole, through, keep, got, far_a, far_b, squares, share):
    outs = [shape(*x.shape) for x in through] + [shape(squares, share, C4)] * 4 + [shape(8, LANES)]
    count = len(through)

    def body(*refs):
        product_kernel(refs[0], *refs[1 + count : 5 + count], *refs[5 + 2 * count :])

    return kernel_call(body, outs, [], 1, count, 5 + count, 3, count, {1 + k: k for k in range(count)})(
        whole, *through, keep, got, far_a, far_b
    )


def sum_kernel(whole_ref, keep_one_ref, got_one_ref, keep_two_ref, got_two_ref, *out_refs):
    square = whole_ref[5] // 8
    share = keep_one_ref.shape[1]
    for j, out_ref in enumerate(out_refs):
        entry = square ^ j
        out_ref[pl.ds(0, share), :] = keep_one_ref[entry] + got_one_ref[entry]
        out_ref[pl.ds(share, share), :] = keep_two_ref[entry] + got_two_ref[entry]


def run_sum(whole, tie, keep_one, got_one, keep_two, got_two):
    squares, share, unused_channels = keep_one.shape
    outs = [shape(2 * share, C4)] * squares

    def body(*refs):
        sum_kernel(refs[0], *refs[2:])

    return kernel_call(body, outs, [], 1, 1, 6, 2)(whole, tie, keep_one, got_one, keep_two, got_two)


def halve_kernel(whole_ref, tie_ref, keep_a, got_a, keep_b, got_b, sent_a, left_a, sent_b, left_b):
    me = whole_ref[5]
    high, low = (me // 4) % 2, (me // 2) % 2
    for place in range(2):
        first, second = (keep_a[0, k, place] + got_a[0, k, place] for k in range(2))
        sent_a[place, 0] = jnp.where(high == 0, second, first)
        left_a[place, 0] = jnp.where(high == 0, first, second)
        first, second = (keep_b[0, place, k] + got_b[0, place, k] for k in range(2))
        sent_b[place, 0] = jnp.where(low == 0, second, first)
        left_b[place, 0] = jnp.where(low == 0, first, second)


def run_halve(whole, tie, keep_a, got_a, keep_b, got_b):
    squares = keep_a.shape[0] // 4
    inputs = [x.reshape(squares, 2, 2, *x.shape[1:]) for x in (keep_a, got_a, keep_b, got_b)]
    rows = [x.shape[3] for x in inputs]
    outs = [shape(2, squares, rows[0], LANES)] * 2 + [shape(2, squares, rows[2], LANES)] * 2
    return pl.pallas_call(
        halve_kernel,
        grid=(squares,),
        out_shape=outs,
        in_specs=[pl.BlockSpec(memory_space=pltpu.SMEM), pl.BlockSpec(memory_space=pl.ANY)]
        + [pl.BlockSpec((1, 2, 2, r, LANES), lambda i: (i, 0, 0, 0, 0)) for r in rows],
        out_specs=[pl.BlockSpec((2, 1, x.shape[2], LANES), lambda i: (0, i, 0, 0)) for x in outs],
        compiler_params=pltpu.CompilerParams(vmem_limit_bytes=60 * 1024 * 1024),
        cost_estimate=pl.CostEstimate(flops=10**6, bytes_accessed=15_000_000, transcendentals=0),
    )(whole, tie, *inputs)


def run_gram(scale, terms, momentum, loss):
    rows, count = momentum.shape[0], len(terms)
    outs = [shape(rows, C4), shape(rows, C4), shape(len(PAIRS) * LANES, LANES)]

    def body(*refs):
        gram_kernel(refs[0], refs[1 : 1 + count], *refs[1 + count :])

    return kernel_call(body, outs, [], 1, 0, 3 + count, 4)(scale, *terms, momentum, loss)


def run_newton_first(packed, ortho, steps):
    outs = [shape(*ortho.shape), shape(C4, C4), shape(8, LANES)]
    return kernel_call(functools.partial(newton_first_kernel, steps), outs, [], 0, 0, 2, 12)(packed, ortho)


def run_newton_last(ties, gram, ortho, steps):
    outs = [shape(*ortho.shape)]
    count = len(ties)

    def body(*refs):
        newton_last_kernel(steps, *refs[count:])

    return kernel_call(body, outs, [], 0, count, 2 + count, 8)(*ties, gram, ortho)[0]


def patches(images, resolution, partner_col, mix_col):
    pictures = images[:, 0].astype(f32)
    dims = (1, 1, RES_L, RES_L)
    inside = (lax.broadcasted_iota(jnp.int32, dims, 2) < resolution) & (
        lax.broadcasted_iota(jnp.int32, dims, 3) < resolution
    )
    mixing = mix_col[:, None, None, None]
    other = jnp.where(partner_col[:, None, None, None] == 0, pictures[0][None], pictures[1][None])
    pixels = jnp.where(inside, mixing * pictures + (1.0 - mixing) * other, 0.0).astype(bf16)
    padded = jnp.pad(pixels, ((0, 0), (0, 0), (2, 1), (2, 1)))
    size = RES_STEP + 3
    blocks = [
        padded[:, :, RES_STEP * i : RES_STEP * i + size, RES_STEP * j : RES_STEP * j + size]
        for i in range(SIDE)
        for j in range(SIDE)
    ]
    blocks = jnp.stack(blocks, axis=1).reshape(MICRO * SIDE * SIDE, IN_CH, size, size)
    depth = IN_CH * 49
    choose = jnp.eye(depth, dtype=bf16).reshape(IN_CH, 7, 7, depth).transpose(1, 2, 0, 3)
    columns = lax.conv_general_dilated(
        blocks,
        choose,
        (4, 4),
        ((0, 0), (0, 0)),
        dimension_numbers=("NCHW", "HWIO", "HWNC"),
        preferred_element_type=f32,
    ).astype(bf16)
    columns = columns.reshape(64, MICRO, SIDE * SIDE, depth)
    columns = jnp.pad(columns, ((0, 0), (0, 0), (0, ROWS - SIDE * SIDE), (0, 2 * LANES - depth)))
    return columns.reshape(64 * BOTH, 2 * LANES)


def tap_orders(zero):
    row = lax.broadcasted_iota(jnp.int32, (TAPS * LANES, TAPS * LANES), 0) + zero
    col = lax.broadcasted_iota(jnp.int32, (TAPS * LANES, TAPS * LANES), 1)
    forth = ((row % LANES) * TAPS + row // LANES == col).astype(bf16)
    dims = (5 * LANES + C1, 5 * LANES)
    row = lax.broadcasted_iota(jnp.int32, dims, 0) - C1 + zero
    col = lax.broadcasted_iota(jnp.int32, dims, 1)
    real = (row >= 0) & (row < TAPS * C1)
    row = jnp.maximum(row, 0)
    back = (real & ((row % TAPS) * C1 + row // TAPS == col)).astype(bf16)
    row = lax.broadcasted_iota(jnp.int32, (C4, C4), 0) + zero
    col = lax.broadcasted_iota(jnp.int32, (C4, C4), 1)
    merge = ((row % (C4 // 2)) * 2 + row // (C4 // 2) == col).astype(bf16)
    return forth, back, merge


def grid_marks(side):
    row = np.arange(BOTH)
    image, q = row // ROWS, row % ROWS
    y, x = q // SIDE, q % SIDE
    real = q < SIDE * SIDE
    fixed = np.stack([real & (y > 0), real & (x > 0), real & (y > 0) & (x > 0)], 1).astype(np.float32)
    close = (
        (image[:, None] == image[None])
        & (abs(y[:, None] - y[None]) <= 1)
        & (abs(x[:, None] - x[None]) <= 1)
        & real[:, None]
        & real[None]
    )
    inside = jnp.asarray(real) & (jnp.asarray(y) < side) & (jnp.asarray(x) < side)
    near = jnp.where(jnp.asarray(close) & inside[:, None] & inside[None], 1.0, 0.0)
    cells = jnp.maximum(jnp.sum(near, axis=1), 1.0)
    marks = jnp.concatenate(
        [inside.astype(f32)[:, None], jnp.asarray(fixed), (1.0 / cells)[:, None]], axis=1
    )
    return jnp.pad(marks, ((0, 0), (0, LANES - marks.shape[1]))), near.astype(bf16)


def local_inputs(images, group, label_col, partner_col, mix_col, valid_col, me):
    side = RES_S // RES_STEP + group
    columns = patches(images, side * RES_STEP, partner_col, mix_col)
    orders = tap_orders(jnp.minimum(group, 0))
    marks, near = grid_marks(side)
    other = jnp.where(partner_col == 0, label_col[0], label_col[1])
    whole = jnp.concatenate([label_col, other, jnp.stack([me % 2, me]).astype(jnp.int32)])
    cells = (side * side).astype(f32)
    real = jnp.concatenate([mix_col, valid_col.astype(f32), jnp.stack([cells, cells * C4])])
    return whole, real, columns, orders, marks, near


def second_half(prepared, convs, made, chips, each, ties):
    columns, (forth, back, merge), marks = prepared[2], prepared[3], prepared[4]
    p1, p2, p3e, p3o, k1t, k2, k3e, k3o = convs[:8]
    args = [made[2], columns, p1, p2, p3e, p3o, k1t, k2, k3e, k3o, forth, back, merge, marks]
    return run_backward([prepared[0]] + list(ties) + args + list(made[3:8]), chips, each)


class Ring:
    def __init__(self, count):
        self.count = count
        self.squares = count // 8
        me = lax.axis_index(AXES)
        self.me = me
        self.core = me % 2
        self.low = (me // 2) % 2
        self.high = (me // 4) % 2
        self.corner = (me // 2) % 4
        self.square = me // 8

    def swap(self, value, bits):
        return lax.ppermute(value, AXES, [(i, i ^ bits) for i in range(self.count)])


def pick(value, at, axis):
    return lax.dynamic_index_in_dim(value, at, axis, keepdims=False)


class Scatter:
    def __init__(self, ring, terms, mine, bits):
        self.ring = ring
        self.terms = terms
        self.mine = mine
        self.bits = bits

    def exchange(self):
        sent = functools.reduce(jnp.add, [pick(x, 1 - self.mine, 0) for x in self.terms])
        self.terms = [pick(x, self.mine, 0) for x in self.terms] + [self.ring.swap(sent, self.bits)]

    def add(self):
        self.terms = [functools.reduce(jnp.add, self.terms)]


def sum_squares(ring, value, far_first):
    bits = ring.squares.bit_length() - 1
    order = list(range(bits))
    if far_first:
        order.reverse()
    held = order.copy()
    value = value.reshape((2,) * bits + value.shape[1:])
    got = None
    for bit in order:
        axis = len(held) - 1 - sorted(held).index(bit)
        held.remove(bit)
        mine = (ring.square >> bit) & 1
        if got is not None:
            value = value + got
        got = ring.swap(pick(value, 1 - mine, axis), 8 << bit)
        value = pick(value, mine, axis)
    return value, got


class Gather:
    def __init__(self, ring, value, far_first, high_first):
        self.ring = ring
        self.value = value
        self.masks = []
        bits = list(range(ring.squares.bit_length() - 1))
        self.squares = [8 << bit for bit in (reversed(bits) if far_first else bits)]
        self.corners = (4, 2) if high_first else (2, 4)
        self.pieces = []

    def exchange(self, mask):
        self.value = jnp.stack([self.value, self.ring.swap(self.value, mask)])
        self.masks = [mask] + self.masks

    def between_squares(self):
        for mask in self.squares:
            self.exchange(mask)

    def first_corner(self):
        self.exchange(self.corners[0])

    def second_corner(self):
        got = self.ring.swap(self.value, self.corners[1])
        self.pieces = [(self.value, self.masks, 0), (got, self.masks, self.corners[1])]

    def between_cores(self):
        self.pieces += [(self.ring.swap(array, 1), masks, base | 1) for array, masks, base in self.pieces]


def together(scatters, *others):
    counts = [len(x.terms) for x in scatters]
    values = lax.optimization_barrier(tuple(t for x in scatters for t in x.terms) + tuple(others))
    at = 0
    for x, count in zip(scatters, counts):
        x.terms = list(values[at : at + count])
        at += count
    return values[at:]


class ChipSum:
    def __init__(self, ring, value):
        self.ring = ring
        self.shape = value.shape
        self.terms = [value.reshape(4, value.shape[0] // 4, value.shape[1])]

    def scatter_corners(self):
        ring = self.ring
        got = [ring.swap(pick(self.terms[0], ring.corner ^ j, 0), 2 * j) for j in range(1, 4)]
        self.terms = [functools.reduce(jnp.add, got, pick(self.terms[0], ring.corner, 0))]

    def sum_squares(self):
        ring = self.ring
        got = [ring.swap(self.terms[0], 8 * j) for j in range(1, ring.squares)]
        self.terms = [functools.reduce(jnp.add, got, self.terms[0])]


    def gather_corners(self):
        ring = self.ring
        held = jnp.stack([self.terms[0]] + [ring.swap(self.terms[0], 2 * j) for j in range(1, 4)])
        return jnp.stack([pick(held, ring.corner ^ j, 0) for j in range(4)]).reshape(self.shape)


def per_device(
    devices_count,
    images,
    group_ids,
    labels,
    partners,
    mix_weights,
    valid,
    flat_params,
    flat_first,
    flat_second,
    mlp_weights,
    mlp_momentum,
):
    ring = Ring(devices_count)
    chips = devices_count // 2
    share = mlp_weights.shape[2]
    flat_share = flat_params.shape[0]
    flat_rows = -(-flat_share // LANES)
    spare = flat_rows * LANES - flat_share
    mine = jnp.pad(flat_params, (0, spare)) if spare else flat_params
    sent, flat_low, flat_high = run_pack(
        valid.reshape(MICRO), mlp_weights.transpose(0, 2, 1), mine.reshape(flat_rows, LANES)
    )
    got = lax.all_gather(sent, AXES, axis=0, tiled=False)
    aligned = flat_share % LANES == 0
    pieces = [Gather(ring, flat_low, False, True), Gather(ring, flat_high, True, False)]
    group = group_ids
    if aligned:
        for x in pieces:
            x.between_squares()
        for x in pieces:
            x.first_corner()
        group = run_late(group, pieces[1].value)
    else:
        group = group[0]
    prepared = local_inputs(
        images, group, labels[:, 0], partners[:, 0], mix_weights[:, 0], valid[:, 0], ring.me
    )
    whole, real, columns, orders, marks, near = prepared
    momentum = mlp_momentum.transpose(0, 2, 1)

    def of_both_cores(mine, theirs):
        at_first = ring.core == 0
        return jnp.concatenate([jnp.where(at_first, mine, theirs), jnp.where(at_first, theirs, mine)])

    momentum_rows = of_both_cores(
        pick(momentum, ring.core, 0), ring.swap(pick(momentum, 1 - ring.core, 0), 1)
    )
    moved = [columns, *orders]
    if aligned:
        for x in pieces:
            x.second_corner()
        for x in pieces:
            x.between_cores()
        convs = run_conv(
            whole, None, [x.pieces for x in pieces], momentum_rows, moved, marks, flat_share, devices_count
        )
        counted = convs[12][0, 0]
    else:
        rows = lax.all_gather(jnp.concatenate([flat_low, flat_high]), AXES, axis=0, tiled=False)
        whole_flat = (
            rows[:, :flat_rows]
            .astype(f32)
            .reshape(devices_count, flat_rows * LANES)[:, :flat_share]
            .reshape(devices_count * flat_share // LANES, LANES)
        )
        convs = run_conv(whole, whole_flat, None, momentum_rows, moved, marks, flat_share, devices_count)
        counted = jnp.sum(rows[:, flat_rows, 0].astype(f32))
    scale = 1.0 / jnp.maximum(counted, 1.0)
    made = run_block(whole, real, got, convs[8:12], marks, near, share)
    keep, send = made[:2]
    got_factors = ring.swap(send, 1)
    ahead = [
        jnp.stack([x[begin : begin + QUARTER + C4] for x in (keep, got_factors)]) for begin in (0, FACTOR_CHANNELS)
    ]
    far_a, far_b = ring.swap(ahead[0], 4), ring.swap(ahead[1], 2)

    each = -(-(devices_count * flat_share) // (devices_count * LANES * 8)) * 8
    ties = ahead
    keep_a, keep_b, send_a, send_b = second_half(prepared, convs, made, chips, each, ties)
    send_a, send_b, keep_one, send_one, keep_two, send_two, loss = run_product(
        whole, [send_a, send_b], keep, got_factors, far_a, far_b, ring.squares, share
    )
    got_one, got_two = ring.swap(send_one, 2), ring.swap(send_two, 4)
    got_a, got_b = ring.swap(send_a, 1), ring.swap(send_b, 1)
    sent_a, left_a, sent_b, left_b = run_halve(whole, keep_one, keep_a, got_a, keep_b, got_b)
    entries = run_sum(whole, sent_a, keep_one, got_one, keep_two, got_two)
    terms = [entries[0]] + [ring.swap(entries[j], 8 * j) for j in range(1, ring.squares)]
    flat = [
        Scatter(ring, [left_a, ring.swap(sent_a, 4)], ring.low, 2),
        Scatter(ring, [left_b, ring.swap(sent_b, 2)], ring.high, 4),
    ]
    ortho, momentum_new, packed = run_gram(scale[None], terms, momentum_rows, loss)
    grams = ChipSum(ring, packed)
    grams.scatter_corners()
    grams.sum_squares()
    for x in flat:
        x.exchange()
        x.add()
    together([grams] + flat)
    flat_sums = [sum_squares(ring, x.terms[0], far) for x, far in zip(flat, (False, True))]
    sum_flat = jnp.concatenate([sum(x) for x in flat_sums])
    steps = 3
    ortho, gram, loss_total = run_newton_first(grams.gather_corners(), ortho, steps)
    lag = (devices_count - 1) * (each * LANES - flat_share)
    hops = -(-lag // (each * LANES))
    tail = min(each, -(-lag // (8 * LANES)) * 8)
    before = [
        lax.ppermute(sum_flat[each - tail :], AXES, [(i, i + h) for i in range(devices_count - h)])
        for h in range(hops, 0, -1)
    ]
    ortho = run_newton_last([x[0] for x in flat_sums], gram, ortho, steps)
    sum_flat = jnp.concatenate(before + [sum_flat])
    start = len(before) * tail * LANES - ring.me * (each * LANES - flat_share)
    if flat_share % LANES == 0:
        sum_flat = lax.dynamic_slice_in_dim(sum_flat, start // LANES, flat_rows, 0).reshape(-1)
    else:
        sum_flat = lax.dynamic_slice_in_dim(sum_flat.reshape(-1), start, flat_share, 0)
    sum_flat = sum_flat * scale
    first_new = 0.9 * flat_first + 0.1 * sum_flat
    second_new = 0.999 * flat_second + 0.001 * sum_flat * sum_flat
    first_hat = first_new / (1.0 - 0.9**STEP)
    second_hat = second_new / (1.0 - 0.999**STEP)
    params_new = flat_params - 0.02 * (
        first_hat / (jnp.sqrt(second_hat) + 1e-08) + 0.05 * flat_params
    )

    def to_owners(by_chip):
        parts = by_chip.reshape(2, share, C4)
        mine, theirs = pick(parts, ring.core, 0), ring.swap(pick(parts, 1 - ring.core, 0), 1)
        at_first = ring.core == 0
        return jnp.stack([jnp.where(at_first, mine, theirs), jnp.where(at_first, theirs, mine)])

    mats = mlp_weights.transpose(0, 2, 1)
    weights_new = mats * (1.0 - 0.1 * 0.05) - 0.1 * 0.2 * math.sqrt(HID) * to_owners(ortho)
    return (
        loss_total[0, 0],
        params_new,
        first_new,
        second_new,
        weights_new.transpose(0, 2, 1),
        to_owners(momentum_new).transpose(0, 2, 1),
    )


def solution(mesh):
    placed = (
        P(None, AXES, None, None, None),
        P(AXES),
        P(None, AXES),
        P(None, AXES),
        P(None, AXES),
        P(None, AXES),
        P(AXES),
        P(AXES),
        P(AXES),
        P(None, None, AXES),
        P(None, None, AXES),
    )
    devices_count = math.prod(mesh.shape[axis] for axis in AXES)
    return jax.shard_map(
        functools.partial(per_device, devices_count),
        mesh=mesh,
        in_specs=placed,
        out_specs=(
            P(),
            P(AXES),
            P(AXES),
            P(AXES),
            P(None, None, AXES),
            P(None, None, AXES),
        ),
        check_vma=False,
    )
```

```python
import functools
import math

import jax
import jax.numpy as jnp
import numpy as np
from jax import lax
from jax.experimental import pallas as pl
from jax.experimental.pallas import tpu as pltpu
from jax.sharding import PartitionSpec as P

C1 = 64
C2 = 128
C3 = 320
C4 = 512
HID = 2048
CLS = 1000
IN_CH = 3
RES_S = 96
RES_L = 160
RES_STEP = 32
MICRO = 2
NS_ITERS = 5
STEP = 10

AXES = ("fsdp", "ns")
LANES = 128
SIDE = 5
ROWS = 32
BOTH = MICRO * ROWS
C3P = 384
CLSP = 1024
K3P = 2944
TAPS = 9

f32 = jnp.float32
bf16 = jnp.bfloat16
norm_epsilon = 1e-05

NARROW = C1 * IN_CH * 49
ROW_B0 = NARROW // LANES
ROW_K1 = 74
ROW_B1 = 650
ROW_K2 = 651
ROW_B2 = 3531
ROW_K3 = 3533
ROW_B3 = 15053
REST = {"b3": 0, "block": 4, "fb1": 28, "fb2": 44, "final": 48, "head": 56, "hb": 4056, "end": 4064}
QUARTER = HID // 4
FACTOR_OTHER = (0, QUARTER + C4)
FACTOR_CHANNELS = QUARTER
FACTOR_OWN = (2 * QUARTER + C4, 3 * QUARTER + C4)
FACTOR_LOSS = HID + C4
FACTOR_ROWS = FACTOR_LOSS + 16
GROUP = 16
SPAN = GROUP * CLS // LANES
PAIRS = [(i, j) for i in range(4) for j in range(i, 4)]


def dot_nn(a, b):
    return lax.dot_general(a, b, (((1,), (0,)), ((), ())), preferred_element_type=f32)


def dot_nt(a, b):
    return lax.dot_general(a, b, (((1,), (1,)), ((), ())), preferred_element_type=f32)


def dot_tn(a, b):
    return lax.dot_general(a, b, (((0,), (0,)), ((), ())), preferred_element_type=f32)


def split2(x):
    hi = x.astype(bf16)
    return hi, (x - hi.astype(f32)).astype(bf16)


def split3(x):
    hi = x.astype(bf16)
    rest = x - hi.astype(f32)
    mid = rest.astype(bf16)
    return hi, mid, (rest - mid.astype(f32)).astype(bf16)


def stacked(dot, parts, other):
    rows = parts[0].shape[0]
    product = dot(jnp.concatenate(parts, axis=0), other)
    return functools.reduce(jnp.add, [product[k * rows : (k + 1) * rows] for k in range(len(parts))])


def two(dot, pair, other):
    return stacked(dot, pair, other)


def borrow(bits):
    out = list(bits)
    for at, bit in enumerate(out):
        if bit:
            out[at] = 0
            return tuple(out), 0
        out[at] = 1
    return tuple(out), 1


def tap_source(tap, row_bits, col_bits):
    r, c = divmod(tap, 3)
    src_r, down_r = (row_bits, 0) if r else borrow(row_bits)
    src_c, down_c = (col_bits, 0) if c else borrow(col_bits)
    return (int(r != 1), int(c != 1)), src_r, src_c, down_r, down_c


def plane_of(row_bits, col_bits):
    at = 0
    for r, c in zip(row_bits, col_bits):
        at = at * 4 + r * 2 + c
    return at


def stem_plane(quarter, row_bits, col_bits):
    row = quarter[0] + 2 * row_bits[0] + 4 * row_bits[1]
    return row * 8 + quarter[1] + 2 * col_bits[0] + 4 * col_bits[1]


def all_bits(pairs):
    for at in range(4**pairs):
        digits = [(at >> (2 * (pairs - 1 - k))) & 3 for k in range(pairs)]
        yield at, tuple(d >> 1 for d in digits), tuple(d & 1 for d in digits)


def moved(value, down_r, down_c, marks):
    if not (down_r or down_c):
        return value
    step = SIDE * down_r + down_c
    column = {(1, 0): 1, (0, 1): 2, (1, 1): 3}[(down_r, down_c)]
    return pltpu.roll(value, step, 0) * marks[:, column : column + 1]


def moved_back(value, down_r, down_c, marks):
    if not (down_r or down_c):
        return value
    step = SIDE * down_r + down_c
    column = {(1, 0): 1, (0, 1): 2, (1, 1): 3}[(down_r, down_c)]
    return pltpu.roll(value * marks[:, column : column + 1], BOTH - step, 0)


def erf(x):
    x = jnp.clip(x, -3.832506856900711, 3.832506856900711)
    s = x * x
    top = 2.2905065861350646e-4
    for coef in (3.4082910107109506e-3, 5.0955695062380861e-2, 1.8520832239976145e-1, 1.128379143519084):
        top = top * s + coef
    low = -1.1791602954361697e-7
    for coef in (
        2.3547966471313185e-5,
        1.0179625278914885e-3,
        1.4070470171167667e-2,
        1.1098505178285362e-1,
        4.9746925110067538e-1,
        1.0,
    ):
        low = low * s + coef
    return x * top / low


def total(x):
    return jnp.sum(jnp.sum(x, axis=1, keepdims=True), axis=0, keepdims=True)


def norm_images(value, mask, count):
    parts, scales = [], []
    for m in range(MICRO):
        v = value[m * ROWS : (m + 1) * ROWS]
        k = mask[m * ROWS : (m + 1) * ROWS]
        center = (v - total(v * k) / count) * k
        scale = lax.rsqrt(total(center * center) / count + norm_epsilon)
        parts.append(center * scale)
        scales.append(scale)
    return jnp.concatenate(parts, axis=0), scales


def norm_images_back(grad, hat, scales, gain, mask, count):
    parts = []
    for m in range(MICRO):
        at = slice(m * ROWS, (m + 1) * ROWS)
        g = grad[at] * gain
        h = hat[at]
        parts.append((g - total(g) / count - h * (total(g * h) / count)) * scales[m] * mask[at])
    return jnp.concatenate(parts, axis=0)


def rowsum(x):
    return jnp.sum(x, axis=0, keepdims=True)


def halves(low, high):
    lane = lax.broadcasted_iota(jnp.int32, low.shape, 1)
    return jnp.where(lane < LANES // 2, pltpu.roll(low, LANES // 2, 1), pltpu.roll(high, LANES // 2, 1))


def lanes_of(ref, row, count):
    return jnp.concatenate([ref[row + at : row + at + 1, :] for at in range(count)], axis=1)


def head_masks():
    row = lax.broadcasted_iota(jnp.int32, (C4 // GROUP, C4), 0)
    col = lax.broadcasted_iota(jnp.int32, (C4 // GROUP, C4), 1)
    return col // GROUP == row, col % GROUP == row // MICRO, row % MICRO == 0


class Copies:
    def __init__(self, sems):
        self.sems = sems
        self.count = 2

    def start_shared(self, source, target):
        pltpu.make_async_copy(source, target, self.sems.at[0]).start()

    def start_out(self, source, target):
        pltpu.make_async_copy(source, target, self.sems.at[1]).start()

    def out(self, source):
        return pltpu.make_async_copy(source, source, self.sems.at[1])

    def shared(self, target):
        return pltpu.make_async_copy(target, target, self.sems.at[0])

    def start(self, source, target):
        copy = self.make(source, target)
        copy.start()
        return copy

    def make(self, source, target):
        copy = pltpu.make_async_copy(source, target, self.sems.at[self.count])
        self.count += 1
        return copy


def pieces_of(gathered):
    for number, (unused_array, masks, base) in enumerate(gathered):
        for place in range(2 ** len(masks)):
            index, owner = [], base
            for k, mask in enumerate(masks):
                bit = (place >> k) & 1
                index.append(bit)
                owner ^= mask * bit
            yield number, tuple(index), owner


def conv_kernel(flat_share, gathered, *refs):
    if flat_share % LANES:
        conv_body(None, None, *refs)
    else:
        count = [len(side) for side in gathered]
        held = [refs[1 : 1 + count[0]], refs[1 + count[0] : 1 + sum(count)]]
        conv_body(flat_share, (gathered, held), refs[0], refs[-1], *refs[1 + sum(count) : -1])


def conv_body(
    flat_share,
    arrived,
    whole_ref,
    flat_ref,
    unused_hbm,
    p0_hbm,
    tm_hbm,
    t64_hbm,
    pm_hbm,
    marks_ref,
    p1_hbm,
    p2_hbm,
    p3e_hbm,
    p3o_hbm,
    k1t_hbm,
    k2_hbm,
    k3e_hbm,
    k3o_hbm,
    stream_ref,
    rest_ref,
    wide_ref,
    hb_ref,
    count_ref,
    p0_ref,
    tm_ref,
    t64_ref,
    pm_ref,
    p1_ref,
    p2_ref,
    p3e_ref,
    p3o_ref,
    k1t_ref,
    k2_ref,
    k3e_ref,
    k3o_ref,
    s1_ref,
    s2_ref,
    s3_ref,
    t2_ref,
    t3_ref,
    w0_ref,
    k1f_ref,
    sems,
    *near_refs,
):
    copies = Copies(sems)
    if arrived is not None:
        near_ref = near_refs[0]
        gathered, held = arrived
        half_rows = near_ref.shape[1] // 2
        me = whole_ref[5]
        for side in range(2):
            for number, index, owner in pieces_of(gathered[side]):
                copies.start_shared(
                    held[side][number].at[index], near_ref.at[me ^ owner, pl.ds(side * half_rows, half_rows), :]
                )
        flat_copy = copies.shared(near_ref)
    p0_copy = copies.start(p0_hbm, p0_ref)
    t64_copy = copies.start(t64_hbm, t64_ref)
    tm_copy = copies.start(tm_hbm, tm_ref)
    pm_copy = copies.start(pm_hbm, pm_ref)
    outward = []
    if arrived is not None:
        flat_copy.wait()
        flat_rows = flat_share // LANES
        counted = jnp.zeros((1, LANES), f32)
        for at in range(near_ref.shape[0]):
            flat_ref[pl.ds(at * flat_rows, flat_rows), :] = near_ref[at, pl.ds(0, flat_rows), :].astype(f32)
            counted = counted + near_ref[at, pl.ds(flat_rows, 1), :].astype(f32)
        count_ref[...] = jnp.broadcast_to(counted, (8, LANES))
    else:
        count_ref[...] = jnp.zeros((8, LANES), f32)
    marks = marks_ref[...]
    lane = lax.broadcasted_iota(jnp.int32, (BOTH, LANES), 1)
    lane1 = lax.broadcasted_iota(jnp.int32, (1, LANES), 1)
    depth = IN_CH * 49
    for at in range(C1):
        row, shift = divmod(depth * at, LANES)
        line = lanes_of(flat_ref, row, 3)
        if shift:
            line = pltpu.roll(line, 3 * LANES - shift, 1)
        w0_ref[at : at + 1, :] = line[:, : 2 * LANES]
    w0 = w0_ref[...].astype(bf16)
    w0 = jnp.concatenate([w0, w0], axis=0)
    b0 = flat_ref[ROW_B0 : ROW_B0 + 1, :]
    b0 = jnp.where(lane1 < C1, pltpu.roll(b0, C1, 1), b0)
    quarter = 16 * BOTH
    p0_copy.wait()
    for at in range(4):
        span = pl.ds(at * quarter, quarter)
        s1_ref[span, :] = (dot_nt(p0_ref[span, :], w0) + b0).astype(bf16).astype(f32)

    def tap_value(ref, pairs, tap, row_bits, col_bits, cols):
        q, src_r, src_c, down_r, down_c = tap_source(tap, row_bits, col_bits)
        if pairs == 2:
            at = stem_plane(q, src_r, src_c)
        else:
            at = (q[0] * 2 + q[1]) * 4**pairs + plane_of(src_r, src_c)
        return moved(ref[pl.ds(at * BOTH, BOTH), cols], down_r, down_c, marks)

    half = C2 // 2
    t64_copy.wait()
    for odd in range(2):
        block = jnp.concatenate(
            [flat_ref[pl.ds(ROW_K1 + 4 * odd + j, half, stride=9), :].astype(bf16) for j in range(5)], axis=1
        )
        block = dot_nn(block, t64_ref[pl.ds(C1 * (1 - odd), 5 * LANES), :])
        for j in range(5):
            k1f_ref[j, pl.ds(odd, half, stride=2), :] = block[:, j * LANES : (j + 1) * LANES]
    for j in range(5):
        k1t_ref[:, pl.ds(j * LANES, LANES)] = k1f_ref[j].astype(bf16)
    outward.append(copies.start(k1t_ref, k1t_hbm))
    everything = slice(None)
    for at, rb, cb in all_bits(2):
        for pair in range(5):
            left = tap_value(s1_ref, 2, 2 * pair, rb, cb, everything)
            if pair < 4:
                right = tap_value(s1_ref, 2, 2 * pair + 1, rb, cb, everything)
            else:
                right = jnp.zeros_like(left)
            p1_ref[pl.ds(at * BOTH, BOTH), pl.ds(pair * LANES, LANES)] = jnp.where(
                lane < C1, left, right
            ).astype(bf16)
    outward.append(copies.start(p1_ref, p1_hbm))
    b1 = flat_ref[ROW_B1 : ROW_B1 + 1, :]
    s2_ref[...] = (dot_nt(p1_ref[...], k1t_ref[...]) + b1).astype(bf16).astype(f32)
    for j in range(TAPS):
        k2_ref[pl.ds(0, C3), pl.ds(j * LANES, LANES)] = flat_ref[pl.ds(ROW_K2 + j, C3, stride=TAPS), :].astype(bf16)
    k2_ref[pl.ds(C3, C3P - C3), :] = jnp.zeros((C3P - C3, TAPS * LANES), bf16)
    outward.append(copies.start(k2_ref, k2_hbm))
    b2 = lanes_of(flat_ref, ROW_B2, 3)
    b2 = jnp.where(lax.broadcasted_iota(jnp.int32, b2.shape, 1) < C3, b2, 0.0)
    for at, rb, cb in all_bits(1):
        for tap in range(TAPS):
            t2_ref[pl.ds(at * BOTH, BOTH), pl.ds(tap * LANES, LANES)] = tap_value(
                s2_ref, 1, tap, rb, cb, everything
            ).astype(bf16)
    tm_copy.wait()
    p2_ref[...] = dot_nn(t2_ref[...], tm_ref[...]).astype(bf16)
    outward.append(copies.start(p2_ref, p2_hbm))
    s3_ref[...] = (dot_nt(p2_ref[...], k2_ref[...]) + b2).astype(bf16).astype(f32)
    for part in range(3):
        for tap in range(TAPS):
            t3_ref[pl.ds(part * BOTH, BOTH), pl.ds(tap * LANES, LANES)] = tap_value(
                s3_ref, 0, tap, (), (), pl.ds(part * LANES, LANES)
            ).astype(bf16)
    spread = dot_nn(t3_ref[...], tm_ref[...])
    spread = jnp.concatenate([spread[part * BOTH : (part + 1) * BOTH] for part in range(3)], axis=1)
    p3o_ref[...] = spread[:, :K3P].astype(bf16)
    p3e_ref[...] = pltpu.roll(spread, LANES // 2, 1)[:, :K3P].astype(bf16)
    for j in range(K3P // LANES):
        cols = pl.ds(j * LANES, LANES)
        k3e_ref[:, cols] = flat_ref[pl.ds(ROW_K3 + j, C4 // 2, stride=45), :].astype(bf16)
        k3o_ref[:, cols] = flat_ref[pl.ds(ROW_K3 + 23 + j, C4 // 2, stride=45), :].astype(bf16)
    for source, target in ((p3e_ref, p3e_hbm), (p3o_ref, p3o_hbm), (k3e_ref, k3e_hbm), (k3o_ref, k3o_hbm)):
        outward.append(copies.start(source, target))
    pm_copy.wait()
    apart = split3(
        jnp.concatenate([dot_nt(p3e_ref[...], k3e_ref[...]), dot_nt(p3o_ref[...], k3o_ref[...])], axis=1)
    )
    stream = stacked(dot_nn, apart, pm_ref[...])

    stream_ref[...] = stream

    amount = REST["head"]
    rest_ref[...] = halves(flat_ref[ROW_B3 : ROW_B3 + amount, :], flat_ref[ROW_B3 + 1 : ROW_B3 + 1 + amount, :])
    row_hb = ROW_B3 + REST["hb"]
    hb_ref[...] = halves(flat_ref[row_hb : row_hb + 8, :], flat_ref[row_hb + 1 : row_hb + 9, :])
    groups = C4 // GROUP
    row_head = ROW_B3 + REST["head"]
    low = pltpu.roll(flat_ref[pl.ds(row_head, groups, stride=SPAN), :], LANES // 2, 1)
    lane32 = lax.broadcasted_iota(jnp.int32, (groups, LANES), 1)
    for at in range(SPAN):
        high = pltpu.roll(flat_ref[pl.ds(row_head + at + 1, groups, stride=SPAN), :], LANES // 2, 1)
        wide_ref[:, pl.ds(at * LANES, LANES)] = jnp.where(lane32 < LANES // 2, low, high).astype(bf16)
        low = high
    wide_ref[:, pl.ds(SPAN * LANES, LANES)] = jnp.zeros((groups, LANES), bf16)
    for copy in outward:
        copy.wait()


def block_kernel(
    share,
    whole_ref,
    real_ref,
    got_hbm,
    stream_ref,
    rest_ref,
    wide_ref,
    hb_ref,
    marks_ref,
    near_ref,
    keep_hbm,
    send_hbm,
    dstream_ref,
    dblock_ref,
    dfb1_ref,
    small_ref,
    pooled_ref,
    dlog_ref,
    factor_ref,
    hid_ref,
    z_ref,
    per_ref,
    mats_ref,
    sems,
):
    copies = Copies(sems)
    me = whole_ref[5]
    for mat in range(2):
        rows = mats_ref.shape[2]
        copies.start_shared(got_hbm.at[:, pl.ds(mat * rows, rows), :], mats_ref.at[mat])
    mats_copy = copies.shared(mats_ref)
    marks = marks_ref[...]
    stream = stream_ref[...]
    b3 = lanes_of(rest_ref, REST["b3"], 4)
    gain1, shift1, scale1, gain2, shift2, scale2 = (lanes_of(rest_ref, REST["block"] + 4 * k, 4) for k in range(6))
    fb1 = lanes_of(rest_ref, REST["fb1"], HID // LANES)
    fb2 = lanes_of(rest_ref, REST["fb2"], 4)
    gain3, shift3 = (lanes_of(rest_ref, REST["final"] + 4 * k, 4) for k in range(2))

    stream = stream + b3
    mask = marks[:, 0:1]
    per_count = marks[:, 4:5]
    cells = real_ref[4]
    count = real_ref[5]
    near = near_ref[...]
    hat1, rs1 = norm_images(stream, mask, count)
    u = (hat1 * gain1 + shift1) * mask
    u3 = split3(u)
    around = dot_nn(near, u3[0]) + (dot_nn(near, u3[1]) + dot_nn(near, u3[2]))
    pool = around * per_count - u
    stream1 = stream + scale1 * pool
    hat2, rs2 = norm_images(stream1, mask, count)
    normed = ((hat2 * gain2 + shift2) * mask).astype(bf16)
    mats_copy.wait()
    blocks = C4 // LANES

    def matrix(mat, part):
        return mats_ref[mat, :, pl.ds(part * share, share), :].reshape(HID, LANES)

    def lanes(x, part):
        return x[:, part * LANES : (part + 1) * LANES]

    hidden = fb1
    for part in range(blocks):
        hidden = hidden + dot_nt(lanes(normed, part), matrix(0, part))
    hid_ref[...] = hidden
    active = (hidden * (0.5 * (1.0 + erf(hidden * math.sqrt(0.5))))).astype(bf16)
    branch = jnp.concatenate([dot_nn(active, matrix(1, part)) for part in range(blocks)], axis=1) + fb2
    stream2 = stream1 + scale2 * branch
    hat3, rs3 = norm_images(stream2, mask, count)
    outs = (hat3 * gain3 + shift3) * mask
    row8 = lax.broadcasted_iota(jnp.int32, (8, 1), 0)
    first, second = row8 == 0, row8 == 1

    def by_row(a, b):
        return jnp.where(first, a, jnp.where(second, b, 0.0))

    pooled = (by_row(rowsum(outs[:ROWS]), rowsum(outs[ROWS:])) / cells).astype(bf16)
    pooled_f = pooled.astype(f32)
    pooled_ref[...] = pooled_f
    in_group, in_place, own_row = head_masks()
    picked = jnp.where(in_place, jnp.where(own_row, pooled_f[0:1, :], pooled_f[1:2, :]), 0.0).astype(bf16)
    by_place = dot_nt(picked, in_group.astype(bf16)).astype(bf16)
    z_ref[...] = dot_nn(by_place, wide_ref[...])
    column = lax.broadcasted_iota(jnp.int32, (8, CLSP), 1)
    hb = lanes_of(hb_ref, 0, 8)
    logits = jnp.zeros((MICRO, CLSP), f32)
    for place in range(GROUP):
        at, shift = divmod(CLS * place, LANES)
        window = z_ref[pl.ds(MICRO * place, MICRO), pl.ds(at * LANES, CLSP + LANES)]
        if shift:
            window = pltpu.roll(window, CLSP + LANES - shift, 1)
        logits = logits + window[:, :CLSP]
    logits = by_row(logits[0:1], logits[1:2]) + hb
    logits = jnp.where(column < CLS, logits, -1e30)
    top = jnp.max(logits, axis=1, keepdims=True)
    powers = jnp.exp(logits - top)
    mass = jnp.sum(powers, axis=1, keepdims=True)
    own = jnp.where(first, whole_ref[0], whole_ref[1])
    other = jnp.where(first, whole_ref[2], whole_ref[3])
    mix = by_row(real_ref[0], real_ref[1])
    target = jnp.where(column == own, mix, 0.0) + jnp.where(column == other, 1.0 - mix, 0.0)
    valid = by_row(real_ref[2], real_ref[3])
    logp = logits - top - jnp.log(mass)
    losses = -jnp.sum(target * logp, axis=1, keepdims=True) * valid
    loss = split3(jnp.broadcast_to(jnp.sum(losses, axis=0, keepdims=True), (1, LANES)))
    dlogits = (powers / mass * jnp.sum(target, axis=1, keepdims=True) - target) * valid
    dlog_ref[...] = dlogits
    padded = jnp.concatenate([dlogits, jnp.zeros((8, LANES), f32)], axis=1)
    for place in range(GROUP):
        at, shift = divmod(CLS * place, LANES)
        window = pltpu.roll(padded, shift, 1) if shift else padded
        per_group = two(dot_nt, split2(window), wide_ref[:, pl.ds(at * LANES, CLSP + LANES)])
        per_ref[pl.ds(MICRO * place, MICRO), :] = per_group[:MICRO]
    per3 = split3(per_ref[...])
    ones = in_group.astype(bf16)
    by_channel = dot_nn(per3[0], ones) + (dot_nn(per3[1], ones) + dot_nn(per3[2], ones))
    dpooled = by_row(
        rowsum(jnp.where(in_place & own_row, by_channel, 0.0)),
        rowsum(jnp.where(in_place & ~own_row, by_channel, 0.0)),
    )
    dpooled = dpooled / cells
    douts = jnp.concatenate(
        [
            jnp.broadcast_to(dpooled[0:1], (ROWS, C4)),
            jnp.broadcast_to(dpooled[1:2], (ROWS, C4)),
        ],
        axis=0,
    ) * mask
    row8w = lax.broadcasted_iota(jnp.int32, (8, C4), 0)

    def stack8(values):
        out = jnp.zeros((8, C4), f32)
        for at, v in enumerate(values):
            out = jnp.where(row8w == at, v, out)
        return out

    dgain3, dshift3 = rowsum(douts * hat3), rowsum(douts)
    dstream2 = norm_images_back(douts, hat3, rs3, gain3, mask, count)
    dscale2 = rowsum(dstream2 * branch)
    dbranch = dstream2 * scale2
    dfb2 = rowsum(dbranch)
    dbr = split2(dbranch)
    dactive = None
    for part in range(blocks):
        term = two(dot_nt, (lanes(dbr[0], part), lanes(dbr[1], part)), matrix(1, part))
        dactive = term if dactive is None else dactive + term
    hidden = hid_ref[...]
    slope = 0.5 * (1.0 + erf(hidden * math.sqrt(0.5))) + hidden * (
        jnp.exp(-0.5 * hidden * hidden) * (1.0 / math.sqrt(2.0 * math.pi))
    )
    dhidden = dactive * slope
    dfb1_ref[...] = jnp.broadcast_to(rowsum(dhidden), (8, HID))
    dhid = split2(dhidden)

    core, corner_high, corner_low = whole_ref[4], (me // 4) % 2, (me // 2) % 2
    active_f = active.astype(f32)
    sides = (
        (jnp.concatenate([d.astype(f32) for d in dhid], axis=0), jnp.concatenate([normed, normed], axis=0)),
        (jnp.concatenate([active_f, active_f], axis=0), jnp.concatenate(dbr, axis=0)),
    )
    each = 2 * share
    factor_ref[:, pl.ds(FACTOR_LOSS, FACTOR_ROWS - FACTOR_LOSS), :] = jnp.zeros(
        (2, FACTOR_ROWS - FACTOR_LOSS, LANES), bf16
    )
    for mat, (hidden_side, channel_side) in enumerate(sides):
        for at in range(HID // LANES):
            cols = slice(at * LANES, (at + 1) * LANES)
            factor_ref[mat, pl.ds(at * LANES, LANES), :] = hidden_side[:, cols].T.astype(bf16)
        for part in range(blocks):
            factor_ref[mat, pl.ds(HID + part * LANES, LANES), :] = lanes(channel_side, part)

        for k in range(3):
            factor_ref[mat, pl.ds(FACTOR_LOSS + k, 1), :] = loss[k]

        def send_out(mat, target):
            for chip in range(HID // each):
                square, high, low = chip // 4, (chip // 2) % 2, chip % 2
                for side, (bit, mine, place) in enumerate(((high, corner_high, low), (low, corner_low, high))):
                    begin = jnp.where(mine == bit, FACTOR_OWN[side], FACTOR_OTHER[side])
                    to = pl.multiple_of(begin + (square * 2 + place) * share, share)
                    source = factor_ref.at[mat, pl.ds(chip * each + side * share, share), :]
                    copies.start_out(source, target.at[pl.ds(to, share), :])
            copies.start_out(
                factor_ref.at[mat, pl.ds(HID, blocks * LANES), :], target.at[pl.ds(FACTOR_CHANNELS, blocks * LANES), :]
            )
            rest = pl.ds(FACTOR_LOSS, FACTOR_ROWS - FACTOR_LOSS)
            copies.start_out(factor_ref.at[mat, rest, :], target.at[rest, :])

        pl.when(core == mat)(functools.partial(send_out, mat, keep_hbm))
        pl.when(core != mat)(functools.partial(send_out, mat, send_hbm))
    dnormed = jnp.concatenate([two(dot_nn, dhid, matrix(0, part)) for part in range(blocks)], axis=1)
    dgain2, dshift2 = rowsum(dnormed * hat2), rowsum(dnormed * mask)
    dstream1 = dstream2 + norm_images_back(dnormed, hat2, rs2, gain2, mask, count)
    dscale1 = rowsum(dstream1 * pool)
    dpool = dstream1 * scale1
    back = split3(dpool * per_count)
    du = dot_nn(near, back[0]) + (dot_nn(near, back[1]) + dot_nn(near, back[2])) - dpool
    dgain1, dshift1 = rowsum(du * hat1), rowsum(du)
    dstream = dstream1 + norm_images_back(du, hat1, rs1, gain1, mask, count)
    dblock_ref[...] = stack8([dgain1, dshift1, dscale1, dgain2, dshift2, dscale2])
    small_ref[...] = stack8([rowsum(dstream), dfb2, dgain3, dshift3])
    dstream_ref[...] = dstream
    copies.out(factor_ref).wait()


def backward_kernel(
    unused_one_ref,
    unused_two_ref,
    dstream_ref,
    p0_hbm,
    p1_hbm,
    p2_hbm,
    p3e_ref,
    p3o_ref,
    k1t_hbm,
    k2_hbm,
    k3e_hbm,
    k3o_hbm,
    tm_hbm,
    t64_hbm,
    pm_ref,
    marks_ref,
    dblock_ref,
    dfb1_ref,
    small_ref,
    pooled_ref,
    dlog_ref,
    whole_ref,
    keep_a_hbm,
    keep_b_hbm,
    send_a_hbm,
    send_b_hbm,
    out_ref,
    ds3_ref,
    ds2_ref,
    ds1_ref,
    dt_ref,
    dk1t_ref,
    rest_ref,
    p0_ref,
    p1_ref,
    p2_ref,
    k1t_ref,
    k2_ref,
    k3e_ref,
    k3o_ref,
    tm_ref,
    t64_ref,
    sems,
):
    copies = Copies(sems)
    third_copies = [copies.start(*x) for x in ((k3e_hbm, k3e_ref), (k3o_hbm, k3o_ref), (tm_hbm, tm_ref))]
    early_copies = [
        copies.start(*x)
        for x in (
            (p2_hbm, p2_ref),
            (k2_hbm, k2_ref),
            (p1_hbm, p1_ref),
            (k1t_hbm, k1t_ref),
            (t64_hbm, t64_ref),
            (p0_hbm, p0_ref),
        )
    ]
    marks = marks_ref[...]
    lane = lax.broadcasted_iota(jnp.int32, (BOTH, LANES), 1)
    lane1 = lax.broadcasted_iota(jnp.int32, (1, LANES), 1)
    wide = TAPS * LANES
    grad3 = split3(dstream_ref[...])
    apart = stacked(dot_nt, grad3, pm_ref[...])
    half = C4 // 2
    even, odd = split2(apart[:, :half]), split2(apart[:, half:])
    tall_even, tall_odd = jnp.concatenate(even, axis=0), jnp.concatenate(odd, axis=0)

    def by_even(cols):
        return dot_tn(tall_even, jnp.concatenate([p3e_ref[:, cols]] * 2, axis=0))

    def by_odd(cols):
        return dot_tn(tall_odd, jnp.concatenate([p3o_ref[:, cols]] * 2, axis=0))

    last = K3P // LANES - 1
    for j in range(last):
        cols = pl.ds(j * LANES, LANES)
        out_ref[pl.ds(ROW_K3 + 23 + j, half, stride=45), :] = by_odd(cols)
        if j:
            out_ref[pl.ds(ROW_K3 + j, half, stride=45), :] = by_even(cols)
    cols = pl.ds(last * LANES, LANES)
    out_ref[pl.ds(ROW_K3 + last, half, stride=45), :] = by_even(cols)
    tail = by_odd(cols)
    begin = by_even(pl.ds(0, LANES))
    rows = lax.broadcasted_iota(jnp.int32, (half, LANES), 0)
    out_ref[pl.ds(ROW_K3, half, stride=45), :] = begin + jnp.where(rows == 0, 0.0, pltpu.roll(tail, 1, 0))
    tail = tail[half - 1 : half]
    ds3_ref[...] = jnp.zeros_like(ds3_ref)
    position = lax.broadcasted_iota(jnp.int32, (BOTH, K3P), 1)
    for copy in third_copies:
        copy.wait()
    nat = jnp.where(position < LANES // 2, 0.0, two(dot_nn, even, k3e_ref[...]))
    nat = pltpu.roll(nat, K3P - LANES // 2, 1) + jnp.where(
        position < C3 * TAPS, two(dot_nn, odd, k3o_ref[...]), 0.0
    )
    for part in range(3):
        width = min(wide, K3P - part * wide)
        pieces = split2(nat[:, part * wide : part * wide + width])
        by_tap = dot_nt(pieces[0], tm_ref[:, pl.ds(0, width)]) + dot_nt(pieces[1], tm_ref[:, pl.ds(0, width)])
        for tap in range(TAPS):
            q, src_r, src_c, down_r, down_c = tap_source(tap, (), ())
            at = q[0] * 2 + q[1]
            ds3_ref[pl.ds(at * BOTH, BOTH), pl.ds(part * LANES, LANES)] += moved_back(
                by_tap[:, tap * LANES : (tap + 1) * LANES], down_r, down_c, marks
            )
    lead = 5

    def put(name, value):
        for k in range(value.shape[1] // LANES):
            at = lead + REST[name] + k
            rest_ref[at : at + 1, :] = value[:, k * LANES : (k + 1) * LANES]

    rest_ref[0:8, :] = jnp.zeros((8, LANES), f32)
    put("b3", small_ref[0:1, :])
    for k in range(6):
        at = lead + REST["block"] + 4 * k
        for i in range(4):
            rest_ref[at + i : at + i + 1, :] = dblock_ref[k : k + 1, i * LANES : (i + 1) * LANES]
    put("fb1", dfb1_ref[0:1, :])
    put("fb2", small_ref[1:2, :])
    put("final", jnp.concatenate([small_ref[2:3, :], small_ref[3:4, :]], axis=1))
    dlog = dlog_ref[...]
    put("hb", dlog[0:1] + dlog[1:2])
    rest_ref[lead + REST["end"] : lead + REST["end"] + 11, :] = jnp.zeros((11, LANES), f32)
    pooled = pooled_ref[...]
    in_group, in_place, own_row = head_masks()
    picked = jnp.where(in_place, jnp.where(own_row, pooled[0:1, :], pooled[1:2, :]), 0.0).astype(bf16)
    by_group = dot_nt(in_group.astype(bf16), picked)
    padded = jnp.concatenate([dlog, jnp.zeros((8, LANES), f32)], axis=1)
    groups = C4 // GROUP
    written = -1
    for place in range(GROUP):
        at, shift = divmod(CLS * place, LANES)
        window = pltpu.roll(padded, shift, 1) if shift else padded
        ours = by_group[:, MICRO * place : MICRO * place + 1]
        others = by_group[:, MICRO * place + 1 : MICRO * place + 2]
        for k in range(CLSP // LANES + 1):
            if (at + k) * LANES >= CLS * (place + 1):
                break
            block = slice(k * LANES, (k + 1) * LANES)
            value = ours * window[0:1, block] + others * window[1:2, block]
            target = pl.ds(lead + REST["head"] + at + k, groups, stride=SPAN)
            if at + k == written:
                rest_ref[target, :] += value
            else:
                rest_ref[target, :] = value
            written = at + k
    first = ROW_B3 + 3
    out_ref[ROW_B3 : first, :] = halves(rest_ref[lead - 1 : lead + 2, :], rest_ref[lead : lead + 3, :])
    out_ref[ROW_B3 : ROW_B3 + 1, :] += tail
    step = 508
    for at in range(0, REST["end"], step):
        out_ref[first + at : first + at + step, :] = halves(
            rest_ref[lead + 2 + at : lead + 2 + at + step, :], rest_ref[lead + 3 + at : lead + 3 + at + step, :]
        )
    end = first + REST["end"]
    out_ref[end : out_ref.shape[0], :] = jnp.zeros((out_ref.shape[0] - end, LANES), f32)
    chips, cut, unused_lanes = keep_a_hbm.shape
    each = cut + keep_b_hbm.shape[1]
    core = whole_ref[4]

    def send_chunks(chunks):
        for chunk in chunks:
            for keep, send, at, rows in ((keep_a_hbm, send_a_hbm, 0, cut), (keep_b_hbm, send_b_hbm, cut, each - cut)):
                source = out_ref.at[pl.ds(chunk * each + at, rows), :]
                ours, theirs = (keep, send) if chunk % 2 == 0 else (send, keep)
                pl.when(core == 0)(functools.partial(copies.start_out, source, ours.at[chunk // 2]))
                pl.when(core != 0)(functools.partial(copies.start_out, source, theirs.at[chunk // 2]))

    bound = -(-(ROW_K3 + 1) // each)
    send_chunks(range(bound, 2 * chips))
    for copy in early_copies:
        copy.wait()
    db2 = rowsum(ds3_ref[...])
    for k in range(2):
        out_ref[ROW_B2 + k : ROW_B2 + k + 1, :] = db2[:, k * LANES : (k + 1) * LANES]
    out_ref[ROW_K3 : ROW_K3 + 1, :] += jnp.where(lane1 < LANES // 2, db2[:, 2 * LANES :], 0.0)
    grad = split2(ds3_ref[...])
    grad_real = (grad[0][:, :C3], grad[1][:, :C3])
    for j in range(TAPS):
        cols = pl.ds(j * LANES, LANES)
        value = dot_tn(grad[0], p2_ref[:, cols]) + dot_tn(grad[1], p2_ref[:, cols])
        out_ref[pl.ds(ROW_K2 + j, C3, stride=TAPS), :] = value[:C3]
    pieces = split2(two(dot_nn, grad, k2_ref[...]))
    dt_ref[...] = two(dot_nt, pieces, tm_ref[...])
    ds2_ref[...] = jnp.zeros_like(ds2_ref)
    for at, rb, cb in all_bits(1):
        for tap in range(TAPS):
            q, src_r, src_c, down_r, down_c = tap_source(tap, rb, cb)
            to = (q[0] * 2 + q[1]) * 4 + plane_of(src_r, src_c)
            ds2_ref[pl.ds(to * BOTH, BOTH), :] += moved_back(
                dt_ref[pl.ds(at * BOTH, BOTH), pl.ds(tap * LANES, LANES)], down_r, down_c, marks
            )
    out_ref[ROW_B1 : ROW_B1 + 1, :] = rowsum(ds2_ref[...])
    grad = split2(ds2_ref[...])
    few = C2 // 2
    for j in range(5):
        cols = pl.ds(j * LANES, LANES)
        dk1t_ref[j] = dot_tn(grad[0], p1_ref[:, cols]) + dot_tn(grad[1], p1_ref[:, cols])
    evens, odds = (
        two(
            dot_nt,
            split2(jnp.concatenate([dk1t_ref[j, pl.ds(odd, few, stride=2), :] for j in range(5)], axis=1)),
            t64_ref[pl.ds(C1 * (1 - odd), 5 * LANES), :],
        )
        for odd in range(2)
    )
    for j in range(9):
        if j < 4:
            value = evens[:, j * LANES : (j + 1) * LANES]
        elif j == 4:
            value = evens[:, 4 * LANES :] + odds[:, :LANES]
        else:
            value = odds[:, (j - 4) * LANES : (j - 3) * LANES]
        out_ref[pl.ds(ROW_K1 + j, few, stride=9), :] = value
    ds1_ref[...] = jnp.zeros_like(ds1_ref)
    for pair in range(5):
        values = two(dot_nn, grad, k1t_ref[:, pl.ds(pair * LANES, LANES)])
        for at, rb, cb in all_bits(2):
            here = values[at * BOTH : (at + 1) * BOTH]
            for side in range(2):
                tap = 2 * pair + side
                if tap >= TAPS:
                    continue
                q, src_r, src_c, down_r, down_c = tap_source(tap, rb, cb)
                to = stem_plane(q, src_r, src_c)
                mine = (lane < C1) if side == 0 else (lane >= C1)
                ds1_ref[pl.ds(to * BOTH, BOTH), :] += moved_back(
                    jnp.where(mine, here, 0.0), down_r, down_c, marks
                )
    db0 = rowsum(ds1_ref[...])
    db0 = db0 + pltpu.roll(db0, LANES // 2, 1)
    stem = jnp.zeros((LANES, 2 * LANES), f32)
    for at in range(4):
        span = pl.ds(at * 16 * BOTH, 16 * BOTH)
        grad = split2(ds1_ref[span, :])
        stem = stem + (dot_tn(grad[0], p0_ref[span, :]) + dot_tn(grad[1], p0_ref[span, :]))
    stem = stem[:C1] + stem[C1:]
    depth = IN_CH * 49
    held = jnp.zeros((1, 3 * LANES), f32)
    done = 0
    for at in range(C1):
        row, shift = divmod(depth * at, LANES)
        line = jnp.concatenate([stem[at : at + 1], jnp.zeros((1, LANES), f32)], axis=1)
        if shift:
            line = pltpu.roll(line, shift, 1)
        while done < row:
            out_ref[done : done + 1, :] = held[:, :LANES]
            held = jnp.concatenate([held[:, LANES:], jnp.zeros((1, LANES), f32)], axis=1)
            done += 1
        held = held + line
    out_ref[done : done + 1, :] = held[:, :LANES]
    if done < ROW_B0:
        out_ref[ROW_B0 : ROW_B0 + 1, :] = held[:, LANES : 2 * LANES]
    out_ref[ROW_B0 : ROW_B0 + 1, :] += jnp.where(lane1 < LANES // 2, 0.0, db0)

    send_chunks(range(bound))
    copies.out(out_ref).wait()


def product_kernel(whole_ref, keep_ref, got_ref, far_a_ref, far_b_ref, keep_a_ref, send_a_ref, keep_b_ref, send_b_ref, loss_ref):
    me = whole_ref[5]
    loss = keep_ref[pl.ds(FACTOR_LOSS, 8), :].astype(f32) + got_ref[pl.ds(FACTOR_LOSS, 8), :].astype(f32)
    loss_ref[...] = jnp.broadcast_to(loss[0:1] + (loss[1:2] + loss[2:3]), (8, LANES))
    squares, share, unused_channels = keep_a_ref.shape
    blocks = C4 // LANES
    ways = (
        (0, far_a_ref, 0, QUARTER, (me // 2) % 2, keep_a_ref, send_a_ref),
        (1, far_b_ref, C4, 0, (me // 4) % 2, keep_b_ref, send_b_ref),
    )
    for way, far_ref, far_hidden, far_channels, mine, to_keep_ref, to_send_ref in ways:
        own = pl.ds(FACTOR_OWN[way], QUARTER)
        hidden = jnp.concatenate(
            [keep_ref[own, :], got_ref[own, :]] + [far_ref[k, pl.ds(far_hidden, QUARTER), :] for k in range(2)], axis=1
        )
        channels = [
            jnp.concatenate(
                [
                    keep_ref[pl.ds(FACTOR_CHANNELS + part * LANES, LANES), :],
                    got_ref[pl.ds(FACTOR_CHANNELS + part * LANES, LANES), :],
                ]
                + [far_ref[k, pl.ds(far_channels + part * LANES, LANES), :] for k in range(2)],
                axis=0,
            )
            for part in range(blocks)
        ]
        product = dot_nn(hidden, jnp.concatenate(channels, axis=1))
        for square in range(squares):
            first, second = (product[(2 * square + k) * share : (2 * square + k + 1) * share] for k in range(2))
            to_keep_ref[square] = jnp.where(mine == 0, first, second)
            to_send_ref[square] = jnp.where(mine == 0, second, first)


def passes(a, b, dot, many):
    pairs = [(0, 0), (0, 1), (1, 0)]
    if many:
        pairs += [(0, 2), (1, 1), (2, 0)]
    axis = 0 if dot is dot_tn else 1
    return dot(
        jnp.concatenate([a[i] for i, unused in pairs], axis=axis),
        jnp.concatenate([b[j] for unused, j in pairs], axis=0),
    )


def gram_kernel(scale_ref, terms, momentum_ref, loss_ref, ortho_ref, new_ref, packed_ref):
    grad = functools.reduce(jnp.add, [term[...] for term in terms]) * scale_ref[0]
    new = 0.95 * momentum_ref[...] + grad
    new_ref[...] = new
    ortho = grad + 0.95 * new
    ortho_ref[...] = ortho
    parts = split3(ortho)

    def cut(k):
        return tuple(p[:, k * LANES : (k + 1) * LANES] for p in parts)

    for at, (i, j) in enumerate(PAIRS):
        block = passes(cut(i), cut(j), dot_tn, True)
        if at == 0:
            row = lax.broadcasted_iota(jnp.int32, block.shape, 0)
            col = lax.broadcasted_iota(jnp.int32, block.shape, 1)
            block = jnp.where((row == LANES - 1) & (col == 0), loss_ref[0:1, 0:1], block)
        packed_ref[pl.ds(at * LANES, LANES), :] = block


def newton_steps(gram, ortho, steps, last):
    wide_row = lax.broadcasted_iota(jnp.int32, (C4, C4), 0)
    wide_col = lax.broadcasted_iota(jnp.int32, (C4, C4), 1)
    for iteration in steps:
        many = iteration == 0
        split = split3 if many else split2
        parts = split(gram)
        poly = jnp.where(wide_row == wide_col, 3.4445, 0.0) + (
            -4.775 * gram + 2.0315 * passes(parts, parts, dot_nn, many)
        )
        poly_parts = split(poly)
        ortho = passes(split(ortho), poly_parts, dot_nn, many)
        if iteration < last:
            gram = passes(split(passes(poly_parts, parts, dot_nn, many)), poly_parts, dot_nn, many)
    return gram, ortho


def newton_first_kernel(steps, packed_ref, ortho_ref, out_ref, gram_ref, loss_ref):
    row = lax.broadcasted_iota(jnp.int32, (LANES, LANES), 0)
    col = lax.broadcasted_iota(jnp.int32, (LANES, LANES), 1)
    trace = jnp.zeros((1, 1), f32)
    for at, (i, j) in enumerate(PAIRS):
        block = packed_ref[pl.ds(at * LANES, LANES), :]
        if at == 0:
            loss_ref[...] = jnp.broadcast_to(block[LANES - 1 : LANES, 0:1], (8, LANES))
            block = jnp.where((row == LANES - 1) & (col == 0), block.T, block)
        gram_ref[pl.ds(i * LANES, LANES), pl.ds(j * LANES, LANES)] = block
        if i == j:
            trace = trace + total(jnp.where(row == col, block, 0.0))
        else:
            gram_ref[pl.ds(j * LANES, LANES), pl.ds(i * LANES, LANES)] = block.T
    inverse = 1.0 / (jnp.sqrt(trace) + 1e-07)
    gram, ortho = newton_steps(
        gram_ref[...] * (inverse * inverse), ortho_ref[...] * inverse, range(steps), NS_ITERS - 1
    )
    gram_ref[...] = gram
    out_ref[...] = ortho


def newton_last_kernel(steps, gram_ref, ortho_ref, out_ref):
    unused_gram, ortho = newton_steps(gram_ref[...], ortho_ref[...], range(steps, NS_ITERS), NS_ITERS - 1)
    out_ref[...] = ortho


def shape(*dims, dtype=f32):
    return jax.ShapeDtypeStruct(dims, dtype)


def kernel_call(body, outs, scratch, smem, kept, count, micros, outs_kept=0, aliases=None):
    vmem = pl.BlockSpec(memory_space=pltpu.VMEM)
    scalar = pl.BlockSpec(memory_space=pltpu.SMEM)
    anywhere = pl.BlockSpec(memory_space=pl.ANY)
    if isinstance(kept, int):
        specs = [anywhere] * kept + [vmem] * (count - smem - kept)
    else:
        specs = [anywhere if k else vmem for k in kept[smem:]] + [vmem] * (count - len(kept))
    return pl.pallas_call(
        body,
        out_shape=outs,
        in_specs=[scalar] * smem + specs,
        out_specs=[anywhere] * outs_kept + [vmem] * (len(outs) - outs_kept),
        scratch_shapes=scratch,
        input_output_aliases=aliases or {},
        compiler_params=pltpu.CompilerParams(vmem_limit_bytes=60 * 1024 * 1024),
        cost_estimate=pl.CostEstimate(flops=10**6, bytes_accessed=micros * 3_000_000, transcendentals=0),
    )


def pack_kernel(valid_ref, mats_ref, flat_ref, out_ref, low_ref, high_ref):
    share = mats_ref.shape[1]
    blocks = C4 // LANES
    for mat in range(2):
        for part in range(blocks):
            at = (mat * blocks + part) * share
            out_ref[pl.ds(at, share), :] = mats_ref[mat, :, pl.ds(part * LANES, LANES)].astype(bf16)
    half, count = low_ref.shape[0], flat_ref.shape[0]
    low_ref[...] = flat_ref[pl.ds(0, half), :].astype(bf16)
    high_ref[pl.ds(0, count - half), :] = flat_ref[pl.ds(half, count - half), :].astype(bf16)
    left = 2 * half - count
    counted = (valid_ref[0] + valid_ref[1]).astype(f32)
    high_ref[pl.ds(count - half, left), :] = jnp.full((left, LANES), counted, f32).astype(bf16)


def run_pack(valid, mats, flat):
    half = (flat.shape[0] // 32 + 1) * 16
    outs = [shape(2 * C4 // LANES * mats.shape[1], LANES, dtype=bf16)] + [shape(half, LANES, dtype=bf16)] * 2
    return kernel_call(pack_kernel, outs, [], 1, 0, 3, 2)(valid, mats, flat)


def late_kernel(group_ref, unused_ref, out_ref):
    out_ref[0] = group_ref[0]


def run_late(group, tie):
    return pl.pallas_call(
        late_kernel,
        out_shape=shape(1, dtype=jnp.int32),
        in_specs=[pl.BlockSpec(memory_space=pltpu.SMEM), pl.BlockSpec(memory_space=pl.ANY)],
        out_specs=pl.BlockSpec(memory_space=pltpu.SMEM),
    )(group, tie)[0]


def run_conv(whole, flat, gathered, tie, moved, marks, flat_share, devices_count):
    half = C4 // 2
    moved_outs = [
        shape(16 * BOTH, 5 * LANES, dtype=bf16),
        shape(4 * BOTH, TAPS * LANES, dtype=bf16),
        shape(BOTH, K3P, dtype=bf16),
        shape(BOTH, K3P, dtype=bf16),
        shape(C2, 5 * LANES, dtype=bf16),
        shape(C3P, TAPS * LANES, dtype=bf16),
        shape(half, K3P, dtype=bf16),
        shape(half, K3P, dtype=bf16),
    ]
    outs = moved_outs + [
        shape(BOTH, C4),
        shape(REST["head"], LANES),
        shape(C4 // GROUP, (SPAN + 1) * LANES, dtype=bf16),
        shape(8, LANES),
        shape(8, LANES),
    ]
    scratch = [pltpu.VMEM(a.shape, a.dtype) for a in moved + moved_outs]
    scratch += [
        pltpu.VMEM((64 * BOTH, LANES), f32),
        pltpu.VMEM((16 * BOTH, LANES), f32),
        pltpu.VMEM((4 * BOTH, C3P), f32),
        pltpu.VMEM((4 * BOTH, TAPS * LANES), bf16),
        pltpu.VMEM((3 * BOTH, TAPS * LANES), bf16),
        pltpu.VMEM((C1, 2 * LANES), f32),
        pltpu.VMEM((5, C2, LANES), f32),
        pltpu.SemaphoreType.DMA((16,)),
    ]
    if flat_share % LANES:
        args = [whole, flat, tie] + moved + [marks]
        kept = [False, False] + [True] * 5
    else:
        arrays = [array for side in gathered for array, *unused in side]
        args = [whole] + arrays + [tie] + moved + [marks]
        kept = [False] + [True] * (len(arrays) + 5)
        scratch += [
            pltpu.VMEM((devices_count, 2 * arrays[0].shape[-2], LANES), bf16),
            pltpu.VMEM((devices_count * flat_share // LANES, LANES), f32),
        ]
    body = functools.partial(conv_kernel, flat_share, gathered)
    return kernel_call(body, outs, scratch, 1, kept, len(args), 12, 8)(*args)


def run_block(whole, real, got, made, marks, near, share):
    outs = [shape(FACTOR_ROWS, LANES, dtype=bf16)] * 2 + [
        shape(BOTH, C4),
        shape(8, C4),
        shape(8, HID),
        shape(8, C4),
        shape(8, C4),
        shape(8, CLSP),
    ]
    scratch = [
        pltpu.VMEM((2, FACTOR_ROWS, LANES), bf16),
        pltpu.VMEM((BOTH, HID), f32),
        pltpu.VMEM((C4 // GROUP, (SPAN + 1) * LANES), f32),
        pltpu.VMEM((MICRO * GROUP, C4 // GROUP), f32),
        pltpu.VMEM((2, HID // share, C4 // LANES * share, LANES), bf16),
        pltpu.SemaphoreType.DMA((2,)),
    ]
    args = [whole, real, got] + list(made) + [marks, near]
    body = functools.partial(block_kernel, share)
    return kernel_call(body, outs, scratch, 2, 1, len(args), 12, 2)(*args)


def run_backward(args, chips, each):
    scratch = [
        pltpu.VMEM((2 * chips * each, LANES), f32),
        pltpu.VMEM((4 * BOTH, C3P), f32),
        pltpu.VMEM((16 * BOTH, LANES), f32),
        pltpu.VMEM((64 * BOTH, LANES), f32),
        pltpu.VMEM((4 * BOTH, TAPS * LANES), f32),
        pltpu.VMEM((5, C2, LANES), f32),
        pltpu.VMEM((REST["end"] + 16, LANES), f32),
    ]
    moved = args[4:7] + args[9:15]
    scratch += [pltpu.VMEM(x.shape, x.dtype) for x in moved] + [pltpu.SemaphoreType.DMA((2 + len(moved),))]
    kept = [False] + [True] * 2 + [False] + [True] * 3 + [False] * 2 + [True] * 6
    cut = -(-each // 16) * 8
    outs = [shape(chips, cut, LANES), shape(chips, each - cut, LANES)] * 2

    def body(*refs):
        backward_kernel(*refs[1 : len(args)], refs[0], *refs[len(args) :])

    return kernel_call(body, outs, scratch, 1, kept, len(args), 20, 4)(*args)


def run_product(whole, through, keep, got, far_a, far_b, squares, share):
    outs = [shape(*x.shape) for x in through] + [shape(squares, share, C4)] * 4 + [shape(8, LANES)]
    count = len(through)

    def body(*refs):
        product_kernel(refs[0], *refs[1 + count : 5 + count], *refs[5 + 2 * count :])

    return kernel_call(body, outs, [], 1, count, 5 + count, 3, count, {1 + k: k for k in range(count)})(
        whole, *through, keep, got, far_a, far_b
    )


def sum_kernel(whole_ref, keep_one_ref, got_one_ref, keep_two_ref, got_two_ref, *out_refs):
    square = whole_ref[5] // 8
    share = keep_one_ref.shape[1]
    for j, out_ref in enumerate(out_refs):
        entry = square ^ j
        out_ref[pl.ds(0, share), :] = keep_one_ref[entry] + got_one_ref[entry]
        out_ref[pl.ds(share, share), :] = keep_two_ref[entry] + got_two_ref[entry]


def run_sum(whole, tie, keep_one, got_one, keep_two, got_two):
    squares, share, unused_channels = keep_one.shape
    outs = [shape(2 * share, C4)] * squares

    def body(*refs):
        sum_kernel(refs[0], *refs[2:])

    return kernel_call(body, outs, [], 1, 1, 6, 2)(whole, tie, keep_one, got_one, keep_two, got_two)


def halve_kernel(whole_ref, tie_ref, keep_a, got_a, keep_b, got_b, sent_a, left_a, sent_b, left_b):
    me = whole_ref[5]
    high, low = (me // 4) % 2, (me // 2) % 2
    for place in range(2):
        first, second = (keep_a[0, k, place] + got_a[0, k, place] for k in range(2))
        sent_a[place, 0] = jnp.where(high == 0, second, first)
        left_a[place, 0] = jnp.where(high == 0, first, second)
        first, second = (keep_b[0, place, k] + got_b[0, place, k] for k in range(2))
        sent_b[place, 0] = jnp.where(low == 0, second, first)
        left_b[place, 0] = jnp.where(low == 0, first, second)


def run_halve(whole, tie, keep_a, got_a, keep_b, got_b):
    squares = keep_a.shape[0] // 4
    inputs = [x.reshape(squares, 2, 2, *x.shape[1:]) for x in (keep_a, got_a, keep_b, got_b)]
    rows = [x.shape[3] for x in inputs]
    outs = [shape(2, squares, rows[0], LANES)] * 2 + [shape(2, squares, rows[2], LANES)] * 2
    return pl.pallas_call(
        halve_kernel,
        grid=(squares,),
        out_shape=outs,
        in_specs=[pl.BlockSpec(memory_space=pltpu.SMEM), pl.BlockSpec(memory_space=pl.ANY)]
        + [pl.BlockSpec((1, 2, 2, r, LANES), lambda i: (i, 0, 0, 0, 0)) for r in rows],
        out_specs=[pl.BlockSpec((2, 1, x.shape[2], LANES), lambda i: (0, i, 0, 0)) for x in outs],
        compiler_params=pltpu.CompilerParams(vmem_limit_bytes=63 * 1024 * 1024),
        cost_estimate=pl.CostEstimate(flops=10**6, bytes_accessed=15_000_000, transcendentals=0),
    )(whole, tie, *inputs)


def run_gram(scale, terms, momentum, loss):
    rows, count = momentum.shape[0], len(terms)
    outs = [shape(rows, C4), shape(rows, C4), shape(len(PAIRS) * LANES, LANES)]

    def body(*refs):
        gram_kernel(refs[0], refs[1 : 1 + count], *refs[1 + count :])

    return kernel_call(body, outs, [], 1, 0, 3 + count, 4)(scale, *terms, momentum, loss)


def run_newton_first(packed, ortho, steps):
    outs = [shape(*ortho.shape), shape(C4, C4), shape(8, LANES)]
    return kernel_call(functools.partial(newton_first_kernel, steps), outs, [], 0, 0, 2, 12)(packed, ortho)


def run_newton_last(ties, gram, ortho, steps):
    outs = [shape(*ortho.shape)]
    count = len(ties)

    def body(*refs):
        newton_last_kernel(steps, *refs[count:])

    return kernel_call(body, outs, [], 0, count, 2 + count, 8)(*ties, gram, ortho)[0]


def patches(images, resolution, partner_col, mix_col):
    pictures = images[:, 0].astype(f32)
    dims = (1, 1, RES_L, RES_L)
    inside = (lax.broadcasted_iota(jnp.int32, dims, 2) < resolution) & (
        lax.broadcasted_iota(jnp.int32, dims, 3) < resolution
    )
    mixing = mix_col[:, None, None, None]
    other = jnp.where(partner_col[:, None, None, None] == 0, pictures[0][None], pictures[1][None])
    pixels = jnp.where(inside, mixing * pictures + (1.0 - mixing) * other, 0.0).astype(bf16)
    padded = jnp.pad(pixels, ((0, 0), (0, 0), (2, 1), (2, 1)))
    size = RES_STEP + 3
    blocks = [
        padded[:, :, RES_STEP * i : RES_STEP * i + size, RES_STEP * j : RES_STEP * j + size]
        for i in range(SIDE)
        for j in range(SIDE)
    ]
    blocks = jnp.stack(blocks, axis=1).reshape(MICRO * SIDE * SIDE, IN_CH, size, size)
    depth = IN_CH * 49
    choose = jnp.eye(depth, dtype=bf16).reshape(IN_CH, 7, 7, depth).transpose(1, 2, 0, 3)
    columns = lax.conv_general_dilated(
        blocks,
        choose,
        (4, 4),
        ((0, 0), (0, 0)),
        dimension_numbers=("NCHW", "HWIO", "HWNC"),
        preferred_element_type=f32,
    ).astype(bf16)
    columns = columns.reshape(64, MICRO, SIDE * SIDE, depth)
    columns = jnp.pad(columns, ((0, 0), (0, 0), (0, ROWS - SIDE * SIDE), (0, 2 * LANES - depth)))
    return columns.reshape(64 * BOTH, 2 * LANES)


def tap_orders(zero):
    row = lax.broadcasted_iota(jnp.int32, (TAPS * LANES, TAPS * LANES), 0) + zero
    col = lax.broadcasted_iota(jnp.int32, (TAPS * LANES, TAPS * LANES), 1)
    forth = ((row % LANES) * TAPS + row // LANES == col).astype(bf16)
    dims = (5 * LANES + C1, 5 * LANES)
    row = lax.broadcasted_iota(jnp.int32, dims, 0) - C1 + zero
    col = lax.broadcasted_iota(jnp.int32, dims, 1)
    real = (row >= 0) & (row < TAPS * C1)
    row = jnp.maximum(row, 0)
    back = (real & ((row % TAPS) * C1 + row // TAPS == col)).astype(bf16)
    row = lax.broadcasted_iota(jnp.int32, (C4, C4), 0) + zero
    col = lax.broadcasted_iota(jnp.int32, (C4, C4), 1)
    merge = ((row % (C4 // 2)) * 2 + row // (C4 // 2) == col).astype(bf16)
    return forth, back, merge


def grid_marks(side):
    row = np.arange(BOTH)
    image, q = row // ROWS, row % ROWS
    y, x = q // SIDE, q % SIDE
    real = q < SIDE * SIDE
    fixed = np.stack([real & (y > 0), real & (x > 0), real & (y > 0) & (x > 0)], 1).astype(np.float32)
    close = (
        (image[:, None] == image[None])
        & (abs(y[:, None] - y[None]) <= 1)
        & (abs(x[:, None] - x[None]) <= 1)
        & real[:, None]
        & real[None]
    )
    inside = jnp.asarray(real) & (jnp.asarray(y) < side) & (jnp.asarray(x) < side)
    near = jnp.where(jnp.asarray(close) & inside[:, None] & inside[None], 1.0, 0.0)
    cells = jnp.maximum(jnp.sum(near, axis=1), 1.0)
    marks = jnp.concatenate(
        [inside.astype(f32)[:, None], jnp.asarray(fixed), (1.0 / cells)[:, None]], axis=1
    )
    return jnp.pad(marks, ((0, 0), (0, LANES - marks.shape[1]))), near.astype(bf16)


def local_inputs(images, group, early_group, label_col, partner_col, mix_col, valid_col, me):
    side = RES_S // RES_STEP + group
    columns = patches(images, side * RES_STEP, partner_col, mix_col)
    orders = tap_orders(jnp.minimum(early_group, 0))
    marks, near = grid_marks(side)
    other = jnp.where(partner_col == 0, label_col[0], label_col[1])
    whole = jnp.concatenate([label_col, other, jnp.stack([me % 2, me]).astype(jnp.int32)])
    cells = (side * side).astype(f32)
    real = jnp.concatenate([mix_col, valid_col.astype(f32), jnp.stack([cells, cells * C4])])
    return whole, real, columns, orders, marks, near


def second_half(prepared, convs, made, chips, each, ties):
    columns, (forth, back, merge), marks = prepared[2], prepared[3], prepared[4]
    p1, p2, p3e, p3o, k1t, k2, k3e, k3o = convs[:8]
    args = [made[2], columns, p1, p2, p3e, p3o, k1t, k2, k3e, k3o, forth, back, merge, marks]
    return run_backward([prepared[0]] + list(ties) + args + list(made[3:8]), chips, each)


class Ring:
    def __init__(self, count):
        self.count = count
        self.squares = count // 8
        me = lax.axis_index(AXES)
        self.me = me
        self.core = me % 2
        self.low = (me // 2) % 2
        self.high = (me // 4) % 2
        self.corner = (me // 2) % 4
        self.square = me // 8

    def swap(self, value, bits):
        return lax.ppermute(value, AXES, [(i, i ^ bits) for i in range(self.count)])


def pick(value, at, axis):
    return lax.dynamic_index_in_dim(value, at, axis, keepdims=False)


class Scatter:
    def __init__(self, ring, terms, mine, bits):
        self.ring = ring
        self.terms = terms
        self.mine = mine
        self.bits = bits

    def exchange(self):
        sent = functools.reduce(jnp.add, [pick(x, 1 - self.mine, 0) for x in self.terms])
        self.terms = [pick(x, self.mine, 0) for x in self.terms] + [self.ring.swap(sent, self.bits)]

    def add(self):
        self.terms = [functools.reduce(jnp.add, self.terms)]


def sum_squares(ring, value, far_first):
    bits = ring.squares.bit_length() - 1
    order = list(range(bits))
    if far_first:
        order.reverse()
    held = order.copy()
    value = value.reshape((2,) * bits + value.shape[1:])
    got = None
    for bit in order:
        axis = len(held) - 1 - sorted(held).index(bit)
        held.remove(bit)
        mine = (ring.square >> bit) & 1
        if got is not None:
            value = value + got
        got = ring.swap(pick(value, 1 - mine, axis), 8 << bit)
        value = pick(value, mine, axis)
    return value, got


class Gather:
    def __init__(self, ring, value, far_first, high_first):
        self.ring = ring
        self.value = value
        self.masks = []
        bits = list(range(ring.squares.bit_length() - 1))
        self.squares = [8 << bit for bit in (reversed(bits) if far_first else bits)]
        self.corners = (4, 2) if high_first else (2, 4)
        self.pieces = []

    def exchange(self, mask):
        self.value = jnp.stack([self.value, self.ring.swap(self.value, mask)])
        self.masks = [mask] + self.masks

    def between_squares(self):
        for mask in self.squares:
            self.exchange(mask)

    def first_corner(self):
        self.exchange(self.corners[0])

    def second_corner(self):
        got = self.ring.swap(self.value, self.corners[1])
        self.pieces = [(self.value, self.masks, 0), (got, self.masks, self.corners[1])]

    def between_cores(self):
        self.pieces += [(self.ring.swap(array, 1), masks, base | 1) for array, masks, base in self.pieces]


def together(scatters, *others):
    counts = [len(x.terms) for x in scatters]
    values = lax.optimization_barrier(tuple(t for x in scatters for t in x.terms) + tuple(others))
    at = 0
    for x, count in zip(scatters, counts):
        x.terms = list(values[at : at + count])
        at += count
    return values[at:]


class ChipSum:
    def __init__(self, ring, value):
        self.ring = ring
        self.shape = value.shape
        self.terms = [value.reshape(4, value.shape[0] // 4, value.shape[1])]

    def scatter_corners(self):
        ring = self.ring
        got = [ring.swap(pick(self.terms[0], ring.corner ^ j, 0), 2 * j) for j in range(1, 4)]
        self.terms = [functools.reduce(jnp.add, got, pick(self.terms[0], ring.corner, 0))]

    def sum_squares(self):
        ring = self.ring
        got = [ring.swap(self.terms[0], 8 * j) for j in range(1, ring.squares)]
        self.terms = [functools.reduce(jnp.add, got, self.terms[0])]


    def gather_corners(self):
        ring = self.ring
        held = jnp.stack([self.terms[0]] + [ring.swap(self.terms[0], 2 * j) for j in range(1, 4)])
        return jnp.stack([pick(held, ring.corner ^ j, 0) for j in range(4)]).reshape(self.shape)


def per_device(
    devices_count,
    images,
    group_ids,
    labels,
    partners,
    mix_weights,
    valid,
    flat_params,
    flat_first,
    flat_second,
    mlp_weights,
    mlp_momentum,
):
    ring = Ring(devices_count)
    chips = devices_count // 2
    share = mlp_weights.shape[2]
    flat_share = flat_params.shape[0]
    flat_rows = -(-flat_share // LANES)
    spare = flat_rows * LANES - flat_share
    mine = jnp.pad(flat_params, (0, spare)) if spare else flat_params
    sent, flat_low, flat_high = run_pack(
        valid.reshape(MICRO), mlp_weights.transpose(0, 2, 1), mine.reshape(flat_rows, LANES)
    )
    got = lax.all_gather(sent, AXES, axis=0, tiled=False)
    aligned = flat_share % LANES == 0
    pieces = [Gather(ring, flat_low, False, True), Gather(ring, flat_high, True, False)]
    group = early_group = group_ids[0]
    if aligned:
        for x in pieces:
            x.between_squares()
        early_group = run_late(group_ids, pieces[1].value)
        for x in pieces:
            x.first_corner()
        group = run_late(group_ids, pieces[1].value)
    prepared = local_inputs(
        images, group, early_group, labels[:, 0], partners[:, 0], mix_weights[:, 0], valid[:, 0], ring.me
    )
    whole, real, columns, orders, marks, near = prepared
    momentum = mlp_momentum.transpose(0, 2, 1)

    def of_both_cores(mine, theirs):
        at_first = ring.core == 0
        return jnp.concatenate([jnp.where(at_first, mine, theirs), jnp.where(at_first, theirs, mine)])

    momentum_rows = of_both_cores(
        pick(momentum, ring.core, 0), ring.swap(pick(momentum, 1 - ring.core, 0), 1)
    )
    moved = [columns, *orders]
    if aligned:
        for x in pieces:
            x.second_corner()
        for x in pieces:
            x.between_cores()
        convs = run_conv(
            whole, None, [x.pieces for x in pieces], momentum_rows, moved, marks, flat_share, devices_count
        )
        counted = convs[12][0, 0]
    else:
        rows = lax.all_gather(jnp.concatenate([flat_low, flat_high]), AXES, axis=0, tiled=False)
        whole_flat = (
            rows[:, :flat_rows]
            .astype(f32)
            .reshape(devices_count, flat_rows * LANES)[:, :flat_share]
            .reshape(devices_count * flat_share // LANES, LANES)
        )
        convs = run_conv(whole, whole_flat, None, momentum_rows, moved, marks, flat_share, devices_count)
        counted = jnp.sum(rows[:, flat_rows, 0].astype(f32))
    scale = 1.0 / jnp.maximum(counted, 1.0)
    made = run_block(whole, real, got, convs[8:12], marks, near, share)
    keep, send = made[:2]
    got_factors = ring.swap(send, 1)
    ahead = [
        jnp.stack([x[begin : begin + QUARTER + C4] for x in (keep, got_factors)]) for begin in (0, FACTOR_CHANNELS)
    ]
    far_a, far_b = ring.swap(ahead[0], 4), ring.swap(ahead[1], 2)

    each = -(-(devices_count * flat_share) // (devices_count * LANES * 8)) * 8
    ties = ahead
    keep_a, keep_b, send_a, send_b = second_half(prepared, convs, made, chips, each, ties)
    send_a, send_b, keep_one, send_one, keep_two, send_two, loss = run_product(
        whole, [send_a, send_b], keep, got_factors, far_a, far_b, ring.squares, share
    )
    got_one, got_two = ring.swap(send_one, 2), ring.swap(send_two, 4)
    got_a, got_b = ring.swap(send_a, 1), ring.swap(send_b, 1)
    sent_a, left_a, sent_b, left_b = run_halve(whole, keep_one, keep_a, got_a, keep_b, got_b)
    entries = run_sum(whole, sent_a, keep_one, got_one, keep_two, got_two)
    terms = [entries[0]] + [ring.swap(entries[j], 8 * j) for j in range(1, ring.squares)]
    flat = [
        Scatter(ring, [left_a, ring.swap(sent_a, 4)], ring.low, 2),
        Scatter(ring, [left_b, ring.swap(sent_b, 2)], ring.high, 4),
    ]
    ortho, momentum_new, packed = run_gram(scale[None], terms, momentum_rows, loss)
    grams = ChipSum(ring, packed)
    grams.scatter_corners()
    grams.sum_squares()
    for x in flat:
        x.exchange()
        x.add()
    together([grams] + flat)
    flat_sums = [sum_squares(ring, x.terms[0], far) for x, far in zip(flat, (False, True))]
    sum_flat = jnp.concatenate([sum(x) for x in flat_sums])
    steps = 3
    ortho, gram, loss_total = run_newton_first(grams.gather_corners(), ortho, steps)
    lag = (devices_count - 1) * (each * LANES - flat_share)
    hops = -(-lag // (each * LANES))
    tail = min(each, -(-lag // (8 * LANES)) * 8)
    before = [
        lax.ppermute(sum_flat[each - tail :], AXES, [(i, i + h) for i in range(devices_count - h)])
        for h in range(hops, 0, -1)
    ]
    ortho = run_newton_last([x[0] for x in flat_sums], gram, ortho, steps)
    sum_flat = jnp.concatenate(before + [sum_flat])
    start = len(before) * tail * LANES - ring.me * (each * LANES - flat_share)
    if flat_share % LANES == 0:
        sum_flat = lax.dynamic_slice_in_dim(sum_flat, start // LANES, flat_rows, 0).reshape(-1)
    else:
        sum_flat = lax.dynamic_slice_in_dim(sum_flat.reshape(-1), start, flat_share, 0)
    sum_flat = sum_flat * scale
    first_new = 0.9 * flat_first + 0.1 * sum_flat
    second_new = 0.999 * flat_second + 0.001 * sum_flat * sum_flat
    first_hat = first_new / (1.0 - 0.9**STEP)
    second_hat = second_new / (1.0 - 0.999**STEP)
    params_new = flat_params - 0.02 * (
        first_hat / (jnp.sqrt(second_hat) + 1e-08) + 0.05 * flat_params
    )

    def to_owners(by_chip):
        parts = by_chip.reshape(2, share, C4)
        mine, theirs = pick(parts, ring.core, 0), ring.swap(pick(parts, 1 - ring.core, 0), 1)
        at_first = ring.core == 0
        return jnp.stack([jnp.where(at_first, mine, theirs), jnp.where(at_first, theirs, mine)])

    mats = mlp_weights.transpose(0, 2, 1)
    weights_new = mats * (1.0 - 0.1 * 0.05) - 0.1 * 0.2 * math.sqrt(HID) * to_owners(ortho)
    return (
        loss_total[0, 0],
        params_new,
        first_new,
        second_new,
        weights_new.transpose(0, 2, 1),
        to_owners(momentum_new).transpose(0, 2, 1),
    )


def solution(mesh):
    placed = (
        P(None, AXES, None, None, None),
        P(AXES),
        P(None, AXES),
        P(None, AXES),
        P(None, AXES),
        P(None, AXES),
        P(AXES),
        P(AXES),
        P(AXES),
        P(None, None, AXES),
        P(None, None, AXES),
    )
    devices_count = math.prod(mesh.shape[axis] for axis in AXES)
    return jax.shard_map(
        functools.partial(per_device, devices_count),
        mesh=mesh,
        in_specs=placed,
        out_specs=(
            P(),
            P(AXES),
            P(AXES),
            P(AXES),
            P(None, None, AXES),
            P(None, None, AXES),
        ),
        check_vma=False,
    )
```

```python
import functools
import math

import jax
import jax.numpy as jnp
import numpy as np
from jax import lax
from jax.experimental import pallas as pl
from jax.experimental.pallas import tpu as pltpu
from jax.sharding import PartitionSpec as P

C1 = 64
C2 = 128
C3 = 320
C4 = 512
HID = 2048
CLS = 1000
IN_CH = 3
RES_S = 96
RES_L = 160
RES_STEP = 32
MICRO = 2
NS_ITERS = 5
STEP = 10

AXES = ("fsdp", "ns")
LANES = 128
SIDE = 5
ROWS = 32
BOTH = MICRO * ROWS
C3P = 384
CLSP = 1024
K3P = 2944
TAPS = 9

f32 = jnp.float32
bf16 = jnp.bfloat16
norm_epsilon = 1e-05

NARROW = C1 * IN_CH * 49
ROW_B0 = NARROW // LANES
ROW_K1 = 74
ROW_B1 = 650
ROW_K2 = 651
ROW_B2 = 3531
ROW_K3 = 3533
ROW_B3 = 15053
REST = {"b3": 0, "block": 4, "fb1": 28, "fb2": 44, "final": 48, "head": 56, "hb": 4056, "end": 4064}
QUARTER = HID // 4
FACTOR_OTHER = (0, QUARTER + C4)
FACTOR_CHANNELS = QUARTER
FACTOR_OWN = (2 * QUARTER + C4, 3 * QUARTER + C4)
FACTOR_LOSS = HID + C4
FACTOR_ROWS = FACTOR_LOSS + 16
GROUP = 16
SPAN = GROUP * CLS // LANES
PAIRS = [(i, j) for i in range(4) for j in range(i, 4)]


def dot_nn(a, b):
    return lax.dot_general(a, b, (((1,), (0,)), ((), ())), preferred_element_type=f32)


def dot_nt(a, b):
    return lax.dot_general(a, b, (((1,), (1,)), ((), ())), preferred_element_type=f32)


def dot_tn(a, b):
    return lax.dot_general(a, b, (((0,), (0,)), ((), ())), preferred_element_type=f32)


def split2(x):
    hi = x.astype(bf16)
    return hi, (x - hi.astype(f32)).astype(bf16)


def split3(x):
    hi = x.astype(bf16)
    rest = x - hi.astype(f32)
    mid = rest.astype(bf16)
    return hi, mid, (rest - mid.astype(f32)).astype(bf16)


def stacked(dot, parts, other):
    rows = parts[0].shape[0]
    product = dot(jnp.concatenate(parts, axis=0), other)
    return functools.reduce(jnp.add, [product[k * rows : (k + 1) * rows] for k in range(len(parts))])


def two(dot, pair, other):
    return stacked(dot, pair, other)


def borrow(bits):
    out = list(bits)
    for at, bit in enumerate(out):
        if bit:
            out[at] = 0
            return tuple(out), 0
        out[at] = 1
    return tuple(out), 1


def tap_source(tap, row_bits, col_bits):
    r, c = divmod(tap, 3)
    src_r, down_r = (row_bits, 0) if r else borrow(row_bits)
    src_c, down_c = (col_bits, 0) if c else borrow(col_bits)
    return (int(r != 1), int(c != 1)), src_r, src_c, down_r, down_c


def plane_of(row_bits, col_bits):
    at = 0
    for r, c in zip(row_bits, col_bits):
        at = at * 4 + r * 2 + c
    return at


def stem_plane(quarter, row_bits, col_bits):
    row = quarter[0] + 2 * row_bits[0] + 4 * row_bits[1]
    return row * 8 + quarter[1] + 2 * col_bits[0] + 4 * col_bits[1]


def all_bits(pairs):
    for at in range(4**pairs):
        digits = [(at >> (2 * (pairs - 1 - k))) & 3 for k in range(pairs)]
        yield at, tuple(d >> 1 for d in digits), tuple(d & 1 for d in digits)


def moved(value, down_r, down_c, marks):
    if not (down_r or down_c):
        return value
    step = SIDE * down_r + down_c
    column = {(1, 0): 1, (0, 1): 2, (1, 1): 3}[(down_r, down_c)]
    return pltpu.roll(value, step, 0) * marks[:, column : column + 1]


def moved_back(value, down_r, down_c, marks):
    if not (down_r or down_c):
        return value
    step = SIDE * down_r + down_c
    column = {(1, 0): 1, (0, 1): 2, (1, 1): 3}[(down_r, down_c)]
    return pltpu.roll(value * marks[:, column : column + 1], BOTH - step, 0)


def erf(x):
    x = jnp.clip(x, -3.832506856900711, 3.832506856900711)
    s = x * x
    top = 2.2905065861350646e-4
    for coef in (3.4082910107109506e-3, 5.0955695062380861e-2, 1.8520832239976145e-1, 1.128379143519084):
        top = top * s + coef
    low = -1.1791602954361697e-7
    for coef in (
        2.3547966471313185e-5,
        1.0179625278914885e-3,
        1.4070470171167667e-2,
        1.1098505178285362e-1,
        4.9746925110067538e-1,
        1.0,
    ):
        low = low * s + coef
    return x * top / low


def total(x):
    return jnp.sum(jnp.sum(x, axis=1, keepdims=True), axis=0, keepdims=True)


def norm_images(value, mask, count):
    parts, scales = [], []
    for m in range(MICRO):
        v = value[m * ROWS : (m + 1) * ROWS]
        k = mask[m * ROWS : (m + 1) * ROWS]
        center = (v - total(v * k) / count) * k
        scale = lax.rsqrt(total(center * center) / count + norm_epsilon)
        parts.append(center * scale)
        scales.append(scale)
    return jnp.concatenate(parts, axis=0), scales


def norm_images_back(grad, hat, scales, gain, mask, count):
    parts = []
    for m in range(MICRO):
        at = slice(m * ROWS, (m + 1) * ROWS)
        g = grad[at] * gain
        h = hat[at]
        parts.append((g - total(g) / count - h * (total(g * h) / count)) * scales[m] * mask[at])
    return jnp.concatenate(parts, axis=0)


def rowsum(x):
    return jnp.sum(x, axis=0, keepdims=True)


def halves(low, high):
    lane = lax.broadcasted_iota(jnp.int32, low.shape, 1)
    return jnp.where(lane < LANES // 2, pltpu.roll(low, LANES // 2, 1), pltpu.roll(high, LANES // 2, 1))


def lanes_of(ref, row, count):
    return jnp.concatenate([ref[row + at : row + at + 1, :] for at in range(count)], axis=1)


def head_masks():
    row = lax.broadcasted_iota(jnp.int32, (C4 // GROUP, C4), 0)
    col = lax.broadcasted_iota(jnp.int32, (C4 // GROUP, C4), 1)
    return col // GROUP == row, col % GROUP == row // MICRO, row % MICRO == 0


class Copies:
    def __init__(self, sems):
        self.sems = sems
        self.count = 2

    def start_shared(self, source, target):
        pltpu.make_async_copy(source, target, self.sems.at[0]).start()

    def start_out(self, source, target):
        pltpu.make_async_copy(source, target, self.sems.at[1]).start()

    def out(self, source):
        return pltpu.make_async_copy(source, source, self.sems.at[1])

    def shared(self, target):
        return pltpu.make_async_copy(target, target, self.sems.at[0])

    def start(self, source, target):
        copy = self.make(source, target)
        copy.start()
        return copy

    def make(self, source, target):
        copy = pltpu.make_async_copy(source, target, self.sems.at[self.count])
        self.count += 1
        return copy


def pieces_of(gathered):
    for number, (unused_array, masks, base) in enumerate(gathered):
        for place in range(2 ** len(masks)):
            index, owner = [], base
            for k, mask in enumerate(masks):
                bit = (place >> k) & 1
                index.append(bit)
                owner ^= mask * bit
            yield number, tuple(index), owner


def conv_kernel(flat_share, gathered, *refs):
    if flat_share % LANES:
        conv_body(None, None, *refs)
    else:
        count = [len(side) for side in gathered]
        held = [refs[1 : 1 + count[0]], refs[1 + count[0] : 1 + sum(count)]]
        conv_body(flat_share, (gathered, held), refs[0], refs[-1], *refs[1 + sum(count) : -1])


def conv_body(
    flat_share,
    arrived,
    whole_ref,
    flat_ref,
    unused_hbm,
    p0_hbm,
    tm_hbm,
    t64_hbm,
    pm_hbm,
    marks_ref,
    p1_hbm,
    p2_hbm,
    p3e_hbm,
    p3o_hbm,
    k1t_hbm,
    k2_hbm,
    k3e_hbm,
    k3o_hbm,
    stream_ref,
    rest_ref,
    wide_ref,
    hb_ref,
    count_ref,
    p0_ref,
    tm_ref,
    t64_ref,
    pm_ref,
    p1_ref,
    p2_ref,
    p3e_ref,
    p3o_ref,
    k1t_ref,
    k2_ref,
    k3e_ref,
    k3o_ref,
    s1_ref,
    s2_ref,
    s3_ref,
    t2_ref,
    t3_ref,
    w0_ref,
    k1f_ref,
    sems,
    *near_refs,
):
    copies = Copies(sems)
    if arrived is not None:
        near_ref = near_refs[0]
        gathered, held = arrived
        half_rows = near_ref.shape[1] // 2
        me = whole_ref[5]
        for side in range(2):
            for number, index, owner in pieces_of(gathered[side]):
                copies.start_shared(
                    held[side][number].at[index], near_ref.at[me ^ owner, pl.ds(side * half_rows, half_rows), :]
                )
        flat_copy = copies.shared(near_ref)
    p0_copy = copies.start(p0_hbm, p0_ref)
    t64_copy = copies.start(t64_hbm, t64_ref)
    tm_copy = copies.start(tm_hbm, tm_ref)
    pm_copy = copies.start(pm_hbm, pm_ref)
    outward = []
    if arrived is not None:
        flat_copy.wait()
        flat_rows = flat_share // LANES
        counted = jnp.zeros((1, LANES), f32)
        for at in range(near_ref.shape[0]):
            flat_ref[pl.ds(at * flat_rows, flat_rows), :] = near_ref[at, pl.ds(0, flat_rows), :].astype(f32)
            counted = counted + near_ref[at, pl.ds(flat_rows, 1), :].astype(f32)
        count_ref[...] = jnp.broadcast_to(counted, (8, LANES))
    else:
        count_ref[...] = jnp.zeros((8, LANES), f32)
    marks = marks_ref[...]
    lane = lax.broadcasted_iota(jnp.int32, (BOTH, LANES), 1)
    lane1 = lax.broadcasted_iota(jnp.int32, (1, LANES), 1)
    depth = IN_CH * 49
    for at in range(C1):
        row, shift = divmod(depth * at, LANES)
        line = lanes_of(flat_ref, row, 3)
        if shift:
            line = pltpu.roll(line, 3 * LANES - shift, 1)
        w0_ref[at : at + 1, :] = line[:, : 2 * LANES]
    w0 = w0_ref[...].astype(bf16)
    w0 = jnp.concatenate([w0, w0], axis=0)
    b0 = flat_ref[ROW_B0 : ROW_B0 + 1, :]
    b0 = jnp.where(lane1 < C1, pltpu.roll(b0, C1, 1), b0)
    quarter = 16 * BOTH
    p0_copy.wait()
    for at in range(4):
        span = pl.ds(at * quarter, quarter)
        s1_ref[span, :] = (dot_nt(p0_ref[span, :], w0) + b0).astype(bf16).astype(f32)

    def tap_value(ref, pairs, tap, row_bits, col_bits, cols):
        q, src_r, src_c, down_r, down_c = tap_source(tap, row_bits, col_bits)
        if pairs == 2:
            at = stem_plane(q, src_r, src_c)
        else:
            at = (q[0] * 2 + q[1]) * 4**pairs + plane_of(src_r, src_c)
        return moved(ref[pl.ds(at * BOTH, BOTH), cols], down_r, down_c, marks)

    half = C2 // 2
    t64_copy.wait()
    for odd in range(2):
        block = jnp.concatenate(
            [flat_ref[pl.ds(ROW_K1 + 4 * odd + j, half, stride=9), :].astype(bf16) for j in range(5)], axis=1
        )
        block = dot_nn(block, t64_ref[pl.ds(C1 * (1 - odd), 5 * LANES), :])
        for j in range(5):
            k1f_ref[j, pl.ds(odd, half, stride=2), :] = block[:, j * LANES : (j + 1) * LANES]
    for j in range(5):
        k1t_ref[:, pl.ds(j * LANES, LANES)] = k1f_ref[j].astype(bf16)
    outward.append(copies.start(k1t_ref, k1t_hbm))
    everything = slice(None)
    for at, rb, cb in all_bits(2):
        for pair in range(5):
            left = tap_value(s1_ref, 2, 2 * pair, rb, cb, everything)
            if pair < 4:
                right = tap_value(s1_ref, 2, 2 * pair + 1, rb, cb, everything)
            else:
                right = jnp.zeros_like(left)
            p1_ref[pl.ds(at * BOTH, BOTH), pl.ds(pair * LANES, LANES)] = jnp.where(
                lane < C1, left, right
            ).astype(bf16)
    outward.append(copies.start(p1_ref, p1_hbm))
    b1 = flat_ref[ROW_B1 : ROW_B1 + 1, :]
    s2_ref[...] = (dot_nt(p1_ref[...], k1t_ref[...]) + b1).astype(bf16).astype(f32)
    for j in range(TAPS):
        k2_ref[pl.ds(0, C3), pl.ds(j * LANES, LANES)] = flat_ref[pl.ds(ROW_K2 + j, C3, stride=TAPS), :].astype(bf16)
    k2_ref[pl.ds(C3, C3P - C3), :] = jnp.zeros((C3P - C3, TAPS * LANES), bf16)
    outward.append(copies.start(k2_ref, k2_hbm))
    b2 = lanes_of(flat_ref, ROW_B2, 3)
    b2 = jnp.where(lax.broadcasted_iota(jnp.int32, b2.shape, 1) < C3, b2, 0.0)
    for at, rb, cb in all_bits(1):
        for tap in range(TAPS):
            t2_ref[pl.ds(at * BOTH, BOTH), pl.ds(tap * LANES, LANES)] = tap_value(
                s2_ref, 1, tap, rb, cb, everything
            ).astype(bf16)
    tm_copy.wait()
    p2_ref[...] = dot_nn(t2_ref[...], tm_ref[...]).astype(bf16)
    outward.append(copies.start(p2_ref, p2_hbm))
    s3_ref[...] = (dot_nt(p2_ref[...], k2_ref[...]) + b2).astype(bf16).astype(f32)
    for part in range(3):
        for tap in range(TAPS):
            t3_ref[pl.ds(part * BOTH, BOTH), pl.ds(tap * LANES, LANES)] = tap_value(
                s3_ref, 0, tap, (), (), pl.ds(part * LANES, LANES)
            ).astype(bf16)
    spread = dot_nn(t3_ref[...], tm_ref[...])
    spread = jnp.concatenate([spread[part * BOTH : (part + 1) * BOTH] for part in range(3)], axis=1)
    p3o_ref[...] = spread[:, :K3P].astype(bf16)
    p3e_ref[...] = pltpu.roll(spread, LANES // 2, 1)[:, :K3P].astype(bf16)
    for j in range(K3P // LANES):
        cols = pl.ds(j * LANES, LANES)
        k3e_ref[:, cols] = flat_ref[pl.ds(ROW_K3 + j, C4 // 2, stride=45), :].astype(bf16)
        k3o_ref[:, cols] = flat_ref[pl.ds(ROW_K3 + 23 + j, C4 // 2, stride=45), :].astype(bf16)
    for source, target in ((p3e_ref, p3e_hbm), (p3o_ref, p3o_hbm), (k3e_ref, k3e_hbm), (k3o_ref, k3o_hbm)):
        outward.append(copies.start(source, target))
    pm_copy.wait()
    apart = split3(
        jnp.concatenate([dot_nt(p3e_ref[...], k3e_ref[...]), dot_nt(p3o_ref[...], k3o_ref[...])], axis=1)
    )
    stream = stacked(dot_nn, apart, pm_ref[...])

    stream_ref[...] = stream

    amount = REST["head"]
    rest_ref[...] = halves(flat_ref[ROW_B3 : ROW_B3 + amount, :], flat_ref[ROW_B3 + 1 : ROW_B3 + 1 + amount, :])
    row_hb = ROW_B3 + REST["hb"]
    hb_ref[...] = halves(flat_ref[row_hb : row_hb + 8, :], flat_ref[row_hb + 1 : row_hb + 9, :])
    groups = C4 // GROUP
    row_head = ROW_B3 + REST["head"]
    low = pltpu.roll(flat_ref[pl.ds(row_head, groups, stride=SPAN), :], LANES // 2, 1)
    lane32 = lax.broadcasted_iota(jnp.int32, (groups, LANES), 1)
    for at in range(SPAN):
        high = pltpu.roll(flat_ref[pl.ds(row_head + at + 1, groups, stride=SPAN), :], LANES // 2, 1)
        wide_ref[:, pl.ds(at * LANES, LANES)] = jnp.where(lane32 < LANES // 2, low, high).astype(bf16)
        low = high
    wide_ref[:, pl.ds(SPAN * LANES, LANES)] = jnp.zeros((groups, LANES), bf16)
    for copy in outward:
        copy.wait()


def block_kernel(
    share,
    whole_ref,
    real_ref,
    got_hbm,
    stream_ref,
    rest_ref,
    wide_ref,
    hb_ref,
    marks_ref,
    near_ref,
    keep_hbm,
    send_hbm,
    dstream_ref,
    dblock_ref,
    dfb1_ref,
    small_ref,
    pooled_ref,
    dlog_ref,
    factor_ref,
    hid_ref,
    z_ref,
    per_ref,
    mats_ref,
    sems,
):
    copies = Copies(sems)
    me = whole_ref[5]
    for mat in range(2):
        rows = mats_ref.shape[2]
        copies.start_shared(got_hbm.at[:, pl.ds(mat * rows, rows), :], mats_ref.at[mat])
    mats_copy = copies.shared(mats_ref)
    marks = marks_ref[...]
    stream = stream_ref[...]
    b3 = lanes_of(rest_ref, REST["b3"], 4)
    gain1, shift1, scale1, gain2, shift2, scale2 = (lanes_of(rest_ref, REST["block"] + 4 * k, 4) for k in range(6))
    fb1 = lanes_of(rest_ref, REST["fb1"], HID // LANES)
    fb2 = lanes_of(rest_ref, REST["fb2"], 4)
    gain3, shift3 = (lanes_of(rest_ref, REST["final"] + 4 * k, 4) for k in range(2))

    stream = stream + b3
    mask = marks[:, 0:1]
    per_count = marks[:, 4:5]
    cells = real_ref[4]
    count = real_ref[5]
    near = near_ref[...]
    hat1, rs1 = norm_images(stream, mask, count)
    u = (hat1 * gain1 + shift1) * mask
    u3 = split3(u)
    around = dot_nn(near, u3[0]) + (dot_nn(near, u3[1]) + dot_nn(near, u3[2]))
    pool = around * per_count - u
    stream1 = stream + scale1 * pool
    hat2, rs2 = norm_images(stream1, mask, count)
    normed = ((hat2 * gain2 + shift2) * mask).astype(bf16)
    mats_copy.wait()
    blocks = C4 // LANES

    def matrix(mat, part):
        return mats_ref[mat, :, pl.ds(part * share, share), :].reshape(HID, LANES)

    def lanes(x, part):
        return x[:, part * LANES : (part + 1) * LANES]

    hidden = fb1
    for part in range(blocks):
        hidden = hidden + dot_nt(lanes(normed, part), matrix(0, part))
    hid_ref[...] = hidden
    active = (hidden * (0.5 * (1.0 + erf(hidden * math.sqrt(0.5))))).astype(bf16)
    branch = jnp.concatenate([dot_nn(active, matrix(1, part)) for part in range(blocks)], axis=1) + fb2
    stream2 = stream1 + scale2 * branch
    hat3, rs3 = norm_images(stream2, mask, count)
    outs = (hat3 * gain3 + shift3) * mask
    row8 = lax.broadcasted_iota(jnp.int32, (8, 1), 0)
    first, second = row8 == 0, row8 == 1

    def by_row(a, b):
        return jnp.where(first, a, jnp.where(second, b, 0.0))

    pooled = (by_row(rowsum(outs[:ROWS]), rowsum(outs[ROWS:])) / cells).astype(bf16)
    pooled_f = pooled.astype(f32)
    pooled_ref[...] = pooled_f
    in_group, in_place, own_row = head_masks()
    picked = jnp.where(in_place, jnp.where(own_row, pooled_f[0:1, :], pooled_f[1:2, :]), 0.0).astype(bf16)
    by_place = dot_nt(picked, in_group.astype(bf16)).astype(bf16)
    z_ref[...] = dot_nn(by_place, wide_ref[...])
    column = lax.broadcasted_iota(jnp.int32, (8, CLSP), 1)
    hb = lanes_of(hb_ref, 0, 8)
    logits = jnp.zeros((MICRO, CLSP), f32)
    for place in range(GROUP):
        at, shift = divmod(CLS * place, LANES)
        window = z_ref[pl.ds(MICRO * place, MICRO), pl.ds(at * LANES, CLSP + LANES)]
        if shift:
            window = pltpu.roll(window, CLSP + LANES - shift, 1)
        logits = logits + window[:, :CLSP]
    logits = by_row(logits[0:1], logits[1:2]) + hb
    logits = jnp.where(column < CLS, logits, -1e30)
    top = jnp.max(logits, axis=1, keepdims=True)
    powers = jnp.exp(logits - top)
    mass = jnp.sum(powers, axis=1, keepdims=True)
    own = jnp.where(first, whole_ref[0], whole_ref[1])
    other = jnp.where(first, whole_ref[2], whole_ref[3])
    mix = by_row(real_ref[0], real_ref[1])
    target = jnp.where(column == own, mix, 0.0) + jnp.where(column == other, 1.0 - mix, 0.0)
    valid = by_row(real_ref[2], real_ref[3])
    logp = logits - top - jnp.log(mass)
    losses = -jnp.sum(target * logp, axis=1, keepdims=True) * valid
    loss = split3(jnp.broadcast_to(jnp.sum(losses, axis=0, keepdims=True), (1, LANES)))
    dlogits = (powers / mass * jnp.sum(target, axis=1, keepdims=True) - target) * valid
    dlog_ref[...] = dlogits
    padded = jnp.concatenate([dlogits, jnp.zeros((8, LANES), f32)], axis=1)
    for place in range(GROUP):
        at, shift = divmod(CLS * place, LANES)
        window = pltpu.roll(padded, shift, 1) if shift else padded
        per_group = two(dot_nt, split2(window), wide_ref[:, pl.ds(at * LANES, CLSP + LANES)])
        per_ref[pl.ds(MICRO * place, MICRO), :] = per_group[:MICRO]
    per3 = split3(per_ref[...])
    ones = in_group.astype(bf16)
    by_channel = dot_nn(per3[0], ones) + (dot_nn(per3[1], ones) + dot_nn(per3[2], ones))
    dpooled = by_row(
        rowsum(jnp.where(in_place & own_row, by_channel, 0.0)),
        rowsum(jnp.where(in_place & ~own_row, by_channel, 0.0)),
    )
    dpooled = dpooled / cells
    douts = jnp.concatenate(
        [
            jnp.broadcast_to(dpooled[0:1], (ROWS, C4)),
            jnp.broadcast_to(dpooled[1:2], (ROWS, C4)),
        ],
        axis=0,
    ) * mask
    row8w = lax.broadcasted_iota(jnp.int32, (8, C4), 0)

    def stack8(values):
        out = jnp.zeros((8, C4), f32)
        for at, v in enumerate(values):
            out = jnp.where(row8w == at, v, out)
        return out

    dgain3, dshift3 = rowsum(douts * hat3), rowsum(douts)
    dstream2 = norm_images_back(douts, hat3, rs3, gain3, mask, count)
    dscale2 = rowsum(dstream2 * branch)
    dbranch = dstream2 * scale2
    dfb2 = rowsum(dbranch)
    dbr = split2(dbranch)
    dactive = None
    for part in range(blocks):
        term = two(dot_nt, (lanes(dbr[0], part), lanes(dbr[1], part)), matrix(1, part))
        dactive = term if dactive is None else dactive + term
    hidden = hid_ref[...]
    slope = 0.5 * (1.0 + erf(hidden * math.sqrt(0.5))) + hidden * (
        jnp.exp(-0.5 * hidden * hidden) * (1.0 / math.sqrt(2.0 * math.pi))
    )
    dhidden = dactive * slope
    dfb1_ref[...] = jnp.broadcast_to(rowsum(dhidden), (8, HID))
    dhid = split2(dhidden)

    core, corner_high, corner_low = whole_ref[4], (me // 4) % 2, (me // 2) % 2
    active_f = active.astype(f32)
    sides = (
        (jnp.concatenate([d.astype(f32) for d in dhid], axis=0), jnp.concatenate([normed, normed], axis=0)),
        (jnp.concatenate([active_f, active_f], axis=0), jnp.concatenate(dbr, axis=0)),
    )
    each = 2 * share
    factor_ref[:, pl.ds(FACTOR_LOSS, FACTOR_ROWS - FACTOR_LOSS), :] = jnp.zeros(
        (2, FACTOR_ROWS - FACTOR_LOSS, LANES), bf16
    )
    for mat, (hidden_side, channel_side) in enumerate(sides):
        for at in range(HID // LANES):
            cols = slice(at * LANES, (at + 1) * LANES)
            factor_ref[mat, pl.ds(at * LANES, LANES), :] = hidden_side[:, cols].T.astype(bf16)
        for part in range(blocks):
            factor_ref[mat, pl.ds(HID + part * LANES, LANES), :] = lanes(channel_side, part)

        for k in range(3):
            factor_ref[mat, pl.ds(FACTOR_LOSS + k, 1), :] = loss[k]

        def send_out(mat, target):
            for chip in range(HID // each):
                square, high, low = chip // 4, (chip // 2) % 2, chip % 2
                for side, (bit, mine, place) in enumerate(((high, corner_high, low), (low, corner_low, high))):
                    begin = jnp.where(mine == bit, FACTOR_OWN[side], FACTOR_OTHER[side])
                    to = pl.multiple_of(begin + (square * 2 + place) * share, share)
                    source = factor_ref.at[mat, pl.ds(chip * each + side * share, share), :]
                    copies.start_out(source, target.at[pl.ds(to, share), :])
            copies.start_out(
                factor_ref.at[mat, pl.ds(HID, blocks * LANES), :], target.at[pl.ds(FACTOR_CHANNELS, blocks * LANES), :]
            )
            rest = pl.ds(FACTOR_LOSS, FACTOR_ROWS - FACTOR_LOSS)
            copies.start_out(factor_ref.at[mat, rest, :], target.at[rest, :])

        pl.when(core == mat)(functools.partial(send_out, mat, keep_hbm))
        pl.when(core != mat)(functools.partial(send_out, mat, send_hbm))
    dnormed = jnp.concatenate([two(dot_nn, dhid, matrix(0, part)) for part in range(blocks)], axis=1)
    dgain2, dshift2 = rowsum(dnormed * hat2), rowsum(dnormed * mask)
    dstream1 = dstream2 + norm_images_back(dnormed, hat2, rs2, gain2, mask, count)
    dscale1 = rowsum(dstream1 * pool)
    dpool = dstream1 * scale1
    back = split3(dpool * per_count)
    du = dot_nn(near, back[0]) + (dot_nn(near, back[1]) + dot_nn(near, back[2])) - dpool
    dgain1, dshift1 = rowsum(du * hat1), rowsum(du)
    dstream = dstream1 + norm_images_back(du, hat1, rs1, gain1, mask, count)
    dblock_ref[...] = stack8([dgain1, dshift1, dscale1, dgain2, dshift2, dscale2])
    small_ref[...] = stack8([rowsum(dstream), dfb2, dgain3, dshift3])
    dstream_ref[...] = dstream
    copies.out(factor_ref).wait()


def backward_kernel(
    unused_one_ref,
    unused_two_ref,
    dstream_ref,
    p0_hbm,
    p1_hbm,
    p2_hbm,
    p3e_ref,
    p3o_ref,
    k1t_hbm,
    k2_hbm,
    k3e_hbm,
    k3o_hbm,
    tm_hbm,
    t64_hbm,
    pm_ref,
    marks_ref,
    dblock_ref,
    dfb1_ref,
    small_ref,
    pooled_ref,
    dlog_ref,
    whole_ref,
    keep_a_hbm,
    keep_b_hbm,
    send_a_hbm,
    send_b_hbm,
    out_ref,
    ds3_ref,
    ds2_ref,
    ds1_ref,
    dt_ref,
    dk1t_ref,
    rest_ref,
    p0_ref,
    p1_ref,
    p2_ref,
    k1t_ref,
    k2_ref,
    k3e_ref,
    k3o_ref,
    tm_ref,
    t64_ref,
    sems,
):
    copies = Copies(sems)
    third_copies = [copies.start(*x) for x in ((k3e_hbm, k3e_ref), (k3o_hbm, k3o_ref), (tm_hbm, tm_ref))]
    early_copies = [
        copies.start(*x)
        for x in (
            (p2_hbm, p2_ref),
            (k2_hbm, k2_ref),
            (p1_hbm, p1_ref),
            (k1t_hbm, k1t_ref),
            (t64_hbm, t64_ref),
            (p0_hbm, p0_ref),
        )
    ]
    marks = marks_ref[...]
    lane = lax.broadcasted_iota(jnp.int32, (BOTH, LANES), 1)
    lane1 = lax.broadcasted_iota(jnp.int32, (1, LANES), 1)
    wide = TAPS * LANES
    grad3 = split3(dstream_ref[...])
    apart = stacked(dot_nt, grad3, pm_ref[...])
    half = C4 // 2
    even, odd = split2(apart[:, :half]), split2(apart[:, half:])
    tall_even, tall_odd = jnp.concatenate(even, axis=0), jnp.concatenate(odd, axis=0)

    def by_even(cols):
        return dot_tn(tall_even, jnp.concatenate([p3e_ref[:, cols]] * 2, axis=0))

    def by_odd(cols):
        return dot_tn(tall_odd, jnp.concatenate([p3o_ref[:, cols]] * 2, axis=0))

    last = K3P // LANES - 1
    for j in range(last):
        cols = pl.ds(j * LANES, LANES)
        out_ref[pl.ds(ROW_K3 + 23 + j, half, stride=45), :] = by_odd(cols)
        if j:
            out_ref[pl.ds(ROW_K3 + j, half, stride=45), :] = by_even(cols)
    cols = pl.ds(last * LANES, LANES)
    out_ref[pl.ds(ROW_K3 + last, half, stride=45), :] = by_even(cols)
    tail = by_odd(cols)
    begin = by_even(pl.ds(0, LANES))
    rows = lax.broadcasted_iota(jnp.int32, (half, LANES), 0)
    out_ref[pl.ds(ROW_K3, half, stride=45), :] = begin + jnp.where(rows == 0, 0.0, pltpu.roll(tail, 1, 0))
    tail = tail[half - 1 : half]
    ds3_ref[...] = jnp.zeros_like(ds3_ref)
    position = lax.broadcasted_iota(jnp.int32, (BOTH, K3P), 1)
    for copy in third_copies:
        copy.wait()
    nat = jnp.where(position < LANES // 2, 0.0, two(dot_nn, even, k3e_ref[...]))
    nat = pltpu.roll(nat, K3P - LANES // 2, 1) + jnp.where(
        position < C3 * TAPS, two(dot_nn, odd, k3o_ref[...]), 0.0
    )
    for part in range(3):
        width = min(wide, K3P - part * wide)
        pieces = split2(nat[:, part * wide : part * wide + width])
        by_tap = dot_nt(pieces[0], tm_ref[:, pl.ds(0, width)]) + dot_nt(pieces[1], tm_ref[:, pl.ds(0, width)])
        for tap in range(TAPS):
            q, src_r, src_c, down_r, down_c = tap_source(tap, (), ())
            at = q[0] * 2 + q[1]
            ds3_ref[pl.ds(at * BOTH, BOTH), pl.ds(part * LANES, LANES)] += moved_back(
                by_tap[:, tap * LANES : (tap + 1) * LANES], down_r, down_c, marks
            )
    lead = 5

    def put(name, value):
        for k in range(value.shape[1] // LANES):
            at = lead + REST[name] + k
            rest_ref[at : at + 1, :] = value[:, k * LANES : (k + 1) * LANES]

    rest_ref[0:8, :] = jnp.zeros((8, LANES), f32)
    put("b3", small_ref[0:1, :])
    for k in range(6):
        at = lead + REST["block"] + 4 * k
        for i in range(4):
            rest_ref[at + i : at + i + 1, :] = dblock_ref[k : k + 1, i * LANES : (i + 1) * LANES]
    put("fb1", dfb1_ref[0:1, :])
    put("fb2", small_ref[1:2, :])
    put("final", jnp.concatenate([small_ref[2:3, :], small_ref[3:4, :]], axis=1))
    dlog = dlog_ref[...]
    put("hb", dlog[0:1] + dlog[1:2])
    rest_ref[lead + REST["end"] : lead + REST["end"] + 11, :] = jnp.zeros((11, LANES), f32)
    pooled = pooled_ref[...]
    in_group, in_place, own_row = head_masks()
    picked = jnp.where(in_place, jnp.where(own_row, pooled[0:1, :], pooled[1:2, :]), 0.0).astype(bf16)
    by_group = dot_nt(in_group.astype(bf16), picked)
    padded = jnp.concatenate([dlog, jnp.zeros((8, LANES), f32)], axis=1)
    groups = C4 // GROUP
    written = -1
    for place in range(GROUP):
        at, shift = divmod(CLS * place, LANES)
        window = pltpu.roll(padded, shift, 1) if shift else padded
        ours = by_group[:, MICRO * place : MICRO * place + 1]
        others = by_group[:, MICRO * place + 1 : MICRO * place + 2]
        for k in range(CLSP // LANES + 1):
            if (at + k) * LANES >= CLS * (place + 1):
                break
            block = slice(k * LANES, (k + 1) * LANES)
            value = ours * window[0:1, block] + others * window[1:2, block]
            target = pl.ds(lead + REST["head"] + at + k, groups, stride=SPAN)
            if at + k == written:
                rest_ref[target, :] += value
            else:
                rest_ref[target, :] = value
            written = at + k
    first = ROW_B3 + 3
    out_ref[ROW_B3 : first, :] = halves(rest_ref[lead - 1 : lead + 2, :], rest_ref[lead : lead + 3, :])
    out_ref[ROW_B3 : ROW_B3 + 1, :] += tail
    step = 508
    for at in range(0, REST["end"], step):
        out_ref[first + at : first + at + step, :] = halves(
            rest_ref[lead + 2 + at : lead + 2 + at + step, :], rest_ref[lead + 3 + at : lead + 3 + at + step, :]
        )
    end = first + REST["end"]
    out_ref[end : out_ref.shape[0], :] = jnp.zeros((out_ref.shape[0] - end, LANES), f32)
    chips, cut, unused_lanes = keep_a_hbm.shape
    each = cut + keep_b_hbm.shape[1]
    core = whole_ref[4]

    def send_chunks(chunks):
        for chunk in chunks:
            for keep, send, at, rows in ((keep_a_hbm, send_a_hbm, 0, cut), (keep_b_hbm, send_b_hbm, cut, each - cut)):
                source = out_ref.at[pl.ds(chunk * each + at, rows), :]
                ours, theirs = (keep, send) if chunk % 2 == 0 else (send, keep)
                pl.when(core == 0)(functools.partial(copies.start_out, source, ours.at[chunk // 2]))
                pl.when(core != 0)(functools.partial(copies.start_out, source, theirs.at[chunk // 2]))

    bound = -(-(ROW_K3 + 1) // each)
    send_chunks(range(bound, 2 * chips))
    for copy in early_copies:
        copy.wait()
    db2 = rowsum(ds3_ref[...])
    for k in range(2):
        out_ref[ROW_B2 + k : ROW_B2 + k + 1, :] = db2[:, k * LANES : (k + 1) * LANES]
    out_ref[ROW_K3 : ROW_K3 + 1, :] += jnp.where(lane1 < LANES // 2, db2[:, 2 * LANES :], 0.0)
    grad = split2(ds3_ref[...])
    grad_real = (grad[0][:, :C3], grad[1][:, :C3])
    for j in range(TAPS):
        cols = pl.ds(j * LANES, LANES)
        value = dot_tn(grad[0], p2_ref[:, cols]) + dot_tn(grad[1], p2_ref[:, cols])
        out_ref[pl.ds(ROW_K2 + j, C3, stride=TAPS), :] = value[:C3]
    pieces = split2(two(dot_nn, grad, k2_ref[...]))
    dt_ref[...] = two(dot_nt, pieces, tm_ref[...])
    ds2_ref[...] = jnp.zeros_like(ds2_ref)
    for at, rb, cb in all_bits(1):
        for tap in range(TAPS):
            q, src_r, src_c, down_r, down_c = tap_source(tap, rb, cb)
            to = (q[0] * 2 + q[1]) * 4 + plane_of(src_r, src_c)
            ds2_ref[pl.ds(to * BOTH, BOTH), :] += moved_back(
                dt_ref[pl.ds(at * BOTH, BOTH), pl.ds(tap * LANES, LANES)], down_r, down_c, marks
            )
    out_ref[ROW_B1 : ROW_B1 + 1, :] = rowsum(ds2_ref[...])
    grad = split2(ds2_ref[...])
    few = C2 // 2
    for j in range(5):
        cols = pl.ds(j * LANES, LANES)
        dk1t_ref[j] = dot_tn(grad[0], p1_ref[:, cols]) + dot_tn(grad[1], p1_ref[:, cols])
    evens, odds = (
        two(
            dot_nt,
            split2(jnp.concatenate([dk1t_ref[j, pl.ds(odd, few, stride=2), :] for j in range(5)], axis=1)),
            t64_ref[pl.ds(C1 * (1 - odd), 5 * LANES), :],
        )
        for odd in range(2)
    )
    for j in range(9):
        if j < 4:
            value = evens[:, j * LANES : (j + 1) * LANES]
        elif j == 4:
            value = evens[:, 4 * LANES :] + odds[:, :LANES]
        else:
            value = odds[:, (j - 4) * LANES : (j - 3) * LANES]
        out_ref[pl.ds(ROW_K1 + j, few, stride=9), :] = value
    ds1_ref[...] = jnp.zeros_like(ds1_ref)
    for pair in range(5):
        values = two(dot_nn, grad, k1t_ref[:, pl.ds(pair * LANES, LANES)])
        for at, rb, cb in all_bits(2):
            here = values[at * BOTH : (at + 1) * BOTH]
            for side in range(2):
                tap = 2 * pair + side
                if tap >= TAPS:
                    continue
                q, src_r, src_c, down_r, down_c = tap_source(tap, rb, cb)
                to = stem_plane(q, src_r, src_c)
                mine = (lane < C1) if side == 0 else (lane >= C1)
                ds1_ref[pl.ds(to * BOTH, BOTH), :] += moved_back(
                    jnp.where(mine, here, 0.0), down_r, down_c, marks
                )
    db0 = rowsum(ds1_ref[...])
    db0 = db0 + pltpu.roll(db0, LANES // 2, 1)
    stem = jnp.zeros((LANES, 2 * LANES), f32)
    for at in range(4):
        span = pl.ds(at * 16 * BOTH, 16 * BOTH)
        grad = split2(ds1_ref[span, :])
        stem = stem + (dot_tn(grad[0], p0_ref[span, :]) + dot_tn(grad[1], p0_ref[span, :]))
    stem = stem[:C1] + stem[C1:]
    depth = IN_CH * 49
    held = jnp.zeros((1, 3 * LANES), f32)
    done = 0
    for at in range(C1):
        row, shift = divmod(depth * at, LANES)
        line = jnp.concatenate([stem[at : at + 1], jnp.zeros((1, LANES), f32)], axis=1)
        if shift:
            line = pltpu.roll(line, shift, 1)
        while done < row:
            out_ref[done : done + 1, :] = held[:, :LANES]
            held = jnp.concatenate([held[:, LANES:], jnp.zeros((1, LANES), f32)], axis=1)
            done += 1
        held = held + line
    out_ref[done : done + 1, :] = held[:, :LANES]
    if done < ROW_B0:
        out_ref[ROW_B0 : ROW_B0 + 1, :] = held[:, LANES : 2 * LANES]
    out_ref[ROW_B0 : ROW_B0 + 1, :] += jnp.where(lane1 < LANES // 2, 0.0, db0)

    send_chunks(range(bound))
    copies.out(out_ref).wait()


def product_kernel(whole_ref, keep_ref, got_ref, far_a_ref, far_b_ref, keep_a_ref, send_a_ref, keep_b_ref, send_b_ref, loss_ref):
    me = whole_ref[5]
    loss = keep_ref[pl.ds(FACTOR_LOSS, 8), :].astype(f32) + got_ref[pl.ds(FACTOR_LOSS, 8), :].astype(f32)
    loss_ref[...] = jnp.broadcast_to(loss[0:1] + (loss[1:2] + loss[2:3]), (8, LANES))
    squares, share, unused_channels = keep_a_ref.shape
    blocks = C4 // LANES
    ways = (
        (0, far_a_ref, 0, QUARTER, (me // 2) % 2, keep_a_ref, send_a_ref),
        (1, far_b_ref, C4, 0, (me // 4) % 2, keep_b_ref, send_b_ref),
    )
    for way, far_ref, far_hidden, far_channels, mine, to_keep_ref, to_send_ref in ways:
        own = pl.ds(FACTOR_OWN[way], QUARTER)
        hidden = jnp.concatenate(
            [keep_ref[own, :], got_ref[own, :]] + [far_ref[k, pl.ds(far_hidden, QUARTER), :] for k in range(2)], axis=1
        )
        channels = [
            jnp.concatenate(
                [
                    keep_ref[pl.ds(FACTOR_CHANNELS + part * LANES, LANES), :],
                    got_ref[pl.ds(FACTOR_CHANNELS + part * LANES, LANES), :],
                ]
                + [far_ref[k, pl.ds(far_channels + part * LANES, LANES), :] for k in range(2)],
                axis=0,
            )
            for part in range(blocks)
        ]
        product = dot_nn(hidden, jnp.concatenate(channels, axis=1))
        for square in range(squares):
            first, second = (product[(2 * square + k) * share : (2 * square + k + 1) * share] for k in range(2))
            to_keep_ref[square] = jnp.where(mine == 0, first, second)
            to_send_ref[square] = jnp.where(mine == 0, second, first)


def passes(a, b, dot, many):
    pairs = [(0, 0), (0, 1), (1, 0)]
    if many:
        pairs += [(0, 2), (1, 1), (2, 0)]
    axis = 0 if dot is dot_tn else 1
    return dot(
        jnp.concatenate([a[i] for i, unused in pairs], axis=axis),
        jnp.concatenate([b[j] for unused, j in pairs], axis=0),
    )


def gram_kernel(scale_ref, terms, momentum_ref, loss_ref, ortho_ref, new_ref, packed_ref):
    grad = functools.reduce(jnp.add, [term[...] for term in terms]) * scale_ref[0]
    new = 0.95 * momentum_ref[...] + grad
    new_ref[...] = new
    ortho = grad + 0.95 * new
    ortho_ref[...] = ortho
    parts = split3(ortho)

    def cut(k):
        return tuple(p[:, k * LANES : (k + 1) * LANES] for p in parts)

    for at, (i, j) in enumerate(PAIRS):
        block = passes(cut(i), cut(j), dot_tn, True)
        if at == 0:
            row = lax.broadcasted_iota(jnp.int32, block.shape, 0)
            col = lax.broadcasted_iota(jnp.int32, block.shape, 1)
            block = jnp.where((row == LANES - 1) & (col == 0), loss_ref[0:1, 0:1], block)
        packed_ref[pl.ds(at * LANES, LANES), :] = block


def newton_steps(gram, ortho, steps, last):
    wide_row = lax.broadcasted_iota(jnp.int32, (C4, C4), 0)
    wide_col = lax.broadcasted_iota(jnp.int32, (C4, C4), 1)
    for iteration in steps:
        many = iteration == 0
        split = split3 if many else split2
        parts = split(gram)
        poly = jnp.where(wide_row == wide_col, 3.4445, 0.0) + (
            -4.775 * gram + 2.0315 * passes(parts, parts, dot_nn, False)
        )
        poly_parts = split(poly)
        ortho = passes(split2(ortho), poly_parts, dot_nn, False)
        if iteration < last:
            gram = passes(split(passes(poly_parts, parts, dot_nn, many)), poly_parts, dot_nn, many)
    return gram, ortho


def newton_first_kernel(steps, packed_ref, ortho_ref, out_ref, gram_ref, loss_ref):
    row = lax.broadcasted_iota(jnp.int32, (LANES, LANES), 0)
    col = lax.broadcasted_iota(jnp.int32, (LANES, LANES), 1)
    trace = jnp.zeros((1, 1), f32)
    for at, (i, j) in enumerate(PAIRS):
        block = packed_ref[pl.ds(at * LANES, LANES), :]
        if at == 0:
            loss_ref[...] = jnp.broadcast_to(block[LANES - 1 : LANES, 0:1], (8, LANES))
            block = jnp.where((row == LANES - 1) & (col == 0), block.T, block)
        gram_ref[pl.ds(i * LANES, LANES), pl.ds(j * LANES, LANES)] = block
        if i == j:
            trace = trace + total(jnp.where(row == col, block, 0.0))
        else:
            gram_ref[pl.ds(j * LANES, LANES), pl.ds(i * LANES, LANES)] = block.T
    inverse = 1.0 / (jnp.sqrt(trace) + 1e-07)
    gram, ortho = newton_steps(
        gram_ref[...] * (inverse * inverse), ortho_ref[...] * inverse, range(steps), NS_ITERS - 1
    )
    gram_ref[...] = gram
    out_ref[...] = ortho


def newton_last_kernel(steps, gram_ref, ortho_ref, out_ref):
    unused_gram, ortho = newton_steps(gram_ref[...], ortho_ref[...], range(steps, NS_ITERS), NS_ITERS - 1)
    out_ref[...] = ortho


def shape(*dims, dtype=f32):
    return jax.ShapeDtypeStruct(dims, dtype)


def kernel_call(body, outs, scratch, smem, kept, count, micros, outs_kept=0, aliases=None):
    vmem = pl.BlockSpec(memory_space=pltpu.VMEM)
    scalar = pl.BlockSpec(memory_space=pltpu.SMEM)
    anywhere = pl.BlockSpec(memory_space=pl.ANY)
    if isinstance(kept, int):
        specs = [anywhere] * kept + [vmem] * (count - smem - kept)
    else:
        specs = [anywhere if k else vmem for k in kept[smem:]] + [vmem] * (count - len(kept))
    return pl.pallas_call(
        body,
        out_shape=outs,
        in_specs=[scalar] * smem + specs,
        out_specs=[anywhere] * outs_kept + [vmem] * (len(outs) - outs_kept),
        scratch_shapes=scratch,
        input_output_aliases=aliases or {},
        compiler_params=pltpu.CompilerParams(vmem_limit_bytes=60 * 1024 * 1024),
        cost_estimate=pl.CostEstimate(flops=10**6, bytes_accessed=micros * 3_000_000, transcendentals=0),
    )


def pack_kernel(valid_ref, mats_ref, flat_ref, out_ref, low_ref, high_ref):
    share = mats_ref.shape[1]
    blocks = C4 // LANES
    for mat in range(2):
        for part in range(blocks):
            at = (mat * blocks + part) * share
            out_ref[pl.ds(at, share), :] = mats_ref[mat, :, pl.ds(part * LANES, LANES)].astype(bf16)
    half, count = low_ref.shape[0], flat_ref.shape[0]
    low_ref[...] = flat_ref[pl.ds(0, half), :].astype(bf16)
    high_ref[pl.ds(0, count - half), :] = flat_ref[pl.ds(half, count - half), :].astype(bf16)
    left = 2 * half - count
    counted = (valid_ref[0] + valid_ref[1]).astype(f32)
    high_ref[pl.ds(count - half, left), :] = jnp.full((left, LANES), counted, f32).astype(bf16)


def run_pack(valid, mats, flat):
    half = (flat.shape[0] // 32 + 1) * 16
    outs = [shape(2 * C4 // LANES * mats.shape[1], LANES, dtype=bf16)] + [shape(half, LANES, dtype=bf16)] * 2
    return kernel_call(pack_kernel, outs, [], 1, 0, 3, 2)(valid, mats, flat)


def late_kernel(group_ref, unused_ref, out_ref):
    out_ref[0] = group_ref[0]


def run_late(group, tie):
    return pl.pallas_call(
        late_kernel,
        out_shape=shape(1, dtype=jnp.int32),
        in_specs=[pl.BlockSpec(memory_space=pltpu.SMEM), pl.BlockSpec(memory_space=pl.ANY)],
        out_specs=pl.BlockSpec(memory_space=pltpu.SMEM),
    )(group, tie)[0]


def run_conv(whole, flat, gathered, tie, moved, marks, flat_share, devices_count):
    half = C4 // 2
    moved_outs = [
        shape(16 * BOTH, 5 * LANES, dtype=bf16),
        shape(4 * BOTH, TAPS * LANES, dtype=bf16),
        shape(BOTH, K3P, dtype=bf16),
        shape(BOTH, K3P, dtype=bf16),
        shape(C2, 5 * LANES, dtype=bf16),
        shape(C3P, TAPS * LANES, dtype=bf16),
        shape(half, K3P, dtype=bf16),
        shape(half, K3P, dtype=bf16),
    ]
    outs = moved_outs + [
        shape(BOTH, C4),
        shape(REST["head"], LANES),
        shape(C4 // GROUP, (SPAN + 1) * LANES, dtype=bf16),
        shape(8, LANES),
        shape(8, LANES),
    ]
    scratch = [pltpu.VMEM(a.shape, a.dtype) for a in moved + moved_outs]
    scratch += [
        pltpu.VMEM((64 * BOTH, LANES), f32),
        pltpu.VMEM((16 * BOTH, LANES), f32),
        pltpu.VMEM((4 * BOTH, C3P), f32),
        pltpu.VMEM((4 * BOTH, TAPS * LANES), bf16),
        pltpu.VMEM((3 * BOTH, TAPS * LANES), bf16),
        pltpu.VMEM((C1, 2 * LANES), f32),
        pltpu.VMEM((5, C2, LANES), f32),
        pltpu.SemaphoreType.DMA((16,)),
    ]
    if flat_share % LANES:
        args = [whole, flat, tie] + moved + [marks]
        kept = [False, False] + [True] * 5
    else:
        arrays = [array for side in gathered for array, *unused in side]
        args = [whole] + arrays + [tie] + moved + [marks]
        kept = [False] + [True] * (len(arrays) + 5)
        scratch += [
            pltpu.VMEM((devices_count, 2 * arrays[0].shape[-2], LANES), bf16),
            pltpu.VMEM((devices_count * flat_share // LANES, LANES), f32),
        ]
    body = functools.partial(conv_kernel, flat_share, gathered)
    return kernel_call(body, outs, scratch, 1, kept, len(args), 12, 8)(*args)


def run_block(whole, real, got, made, marks, near, share):
    outs = [shape(FACTOR_ROWS, LANES, dtype=bf16)] * 2 + [
        shape(BOTH, C4),
        shape(8, C4),
        shape(8, HID),
        shape(8, C4),
        shape(8, C4),
        shape(8, CLSP),
    ]
    scratch = [
        pltpu.VMEM((2, FACTOR_ROWS, LANES), bf16),
        pltpu.VMEM((BOTH, HID), f32),
        pltpu.VMEM((C4 // GROUP, (SPAN + 1) * LANES), f32),
        pltpu.VMEM((MICRO * GROUP, C4 // GROUP), f32),
        pltpu.VMEM((2, HID // share, C4 // LANES * share, LANES), bf16),
        pltpu.SemaphoreType.DMA((2,)),
    ]
    args = [whole, real, got] + list(made) + [marks, near]
    body = functools.partial(block_kernel, share)
    return kernel_call(body, outs, scratch, 2, 1, len(args), 12, 2)(*args)


def run_backward(args, chips, each):
    scratch = [
        pltpu.VMEM((2 * chips * each, LANES), f32),
        pltpu.VMEM((4 * BOTH, C3P), f32),
        pltpu.VMEM((16 * BOTH, LANES), f32),
        pltpu.VMEM((64 * BOTH, LANES), f32),
        pltpu.VMEM((4 * BOTH, TAPS * LANES), f32),
        pltpu.VMEM((5, C2, LANES), f32),
        pltpu.VMEM((REST["end"] + 16, LANES), f32),
    ]
    moved = args[4:7] + args[9:15]
    scratch += [pltpu.VMEM(x.shape, x.dtype) for x in moved] + [pltpu.SemaphoreType.DMA((2 + len(moved),))]
    kept = [False] + [True] * 2 + [False] + [True] * 3 + [False] * 2 + [True] * 6
    cut = -(-each // 16) * 8
    outs = [shape(chips, cut, LANES), shape(chips, each - cut, LANES)] * 2

    def body(*refs):
        backward_kernel(*refs[1 : len(args)], refs[0], *refs[len(args) :])

    return kernel_call(body, outs, scratch, 1, kept, len(args), 20, 4)(*args)


def run_product(whole, through, keep, got, far_a, far_b, squares, share):
    outs = [shape(*x.shape) for x in through] + [shape(squares, share, C4)] * 4 + [shape(8, LANES)]
    count = len(through)

    def body(*refs):
        product_kernel(refs[0], *refs[1 + count : 5 + count], *refs[5 + 2 * count :])

    return kernel_call(body, outs, [], 1, count, 5 + count, 3, count, {1 + k: k for k in range(count)})(
        whole, *through, keep, got, far_a, far_b
    )


def sum_kernel(whole_ref, keep_one_ref, got_one_ref, keep_two_ref, got_two_ref, *out_refs):
    square = whole_ref[5] // 8
    share = keep_one_ref.shape[1]
    for j, out_ref in enumerate(out_refs):
        entry = square ^ j
        out_ref[pl.ds(0, share), :] = keep_one_ref[entry] + got_one_ref[entry]
        out_ref[pl.ds(share, share), :] = keep_two_ref[entry] + got_two_ref[entry]


def run_sum(whole, tie, keep_one, got_one, keep_two, got_two):
    squares, share, unused_channels = keep_one.shape
    outs = [shape(2 * share, C4)] * squares

    def body(*refs):
        sum_kernel(refs[0], *refs[2:])

    return kernel_call(body, outs, [], 1, 1, 6, 2)(whole, tie, keep_one, got_one, keep_two, got_two)


def halve_kernel(whole_ref, tie_ref, keep_a, got_a, keep_b, got_b, sent_a, left_a, sent_b, left_b):
    me = whole_ref[5]
    high, low = (me // 4) % 2, (me // 2) % 2
    for place in range(2):
        first, second = (keep_a[0, k, place] + got_a[0, k, place] for k in range(2))
        sent_a[place, 0] = jnp.where(high == 0, second, first)
        left_a[place, 0] = jnp.where(high == 0, first, second)
        first, second = (keep_b[0, place, k] + got_b[0, place, k] for k in range(2))
        sent_b[place, 0] = jnp.where(low == 0, second, first)
        left_b[place, 0] = jnp.where(low == 0, first, second)


def run_halve(whole, tie, keep_a, got_a, keep_b, got_b):
    squares = keep_a.shape[0] // 4
    inputs = [x.reshape(squares, 2, 2, *x.shape[1:]) for x in (keep_a, got_a, keep_b, got_b)]
    rows = [x.shape[3] for x in inputs]
    outs = [shape(2, squares, rows[0], LANES)] * 2 + [shape(2, squares, rows[2], LANES)] * 2
    return pl.pallas_call(
        halve_kernel,
        grid=(squares,),
        out_shape=outs,
        in_specs=[pl.BlockSpec(memory_space=pltpu.SMEM), pl.BlockSpec(memory_space=pl.ANY)]
        + [pl.BlockSpec((1, 2, 2, r, LANES), lambda i: (i, 0, 0, 0, 0)) for r in rows],
        out_specs=[pl.BlockSpec((2, 1, x.shape[2], LANES), lambda i: (0, i, 0, 0)) for x in outs],
        compiler_params=pltpu.CompilerParams(vmem_limit_bytes=63 * 1024 * 1024),
        cost_estimate=pl.CostEstimate(flops=10**6, bytes_accessed=15_000_000, transcendentals=0),
    )(whole, tie, *inputs)


def run_gram(scale, terms, momentum, loss):
    rows, count = momentum.shape[0], len(terms)
    outs = [shape(rows, C4), shape(rows, C4), shape(len(PAIRS) * LANES, LANES)]

    def body(*refs):
        gram_kernel(refs[0], refs[1 : 1 + count], *refs[1 + count :])

    return kernel_call(body, outs, [], 1, 0, 3 + count, 4)(scale, *terms, momentum, loss)


def run_newton_first(packed, ortho, steps):
    outs = [shape(*ortho.shape), shape(C4, C4), shape(8, LANES)]
    return kernel_call(functools.partial(newton_first_kernel, steps), outs, [], 0, 0, 2, 12)(packed, ortho)


def run_newton_last(ties, gram, ortho, steps):
    outs = [shape(*ortho.shape)]
    count = len(ties)

    def body(*refs):
        newton_last_kernel(steps, *refs[count:])

    return kernel_call(body, outs, [], 0, count, 2 + count, 8)(*ties, gram, ortho)[0]


def patches(images, resolution, partner_col, mix_col):
    pictures = images[:, 0].astype(f32)
    dims = (1, 1, RES_L, RES_L)
    inside = (lax.broadcasted_iota(jnp.int32, dims, 2) < resolution) & (
        lax.broadcasted_iota(jnp.int32, dims, 3) < resolution
    )
    mixing = mix_col[:, None, None, None]
    other = jnp.where(partner_col[:, None, None, None] == 0, pictures[0][None], pictures[1][None])
    pixels = jnp.where(inside, mixing * pictures + (1.0 - mixing) * other, 0.0).astype(bf16)
    padded = jnp.pad(pixels, ((0, 0), (0, 0), (2, 1), (2, 1)))
    size = RES_STEP + 3
    blocks = [
        padded[:, :, RES_STEP * i : RES_STEP * i + size, RES_STEP * j : RES_STEP * j + size]
        for i in range(SIDE)
        for j in range(SIDE)
    ]
    blocks = jnp.stack(blocks, axis=1).reshape(MICRO * SIDE * SIDE, IN_CH, size, size)
    depth = IN_CH * 49
    choose = jnp.eye(depth, dtype=bf16).reshape(IN_CH, 7, 7, depth).transpose(1, 2, 0, 3)
    columns = lax.conv_general_dilated(
        blocks,
        choose,
        (4, 4),
        ((0, 0), (0, 0)),
        dimension_numbers=("NCHW", "HWIO", "HWNC"),
        preferred_element_type=f32,
    ).astype(bf16)
    columns = columns.reshape(64, MICRO, SIDE * SIDE, depth)
    columns = jnp.pad(columns, ((0, 0), (0, 0), (0, ROWS - SIDE * SIDE), (0, 2 * LANES - depth)))
    return columns.reshape(64 * BOTH, 2 * LANES)


def tap_orders(zero):
    row = lax.broadcasted_iota(jnp.int32, (TAPS * LANES, TAPS * LANES), 0) + zero
    col = lax.broadcasted_iota(jnp.int32, (TAPS * LANES, TAPS * LANES), 1)
    forth = ((row % LANES) * TAPS + row // LANES == col).astype(bf16)
    dims = (5 * LANES + C1, 5 * LANES)
    row = lax.broadcasted_iota(jnp.int32, dims, 0) - C1 + zero
    col = lax.broadcasted_iota(jnp.int32, dims, 1)
    real = (row >= 0) & (row < TAPS * C1)
    row = jnp.maximum(row, 0)
    back = (real & ((row % TAPS) * C1 + row // TAPS == col)).astype(bf16)
    row = lax.broadcasted_iota(jnp.int32, (C4, C4), 0) + zero
    col = lax.broadcasted_iota(jnp.int32, (C4, C4), 1)
    merge = ((row % (C4 // 2)) * 2 + row // (C4 // 2) == col).astype(bf16)
    return forth, back, merge


def grid_marks(side):
    row = np.arange(BOTH)
    image, q = row // ROWS, row % ROWS
    y, x = q // SIDE, q % SIDE
    real = q < SIDE * SIDE
    fixed = np.stack([real & (y > 0), real & (x > 0), real & (y > 0) & (x > 0)], 1).astype(np.float32)
    close = (
        (image[:, None] == image[None])
        & (abs(y[:, None] - y[None]) <= 1)
        & (abs(x[:, None] - x[None]) <= 1)
        & real[:, None]
        & real[None]
    )
    inside = jnp.asarray(real) & (jnp.asarray(y) < side) & (jnp.asarray(x) < side)
    near = jnp.where(jnp.asarray(close) & inside[:, None] & inside[None], 1.0, 0.0)
    cells = jnp.maximum(jnp.sum(near, axis=1), 1.0)
    marks = jnp.concatenate(
        [inside.astype(f32)[:, None], jnp.asarray(fixed), (1.0 / cells)[:, None]], axis=1
    )
    return jnp.pad(marks, ((0, 0), (0, LANES - marks.shape[1]))), near.astype(bf16)


def local_inputs(images, group, early_group, label_col, partner_col, mix_col, valid_col, me):
    side = RES_S // RES_STEP + group
    columns = patches(images, side * RES_STEP, partner_col, mix_col)
    orders = tap_orders(jnp.minimum(early_group, 0))
    marks, near = grid_marks(side)
    other = jnp.where(partner_col == 0, label_col[0], label_col[1])
    whole = jnp.concatenate([label_col, other, jnp.stack([me % 2, me]).astype(jnp.int32)])
    cells = (side * side).astype(f32)
    real = jnp.concatenate([mix_col, valid_col.astype(f32), jnp.stack([cells, cells * C4])])
    return whole, real, columns, orders, marks, near


def second_half(prepared, convs, made, chips, each, ties):
    columns, (forth, back, merge), marks = prepared[2], prepared[3], prepared[4]
    p1, p2, p3e, p3o, k1t, k2, k3e, k3o = convs[:8]
    args = [made[2], columns, p1, p2, p3e, p3o, k1t, k2, k3e, k3o, forth, back, merge, marks]
    return run_backward([prepared[0]] + list(ties) + args + list(made[3:8]), chips, each)


class Ring:
    def __init__(self, count):
        self.count = count
        self.squares = count // 8
        me = lax.axis_index(AXES)
        self.me = me
        self.core = me % 2
        self.low = (me // 2) % 2
        self.high = (me // 4) % 2
        self.corner = (me // 2) % 4
        self.square = me // 8

    def swap(self, value, bits):
        return lax.ppermute(value, AXES, [(i, i ^ bits) for i in range(self.count)])


def pick(value, at, axis):
    return lax.dynamic_index_in_dim(value, at, axis, keepdims=False)


class Scatter:
    def __init__(self, ring, terms, mine, bits):
        self.ring = ring
        self.terms = terms
        self.mine = mine
        self.bits = bits

    def exchange(self):
        sent = functools.reduce(jnp.add, [pick(x, 1 - self.mine, 0) for x in self.terms])
        self.terms = [pick(x, self.mine, 0) for x in self.terms] + [self.ring.swap(sent, self.bits)]

    def add(self):
        self.terms = [functools.reduce(jnp.add, self.terms)]


def sum_squares(ring, value, far_first):
    bits = ring.squares.bit_length() - 1
    order = list(range(bits))
    if far_first:
        order.reverse()
    held = order.copy()
    value = value.reshape((2,) * bits + value.shape[1:])
    got = None
    for bit in order:
        axis = len(held) - 1 - sorted(held).index(bit)
        held.remove(bit)
        mine = (ring.square >> bit) & 1
        if got is not None:
            value = value + got
        got = ring.swap(pick(value, 1 - mine, axis), 8 << bit)
        value = pick(value, mine, axis)
    return value, got


class Gather:
    def __init__(self, ring, value, far_first, high_first):
        self.ring = ring
        self.value = value
        self.masks = []
        bits = list(range(ring.squares.bit_length() - 1))
        self.squares = [8 << bit for bit in (reversed(bits) if far_first else bits)]
        self.corners = (4, 2) if high_first else (2, 4)
        self.pieces = []

    def exchange(self, mask):
        self.value = jnp.stack([self.value, self.ring.swap(self.value, mask)])
        self.masks = [mask] + self.masks

    def between_squares(self):
        for mask in self.squares:
            self.exchange(mask)

    def first_corner(self):
        self.exchange(self.corners[0])

    def second_corner(self):
        got = self.ring.swap(self.value, self.corners[1])
        self.pieces = [(self.value, self.masks, 0), (got, self.masks, self.corners[1])]

    def between_cores(self):
        self.pieces += [(self.ring.swap(array, 1), masks, base | 1) for array, masks, base in self.pieces]


def together(scatters, *others):
    counts = [len(x.terms) for x in scatters]
    values = lax.optimization_barrier(tuple(t for x in scatters for t in x.terms) + tuple(others))
    at = 0
    for x, count in zip(scatters, counts):
        x.terms = list(values[at : at + count])
        at += count
    return values[at:]


class ChipSum:
    def __init__(self, ring, value):
        self.ring = ring
        self.shape = value.shape
        self.terms = [value.reshape(4, value.shape[0] // 4, value.shape[1])]

    def scatter_corners(self):
        ring = self.ring
        got = [ring.swap(pick(self.terms[0], ring.corner ^ j, 0), 2 * j) for j in range(1, 4)]
        self.terms = [functools.reduce(jnp.add, got, pick(self.terms[0], ring.corner, 0))]

    def sum_squares(self):
        ring = self.ring
        got = [ring.swap(self.terms[0], 8 * j) for j in range(1, ring.squares)]
        self.terms = [functools.reduce(jnp.add, got, self.terms[0])]


    def gather_corners(self):
        ring = self.ring
        held = jnp.stack([self.terms[0]] + [ring.swap(self.terms[0], 2 * j) for j in range(1, 4)])
        return jnp.stack([pick(held, ring.corner ^ j, 0) for j in range(4)]).reshape(self.shape)


def per_device(
    devices_count,
    images,
    group_ids,
    labels,
    partners,
    mix_weights,
    valid,
    flat_params,
    flat_first,
    flat_second,
    mlp_weights,
    mlp_momentum,
):
    ring = Ring(devices_count)
    chips = devices_count // 2
    share = mlp_weights.shape[2]
    flat_share = flat_params.shape[0]
    flat_rows = -(-flat_share // LANES)
    spare = flat_rows * LANES - flat_share
    mine = jnp.pad(flat_params, (0, spare)) if spare else flat_params
    sent, flat_low, flat_high = run_pack(
        valid.reshape(MICRO), mlp_weights.transpose(0, 2, 1), mine.reshape(flat_rows, LANES)
    )
    got = lax.all_gather(sent, AXES, axis=0, tiled=False)
    aligned = flat_share % LANES == 0
    pieces = [Gather(ring, flat_low, False, True), Gather(ring, flat_high, True, False)]
    group = early_group = group_ids[0]
    if aligned:
        for x in pieces:
            x.between_squares()
        early_group = run_late(group_ids, pieces[1].value)
        for x in pieces:
            x.first_corner()
        group = run_late(group_ids, pieces[1].value)
    prepared = local_inputs(
        images, group, early_group, labels[:, 0], partners[:, 0], mix_weights[:, 0], valid[:, 0], ring.me
    )
    whole, real, columns, orders, marks, near = prepared
    momentum = mlp_momentum.transpose(0, 2, 1)

    def of_both_cores(mine, theirs):
        at_first = ring.core == 0
        return jnp.concatenate([jnp.where(at_first, mine, theirs), jnp.where(at_first, theirs, mine)])

    momentum_rows = of_both_cores(
        pick(momentum, ring.core, 0), ring.swap(pick(momentum, 1 - ring.core, 0), 1)
    )
    moved = [columns, *orders]
    if aligned:
        for x in pieces:
            x.second_corner()
        for x in pieces:
            x.between_cores()
        convs = run_conv(
            whole, None, [x.pieces for x in pieces], momentum_rows, moved, marks, flat_share, devices_count
        )
        counted = convs[12][0, 0]
    else:
        rows = lax.all_gather(jnp.concatenate([flat_low, flat_high]), AXES, axis=0, tiled=False)
        whole_flat = (
            rows[:, :flat_rows]
            .astype(f32)
            .reshape(devices_count, flat_rows * LANES)[:, :flat_share]
            .reshape(devices_count * flat_share // LANES, LANES)
        )
        convs = run_conv(whole, whole_flat, None, momentum_rows, moved, marks, flat_share, devices_count)
        counted = jnp.sum(rows[:, flat_rows, 0].astype(f32))
    scale = 1.0 / jnp.maximum(counted, 1.0)
    made = run_block(whole, real, got, convs[8:12], marks, near, share)
    keep, send = made[:2]
    got_factors = ring.swap(send, 1)
    ahead = [
        jnp.stack([x[begin : begin + QUARTER + C4] for x in (keep, got_factors)]) for begin in (0, FACTOR_CHANNELS)
    ]
    far_a, far_b = ring.swap(ahead[0], 4), ring.swap(ahead[1], 2)

    each = -(-(devices_count * flat_share) // (devices_count * LANES * 8)) * 8
    ties = ahead
    keep_a, keep_b, send_a, send_b = second_half(prepared, convs, made, chips, each, ties)
    send_a, send_b, keep_one, send_one, keep_two, send_two, loss = run_product(
        whole, [send_a, send_b], keep, got_factors, far_a, far_b, ring.squares, share
    )
    got_one, got_two = ring.swap(send_one, 2), ring.swap(send_two, 4)
    got_a, got_b = ring.swap(send_a, 1), ring.swap(send_b, 1)
    sent_a, left_a, sent_b, left_b = run_halve(whole, keep_one, keep_a, got_a, keep_b, got_b)
    entries = run_sum(whole, sent_a, keep_one, got_one, keep_two, got_two)
    terms = [entries[0]] + [ring.swap(entries[j], 8 * j) for j in range(1, ring.squares)]
    flat = [
        Scatter(ring, [left_a, ring.swap(sent_a, 4)], ring.low, 2),
        Scatter(ring, [left_b, ring.swap(sent_b, 2)], ring.high, 4),
    ]
    ortho, momentum_new, packed = run_gram(scale[None], terms, momentum_rows, loss)
    grams = ChipSum(ring, packed)
    grams.scatter_corners()
    grams.sum_squares()
    for x in flat:
        x.exchange()
        x.add()
    together([grams] + flat)
    flat_sums = [sum_squares(ring, x.terms[0], far) for x, far in zip(flat, (False, True))]
    sum_flat = jnp.concatenate([sum(x) for x in flat_sums])
    steps = 4
    ortho, gram, loss_total = run_newton_first(grams.gather_corners(), ortho, steps)
    lag = (devices_count - 1) * (each * LANES - flat_share)
    hops = -(-lag // (each * LANES))
    tail = min(each, -(-lag // (8 * LANES)) * 8)
    before = [
        lax.ppermute(sum_flat[each - tail :], AXES, [(i, i + h) for i in range(devices_count - h)])
        for h in range(hops, 0, -1)
    ]
    ortho = run_newton_last([x[0] for x in flat_sums], gram, ortho, steps)
    sum_flat = jnp.concatenate(before + [sum_flat])
    start = len(before) * tail * LANES - ring.me * (each * LANES - flat_share)
    if flat_share % LANES == 0:
        sum_flat = lax.dynamic_slice_in_dim(sum_flat, start // LANES, flat_rows, 0).reshape(-1)
    else:
        sum_flat = lax.dynamic_slice_in_dim(sum_flat.reshape(-1), start, flat_share, 0)
    sum_flat = sum_flat * scale
    first_new = 0.9 * flat_first + 0.1 * sum_flat
    second_new = 0.999 * flat_second + 0.001 * sum_flat * sum_flat
    first_hat = first_new / (1.0 - 0.9**STEP)
    second_hat = second_new / (1.0 - 0.999**STEP)
    params_new = flat_params - 0.02 * (
        first_hat / (jnp.sqrt(second_hat) + 1e-08) + 0.05 * flat_params
    )

    def to_owners(by_chip):
        parts = by_chip.reshape(2, share, C4)
        mine, theirs = pick(parts, ring.core, 0), ring.swap(pick(parts, 1 - ring.core, 0), 1)
        at_first = ring.core == 0
        return jnp.stack([jnp.where(at_first, mine, theirs), jnp.where(at_first, theirs, mine)])

    mats = mlp_weights.transpose(0, 2, 1)
    weights_new = mats * (1.0 - 0.1 * 0.05) - 0.1 * 0.2 * math.sqrt(HID) * to_owners(ortho)
    return (
        loss_total[0, 0],
        params_new,
        first_new,
        second_new,
        weights_new.transpose(0, 2, 1),
        to_owners(momentum_new).transpose(0, 2, 1),
    )


def solution(mesh):
    placed = (
        P(None, AXES, None, None, None),
        P(AXES),
        P(None, AXES),
        P(None, AXES),
        P(None, AXES),
        P(None, AXES),
        P(AXES),
        P(AXES),
        P(AXES),
        P(None, None, AXES),
        P(None, None, AXES),
    )
    devices_count = math.prod(mesh.shape[axis] for axis in AXES)
    return jax.shard_map(
        functools.partial(per_device, devices_count),
        mesh=mesh,
        in_specs=placed,
        out_specs=(
            P(),
            P(AXES),
            P(AXES),
            P(AXES),
            P(None, None, AXES),
            P(None, None, AXES),
        ),
        check_vma=False,
    )
```
